32 devices in a mesh: dir: 4 (over z), row: 8 (over y, x, core).
Axes of the slice: x: 2, y: 2, z: 4, core: 2. Of those that a mesh axis runs over, the one named last changes fastest.
Arguments:
- influence: bfloat16 [3, 32, 192, 144], P(None, 'row'), may hold values from -0.5 to 0.5
- foot_rows: int32 [4, 3, 32], P('dir', None, 'row'), may hold values from 0 to 31, as said below
- foot_columns: int32 [4, 3, 160], P('dir'), may hold values from 0 to 191
- actuator_codes: int32 [3, 48, 48], replicated, may hold values from 0 to 8191, as said below
- poke_rows: int32 [2048], replicated, may hold values from 0 to 8191, as said below
- subaperture_valid: int32 [4, 16, 80], P('dir', 'row'), may hold values 0 or 1
Outputs:
- interaction: bfloat16 [6912, 4, 2560], P(('dir', 'row'))
The draws below stay inside these ranges and needn't reach their ends.
Inputs may be any that keep to these rules, and one draw needn't show every extreme that they name: `foot_rows`: for every direction, mirror and pupil row y the surface row lies within 2 rows of y, and in every draw some lie exactly 2 rows above and some exactly 2 rows below their pupil row. `actuator_codes`: all entries are distinct. `poke_rows`: all entries are distinct.
All inputs are finite; a program needn't handle non-finite values. No bound on the sum of `subaperture_valid` on one device may be relied on, other than what follows from the above.
Results may differ from the reference program's by a relative error of at most 0.01.
Values may be sent and summed in bfloat16 or wider, within the bound.
No kernel may reach another device: no remote copies, remote signals or barrier semaphores. Data moves between devices by JAX's collectives and lax.ppermute only.
A program may use at most 64 MiB of HBM per device.

```python
import jax
import jax.numpy as jnp
from jax import lax

NDM = 3
NAR = 48
NA = 48
BAND = 3
NSUBC = 80
NSC = 192
REACH = 2
NCODE = 8192
POKES = 2048
ACTS = 6912
NAS = 144
NPC = 160
NSUB = 16
NSR = 32
NDIR = 4


def draw_foot_rows(key, part):
    offsets = jax.random.randint(jax.random.fold_in(key, 11), (NDIR, NDM, 1), -REACH, REACH + 1)
    offsets = offsets.at[0, 0, 0].set(REACH).at[0, 1, 0].set(-REACH)
    jitter = jax.random.randint(jax.random.fold_in(key, 12), (NDIR, NDM, NSR), -1, 2)
    pupil_rows = jnp.arange(NSR, dtype=jnp.int32)[None, None, :]
    target = jnp.clip(pupil_rows + offsets + jitter, pupil_rows - REACH, pupil_rows + REACH)
    return jnp.clip(target, 0, NSR - 1).astype(jnp.int32)


def draw_foot_columns(key, part):
    margin = (NSC - NPC) // 2
    offsets = jax.random.randint(jax.random.fold_in(key, 21), (NDIR, NDM, 1), -margin, margin + 1)
    jitter = jax.random.randint(jax.random.fold_in(key, 22), (NDIR, NDM, NPC), -1, 2)
    pupil_columns = jnp.arange(NPC, dtype=jnp.int32)[None, None, :]
    return jnp.clip(pupil_columns + margin + offsets + jitter, 0, NSC - 1).astype(jnp.int32)


def draw_actuator_codes(key, part):
    shuffled = jax.random.permutation(jax.random.fold_in(key, 31), NCODE)
    return shuffled[:ACTS].reshape(NDM, NAR, NA).astype(jnp.int32)


def draw_poke_rows(key, part):
    shuffled = jax.random.permutation(jax.random.fold_in(key, 41), NCODE)
    return shuffled[:POKES].astype(jnp.int32)


def plant(array, key, smallest, high):
    index_at = [jax.random.randint(jax.random.fold_in(key, axis), (), 0, length) for axis, length in enumerate(array.shape)]
    widest = array.shape.index(max(array.shape))
    beside = index_at[:widest] + [(index_at[widest] + 1) % array.shape[widest]] + index_at[widest + 1:]
    return array.at[tuple(index_at)].set(smallest).at[tuple(beside)].set(high)


def steps_of(own_key, extent, pieces, low, high):
    def one(position, blocks):
        steps = jax.random.uniform(jax.random.fold_in(jax.random.fold_in(own_key, 6), position), (blocks,), jnp.float32, low / len(pieces), high / len(pieces))
        return jnp.repeat(jnp.exp(steps), extent[position] // blocks).reshape((-1,) + (1,) * (len(extent) - position - 1))

    level = one(*pieces[0])
    for cut in pieces[1:]:
        level = level * one(*cut)
    return level


def noise(stream_key, extent, deviation, reach, cuts=(), kind=jnp.bfloat16):
    factor_of = steps_of(stream_key, extent, cuts, -0.22, 0.18) if cuts else 1.0
    array = jax.random.normal(stream_key, extent, jnp.float32) * deviation * factor_of
    return jnp.minimum(jnp.maximum(array, -reach), reach).astype(kind)


def setup_inputs(seed: int = 0) -> dict:
    streams_of = jax.random.split(jax.random.key(seed), 7)
    influence = noise(streams_of[0], (NDM, NSR, NSC, NAS), NAS ** -0.5, 0.5, ((1, 8),))
    foot_rows = draw_foot_rows(jax.random.fold_in(streams_of[6], 71), 0)
    foot_columns = draw_foot_columns(jax.random.fold_in(streams_of[6], 71), 0)
    actuator_codes = draw_actuator_codes(jax.random.fold_in(streams_of[6], 71), 0)
    poke_rows = draw_poke_rows(jax.random.fold_in(streams_of[6], 71), 0)
    subaperture_valid = plant((jax.random.randint(streams_of[5], (NDIR, NSUB, NSUBC), 0, 5) < 4).astype(jnp.int32), jax.random.fold_in(streams_of[5], 1), 0, 1)
    return {"influence": influence, "foot_rows": foot_rows, "foot_columns": foot_columns, "actuator_codes": actuator_codes, "poke_rows": poke_rows, "subaperture_valid": subaperture_valid}


def parity_sign(code_values, row_values):
    folded = jnp.bitwise_and(code_values, row_values)
    for stride in (16, 8, 4, 2, 1):
        folded = jnp.bitwise_xor(folded, jnp.right_shift(folded, stride))
    return (1 - 2 * jnp.bitwise_and(folded, 1)).astype(jnp.float32)


def direction_slopes(influence, rows_one, columns_one, valid_one, actuator_codes, poke_rows):
    pupil_phase = jnp.zeros((NSR, NPC, POKES), jnp.float32)
    slot_index = jnp.arange(BAND * NA, dtype=jnp.int32)
    for mirror in range(NDM):
        sampled = influence[mirror][rows_one[mirror]][:, columns_one[mirror]].astype(jnp.float32)
        band_start = jnp.clip(rows_one[mirror] * NAR // NSR - 1, 0, NAR - BAND).astype(jnp.int32)
        code_index = band_start[:, None] * NA + slot_index[None, :]
        column_code = actuator_codes[mirror].reshape(-1)[code_index]
        commands = parity_sign(column_code[:, :, None], poke_rows[None, None, :])
        surface = jnp.einsum("yxa,yap->yxp", sampled, commands, precision=lax.Precision.HIGHEST).astype(jnp.bfloat16)
        pupil_phase = pupil_phase + surface.astype(jnp.float32)
    blocks = pupil_phase.reshape(NSUB, 2, NSUBC, 2, POKES)
    slope_across = 0.5 * ((blocks[:, 0, :, 1] - blocks[:, 0, :, 0]) + (blocks[:, 1, :, 1] - blocks[:, 1, :, 0]))
    slope_down = 0.5 * ((blocks[:, 1, :, 0] - blocks[:, 0, :, 0]) + (blocks[:, 1, :, 1] - blocks[:, 0, :, 1]))
    valid_mask = valid_one.astype(jnp.float32)[:, None, :, None]
    slopes = (jnp.stack([slope_across, slope_down], axis=1) * valid_mask).astype(jnp.bfloat16)
    return slopes.reshape(NSUB * 2 * NSUBC, POKES)


def reference(influence, foot_rows, foot_columns, actuator_codes, poke_rows, subaperture_valid):
    sign_table = parity_sign(actuator_codes.reshape(-1)[:, None], poke_rows[None, :])
    norm_factor = POKES ** -0.5

    def one_direction(direction):
        slopes = direction_slopes(influence, foot_rows[direction], foot_columns[direction],
                                  subaperture_valid[direction], actuator_codes, poke_rows)
        decoded = jnp.dot(sign_table, slopes.astype(jnp.float32).T, precision=lax.Precision.HIGHEST)
        return (decoded * norm_factor).astype(jnp.bfloat16)

    per_direction = lax.map(one_direction, jnp.arange(NDIR, dtype=jnp.int32))
    return jnp.transpose(per_direction, (1, 0, 2))
```

```python
import functools
import math

import jax
import jax.numpy as jnp
import numpy as np
from jax import lax
from jax.experimental import pallas as pl
from jax.experimental.pallas import tpu as pltpu
from jax.sharding import PartitionSpec as P

NAR = 48
NA = 48
BAND = 3
LANES = 128
WINDOW = 256
VMEM_BYTES = 56 * 1024 * 1024


def parity(codes, rows):
    return lax.population_count(codes & rows) & 1


def pack_kernel(block_ref, packed_ref):
    mirrors, rows, slots, samples = block_ref.shape
    tail = samples - LANES
    for unit in range(mirrors * rows // 2):
        base = unit * 3 * slots
        tails = []
        for side in range(2):
            k, l = divmod(2 * unit + side, rows)
            packed_ref[pl.ds(base + side * slots, slots), :] = block_ref[k, l, :, :LANES]
            tails.append(block_ref[k, l, :, LANES:])
        packed_ref[pl.ds(base + 2 * slots, slots), :] = jnp.concatenate(tails, axis=1)


def pack(block):
    mirrors, rows, slots, samples = block.shape
    return pl.pallas_call(
        pack_kernel,
        out_shape=jax.ShapeDtypeStruct((mirrors * rows * slots * samples // LANES, LANES), block.dtype),
        in_specs=[pl.BlockSpec(memory_space=pltpu.VMEM)],
        out_specs=pl.BlockSpec(memory_space=pltpu.VMEM),
        compiler_params=pltpu.CompilerParams(vmem_limit_bytes=VMEM_BYTES),
        cost_estimate=pl.CostEstimate(flops=0, bytes_accessed=3 * block.size, transcendentals=0),
        name="pack_influence",
    )(block)


def column_of(row, length):
    return jnp.transpose(jnp.broadcast_to(row, (LANES, length)), (1, 0))


def gram_kernel(own_ref, codes_ref, pokes_ref, gram_ref, poke_columns, own_signs, own_sums):
    pokes = pokes_ref.shape[1]
    own = own_signs.shape[0]

    @pl.when(pl.program_id(0) == 0)
    def _():
        for at in range(0, pokes, LANES):
            poke_columns[pl.ds(at, LANES), :] = column_of(pokes_ref[:, at:at + LANES], LANES)
        own_column = jnp.concatenate(
            [column_of(own_ref[:, at:at + LANES], LANES) for at in range(0, own_ref.shape[1], LANES)], axis=0
        )[:own]
        total = jnp.zeros((own, LANES), jnp.float32)
        for at in range(0, pokes, LANES):
            signs = (1 - 2 * parity(own_column, pokes_ref[:, at:at + LANES])).astype(jnp.float32)
            own_signs[:, at:at + LANES] = signs.astype(jnp.bfloat16)
            total = total + signs
        own_sums[...] = jnp.broadcast_to(jnp.sum(total, axis=1, keepdims=True), own_sums.shape)

    width = codes_ref.shape[1]
    depth = 256
    total = jnp.zeros((own, width), jnp.float32)
    for at in range(0, pokes, depth):
        column = poke_columns[pl.ds(at, depth), :]
        bits = [
            parity(codes_ref[:, lane:lane + LANES], column).astype(jnp.float32).astype(jnp.bfloat16)
            for lane in range(0, width, LANES)
        ]
        total = total + jnp.dot(
            own_signs[:, at:at + depth], jnp.concatenate(bits, axis=1), preferred_element_type=jnp.float32
        )
    sums = jnp.concatenate([own_sums[...]] * (width // LANES), axis=1)
    gram_ref[...] = (sums - 2.0 * total).astype(jnp.bfloat16)


def gram(own_codes, codes, pokes):
    own = own_codes.shape[0]
    padded = -(-own // LANES) * LANES
    own_row = jnp.pad(own_codes, (0, padded - own))[None]
    acts, count = codes.shape[0], pokes.shape[0]
    return pl.pallas_call(
        gram_kernel,
        grid=(acts // WINDOW,),
        out_shape=jax.ShapeDtypeStruct((own, acts), jnp.bfloat16),
        in_specs=[
            pl.BlockSpec((1, padded), lambda s: (0, 0)),
            pl.BlockSpec((1, WINDOW), lambda s: (0, s)),
            pl.BlockSpec((1, count), lambda s: (0, 0)),
        ],
        out_specs=pl.BlockSpec((own, WINDOW), lambda s: (0, s)),
        scratch_shapes=[
            pltpu.VMEM((count, LANES), jnp.int32),
            pltpu.VMEM((own, count), jnp.bfloat16),
            pltpu.VMEM((own, LANES), jnp.float32),
        ],
        compiler_params=pltpu.CompilerParams(vmem_limit_bytes=VMEM_BYTES),
        cost_estimate=pl.CostEstimate(
            flops=2 * own * acts * count, bytes_accessed=2 * own * acts, transcendentals=0
        ),
        name="gram_rows",
    )(own_row, codes[None], pokes[None])


def decode_kernel(
    shard_rows, surface_rows, samples, phases, foot_ref, gram_ref, block_ref, columns_ref, signs_ref, scale_ref,
    out_ref, window, decoded, differences, total
):
    step = pl.program_id(0)
    blocks = surface_rows // shard_rows
    mirrors = decoded.shape[0]
    own = gram_ref.shape[0]
    directions = scale_ref.shape[0]
    slots = BAND * NA
    tail = samples - LANES
    slope_lanes = columns_ref.shape[-1]

    @pl.when(step == 0)
    def _():
        window[...] = jnp.zeros_like(window)

        def build(index, _):
            phase = lax.rem(index, phases)
            for k in range(mirrors):
                first = columns_ref[index, 2 * k:2 * k + 1, :]
                second = columns_ref[index, 2 * k + 1:2 * k + 2, :]
                for y in range(2):
                    plus = signs_ref[phase, 2 * y:2 * y + 1, :]
                    minus = signs_ref[phase, 2 * y + 1:2 * y + 2, :]

                    def piece(start, length):
                        x = start + lax.broadcasted_iota(jnp.int32, (length, slope_lanes), 0)
                        return (
                            jnp.where(x == second, plus, 0.0) + jnp.where(x == first, minus, 0.0)
                        ).astype(jnp.bfloat16)

                    differences[index, pl.ds((2 * k + y) * LANES, LANES), :] = piece(0, LANES)
                    differences[index, pl.ds(2 * mirrors * LANES + k * LANES + y * tail, tail), :] = piece(LANES, tail)
            return 0

        lax.fori_loop(0, directions * phases, build, 0)

    @pl.when(step < blocks)
    def _():
        lane = lax.broadcasted_iota(jnp.int32, (own, LANES), 1)
        for q in range(mirrors * shard_rows):
            k, l = divmod(q, shard_rows)
            r = step * shard_rows + l
            band = jnp.clip(r * NAR // surface_rows - 1, 0, NAR - BAND)
            column = (k * NAR + band) * NA
            base = pl.multiple_of(column // LANES * LANES, LANES)
            shift = pl.multiple_of(column - base, 16)
            unit, side = divmod(q, 2)
            slot = q % window.shape[0]
            window[slot] = jnp.zeros(window.shape[1:], window.dtype)
            at = unit * 3 * slots
            window[slot, pl.ds(shift, slots), :LANES] = block_ref[0, pl.ds(at + side * slots, slots), :]
            window[slot, pl.ds(shift, slots), LANES:] = block_ref[0, pl.ds(at + 2 * slots, slots), :]
            u = jnp.dot(gram_ref[:, pl.ds(base, WINDOW)], window[slot], preferred_element_type=jnp.float32)
            decoded[k, r, :, :LANES] = u[:, :LANES].astype(jnp.bfloat16)
            rest = u[:, LANES:]
            turned = pltpu.roll(rest, LANES // 2, 1)
            low, high = (rest, turned) if side == 0 else (turned, rest)
            decoded[k, r, :, LANES:] = jnp.where(lane < tail, low, high).astype(jnp.bfloat16)

    @pl.when(step >= blocks)
    def _():
        group = step - blocks
        lane = lax.broadcasted_iota(jnp.int32, (own, LANES), 1)

        def one(d, _):
            pieces = []
            for phase in range(phases):
                i = group * phases + phase
                heads, tails = [], []
                for k in range(mirrors):
                    rows = [foot_ref[(d * mirrors + k) * surface_rows + 2 * i + y] for y in range(2)]
                    heads += [decoded[k, row, :, :LANES] for row in rows]
                    tails.append(
                        jnp.where(lane < tail, decoded[k, rows[0], :, LANES:], decoded[k, rows[1], :, LANES:])
                    )
                pieces.append(
                    jnp.dot(
                        jnp.concatenate(heads + tails, axis=1),
                        differences[d * phases + phase],
                        preferred_element_type=jnp.float32,
                    )
                )
            tiles = out_ref.shape[2] // LANES
            for tile in range(tiles):
                value = None
                for phase in range(phases):
                    start = phase * out_ref.shape[2] // phases // LANES
                    if start <= tile < start + slope_lanes // LANES:
                        part = pieces[phase][:, (tile - start) * LANES:(tile - start + 1) * LANES]
                        value = part if value is None else value + part
                value = value * scale_ref[d, :, tile * LANES:(tile + 1) * LANES]
                total[tile, pl.ds(d, own, stride=directions), :] = value
            return 0

        lax.fori_loop(0, directions, one, 0)
        for tile in range(out_ref.shape[2] // LANES):
            value = total[tile].reshape(own, directions, LANES)
            out_ref[:, :, tile * LANES:(tile + 1) * LANES] = value.astype(out_ref.dtype)


def decode(foot_rows, gram_rows, blocks, columns, signs, scale, shard_rows, samples, phases):
    directions, mirrors, surface_rows = foot_rows.shape
    own, acts = gram_rows.shape
    count = blocks.shape[0]
    width = scale.shape[1]
    groups = width // (scale.shape[1] // (surface_rows // 2) * phases)
    lanes = width // groups
    flops = 2 * own * WINDOW * WINDOW * mirrors * surface_rows + 2 * own * mirrors * 3 * LANES * WINDOW * directions * surface_rows // 2
    return pl.pallas_call(
        functools.partial(decode_kernel, shard_rows, surface_rows, samples, phases),
        grid=(count + groups,),
        out_shape=jax.ShapeDtypeStruct((own, directions, width), jnp.bfloat16),
        in_specs=[
            pl.BlockSpec(memory_space=pltpu.SMEM),
            pl.BlockSpec(memory_space=pltpu.VMEM),
            pl.BlockSpec((1,) + blocks.shape[1:], lambda s: (jnp.minimum(s, count - 1), 0, 0)),
            pl.BlockSpec(memory_space=pltpu.VMEM),
            pl.BlockSpec(memory_space=pltpu.VMEM),
            pl.BlockSpec((directions, 1, lanes), lambda s: (0, 0, jnp.maximum(s - count, 0))),
        ],
        out_specs=pl.BlockSpec((own, directions, lanes), lambda s: (0, 0, jnp.maximum(s - count, 0))),
        scratch_shapes=[
            pltpu.VMEM((4, WINDOW, WINDOW), jnp.bfloat16),
            pltpu.VMEM((mirrors, surface_rows, own, WINDOW), jnp.bfloat16),
            pltpu.VMEM((directions * phases, 3 * mirrors * LANES, columns.shape[-1]), jnp.bfloat16),
            pltpu.VMEM((lanes // LANES, own * directions, LANES), jnp.float32),
        ],
        compiler_params=pltpu.CompilerParams(vmem_limit_bytes=VMEM_BYTES),
        cost_estimate=pl.CostEstimate(flops=flops, bytes_accessed=2 * own * directions * width, transcendentals=0),
        name="decode",
    )(foot_rows.reshape(-1), gram_rows, blocks, columns, signs, scale[:, None])


def placed_columns(foot_columns, phases):
    directions, mirrors, pupil = foot_columns.shape
    pairs = foot_columns.reshape(directions, mirrors, pupil // 2, 2).transpose(0, 1, 3, 2)
    both = jnp.concatenate([pairs, pairs], axis=-1)
    placed = []
    for phase in range(phases):
        start = phase * pupil % LANES
        placed.append(
            jnp.pad(both, ((0, 0),) * 3 + ((start, WINDOW - pupil - start),), constant_values=-1)
        )
    return jnp.stack(placed, axis=1).reshape(directions * phases, mirrors * 2, WINDOW)


def placed_signs(pupil, phases):
    signs = np.zeros((phases, 4, WINDOW), np.float32)
    for phase in range(phases):
        start = phase * pupil % LANES
        middle, end = start + pupil // 2, start + pupil
        signs[phase, :, start:middle] = np.array([1, -1, 1, -1])[:, None]
        signs[phase, :, middle:end] = np.array([-1, -1, 1, 1])[:, None]
    return jnp.asarray(signs)


def gather_small(foot_rows, foot_columns, valid):
    directions, devices = lax.axis_size("dir"), lax.axis_size("row")
    own = [foot_rows[0], foot_columns[0], valid[0]]
    flat = jnp.concatenate([piece.reshape(-1) for piece in own])
    every = lax.all_gather(flat, ("dir", "row")).reshape(directions, devices, -1)
    cuts = np.cumsum([piece.size for piece in own])
    rows = every[:, :, :cuts[0]].reshape((directions, devices) + own[0].shape)
    rows = rows.transpose(0, 2, 1, 3).reshape(directions, own[0].shape[0], -1)
    columns = every[:, 0, cuts[0]:cuts[1]].reshape((directions,) + own[1].shape)
    return rows, columns, every[:, :, cuts[1]:].reshape(directions, -1, own[2].shape[1])


def shards(influence, foot_rows, foot_columns, actuator_codes, poke_rows, subaperture_valid):
    mirrors, shard_rows, samples, slots = influence.shape
    pupil = foot_columns.shape[2]
    packed = pack(jnp.swapaxes(influence, 2, 3))
    blocks = lax.all_gather(packed, "row")
    rows, columns, valid = gather_small(foot_rows, foot_columns, subaperture_valid)
    codes = actuator_codes.reshape(-1)
    own = codes.shape[0] // (lax.axis_size("dir") * lax.axis_size("row"))
    device = lax.axis_index("dir") * lax.axis_size("row") + lax.axis_index("row")
    gram_rows = gram(lax.dynamic_slice_in_dim(codes, device * own, own), codes, poke_rows)
    phases = LANES // math.gcd(pupil, LANES)
    norm_factor = 0.5 * poke_rows.shape[0] ** (-0.5)
    scale = valid.astype(jnp.float32) * norm_factor
    scale = jnp.broadcast_to(scale[:, :, None], scale.shape[:2] + (2, scale.shape[2])).reshape(scale.shape[0], -1)
    return decode(
        rows, gram_rows, blocks, placed_columns(columns, phases), placed_signs(pupil, phases), scale,
        shard_rows, samples, phases,
    )


def solution(mesh):
    return jax.shard_map(
        shards,
        mesh=mesh,
        in_specs=(
            P(None, "row", None, None),
            P("dir", None, "row"),
            P("dir", None, None),
            P(),
            P(),
            P("dir", "row", None),
        ),
        out_specs=P(("dir", "row"), None, None),
        check_vma=False,
    )
```

```python
import functools
import math

import jax
import jax.numpy as jnp
import numpy as np
from jax import lax
from jax.experimental import pallas as pl
from jax.experimental.pallas import tpu as pltpu
from jax.sharding import PartitionSpec as P

NAR = 48
NA = 48
BAND = 3
LANES = 128
WINDOW = 256
VMEM_BYTES = 56 * 1024 * 1024


def parity(codes, rows):
    return lax.population_count(codes & rows) & 1


def pack_kernel(block_ref, packed_ref):
    mirrors, rows, slots, samples = block_ref.shape
    for unit in range(mirrors * rows // 2):
        base = unit * 3 * slots
        tails = []
        for side in range(2):
            k, l = divmod(2 * unit + side, rows)
            packed_ref[pl.ds(base + side * slots, slots), :] = block_ref[k, l, :, :LANES]
            tails.append(block_ref[k, l, :, LANES:])
        packed_ref[pl.ds(base + 2 * slots, slots), :] = jnp.concatenate(tails, axis=1)


def pack(block):
    mirrors, rows, slots, samples = block.shape
    return pl.pallas_call(
        pack_kernel,
        out_shape=jax.ShapeDtypeStruct((mirrors * rows * slots * samples // LANES, LANES), block.dtype),
        in_specs=[pl.BlockSpec(memory_space=pltpu.VMEM)],
        out_specs=pl.BlockSpec(memory_space=pltpu.VMEM),
        compiler_params=pltpu.CompilerParams(vmem_limit_bytes=VMEM_BYTES),
        cost_estimate=pl.CostEstimate(flops=0, bytes_accessed=3 * block.size, transcendentals=0),
        name="pack_influence",
    )(block)


def column_of(row, length):
    return jnp.transpose(jnp.broadcast_to(row, (LANES, length)), (1, 0))


def gram_kernel(own_ref, codes_ref, pokes_ref, gram_ref, poke_columns, own_signs, own_sums):
    pokes = pokes_ref.shape[1]
    own = own_signs.shape[0]

    @pl.when(pl.program_id(0) == 0)
    def _():
        for at in range(0, pokes, LANES):
            poke_columns[pl.ds(at, LANES), :] = column_of(pokes_ref[:, at:at + LANES], LANES)
        own_column = jnp.concatenate(
            [column_of(own_ref[:, at:at + LANES], LANES) for at in range(0, own_ref.shape[1], LANES)], axis=0
        )[:own]
        total = jnp.zeros((own, LANES), jnp.float32)
        for at in range(0, pokes, LANES):
            signs = (1 - 2 * parity(own_column, pokes_ref[:, at:at + LANES])).astype(jnp.float32)
            own_signs[:, at:at + LANES] = signs.astype(jnp.bfloat16)
            total = total + signs
        own_sums[...] = jnp.broadcast_to(jnp.sum(total, axis=1, keepdims=True), own_sums.shape)

    width = codes_ref.shape[1]
    depth = 256
    total = jnp.zeros((own, width), jnp.float32)
    for at in range(0, pokes, depth):
        column = poke_columns[pl.ds(at, depth), :]
        bits = [
            parity(codes_ref[:, lane:lane + LANES], column).astype(jnp.float32).astype(jnp.bfloat16)
            for lane in range(0, width, LANES)
        ]
        total = total + jnp.dot(
            own_signs[:, at:at + depth], jnp.concatenate(bits, axis=1), preferred_element_type=jnp.float32
        )
    sums = jnp.concatenate([own_sums[...]] * (width // LANES), axis=1)
    gram_ref[...] = (sums - 2.0 * total).astype(jnp.bfloat16)


def gram(own_codes, codes, pokes):
    padded = -(-own_codes.shape[0] // LANES) * LANES
    own_row = jnp.pad(own_codes, (0, padded - own_codes.shape[0]))[None]
    own = -(-own_codes.shape[0] // 16) * 16
    acts, count = codes.shape[0], pokes.shape[0]
    return pl.pallas_call(
        gram_kernel,
        grid=(acts // WINDOW,),
        out_shape=jax.ShapeDtypeStruct((own, acts), jnp.bfloat16),
        in_specs=[
            pl.BlockSpec((1, padded), lambda s: (0, 0)),
            pl.BlockSpec((1, WINDOW), lambda s: (0, s)),
            pl.BlockSpec((1, count), lambda s: (0, 0)),
        ],
        out_specs=pl.BlockSpec((own, WINDOW), lambda s: (0, s)),
        scratch_shapes=[
            pltpu.VMEM((count, LANES), jnp.int32),
            pltpu.VMEM((own, count), jnp.bfloat16),
            pltpu.VMEM((own, LANES), jnp.float32),
        ],
        compiler_params=pltpu.CompilerParams(vmem_limit_bytes=VMEM_BYTES),
        cost_estimate=pl.CostEstimate(
            flops=2 * own * acts * count, bytes_accessed=2 * own * acts, transcendentals=0
        ),
        name="gram_rows",
    )(own_row, codes[None], pokes[None])


def band_product(block_parts, q, row_shape, block, surface_rows, gram_ref, window_ref):
    mirrors, shard_rows, slots, samples = row_shape
    k, l = divmod(q, shard_rows)
    band = jnp.clip((block * shard_rows + l) * NAR // surface_rows - 1, 0, NAR - BAND)
    column = (k * NAR + band) * NA
    base = pl.multiple_of(column // LANES * LANES, LANES)
    shift = pl.multiple_of(column - base, 16)
    unit, side = divmod(q, 2)
    units = mirrors * shard_rows // 2 // len(block_parts)
    part, at = block_parts[unit // units], unit % units * 3 * slots
    window_ref[...] = jnp.zeros(window_ref.shape, window_ref.dtype)
    window_ref[pl.ds(shift, slots), :LANES] = part[pl.ds(at + side * slots, slots), :]
    window_ref[pl.ds(shift, slots), LANES:] = part[pl.ds(at + 2 * slots, slots), :]
    u = jnp.dot(gram_ref[:, pl.ds(base, WINDOW)], window_ref[...], preferred_element_type=jnp.float32)
    rest = u[:, LANES:]
    turned = pltpu.roll(rest, LANES // 2, 1)
    low, high = (rest, turned) if side == 0 else (turned, rest)
    lane = lax.broadcasted_iota(jnp.int32, rest.shape, 1)
    rest = jnp.where(lane < samples - LANES, low, high)
    return u[:, :LANES].astype(jnp.bfloat16), rest.astype(jnp.bfloat16)


def bands_kernel(row_shape, surface_rows, first, counts, own_ref, gram_ref, *refs):
    sources = refs[:len(counts)]
    out_ref, window = refs[-2:]
    step = pl.program_id(0)
    start = 0
    for source, count in zip(sources, counts):
        @pl.when((step >= start) & (step < start + count))
        def _():
            block = (first + step) ^ own_ref[0]
            for q in range(row_shape[0] * row_shape[1]):
                head, rest = band_product(
                    [source.at[0]], q, row_shape, block, surface_rows, gram_ref, window.at[q % window.shape[0]]
                )
                out_ref[0, q, :, :LANES] = head
                out_ref[0, q, :, LANES:] = rest
        start += count


def bands(gram_rows, sources, decoded, first, place, row_shape, surface_rows):
    own = gram_rows.shape[0]
    counts = [source.shape[0] for source in sources]
    starts = np.cumsum([0] + counts)
    total = surface_rows // row_shape[1]
    rows = row_shape[0] * row_shape[1]
    specs = [
        pl.BlockSpec(
            (1,) + source.shape[1:],
            functools.partial(lambda low, high, s: (jnp.clip(s - low, 0, high - 1), 0, 0), int(starts[n]), counts[n]),
        )
        for n, source in enumerate(sources)
    ]
    arguments = [place, gram_rows, *sources]
    in_specs = [pl.BlockSpec(memory_space=pltpu.SMEM), pl.BlockSpec(memory_space=pltpu.VMEM), *specs]
    aliases = {}
    body = functools.partial(bands_kernel, row_shape, surface_rows, first, counts)
    if decoded is not None:
        aliases = {len(arguments): 0}
        arguments.append(decoded)
        in_specs.append(pl.BlockSpec(memory_space=pl.ANY))
    flops = 2 * own * WINDOW * WINDOW * rows * sum(counts)
    return pl.pallas_call(
        body,
        grid=(sum(counts),),
        out_shape=jax.ShapeDtypeStruct((total, rows, own, WINDOW), jnp.bfloat16),
        in_specs=in_specs,
        out_specs=pl.BlockSpec((1, rows, own, WINDOW), lambda s: (first + s, 0, 0, 0)),
        scratch_shapes=[pltpu.VMEM((4, WINDOW, WINDOW), jnp.bfloat16)],
        input_output_aliases=aliases,
        compiler_params=pltpu.CompilerParams(vmem_limit_bytes=VMEM_BYTES),
        cost_estimate=pl.CostEstimate(
            flops=flops, bytes_accessed=2 * own * WINDOW * rows * sum(counts), transcendentals=0
        ),
        name="bands",
    )(*arguments)


def build_differences(columns_ref, signs_ref, differences, mirrors, samples):
    lanes = columns_ref.shape[-1]
    tail = samples - LANES

    def build(d, _):
        for k in range(mirrors):
            first = columns_ref[d, 2 * k:2 * k + 1, :]
            second = columns_ref[d, 2 * k + 1:2 * k + 2, :]
            for y in range(2):
                plus = signs_ref[2 * y:2 * y + 1, :]
                minus = signs_ref[2 * y + 1:2 * y + 2, :]

                def piece(start, length):
                    x = start + lax.broadcasted_iota(jnp.int32, (length, lanes), 0)
                    value = jnp.where(x == second, plus, 0.0) + jnp.where(x == first, minus, 0.0)
                    return value.astype(jnp.bfloat16)

                differences[d, pl.ds((2 * k + y) * LANES, LANES), :] = piece(0, LANES)
                differences[d, pl.ds(2 * mirrors * LANES + k * LANES + y * tail, tail), :] = piece(LANES, tail)
        return 0

    lax.fori_loop(0, differences.shape[0], build, 0)


def decode_kernel(
    row_shape, surface_rows, own, late, place_ref, foot_ref, columns_ref, signs_ref, scale_ref, *refs
):
    mirrors, shard_rows, slots, samples = row_shape
    extras = refs[:late[1] * late[2]]
    gram_ref, decoded_ref, out_ref, decoded, differences, total, window, semaphores = refs[late[1] * late[2]:]
    group = pl.program_id(0)
    directions = differences.shape[0]
    pupil = columns_ref.shape[2]
    phases = out_ref.shape[2] // pupil
    tail = samples - LANES
    ready = late[0]

    @pl.when(group == 0)
    def _():
        copies = [
            pltpu.make_async_copy(decoded_ref.at[block], decoded.at[block], semaphores.at[block])
            for block in range(ready)
        ]
        for copy in copies:
            copy.start()
        build_differences(columns_ref, signs_ref, differences, mirrors, samples)
        for n in range(late[1]):
            block = (ready + n) ^ place_ref[0]
            parts = [extras[n * late[2] + part] for part in range(late[2])]
            for q in range(mirrors * shard_rows):
                head, rest = band_product(
                    parts, q, row_shape, block, surface_rows, gram_ref, window.at[q % window.shape[0]]
                )
                decoded[ready + n, q, :, :LANES] = head
                decoded[ready + n, q, :, LANES:] = rest
        for copy in copies:
            copy.wait()

    lane = lax.broadcasted_iota(jnp.int32, (decoded.shape[2], LANES), 1)

    def one(d, _):
        place = d ^ place_ref[1]
        left = []
        for phase in range(phases):
            i = group * phases + phase
            block = (2 * i // shard_rows) ^ place_ref[0]
            heads, tails = [], []
            for k in range(mirrors):
                picked = []
                for y in range(2):
                    row = foot_ref[((block * directions + place) * mirrors + k) * shard_rows + (2 * i + y) % shard_rows]
                    picked.append(
                        (row // shard_rows ^ place_ref[0], k * shard_rows + row % shard_rows)
                    )
                heads += [decoded[e, q, :, :LANES] for e, q in picked]
                tails.append(
                    jnp.where(lane < tail, *(decoded[e, q, :, LANES:] for e, q in picked))
                )
            left.append(jnp.concatenate(heads + tails, axis=1))
        rows = left[0].shape[0]
        product = jnp.dot(
            jnp.concatenate(left, axis=0), differences[place], preferred_element_type=jnp.float32
        )
        pieces = []
        for phase in range(phases):
            i = group * phases + phase
            block = (2 * i // shard_rows) ^ place_ref[0]
            factor = scale_ref[block, place, pl.ds(i % (shard_rows // 2), 1), :]
            pieces.append(product[phase * rows:phase * rows + own] * factor)
        value = jnp.concatenate(pieces, axis=1)
        for tile in range(out_ref.shape[2] // LANES):
            total[tile, pl.ds(d, own, stride=directions), :] = value[:, tile * LANES:(tile + 1) * LANES]
        return 0

    lax.fori_loop(0, directions, one, 0)
    for tile in range(out_ref.shape[2] // LANES):
        value = total[tile].reshape(own, directions, LANES)
        out_ref[:, :, tile * LANES:(tile + 1) * LANES] = value.astype(out_ref.dtype)


def decode(place, foot_rows, columns, scale, gram_rows, decoded, extras, parts, own, row_shape, surface_rows):
    directions, mirrors = columns.shape[0], row_shape[0]
    pupil = columns.shape[-1]
    padded = gram_rows.shape[0]
    phases = LANES // math.gcd(pupil, LANES)
    width = surface_rows // 2 * pupil
    lanes = phases * pupil
    signs = np.ones((4, pupil), np.float32)
    signs[1, :pupil // 2] = signs[3, :pupil // 2] = signs[0, pupil // 2:] = signs[1, pupil // 2:] = -1
    late = len(extras) // parts
    ready = decoded.shape[0] - late
    flops = 2 * padded * 3 * mirrors * LANES * pupil * directions * surface_rows // 2
    vmem = pl.BlockSpec(memory_space=pltpu.VMEM)
    smem = pl.BlockSpec(memory_space=pltpu.SMEM)
    return pl.pallas_call(
        functools.partial(decode_kernel, row_shape, surface_rows, own, (ready, late, parts)),
        grid=(width // lanes,),
        out_shape=jax.ShapeDtypeStruct((own, directions, width), jnp.bfloat16),
        in_specs=[smem, smem, vmem, vmem, vmem] + [vmem] * len(extras) + [vmem, pl.BlockSpec(memory_space=pl.ANY)],
        out_specs=pl.BlockSpec((own, directions, lanes), lambda s: (0, 0, s)),
        scratch_shapes=[
            pltpu.VMEM(decoded.shape, jnp.bfloat16),
            pltpu.VMEM((directions, 3 * mirrors * LANES, pupil), jnp.bfloat16),
            pltpu.VMEM((lanes // LANES, own * directions, LANES), jnp.float32),
            pltpu.VMEM((4, WINDOW, WINDOW), jnp.bfloat16),
            pltpu.SemaphoreType.DMA((decoded.shape[0],)),
        ],
        compiler_params=pltpu.CompilerParams(vmem_limit_bytes=VMEM_BYTES),
        cost_estimate=pl.CostEstimate(flops=flops, bytes_accessed=2 * own * directions * width, transcendentals=0),
        name="decode",
    )(place, foot_rows.reshape(-1), columns, jnp.asarray(signs), scale, *extras, gram_rows, decoded)


def swap(block, axis, distance):
    return lax.ppermute(block, axis, [(i, i ^ distance) for i in range(lax.axis_size(axis))])


def small_arrays(foot_rows, foot_columns, valid, staged):
    mirrors, shard_rows = foot_rows.shape[1:]
    pupil = foot_columns.shape[2]
    pairs = foot_columns[0].reshape(mirrors, pupil // 2, 2).transpose(0, 2, 1).reshape(2 * mirrors, pupil // 2)
    lines = jnp.concatenate([pairs, valid[0]], axis=0)
    lines = jnp.concatenate([lines, lines], axis=1)
    row_line = jnp.pad(foot_rows[0].reshape(1, -1), ((0, 0), (0, pupil - mirrors * shard_rows)))
    lines = jnp.concatenate([lines, row_line], axis=0)
    if staged:
        directions = lax.axis_size("dir")
        every = jnp.stack([lines] + [swap(lines, "dir", e) for e in range(1, directions)])
        columns, rest = every[:, :2 * mirrors], every[None, :, 2 * mirrors:]
        distance = 1
        while distance < lax.axis_size("row"):
            rest = jnp.concatenate([rest, swap(rest, "row", distance)], axis=0)
            distance *= 2
    else:
        every = lax.all_gather(lax.all_gather(lines, "dir"), "row")
        columns, rest = every[0, :, :2 * mirrors], every[:, :, 2 * mirrors:]
    return rest[:, :, -1, :mirrors * shard_rows], columns, rest[:, :, :-1]


def shards(influence, foot_rows, foot_columns, actuator_codes, poke_rows, subaperture_valid):
    mirrors, shard_rows, samples, slots = influence.shape
    row_shape = (mirrors, shard_rows, slots, samples)
    directions, devices = lax.axis_size("dir"), lax.axis_size("row")
    surface_rows = shard_rows * devices
    staged = devices == 8 and directions & (directions - 1) == 0
    packed = pack(jnp.swapaxes(influence, 2, 3))
    if staged:
        half = packed.shape[0] // 2
        beside, across, sibling = swap(packed, "row", 2), swap(packed, "row", 4), swap(packed, "row", 1)
        upper, lower = swap(beside[:half], "row", 4), swap(across[half:], "row", 2)
        beside_sibling, across_sibling = swap(beside, "row", 1), swap(across, "row", 1)
        late = [upper, lower, swap(upper, "row", 1), swap(lower, "row", 1)]
        early = [[packed, sibling], [beside, beside_sibling, across, across_sibling]]
        place = jnp.stack([lax.axis_index("row"), lax.axis_index("dir")]).astype(jnp.int32)
    else:
        early, late = [[lax.all_gather(packed, "row")]], []
        place = jnp.zeros((2,), jnp.int32)
    rows, columns, valid = small_arrays(foot_rows, foot_columns, subaperture_valid, staged)
    codes = actuator_codes.reshape(-1)
    own = codes.shape[0] // (directions * devices)
    device = lax.axis_index("dir") * devices + lax.axis_index("row")
    gram_rows = gram(lax.dynamic_slice_in_dim(codes, device * own, own), codes, poke_rows)
    scale = valid.astype(jnp.float32) * (0.5 * poke_rows.shape[0] ** (-0.5))
    decoded, first = None, 0
    for sources in early:
        sources = [source if source.ndim == 3 else source[None] for source in sources]
        decoded = bands(gram_rows, sources, decoded, first, place, row_shape, surface_rows)
        first += sum(source.shape[0] for source in sources)
    return decode(place, rows, columns, scale, gram_rows, decoded, late, 2, own, row_shape, surface_rows)


def solution(mesh):
    return jax.shard_map(
        shards,
        mesh=mesh,
        in_specs=(
            P(None, "row", None, None),
            P("dir", None, "row"),
            P("dir", None, None),
            P(),
            P(),
            P("dir", "row", None),
        ),
        out_specs=P(("dir", "row"), None, None),
        check_vma=False,
    )
```

```python
import functools
import math

import jax
import jax.numpy as jnp
import numpy as np
from jax import lax
from jax.experimental import pallas as pl
from jax.experimental.pallas import tpu as pltpu
from jax.sharding import PartitionSpec as P

NAR = 48
NA = 48
BAND = 3
BITS = 13
LANES = 128
WINDOW = 256
VMEM_BYTES = 56 * 1024 * 1024


def parity(codes, rows):
    return lax.population_count(codes & rows) & 1


def pack_kernel(block_ref, rows_ref, columns_ref, valid_ref, packed_ref, lines_ref):
    mirrors, rows, slots, samples = block_ref.shape
    lines_ref[...] = jnp.zeros(lines_ref.shape, lines_ref.dtype)
    lines_ref[:mirrors, :columns_ref.shape[2]] = columns_ref[0]
    lines_ref[mirrors:mirrors + valid_ref.shape[1], :valid_ref.shape[2]] = valid_ref[0]
    lines_ref[mirrors + valid_ref.shape[1]:, :rows] = rows_ref[0]
    for unit in range(mirrors * rows // 2):
        base = unit * 3 * slots
        tails = []
        for side in range(2):
            k, l = divmod(2 * unit + side, rows)
            packed_ref[pl.ds(base + side * slots, slots), :] = block_ref[k, l, :, :LANES]
            tails.append(block_ref[k, l, :, LANES:])
        packed_ref[pl.ds(base + 2 * slots, slots), :] = jnp.concatenate(tails, axis=1)


def pack(block, foot_rows, foot_columns, valid):
    mirrors, rows, slots, samples = block.shape
    vmem = pl.BlockSpec(memory_space=pltpu.VMEM)
    return pl.pallas_call(
        pack_kernel,
        out_shape=[
            jax.ShapeDtypeStruct((mirrors * rows * slots * samples // LANES, LANES), block.dtype),
            jax.ShapeDtypeStruct((2 * mirrors + rows // 2, WINDOW), jnp.int32),
        ],
        in_specs=[vmem] * 4,
        out_specs=[vmem] * 2,
        compiler_params=pltpu.CompilerParams(vmem_limit_bytes=VMEM_BYTES),
        cost_estimate=pl.CostEstimate(flops=0, bytes_accessed=3 * block.size, transcendentals=0),
        name="pack_influence",
    )(block, foot_rows, foot_columns, valid)


def column_of(row):
    return jnp.transpose(jnp.broadcast_to(row, (LANES, LANES)), (1, 0))


def gram_kernel(codes_ref, pokes_ref, gram_ref, words, own_signs, own_sums):
    planes = pokes_ref.shape[0]
    half = LANES // 2
    own = own_signs.shape[0]
    chunks = gram_ref.shape[1] // WINDOW

    @pl.when(pl.program_id(0) == 0)
    def _():
        plane = lax.broadcasted_iota(jnp.int32, pokes_ref.shape, 0)
        for bit in range(BITS):
            low = jnp.sum((pokes_ref[...] >> bit & 1) << plane, axis=0, keepdims=True)
            word = low | pltpu.roll(jnp.broadcast_to(low, (8, LANES)), half, 1)[:1] << planes
            words[bit] = column_of(word)[:half]
        count = codes_ref.shape[0] * LANES // (lax.axis_size("dir") * lax.axis_size("row"))
        first = (lax.axis_index("dir") * lax.axis_size("row") + lax.axis_index("row")) * count
        lane = lax.broadcasted_iota(jnp.int32, (8, LANES), 1)
        shift = first % LANES
        lines = [
            pltpu.roll(
                jnp.broadcast_to(
                    codes_ref[pl.ds(jnp.minimum(first // LANES + n, codes_ref.shape[0] - 1), 1), :], (8, LANES)
                ),
                LANES - shift, 1,
            )
            for n in range(-(-own // LANES) + 1)
        ]
        own_column = jnp.concatenate(
            [
                column_of(jnp.where(lane < LANES - shift, lines[n], lines[n + 1])[:1])
                for n in range(len(lines) - 1)
            ],
            axis=0,
        )[:own]
        lane = lax.broadcasted_iota(jnp.int32, (1, LANES), 1)
        total = jnp.zeros((own, LANES), jnp.float32)
        for at in range(planes):
            signs = (1 - 2 * parity(own_column, pokes_ref[at:at + 1, :])).astype(jnp.float32)
            upper = -(2.0 ** -(at + planes)) if at + planes == 31 else 2.0 ** -(at + planes)
            own_signs[:, at * LANES:(at + 1) * LANES] = (
                signs * jnp.where(lane < half, 2.0 ** -at, upper)
            ).astype(jnp.bfloat16)
            total = total + signs
        own_sums[...] = jnp.broadcast_to(jnp.sum(total, axis=1, keepdims=True), own_sums.shape)

    def chunk(index, _):
        word = []
        for side in range(WINDOW // LANES):
            line = (pl.program_id(0) * chunks + index) * (WINDOW // LANES) + side
            code = jnp.broadcast_to(codes_ref[pl.ds(line, 1), :], (8, LANES))
            value = None
            for bit in range(BITS):
                mask = jnp.concatenate([code << (31 - bit) >> 31] * (half // 8), axis=0)
                part = words[bit] & mask
                value = part if value is None else value ^ part
            word.append(value)
        word = jnp.concatenate(word, axis=1)
        total = jnp.zeros((own, WINDOW), jnp.float32)
        for at in range(0, planes, 2):
            bits = [
                (word & np.int32(np.uint32(1 << plane).view(np.int32))).astype(jnp.float32).astype(jnp.bfloat16)
                for plane in (at, at + planes, at + 1, at + 1 + planes)
            ]
            total = total + jnp.dot(
                own_signs[:, at * LANES:(at + 2) * LANES], jnp.concatenate(bits, axis=0),
                preferred_element_type=jnp.float32,
            )
        sums = jnp.concatenate([own_sums[...]] * (WINDOW // LANES), axis=1)
        gram_ref[:, pl.ds(pl.multiple_of(index * WINDOW, WINDOW), WINDOW)] = (sums - 2.0 * total).astype(jnp.bfloat16)
        return 0

    lax.fori_loop(0, chunks, chunk, 0, unroll=3)


def gram(codes, pokes, own):
    own = -(-own // 16) * 16
    acts, count = codes.size, pokes.shape[0]
    steps = 3
    return pl.pallas_call(
        gram_kernel,
        grid=(steps,),
        out_shape=jax.ShapeDtypeStruct((own, acts), jnp.bfloat16),
        in_specs=[pl.BlockSpec(memory_space=pltpu.VMEM)] * 2,
        out_specs=pl.BlockSpec((own, acts // steps), lambda s: (0, s)),
        scratch_shapes=[
            pltpu.VMEM((BITS, LANES // 2, LANES), jnp.int32),
            pltpu.VMEM((own, count), jnp.bfloat16),
            pltpu.VMEM((own, LANES), jnp.float32),
        ],
        compiler_params=pltpu.CompilerParams(vmem_limit_bytes=VMEM_BYTES),
        cost_estimate=pl.CostEstimate(
            flops=2 * own * acts * count, bytes_accessed=2 * own * acts, transcendentals=0
        ),
        name="gram_rows",
    )(codes.reshape(-1, LANES), pokes.reshape(-1, LANES))


def position(axis, staged):
    return lax.axis_index(axis) if staged else 0


def band_product(block_parts, q, row_shape, block, surface_rows, gram_ref, window_ref):
    mirrors, shard_rows, slots, samples = row_shape
    k, l = divmod(q, shard_rows)
    band = jnp.clip((block * shard_rows + l) * NAR // surface_rows - 1, 0, NAR - BAND)
    column = (k * NAR + band) * NA
    base = pl.multiple_of(column // LANES * LANES, LANES)
    shift = pl.multiple_of(column - base, 16)
    unit, side = divmod(q, 2)
    units = mirrors * shard_rows // 2 // len(block_parts)
    part, at = block_parts[unit // units], unit % units * 3 * slots
    for gap in range(0, WINDOW - slots, 16):
        row = pl.multiple_of((shift + slots + gap) % WINDOW, 16)
        window_ref[pl.ds(row, 16), :] = jnp.zeros((16, WINDOW), window_ref.dtype)
    window_ref[pl.ds(shift, slots), :LANES] = part[pl.ds(at + side * slots, slots), :]
    both = part[pl.ds(at + 2 * slots, slots), :]
    tail = samples - LANES
    mine = both[:, side * tail:(side + 1) * tail]
    window_ref[pl.ds(shift, slots), LANES:] = jnp.concatenate([mine, mine], axis=1)
    u = jnp.dot(gram_ref[:, pl.ds(base, WINDOW)], window_ref[...], preferred_element_type=jnp.float32)
    return u.astype(jnp.bfloat16)


def bands_kernel(row_shape, surface_rows, first, counts, staged, gram_ref, *refs):
    sources = refs[:len(counts)]
    out_ref, window = refs[-2:]
    step = pl.program_id(0)
    start = 0
    for source, count in zip(sources, counts):
        @pl.when((step >= start) & (step < start + count))
        def _():
            block = (first + step) ^ position("row", staged)
            for q in range(row_shape[0] * row_shape[1]):
                out_ref[0, q] = band_product(
                    [source.at[0]], q, row_shape, block, surface_rows, gram_ref, window.at[q % window.shape[0]]
                )
        start += count


def bands(gram_rows, sources, decoded, first, staged, row_shape, surface_rows):
    own = gram_rows.shape[0]
    counts = [source.shape[0] for source in sources]
    starts = np.cumsum([0] + counts)
    total = surface_rows // row_shape[1]
    rows = row_shape[0] * row_shape[1]
    specs = [
        pl.BlockSpec(
            (1,) + source.shape[1:],
            functools.partial(lambda low, high, s: (jnp.clip(s - low, 0, high - 1), 0, 0), int(starts[n]), counts[n]),
        )
        for n, source in enumerate(sources)
    ]
    arguments = [gram_rows, *sources]
    in_specs = [pl.BlockSpec(memory_space=pltpu.VMEM), *specs]
    aliases = {}
    body = functools.partial(bands_kernel, row_shape, surface_rows, first, counts, staged)
    if decoded is not None:
        aliases = {len(arguments): 0}
        arguments.append(decoded)
        in_specs.append(pl.BlockSpec(memory_space=pl.ANY))
    flops = 2 * own * WINDOW * WINDOW * rows * sum(counts)
    return pl.pallas_call(
        body,
        grid=(sum(counts),),
        out_shape=jax.ShapeDtypeStruct((total, rows, own, WINDOW), jnp.bfloat16),
        in_specs=in_specs,
        out_specs=pl.BlockSpec((1, rows, own, WINDOW), lambda s: (first + s, 0, 0, 0)),
        scratch_shapes=[pltpu.VMEM((4, WINDOW, WINDOW), jnp.bfloat16)],
        input_output_aliases=aliases,
        compiler_params=pltpu.CompilerParams(vmem_limit_bytes=VMEM_BYTES),
        cost_estimate=pl.CostEstimate(
            flops=flops, bytes_accessed=2 * own * WINDOW * rows * sum(counts), transcendentals=0
        ),
        name="bands",
    )(*arguments)


def build_differences(lines_ref, differences, mirrors, samples, pupil):
    tail = samples - LANES
    half = pupil // 2
    x = lax.broadcasted_iota(jnp.int32, (pupil, 2 * pupil), 0)
    lane = lax.broadcasted_iota(jnp.int32, (pupil, 2 * pupil), 1)
    spread = (x == lane % half * 2 + lane // pupil).astype(jnp.float32).astype(jnp.bfloat16)
    upper = lax.broadcasted_iota(jnp.int32, (1, pupil), 1) >= half
    for d in range(differences.shape[0]):
        columns = jnp.dot(
            lines_ref[0, d, :, :pupil].astype(jnp.float32).astype(jnp.bfloat16), spread,
            preferred_element_type=jnp.float32,
        ).astype(jnp.int32)
        for k in range(mirrors):
            first, second = columns[k:k + 1, :pupil], columns[k:k + 1, pupil:]

            def pieces(start, length):
                at = start + lax.broadcasted_iota(jnp.int32, (length, pupil), 0)
                ahead, behind = (at == second).astype(jnp.float32), (at == first).astype(jnp.float32)
                across, down = ahead - behind, ahead + behind
                return [jnp.where(upper, sign * down, across).astype(jnp.bfloat16) for sign in (-1.0, 1.0)]

            for y, (head, rest) in enumerate(zip(pieces(0, LANES), pieces(LANES, tail))):
                differences[d, pl.ds((2 * k + y) * LANES, LANES), :] = head
                differences[d, pl.ds(2 * mirrors * LANES + k * LANES + y * tail, tail), :] = rest


def decode_kernel(row_shape, surface_rows, own, late, staged, norm, foot_ref, lines_ref, *refs):
    mirrors, shard_rows, slots, samples = row_shape
    extras = refs[:late[1] * late[2]]
    gram_ref, decoded_ref, out_ref, decoded, differences, total, window, semaphores = refs[late[1] * late[2]:]
    group = pl.program_id(0)
    directions = differences.shape[0]
    pupil = differences.shape[2]
    phases = out_ref.shape[2] // pupil
    tail = samples - LANES
    ready = late[0]
    place = position("row", staged)

    @pl.when(group == 0)
    def _():
        copies = [
            pltpu.make_async_copy(decoded_ref.at[block], decoded.at[block], semaphores.at[block])
            for block in range(ready)
        ]
        for copy in copies:
            copy.start()
        build_differences(lines_ref, differences, mirrors, samples, pupil)
        for n in range(late[1]):
            block = (ready + n) ^ place
            parts = [extras[n * late[2] + part] for part in range(late[2])]
            for q in range(mirrors * shard_rows):
                decoded[ready + n, q] = band_product(
                    parts, q, row_shape, block, surface_rows, gram_ref, window.at[q % window.shape[0]]
                )
        for copy in copies:
            copy.wait()

    lane = lax.broadcasted_iota(jnp.int32, (decoded.shape[2], LANES), 1)
    for d in range(directions):
        held = d ^ position("dir", staged)
        left, factors = [], []
        for phase in range(phases):
            i = group * phases + phase
            block = (2 * i // shard_rows) ^ place
            heads, tails = [], []
            for k in range(mirrors):
                picked = []
                for y in range(2):
                    row = foot_ref[((block * directions + held) * mirrors + k) * shard_rows + (2 * i + y) % shard_rows]
                    picked.append((row // shard_rows ^ place, k * shard_rows + row % shard_rows))
                heads += [decoded[e, q, :, :LANES] for e, q in picked]
                tails.append(
                    jnp.where(lane < tail, *(decoded[e, q, :, LANES:] for e, q in picked))
                )
            left.append(jnp.concatenate(heads + tails, axis=1))
            line = mirrors + phase % (shard_rows // 2)
            valid = lines_ref[block, held, line:line + 1, :pupil // 2]
            factors.append(valid.astype(jnp.float32) * norm)
        rows = left[0].shape[0]
        product = jnp.dot(
            jnp.concatenate(left, axis=0), differences[held], preferred_element_type=jnp.float32
        )
        value = jnp.concatenate([product[phase * rows:phase * rows + own] for phase in range(phases)], axis=1)
        value = value * jnp.concatenate([factor for factor in factors for _ in range(2)], axis=1)
        for tile in range(out_ref.shape[2] // LANES):
            total[tile, pl.ds(d, own, stride=directions), :] = value[:, tile * LANES:(tile + 1) * LANES]
    for tile in range(out_ref.shape[2] // LANES):
        value = total[tile].reshape(own, directions, LANES)
        out_ref[:, :, tile * LANES:(tile + 1) * LANES] = value.astype(out_ref.dtype)


def decode(lines, gram_rows, decoded, extras, parts, own, row_shape, surface_rows, pupil, norm, staged):
    blocks, directions = lines.shape[:2]
    mirrors, shard_rows = row_shape[:2]
    padded = gram_rows.shape[0]
    foot_rows = lines[:, :, mirrors + shard_rows // 2:, :shard_rows].reshape(-1)
    phases = LANES // math.gcd(pupil, LANES)
    width = surface_rows // 2 * pupil
    lanes = phases * pupil
    late = len(extras) // parts
    ready = decoded.shape[0] - late
    flops = 2 * padded * 3 * mirrors * LANES * pupil * directions * surface_rows // 2
    vmem = pl.BlockSpec(memory_space=pltpu.VMEM)
    return pl.pallas_call(
        functools.partial(decode_kernel, row_shape, surface_rows, own, (ready, late, parts), staged, norm),
        grid=(width // lanes,),
        out_shape=jax.ShapeDtypeStruct((own, directions, width), jnp.bfloat16),
        in_specs=[pl.BlockSpec(memory_space=pltpu.SMEM), vmem]
        + [vmem] * len(extras)
        + [vmem, pl.BlockSpec(memory_space=pl.ANY)],
        out_specs=pl.BlockSpec((own, directions, lanes), lambda s: (0, 0, s)),
        scratch_shapes=[
            pltpu.VMEM(decoded.shape, jnp.bfloat16),
            pltpu.VMEM((directions, 3 * mirrors * LANES, pupil), jnp.bfloat16),
            pltpu.VMEM((lanes // LANES, own * directions, LANES), jnp.float32),
            pltpu.VMEM((4, WINDOW, WINDOW), jnp.bfloat16),
            pltpu.SemaphoreType.DMA((decoded.shape[0],)),
        ],
        compiler_params=pltpu.CompilerParams(vmem_limit_bytes=VMEM_BYTES),
        cost_estimate=pl.CostEstimate(flops=flops, bytes_accessed=2 * own * directions * width, transcendentals=0),
        name="decode",
    )(foot_rows, lines, *extras, gram_rows, decoded)


def swap(block, axis, distance):
    return lax.ppermute(block, axis, [(i, i ^ distance) for i in range(lax.axis_size(axis))])


def shards(influence, foot_rows, foot_columns, actuator_codes, poke_rows, subaperture_valid):
    mirrors, shard_rows, samples, slots = influence.shape
    row_shape = (mirrors, shard_rows, slots, samples)
    directions, devices = lax.axis_size("dir"), lax.axis_size("row")
    surface_rows = shard_rows * devices
    pupil = foot_columns.shape[2]
    norm = 0.5 * poke_rows.shape[0] ** (-0.5)
    own = actuator_codes.size // (directions * devices)
    staged = devices == 8 and directions & (directions - 1) == 0
    packed, lines = pack(jnp.swapaxes(influence, 2, 3), foot_rows, foot_columns, subaperture_valid)
    if not staged:
        gram_rows = gram(actuator_codes, poke_rows, own)
        decoded = bands(gram_rows, [lax.all_gather(packed, "row")], None, 0, staged, row_shape, surface_rows)
        lines = lax.all_gather(lax.all_gather(lines, "dir"), "row")
        return decode(lines, gram_rows, decoded, [], 1, own, row_shape, surface_rows, pupil, norm, staged)

    beside, across, sibling = (swap(packed, "row", distance) for distance in (2, 4, 1))
    lines = jnp.stack([lines] + [swap(lines, "dir", e) for e in range(1, directions)])[None]
    gram_rows = gram(actuator_codes, poke_rows, own)
    gram_rows, lines = lax.optimization_barrier((gram_rows, lines))
    lines = jnp.concatenate([lines, swap(lines, "row", 1)], axis=0)
    decoded = bands(gram_rows, [packed[None], sibling[None]], None, 0, staged, row_shape, surface_rows)
    decoded, lines, beside, across = lax.optimization_barrier((decoded, lines, beside, across))
    half = packed.shape[0] // 2
    upper, lower = swap(beside[:half], "row", 4), swap(across[half:], "row", 2)
    beside_sibling, across_sibling = swap(beside, "row", 1), swap(across, "row", 1)
    lines = jnp.concatenate([lines, swap(lines, "row", 2)], axis=0)
    sources = [source[None] for source in (beside, beside_sibling, across, across_sibling)]
    decoded = bands(gram_rows, sources, decoded, 2, staged, row_shape, surface_rows)
    decoded, lines, upper, lower = lax.optimization_barrier((decoded, lines, upper, lower))
    late = [upper, lower, swap(upper, "row", 1), swap(lower, "row", 1)]
    lines = jnp.concatenate([lines, swap(lines, "row", 4)], axis=0)
    return decode(lines, gram_rows, decoded, late, 2, own, row_shape, surface_rows, pupil, norm, staged)


def solution(mesh):
    return jax.shard_map(
        shards,
        mesh=mesh,
        in_specs=(
            P(None, "row", None, None),
            P("dir", None, "row"),
            P("dir", None, None),
            P(),
            P(),
            P("dir", "row", None),
        ),
        out_specs=P(("dir", "row"), None, None),
        check_vma=False,
    )
```

```python
import functools
import math

import jax
import jax.numpy as jnp
import numpy as np
from jax import lax
from jax.experimental import pallas as pl
from jax.experimental.pallas import tpu as pltpu
from jax.sharding import PartitionSpec as P

NAR = 48
NA = 48
BAND = 3
BITS = 13
LANES = 128
WINDOW = 256
VMEM_BYTES = 56 * 1024 * 1024


def parity(codes, rows):
    return lax.population_count(codes & rows) & 1


def lines_kernel(rows_ref, columns_ref, valid_ref, lines_ref):
    mirrors, rows = rows_ref.shape[0], rows_ref.shape[2]
    lines_ref[...] = jnp.zeros(lines_ref.shape, lines_ref.dtype)
    lines_ref[mirrors:mirrors + valid_ref.shape[1], :valid_ref.shape[2]] = valid_ref[0]
    for k in range(mirrors):
        lines_ref[k:k + 1, :columns_ref.shape[2]] = columns_ref[k]
        lines_ref[mirrors + valid_ref.shape[1]:mirrors + valid_ref.shape[1] + 1, k * rows:(k + 1) * rows] = rows_ref[k]


def small_lines(foot_rows, foot_columns, valid):
    vmem = pl.BlockSpec(memory_space=pltpu.VMEM)
    count = foot_rows.shape[1] + valid.shape[1] + 1
    return pl.pallas_call(
        lines_kernel,
        out_shape=jax.ShapeDtypeStruct((-(-count // 8) * 8, WINDOW), jnp.int32),
        in_specs=[vmem] * 3,
        out_specs=vmem,
        name="small_lines",
    )(jnp.swapaxes(foot_rows, 0, 1), jnp.swapaxes(foot_columns, 0, 1), valid)


def pack_kernel(block_ref, *refs):
    lines_refs, packed_ref = refs[:-1], refs[-1]
    mirrors, rows, slots, samples = block_ref.shape
    for unit in range(mirrors * rows // 2):
        base = unit * 3 * slots
        tails = []
        for side in range(2):
            k, l = divmod(2 * unit + side, rows)
            packed_ref[pl.ds(base + side * slots, slots), :] = block_ref[k, l, :, :LANES]
            tails.append(block_ref[k, l, :, LANES:])
        packed_ref[pl.ds(base + 2 * slots, slots), :] = jnp.concatenate(tails, axis=1)
    count = rows // 2 + 1
    lines = [ref[n, mirrors:mirrors + count, :LANES] for ref in lines_refs for n in range(ref.shape[0])]
    extra = packed_ref.shape[0] - mirrors * rows * slots * samples // LANES
    lines.append(jnp.zeros((extra - count * len(lines), LANES), jnp.int32))
    packed_ref[pl.ds(packed_ref.shape[0] - extra, extra), :] = (
        jnp.concatenate(lines, axis=0).astype(jnp.float32).astype(jnp.bfloat16)
    )


def pack(block, lines):
    mirrors, rows, slots, samples = block.shape
    vmem = pl.BlockSpec(memory_space=pltpu.VMEM)
    extra = -(-sum(line.shape[0] for line in lines) * (rows // 2 + 1) // 16) * 16
    return pl.pallas_call(
        pack_kernel,
        out_shape=jax.ShapeDtypeStruct((mirrors * rows * slots * samples // LANES + extra, LANES), block.dtype),
        in_specs=[vmem] * (1 + len(lines)),
        out_specs=vmem,
        compiler_params=pltpu.CompilerParams(vmem_limit_bytes=VMEM_BYTES),
        cost_estimate=pl.CostEstimate(flops=0, bytes_accessed=3 * block.size, transcendentals=0),
        name="pack_influence",
    )(block, *lines)


def column_of(row):
    return jnp.transpose(jnp.broadcast_to(row, (LANES, LANES)), (1, 0))


def gram_kernel(codes_ref, pokes_ref, gram_ref, words, own_signs, own_sums):
    planes = pokes_ref.shape[0]
    half = LANES // 2
    own = own_signs.shape[0]
    chunks = gram_ref.shape[1] // WINDOW

    @pl.when(pl.program_id(0) == 0)
    def _():
        plane = lax.broadcasted_iota(jnp.int32, pokes_ref.shape, 0)
        for bit in range(BITS):
            low = jnp.sum((pokes_ref[...] >> bit & 1) << plane, axis=0, keepdims=True)
            word = low | pltpu.roll(jnp.broadcast_to(low, (8, LANES)), half, 1)[:1] << planes
            words[bit] = column_of(word)[:half]
        count = codes_ref.shape[0] * LANES // (lax.axis_size("dir") * lax.axis_size("row"))
        first = (lax.axis_index("dir") * lax.axis_size("row") + lax.axis_index("row")) * count
        lane = lax.broadcasted_iota(jnp.int32, (8, LANES), 1)
        shift = first % LANES
        lines = [
            pltpu.roll(
                jnp.broadcast_to(
                    codes_ref[pl.ds(jnp.minimum(first // LANES + n, codes_ref.shape[0] - 1), 1), :], (8, LANES)
                ),
                LANES - shift, 1,
            )
            for n in range(-(-own // LANES) + 1)
        ]
        own_column = jnp.concatenate(
            [
                column_of(jnp.where(lane < LANES - shift, lines[n], lines[n + 1])[:1])
                for n in range(len(lines) - 1)
            ],
            axis=0,
        )[:own]
        lane = lax.broadcasted_iota(jnp.int32, (1, LANES), 1)
        total = jnp.zeros((own, LANES), jnp.float32)
        for at in range(planes):
            signs = (1 - 2 * parity(own_column, pokes_ref[at:at + 1, :])).astype(jnp.float32)
            upper = -(2.0 ** -(at + planes)) if at + planes == 31 else 2.0 ** -(at + planes)
            own_signs[:, at * LANES:(at + 1) * LANES] = (
                signs * jnp.where(lane < half, 2.0 ** -at, upper)
            ).astype(jnp.bfloat16)
            total = total + signs
        own_sums[...] = jnp.broadcast_to(jnp.sum(total, axis=1, keepdims=True), own_sums.shape)

    def chunk(index, _):
        word = []
        for side in range(WINDOW // LANES):
            line = (pl.program_id(0) * chunks + index) * (WINDOW // LANES) + side
            code = jnp.broadcast_to(codes_ref[pl.ds(line, 1), :], (8, LANES))
            value = None
            for bit in range(BITS):
                mask = jnp.concatenate([code << (31 - bit) >> 31] * (half // 8), axis=0)
                part = words[bit] & mask
                value = part if value is None else value ^ part
            word.append(value)
        word = jnp.concatenate(word, axis=1)
        total = jnp.zeros((own, WINDOW), jnp.float32)
        for at in range(0, planes, 2):
            bits = [
                (word & np.int32(np.uint32(1 << plane).view(np.int32))).astype(jnp.float32).astype(jnp.bfloat16)
                for plane in (at, at + planes, at + 1, at + 1 + planes)
            ]
            total = total + jnp.dot(
                own_signs[:, at * LANES:(at + 2) * LANES], jnp.concatenate(bits, axis=0),
                preferred_element_type=jnp.float32,
            )
        sums = jnp.concatenate([own_sums[...]] * (WINDOW // LANES), axis=1)
        gram_ref[:, pl.ds(pl.multiple_of(index * WINDOW, WINDOW), WINDOW)] = (sums - 2.0 * total).astype(jnp.bfloat16)
        return 0

    lax.fori_loop(0, chunks, chunk, 0, unroll=3)


def gram(codes, pokes, own):
    own = -(-own // 16) * 16
    acts, count = codes.size, pokes.shape[0]
    steps = 3
    return pl.pallas_call(
        gram_kernel,
        grid=(steps,),
        out_shape=jax.ShapeDtypeStruct((own, acts), jnp.bfloat16),
        in_specs=[pl.BlockSpec(memory_space=pltpu.VMEM)] * 2,
        out_specs=pl.BlockSpec((own, acts // steps), lambda s: (0, s)),
        scratch_shapes=[
            pltpu.VMEM((BITS, LANES // 2, LANES), jnp.int32),
            pltpu.VMEM((own, count), jnp.bfloat16),
            pltpu.VMEM((own, LANES), jnp.float32),
        ],
        compiler_params=pltpu.CompilerParams(vmem_limit_bytes=VMEM_BYTES),
        cost_estimate=pl.CostEstimate(
            flops=2 * own * acts * count, bytes_accessed=2 * own * acts, transcendentals=0
        ),
        name="gram_rows",
    )(codes.reshape(-1, LANES), pokes.reshape(-1, LANES))


def position(axis, staged):
    return lax.axis_index(axis) if staged else 0


def band_products(parts, row_shape, block, surface_rows, gram_ref, window_ref, out_ref):
    mirrors, shard_rows, slots, samples = row_shape
    tail = samples - LANES
    bases = []
    for q in range(mirrors * shard_rows):
        k, l = divmod(q, shard_rows)
        band = jnp.clip((block * shard_rows + l) * NAR // surface_rows - 1, 0, NAR - BAND)
        column = (k * NAR + band) * NA
        bases.append(pl.multiple_of(column // LANES * LANES, LANES))
        shift = pl.multiple_of(column - bases[-1], 16)
        unit, side = divmod(q, 2)
        units = mirrors * shard_rows // 2 // len(parts)
        part, at = parts[unit // units], unit % units * 3 * slots
        for gap in range(0, WINDOW - slots, 16):
            row = pl.multiple_of((shift + slots + gap) % WINDOW, 16)
            window_ref[q, pl.ds(row, 16), :] = jnp.zeros((16, WINDOW), window_ref.dtype)
        window_ref[q, pl.ds(shift, slots), :LANES] = part[pl.ds(at + side * slots, slots), :]
        window_ref[q, pl.ds(shift, slots), LANES:] = part[pl.ds(at + 2 * slots, slots), :]
    for q, base in enumerate(bases):
        u = jnp.dot(gram_ref[:, pl.ds(base, WINDOW)], window_ref[q], preferred_element_type=jnp.float32)
        out_ref[q, :LANES] = jnp.transpose(u[:, :LANES]).astype(jnp.bfloat16)
        rest = jnp.transpose(u[:, LANES:])[q % 2 * tail:(q % 2 + 1) * tail]
        out_ref[q, LANES:] = rest.astype(jnp.bfloat16)


def bands_kernel(row_shape, surface_rows, first, counts, staged, gram_ref, *refs):
    sources = refs[:len(counts)]
    out_ref, window = refs[-2:]
    step = pl.program_id(0)
    start = 0
    for source, count in zip(sources, counts):
        @pl.when((step >= start) & (step < start + count))
        def _():
            block = (first + step) ^ position("row", staged)
            band_products([source.at[0]], row_shape, block, surface_rows, gram_ref, window, out_ref.at[0])
        start += count


def bands(gram_rows, sources, decoded, first, staged, row_shape, surface_rows):
    own = gram_rows.shape[0]
    counts = [source.shape[0] for source in sources]
    starts = np.cumsum([0] + counts)
    total = surface_rows // row_shape[1]
    rows = row_shape[0] * row_shape[1]
    specs = [
        pl.BlockSpec(
            (1,) + source.shape[1:],
            functools.partial(lambda low, high, s: (jnp.clip(s - low, 0, high - 1), 0, 0), int(starts[n]), counts[n]),
        )
        for n, source in enumerate(sources)
    ]
    arguments = [gram_rows, *sources]
    in_specs = [pl.BlockSpec(memory_space=pltpu.VMEM), *specs]
    aliases = {}
    body = functools.partial(bands_kernel, row_shape, surface_rows, first, counts, staged)
    if decoded is not None:
        aliases = {len(arguments): 0}
        arguments.append(decoded)
        in_specs.append(pl.BlockSpec(memory_space=pl.ANY))
    flops = 2 * own * WINDOW * WINDOW * rows * sum(counts)
    return pl.pallas_call(
        body,
        grid=(sum(counts),),
        out_shape=jax.ShapeDtypeStruct((total, rows, row_shape[3], own), jnp.bfloat16),
        in_specs=in_specs,
        out_specs=pl.BlockSpec((1, rows, row_shape[3], own), lambda s: (first + s, 0, 0, 0)),
        scratch_shapes=[pltpu.VMEM((rows, WINDOW, WINDOW), jnp.bfloat16)],
        input_output_aliases=aliases,
        compiler_params=pltpu.CompilerParams(vmem_limit_bytes=VMEM_BYTES),
        cost_estimate=pl.CostEstimate(
            flops=flops, bytes_accessed=2 * own * WINDOW * rows * sum(counts), transcendentals=0
        ),
        name="bands",
    )(*arguments)


def build_differences(columns, differences, mirrors, samples, pupil):
    half = pupil // 2
    slope = lax.broadcasted_iota(jnp.int32, (pupil, pupil), 0)
    lane = lax.broadcasted_iota(jnp.int32, (pupil, pupil), 1)
    upper = lax.broadcasted_iota(jnp.int32, (pupil, samples), 0) >= half
    at = lax.broadcasted_iota(jnp.int32, (pupil, samples), 1)
    for d, lines in enumerate(columns):
        for k in range(mirrors):
            line = jnp.broadcast_to(lines[k:k + 1], (pupil, pupil))
            sides = [
                jnp.sum(jnp.where(lane == slope % half * 2 + side, line, 0), axis=1, keepdims=True) for side in range(2)
            ]
            behind, ahead = ((at == side).astype(jnp.float32) for side in sides)
            across, down = ahead - behind, ahead + behind
            value = jnp.concatenate([jnp.where(upper, -down, across), jnp.where(upper, down, across)], axis=1)
            differences[d, :, 2 * k * samples:2 * (k + 1) * samples] = value.astype(jnp.bfloat16)


def decode_kernel(row_shape, surface_rows, own, late, staged, norm, counts, *refs):
    mirrors, shard_rows, slots, samples = row_shape
    columns_refs, refs = refs[:counts[0]], refs[counts[0]:]
    lines_refs, refs = refs[:counts[1]], refs[counts[1]:]
    late_refs, refs = refs[:counts[2]], refs[counts[2]:]
    gram_ref, decoded_ref, out_ref, decoded, differences, total, window, lines, scalars, semaphores = refs
    group = pl.program_id(0)
    directions, pupil = differences.shape[:2]
    phases = out_ref.shape[2] // pupil
    place = position("row", staged)
    blocks = surface_rows // shard_rows
    ready = blocks - late
    width = shard_rows // 2 + 1

    @pl.when(group == 0)
    def _():
        copies = [
            pltpu.make_async_copy(decoded_ref.at[block], decoded.at[block], semaphores.at[block])
            for block in range(ready)
        ]
        for copy in copies:
            copy.start()
        extra = lines.shape[1]
        ends = [ref.at[n] for ref in lines_refs for n in range(ref.shape[0])]
        parts = [late_refs[n * counts[2] // max(late, 1):(n + 1) * counts[2] // max(late, 1)] for n in range(late)]
        ends += [part[-1].at[pl.ds(part[-1].shape[0] - extra, extra)] for part in parts]
        for block, end in enumerate(ends):
            lines[block] = end[...].astype(jnp.float32).astype(jnp.int32)
        to_scalars = pltpu.make_async_copy(lines, scalars, semaphores.at[blocks])
        to_scalars.start()
        columns = [ref[n, :, :pupil] for ref in columns_refs for n in range(ref.shape[0])]
        build_differences(columns, differences, mirrors, samples, pupil)
        for n, part in enumerate(parts):
            band_products(
                part, row_shape, (ready + n) ^ place, surface_rows, gram_ref, window, decoded.at[ready + n]
            )
        to_scalars.wait()
        for copy in copies:
            copy.wait()

    for d in range(directions):
        held = d ^ position("dir", staged)
        products, factors = [], []
        for phase in range(phases):
            i = group * phases + phase
            block = (2 * i // shard_rows) ^ place
            picked = []
            for k in range(mirrors):
                for y in range(2):
                    row = scalars[block, held * width + width - 1, k * shard_rows + (2 * phase + y) % shard_rows]
                    picked.append(decoded[row // shard_rows ^ place, k * shard_rows + row % shard_rows])
            products.append(
                jnp.dot(differences[held], jnp.concatenate(picked, axis=0), preferred_element_type=jnp.float32)
            )
            valid = lines[block, pl.ds(held * width + phase % (shard_rows // 2), 1), :][:, :pupil // 2]
            factors += [valid.astype(jnp.float32) * norm] * 2
        product = jnp.concatenate(products, axis=0)
        factor = jnp.concatenate(factors, axis=1)
        for tile in range(out_ref.shape[2] // LANES):
            at = tile * LANES
            value = jnp.transpose(product[at:at + LANES])[:own] * factor[:, at:at + LANES]
            total[tile, pl.ds(d, own, stride=directions), :] = value
    for tile in range(out_ref.shape[2] // LANES):
        value = total[tile].reshape(own, directions, LANES)
        out_ref[:, :, tile * LANES:(tile + 1) * LANES] = value.astype(out_ref.dtype)


def decode(columns, sources, late_parts, late, gram_rows, decoded, own, row_shape, surface_rows, pupil, norm, staged):
    blocks = decoded.shape[0]
    mirrors, shard_rows, slots, samples = row_shape
    padded = gram_rows.shape[0]
    directions = sum(line.shape[0] for line in columns)
    extra = -(-directions * (shard_rows // 2 + 1) // 16) * 16
    phases = LANES // math.gcd(pupil, LANES)
    width = surface_rows // 2 * pupil
    lanes = phases * pupil
    flops = 2 * padded * 2 * mirrors * samples * pupil * directions * surface_rows // 2
    vmem = pl.BlockSpec(memory_space=pltpu.VMEM)
    ends = [
        pl.BlockSpec(
            (source.shape[0], extra, LANES),
            functools.partial(lambda last, s: (0, last, 0), source.shape[1] // extra - 1),
        )
        for source in sources
    ]
    counts = (len(columns), len(sources), len(late_parts))
    return pl.pallas_call(
        functools.partial(decode_kernel, row_shape, surface_rows, own, late, staged, norm, counts),
        grid=(width // lanes,),
        out_shape=jax.ShapeDtypeStruct((own, directions, width), jnp.bfloat16),
        in_specs=[vmem] * len(columns) + ends + [vmem] * len(late_parts) + [vmem, pl.BlockSpec(memory_space=pl.ANY)],
        out_specs=pl.BlockSpec((own, directions, lanes), lambda s: (0, 0, s)),
        scratch_shapes=[
            pltpu.VMEM(decoded.shape, jnp.bfloat16),
            pltpu.VMEM((directions, pupil, 2 * mirrors * samples), jnp.bfloat16),
            pltpu.VMEM((lanes // LANES, own * directions, LANES), jnp.float32),
            pltpu.VMEM((mirrors * shard_rows, WINDOW, WINDOW), jnp.bfloat16),
            pltpu.VMEM((blocks, extra, LANES), jnp.int32),
            pltpu.SMEM((blocks, extra, LANES), jnp.int32),
            pltpu.SemaphoreType.DMA((blocks + 1,)),
        ],
        compiler_params=pltpu.CompilerParams(vmem_limit_bytes=VMEM_BYTES),
        cost_estimate=pl.CostEstimate(flops=flops, bytes_accessed=2 * own * directions * width, transcendentals=0),
        name="decode",
    )(*columns, *sources, *late_parts, gram_rows, decoded)


def swap(block, axis, distance):
    return lax.ppermute(block, axis, [(i, i ^ distance) for i in range(lax.axis_size(axis))])


def shards(influence, foot_rows, foot_columns, actuator_codes, poke_rows, subaperture_valid):
    mirrors, shard_rows, samples, slots = influence.shape
    row_shape = (mirrors, shard_rows, slots, samples)
    directions, devices = lax.axis_size("dir"), lax.axis_size("row")
    surface_rows = shard_rows * devices
    pupil = foot_columns.shape[2]
    norm = 0.5 * poke_rows.shape[0] ** (-0.5)
    own = actuator_codes.size // (directions * devices)
    staged = devices == 8 and directions & (directions - 1) == 0
    turned = jnp.swapaxes(influence, 2, 3)
    lines = small_lines(foot_rows, foot_columns, subaperture_valid)
    if not staged:
        lines = [lax.all_gather(lines, "dir")]
        every = lax.all_gather(pack(turned, lines), "row")
        gram_rows = gram(actuator_codes, poke_rows, own)
        decoded = bands(gram_rows, [every], None, 0, staged, row_shape, surface_rows)
        return decode(
            lines, [every], [], 0, gram_rows, decoded, own, row_shape, surface_rows, pupil, norm, staged
        )

    lines = [lines[None]] + [swap(lines, "dir", e)[None] for e in range(1, directions)]
    packed = pack(turned, lines)
    beside, across, sibling = (swap(packed, "row", distance) for distance in (2, 4, 1))
    gram_rows = gram(actuator_codes, poke_rows, own)
    decoded = bands(gram_rows, [packed[None], sibling[None]], None, 0, staged, row_shape, surface_rows)
    decoded, beside, across = lax.optimization_barrier((decoded, beside, across))
    half = mirrors * shard_rows * slots * samples // LANES // 2
    upper, lower = swap(beside[:half], "row", 4), swap(across[half:], "row", 2)
    beside_sibling, across_sibling = swap(beside, "row", 1), swap(across, "row", 1)
    sources = [source[None] for source in (beside, beside_sibling, across, across_sibling)]
    decoded = bands(gram_rows, sources, decoded, 2, staged, row_shape, surface_rows)
    decoded, upper, lower = lax.optimization_barrier((decoded, upper, lower))
    late = [upper, lower, swap(upper, "row", 1), swap(lower, "row", 1)]
    return decode(
        lines, [packed[None], sibling[None], *sources], late, 2, gram_rows, decoded, own, row_shape, surface_rows,
        pupil, norm, staged,
    )


def solution(mesh):
    return jax.shard_map(
        shards,
        mesh=mesh,
        in_specs=(
            P(None, "row", None, None),
            P("dir", None, "row"),
            P("dir", None, None),
            P(),
            P(),
            P("dir", "row", None),
        ),
        out_specs=P(("dir", "row"), None, None),
        check_vma=False,
    )
```

```python
import functools
import math

import jax
import jax.numpy as jnp
import numpy as np
from jax import lax
from jax.experimental import pallas as pl
from jax.experimental.pallas import tpu as pltpu
from jax.sharding import PartitionSpec as P

NAR = 48
NA = 48
BAND = 3
BITS = 13
LANES = 128
WINDOW = 256
VMEM_BYTES = 56 * 1024 * 1024


def parity(codes, rows):
    return lax.population_count(codes & rows) & 1


def lines_kernel(rows_ref, columns_ref, valid_ref, lines_ref):
    mirrors, rows = rows_ref.shape[0], rows_ref.shape[2]
    lines_ref[...] = jnp.zeros(lines_ref.shape, lines_ref.dtype)
    lines_ref[mirrors:mirrors + valid_ref.shape[1], :valid_ref.shape[2]] = valid_ref[0]
    for k in range(mirrors):
        lines_ref[k:k + 1, :columns_ref.shape[2]] = columns_ref[k]
        lines_ref[mirrors + valid_ref.shape[1]:mirrors + valid_ref.shape[1] + 1, k * rows:(k + 1) * rows] = rows_ref[k]


def small_lines(foot_rows, foot_columns, valid):
    vmem = pl.BlockSpec(memory_space=pltpu.VMEM)
    count = foot_rows.shape[1] + valid.shape[1] + 1
    return pl.pallas_call(
        lines_kernel,
        out_shape=jax.ShapeDtypeStruct((-(-count // 8) * 8, WINDOW), jnp.int32),
        in_specs=[vmem] * 3,
        out_specs=vmem,
        name="small_lines",
    )(jnp.swapaxes(foot_rows, 0, 1), jnp.swapaxes(foot_columns, 0, 1), valid)


def pack_kernel(block_ref, *refs):
    lines_refs, packed_ref = refs[:-1], refs[-1]
    mirrors, rows, slots, samples = block_ref.shape
    groups = mirrors * rows // 2
    identity = (
        lax.broadcasted_iota(jnp.int32, (samples, samples), 0) == lax.broadcasted_iota(jnp.int32, (samples, samples), 1)
    ).astype(jnp.float32).astype(jnp.bfloat16)
    for part in range(2):
        base = part * (groups + 1) * samples
        tails = []
        for group in range(groups):
            k, l = divmod(part * groups + group, rows)
            turned = lax.dot_general(
                identity, block_ref[k, l], (((1,), (1,)), ((), ())), preferred_element_type=jnp.float32
            ).astype(jnp.bfloat16)
            packed_ref[pl.ds(base + group * samples, samples), :] = turned[:, :LANES]
            tails.append(turned[:, LANES:])
        tails.append(jnp.zeros((samples, LANES - groups * (slots - LANES)), jnp.bfloat16))
        packed_ref[pl.ds(base + groups * samples, samples), :] = jnp.concatenate(tails, axis=1)
    count = rows // 2 + 1
    lines = [ref[n, mirrors:mirrors + count, :LANES] for ref in lines_refs for n in range(ref.shape[0])]
    extra = packed_ref.shape[0] - 2 * (groups + 1) * samples
    lines.append(jnp.zeros((extra - count * len(lines), LANES), jnp.int32))
    packed_ref[pl.ds(packed_ref.shape[0] - extra, extra), :] = (
        jnp.concatenate(lines, axis=0).astype(jnp.float32).astype(jnp.bfloat16)
    )


def pack(block, lines):
    mirrors, rows, slots, samples = block.shape
    vmem = pl.BlockSpec(memory_space=pltpu.VMEM)
    extra = -(-sum(line.shape[0] for line in lines) * (rows // 2 + 1) // 16) * 16
    return pl.pallas_call(
        pack_kernel,
        out_shape=jax.ShapeDtypeStruct(((mirrors * rows + 2) * samples + extra, LANES), block.dtype),
        in_specs=[vmem] * (1 + len(lines)),
        out_specs=vmem,
        compiler_params=pltpu.CompilerParams(vmem_limit_bytes=VMEM_BYTES),
        cost_estimate=pl.CostEstimate(flops=0, bytes_accessed=3 * block.size, transcendentals=0),
        name="pack_influence",
    )(block, *lines)


def column_of(row):
    return jnp.transpose(jnp.broadcast_to(row, (LANES, LANES)), (1, 0))


def signs_kernel(codes_ref, pokes_ref, words, own_signs, own_sums):
    planes = pokes_ref.shape[0]
    half = LANES // 2
    own = own_signs.shape[0]
    plane = lax.broadcasted_iota(jnp.int32, pokes_ref.shape, 0)
    for bit in range(BITS):
        low = jnp.sum((pokes_ref[...] >> bit & 1) << plane, axis=0, keepdims=True)
        word = low | pltpu.roll(jnp.broadcast_to(low, (8, LANES)), half, 1)[:1] << planes
        words[bit] = column_of(word)[:half]
    count = codes_ref.shape[0] * LANES // (lax.axis_size("dir") * lax.axis_size("row"))
    first = (lax.axis_index("dir") * lax.axis_size("row") + lax.axis_index("row")) * count
    lane = lax.broadcasted_iota(jnp.int32, (8, LANES), 1)
    shift = first % LANES
    lines = [
        pltpu.roll(
            jnp.broadcast_to(
                codes_ref[pl.ds(jnp.minimum(first // LANES + n, codes_ref.shape[0] - 1), 1), :], (8, LANES)
            ),
            LANES - shift, 1,
        )
        for n in range(-(-own // LANES) + 1)
    ]
    own_column = jnp.concatenate(
        [column_of(jnp.where(lane < LANES - shift, lines[n], lines[n + 1])[:1]) for n in range(len(lines) - 1)],
        axis=0,
    )[:own]
    lane = lax.broadcasted_iota(jnp.int32, (1, LANES), 1)
    total = jnp.zeros((own, LANES), jnp.float32)
    for at in range(planes):
        signs = (1 - 2 * parity(own_column, pokes_ref[at:at + 1, :])).astype(jnp.float32)
        upper = -(2.0 ** -(at + planes)) if at + planes == 31 else 2.0 ** -(at + planes)
        own_signs[:, at * LANES:(at + 1) * LANES] = (
            signs * jnp.where(lane < half, 2.0 ** -at, upper)
        ).astype(jnp.bfloat16)
        total = total + signs
    own_sums[...] = jnp.broadcast_to(jnp.sum(total, axis=1, keepdims=True), own_sums.shape)


def own_side(codes, pokes, own):
    own = -(-own // 16) * 16
    vmem = pl.BlockSpec(memory_space=pltpu.VMEM)
    return pl.pallas_call(
        signs_kernel,
        out_shape=[
            jax.ShapeDtypeStruct((BITS, LANES // 2, LANES), jnp.int32),
            jax.ShapeDtypeStruct((own, pokes.size), jnp.bfloat16),
            jax.ShapeDtypeStruct((own, LANES), jnp.float32),
        ],
        in_specs=[vmem] * 2,
        out_specs=[vmem] * 3,
        compiler_params=pltpu.CompilerParams(vmem_limit_bytes=VMEM_BYTES),
        name="own_signs",
    )(codes, pokes)


def gram_kernel(codes_ref, words, own_signs, own_sums, gram_ref):
    half = LANES // 2
    own, pokes = own_signs.shape
    planes = pokes // LANES
    chunks = gram_ref.shape[0] // WINDOW

    def chunk(index, _):
        word = []
        for side in range(WINDOW // LANES):
            line = (pl.program_id(0) * chunks + index) * (WINDOW // LANES) + side
            code = jnp.broadcast_to(codes_ref[pl.ds(line, 1), :], (8, LANES))
            value = None
            for bit in range(BITS):
                mask = jnp.concatenate([code << (31 - bit) >> 31] * (half // 8), axis=0)
                part = words[bit] & mask
                value = part if value is None else value ^ part
            word.append(value)
        word = jnp.concatenate(word, axis=1)
        total = jnp.zeros((own, WINDOW), jnp.float32)
        for at in range(0, planes, 2):
            bits = [
                (word & np.int32(np.uint32(1 << plane).view(np.int32))).astype(jnp.float32).astype(jnp.bfloat16)
                for plane in (at, at + planes, at + 1, at + 1 + planes)
            ]
            total = total + jnp.dot(
                own_signs[:, at * LANES:(at + 2) * LANES], jnp.concatenate(bits, axis=0),
                preferred_element_type=jnp.float32,
            )
        sums = jnp.concatenate([own_sums[...]] * (WINDOW // LANES), axis=1)
        turned = jnp.transpose(sums - 2.0 * total)
        gram_ref[pl.ds(pl.multiple_of(index * WINDOW, WINDOW), WINDOW), :] = turned.astype(jnp.bfloat16)
        return 0

    lax.fori_loop(0, chunks, chunk, 0, unroll=3)


def gram(codes, words, own_signs, own_sums):
    acts, (own, count) = codes.size, own_signs.shape
    steps = 3
    vmem = pl.BlockSpec(memory_space=pltpu.VMEM)
    return pl.pallas_call(
        gram_kernel,
        grid=(steps,),
        out_shape=jax.ShapeDtypeStruct((acts, own), jnp.bfloat16),
        in_specs=[vmem] * 4,
        out_specs=pl.BlockSpec((acts // steps, own), lambda s: (s, 0)),
        compiler_params=pltpu.CompilerParams(vmem_limit_bytes=VMEM_BYTES),
        cost_estimate=pl.CostEstimate(
            flops=2 * own * acts * count, bytes_accessed=2 * own * acts, transcendentals=0
        ),
        name="gram_rows",
    )(codes, words, own_signs, own_sums)


def position(axis, staged):
    return lax.axis_index(axis) if staged else 0


def band_products(parts, row_shape, block, surface_rows, gram_ref, out_ref):
    mirrors, shard_rows, slots, samples = row_shape
    groups = mirrors * shard_rows // 2
    own = gram_ref.shape[1]
    narrow = slots - LANES
    for q in range(mirrors * shard_rows):
        k, l = divmod(q, shard_rows)
        band = jnp.clip((block * shard_rows + l) * NAR // surface_rows - 1, 0, NAR - BAND)
        column = pl.multiple_of((k * NAR + band) * NA, 16)
        part, group = divmod(q, groups)
        source, base = (parts[0], part * (groups + 1) * samples) if len(parts) == 1 else (parts[part], 0)
        left = jnp.concatenate(
            [source[pl.ds(base + group * samples, samples), :], source[pl.ds(base + groups * samples, samples), :]],
            axis=1,
        )
        right = [gram_ref[pl.ds(column, LANES), :]]
        if group:
            right.append(jnp.zeros((group * narrow, own), jnp.bfloat16))
        right.append(gram_ref[pl.ds(column + LANES, narrow), :])
        right.append(jnp.zeros((LANES - (group + 1) * narrow, own), jnp.bfloat16))
        out_ref[q] = jnp.dot(
            left, jnp.concatenate(right, axis=0), preferred_element_type=jnp.float32
        ).astype(jnp.bfloat16)


def bands_kernel(row_shape, surface_rows, first, counts, staged, gram_ref, *refs):
    sources = refs[:len(counts)]
    out_ref = refs[-1]
    step = pl.program_id(0)
    start = 0
    for source, count in zip(sources, counts):
        @pl.when((step >= start) & (step < start + count))
        def _():
            block = (first + step) ^ position("row", staged)
            band_products([source.at[0]], row_shape, block, surface_rows, gram_ref, out_ref.at[0])
        start += count


def bands(gram_rows, sources, decoded, first, staged, row_shape, surface_rows):
    own = gram_rows.shape[1]
    counts = [source.shape[0] for source in sources]
    starts = np.cumsum([0] + counts)
    total = surface_rows // row_shape[1]
    rows = row_shape[0] * row_shape[1]
    specs = [
        pl.BlockSpec(
            (1,) + source.shape[1:],
            functools.partial(lambda low, high, s: (jnp.clip(s - low, 0, high - 1), 0, 0), int(starts[n]), counts[n]),
        )
        for n, source in enumerate(sources)
    ]
    arguments = [gram_rows, *sources]
    in_specs = [pl.BlockSpec(memory_space=pltpu.VMEM), *specs]
    aliases = {}
    body = functools.partial(bands_kernel, row_shape, surface_rows, first, counts, staged)
    if decoded is not None:
        aliases = {len(arguments): 0}
        arguments.append(decoded)
        in_specs.append(pl.BlockSpec(memory_space=pl.ANY))
    flops = 2 * own * WINDOW * WINDOW * rows * sum(counts)
    return pl.pallas_call(
        body,
        grid=(sum(counts),),
        out_shape=jax.ShapeDtypeStruct((total, rows, row_shape[3], own), jnp.bfloat16),
        in_specs=in_specs,
        out_specs=pl.BlockSpec((1, rows, row_shape[3], own), lambda s: (first + s, 0, 0, 0)),
        input_output_aliases=aliases,
        compiler_params=pltpu.CompilerParams(vmem_limit_bytes=VMEM_BYTES),
        cost_estimate=pl.CostEstimate(
            flops=flops, bytes_accessed=2 * own * WINDOW * rows * sum(counts), transcendentals=0
        ),
        name="bands",
    )(*arguments)


def build_differences(columns, differences, mirrors, samples, pupil):
    half = pupil // 2
    slope = lax.broadcasted_iota(jnp.int32, (half, pupil), 0)
    lane = lax.broadcasted_iota(jnp.int32, (half, pupil), 1)
    at = lax.broadcasted_iota(jnp.int32, (half, mirrors * samples), 1)
    for d, lines in enumerate(columns):
        sides = []
        for side in range(2):
            hit = None
            for k in range(mirrors):
                line = jnp.broadcast_to(lines[k:k + 1], (half, pupil))
                column = jnp.sum(jnp.where(lane == slope * 2 + side, line, 0), axis=1, keepdims=True)
                here = (at == column + k * samples).astype(jnp.float32)
                hit = here if hit is None else hit + here
            sides.append(hit)
        differences[d, 0] = (sides[1] - sides[0]).astype(jnp.bfloat16)
        differences[d, 1] = (sides[1] + sides[0]).astype(jnp.bfloat16)


def decode_kernel(row_shape, surface_rows, own, late, staged, norm, counts, *refs):
    mirrors, shard_rows, slots, samples = row_shape
    columns_refs, refs = refs[:counts[0]], refs[counts[0]:]
    lines_refs, refs = refs[:counts[1]], refs[counts[1]:]
    late_refs, refs = refs[:counts[2]], refs[counts[2]:]
    gram_ref, decoded_ref, out_ref, decoded, differences, total, lines, scalars, semaphores = refs
    group = pl.program_id(0)
    directions, pupil = differences.shape[0], 2 * differences.shape[2]
    phases = out_ref.shape[2] // pupil
    place = position("row", staged)
    blocks = surface_rows // shard_rows
    ready = blocks - late
    width = shard_rows // 2 + 1

    @pl.when(group == 0)
    def _():
        copies = [
            pltpu.make_async_copy(decoded_ref.at[block], decoded.at[block], semaphores.at[block])
            for block in range(ready)
        ]
        for copy in copies:
            copy.start()
        extra = lines.shape[1]
        ends = [ref.at[n] for ref in lines_refs for n in range(ref.shape[0])]
        parts = [late_refs[n * counts[2] // max(late, 1):(n + 1) * counts[2] // max(late, 1)] for n in range(late)]
        ends += [part[-1].at[pl.ds(part[-1].shape[0] - extra, extra)] for part in parts]
        for block, end in enumerate(ends):
            lines[block] = end[...].astype(jnp.float32).astype(jnp.int32)
        to_scalars = pltpu.make_async_copy(lines, scalars, semaphores.at[blocks])
        to_scalars.start()
        columns = [ref[n, :, :pupil] for ref in columns_refs for n in range(ref.shape[0])]
        build_differences(columns, differences, mirrors, samples, pupil)
        for n, part in enumerate(parts):
            band_products(part, row_shape, (ready + n) ^ place, surface_rows, gram_ref, decoded.at[ready + n])
        to_scalars.wait()
        for copy in copies:
            copy.wait()

    for d in range(directions):
        held = d ^ position("dir", staged)
        products, factors = [], []
        for phase in range(phases):
            i = group * phases + phase
            block = (2 * i // shard_rows) ^ place
            sums, changes = [], []
            for k in range(mirrors):
                picked = []
                for y in range(2):
                    row = scalars[block, held * width + width - 1, k * shard_rows + (2 * phase + y) % shard_rows]
                    picked.append(decoded[row // shard_rows ^ place, k * shard_rows + row % shard_rows])
                sums.append(picked[0] + picked[1])
                changes.append(picked[1] - picked[0])
            for kind, rows in enumerate((sums, changes)):
                products.append(
                    jnp.dot(
                        differences[held, kind], jnp.concatenate(rows, axis=0), preferred_element_type=jnp.float32
                    )
                )
            valid = lines[block, pl.ds(held * width + phase % (shard_rows // 2), 1), :][:, :pupil // 2]
            factors += [valid.astype(jnp.float32) * norm] * 2
        product = jnp.concatenate(products, axis=0)
        factor = jnp.concatenate(factors, axis=1)
        for tile in range(out_ref.shape[2] // LANES):
            at = tile * LANES
            value = jnp.transpose(product[at:at + LANES])[:own] * factor[:, at:at + LANES]
            total[tile, pl.ds(d, own, stride=directions), :] = value
    for tile in range(out_ref.shape[2] // LANES):
        value = total[tile].reshape(own, directions, LANES)
        out_ref[:, :, tile * LANES:(tile + 1) * LANES] = value.astype(out_ref.dtype)


def decode(columns, sources, late_parts, late, gram_rows, decoded, own, row_shape, surface_rows, pupil, norm, staged):
    blocks = decoded.shape[0]
    mirrors, shard_rows, slots, samples = row_shape
    padded = gram_rows.shape[1]
    directions = sum(line.shape[0] for line in columns)
    extra = -(-directions * (shard_rows // 2 + 1) // 16) * 16
    phases = LANES // math.gcd(pupil, LANES)
    width = surface_rows // 2 * pupil
    lanes = phases * pupil
    flops = 2 * padded * 2 * mirrors * samples * pupil * directions * surface_rows // 2
    vmem = pl.BlockSpec(memory_space=pltpu.VMEM)
    ends = [
        pl.BlockSpec(
            (source.shape[0], extra, LANES),
            functools.partial(lambda last, s: (0, last, 0), source.shape[1] // extra - 1),
        )
        for source in sources
    ]
    counts = (len(columns), len(sources), len(late_parts))
    return pl.pallas_call(
        functools.partial(decode_kernel, row_shape, surface_rows, own, late, staged, norm, counts),
        grid=(width // lanes,),
        out_shape=jax.ShapeDtypeStruct((own, directions, width), jnp.bfloat16),
        in_specs=[vmem] * len(columns) + ends + [vmem] * len(late_parts) + [vmem, pl.BlockSpec(memory_space=pl.ANY)],
        out_specs=pl.BlockSpec((own, directions, lanes), lambda s: (0, 0, s)),
        scratch_shapes=[
            pltpu.VMEM(decoded.shape, jnp.bfloat16),
            pltpu.VMEM((directions, 2, pupil // 2, mirrors * samples), jnp.bfloat16),
            pltpu.VMEM((lanes // LANES, own * directions, LANES), jnp.float32),
            pltpu.VMEM((blocks, extra, LANES), jnp.int32),
            pltpu.SMEM((blocks, extra, LANES), jnp.int32),
            pltpu.SemaphoreType.DMA((blocks + 1,)),
        ],
        compiler_params=pltpu.CompilerParams(vmem_limit_bytes=VMEM_BYTES),
        cost_estimate=pl.CostEstimate(flops=flops, bytes_accessed=2 * own * directions * width, transcendentals=0),
        name="decode",
    )(*columns, *sources, *late_parts, gram_rows, decoded)


def swap(block, axis, distance):
    return lax.ppermute(block, axis, [(i, i ^ distance) for i in range(lax.axis_size(axis))])


def shards(influence, foot_rows, foot_columns, actuator_codes, poke_rows, subaperture_valid):
    mirrors, shard_rows, samples, slots = influence.shape
    row_shape = (mirrors, shard_rows, slots, samples)
    directions, devices = lax.axis_size("dir"), lax.axis_size("row")
    surface_rows = shard_rows * devices
    pupil = foot_columns.shape[2]
    norm = 0.5 * poke_rows.shape[0] ** (-0.5)
    own = actuator_codes.size // (directions * devices)
    staged = devices == 8 and directions & (directions - 1) == 0
    turned = jnp.swapaxes(influence, 2, 3)
    codes, pokes = actuator_codes.reshape(-1, LANES), poke_rows.reshape(-1, LANES)
    lines = small_lines(foot_rows, foot_columns, subaperture_valid)
    if not staged:
        lines = [lax.all_gather(lines, "dir")]
        every = lax.all_gather(pack(turned, lines), "row")
        gram_rows = gram(codes, *own_side(codes, pokes, own))
        decoded = bands(gram_rows, [every], None, 0, staged, row_shape, surface_rows)
        return decode(
            lines, [every], [], 0, gram_rows, decoded, own, row_shape, surface_rows, pupil, norm, staged
        )

    lines = [lines[None]] + [swap(lines, "dir", e)[None] for e in range(1, directions)]
    sides = own_side(codes, pokes, own)
    lines, sides = lax.optimization_barrier((lines, sides))
    packed = pack(turned, lines)
    beside, across, sibling = (swap(packed, "row", distance) for distance in (2, 4, 1))
    gram_rows = gram(codes, *sides)
    decoded = bands(gram_rows, [packed[None], sibling[None]], None, 0, staged, row_shape, surface_rows)
    decoded, beside, across = lax.optimization_barrier((decoded, beside, across))
    half = (mirrors * shard_rows + 2) * samples // 2
    upper, lower = swap(beside[:half], "row", 4), swap(across[half:], "row", 2)
    beside_sibling, across_sibling = swap(beside, "row", 1), swap(across, "row", 1)
    sources = [source[None] for source in (beside, beside_sibling, across, across_sibling)]
    decoded = bands(gram_rows, sources, decoded, 2, staged, row_shape, surface_rows)
    decoded, upper, lower = lax.optimization_barrier((decoded, upper, lower))
    late = [upper, lower, swap(upper, "row", 1), swap(lower, "row", 1)]
    return decode(
        lines, [packed[None], sibling[None], *sources], late, 2, gram_rows, decoded, own, row_shape, surface_rows,
        pupil, norm, staged,
    )


def solution(mesh):
    return jax.shard_map(
        shards,
        mesh=mesh,
        in_specs=(
            P(None, "row", None, None),
            P("dir", None, "row"),
            P("dir", None, None),
            P(),
            P(),
            P("dir", "row", None),
        ),
        out_specs=P(("dir", "row"), None, None),
        check_vma=False,
    )
```

```python
import functools
import math

import jax
import jax.numpy as jnp
import numpy as np
from jax import lax
from jax.experimental import pallas as pl
from jax.experimental.pallas import tpu as pltpu
from jax.sharding import PartitionSpec as P

NAR = 48
NA = 48
BAND = 3
BITS = 13
SCALE = 7
NARROW = jnp.float8_e5m2
LANES = 128
WINDOW = 256
VMEM_BYTES = 56 * 1024 * 1024


def parity(codes, rows):
    return lax.population_count(codes & rows) & 1


def lines_kernel(rows_ref, columns_ref, valid_ref, lines_ref):
    mirrors, rows = rows_ref.shape[0], rows_ref.shape[2]
    lines_ref[...] = jnp.zeros(lines_ref.shape, lines_ref.dtype)
    lines_ref[mirrors:mirrors + valid_ref.shape[1], :valid_ref.shape[2]] = valid_ref[0]
    for k in range(mirrors):
        lines_ref[k:k + 1, :columns_ref.shape[2]] = columns_ref[k]
        lines_ref[mirrors + valid_ref.shape[1]:mirrors + valid_ref.shape[1] + 1, k * rows:(k + 1) * rows] = rows_ref[k]


def small_lines(foot_rows, foot_columns, valid):
    vmem = pl.BlockSpec(memory_space=pltpu.VMEM)
    count = foot_rows.shape[1] + valid.shape[1] + 1
    return pl.pallas_call(
        lines_kernel,
        out_shape=jax.ShapeDtypeStruct((-(-count // 8) * 8, WINDOW), jnp.int32),
        in_specs=[vmem] * 3,
        out_specs=vmem,
        name="small_lines",
    )(jnp.swapaxes(foot_rows, 0, 1), jnp.swapaxes(foot_columns, 0, 1), valid)


def pack_kernel(block_ref, *refs):
    lines_refs, packed_ref = refs[:-1], refs[-1]
    mirrors, rows, slots, samples = block_ref.shape
    groups = mirrors * rows // 2
    identity = (
        lax.broadcasted_iota(jnp.int32, (samples, samples), 0) == lax.broadcasted_iota(jnp.int32, (samples, samples), 1)
    ).astype(jnp.float32).astype(jnp.bfloat16)
    for part in range(2):
        base = part * (groups + 1) * samples
        tails = []
        for group in range(groups):
            k, l = divmod(part * groups + group, rows)
            turned = lax.dot_general(
                identity, block_ref[k, l], (((1,), (1,)), ((), ())), preferred_element_type=jnp.float32
            ).astype(jnp.bfloat16)
            packed_ref[pl.ds(base + group * samples, samples), :] = turned[:, :LANES]
            tails.append(turned[:, LANES:])
        tails.append(jnp.zeros((samples, LANES - groups * (slots - LANES)), jnp.bfloat16))
        packed_ref[pl.ds(base + groups * samples, samples), :] = jnp.concatenate(tails, axis=1)
    count = rows // 2 + 1
    lines = [ref[n, mirrors:mirrors + count, :LANES] for ref in lines_refs for n in range(ref.shape[0])]
    extra = packed_ref.shape[0] - 2 * (groups + 1) * samples
    lines.append(jnp.zeros((extra - count * len(lines), LANES), jnp.int32))
    packed_ref[pl.ds(packed_ref.shape[0] - extra, extra), :] = (
        jnp.concatenate(lines, axis=0).astype(jnp.float32).astype(jnp.bfloat16)
    )


def pack(block, lines):
    mirrors, rows, slots, samples = block.shape
    vmem = pl.BlockSpec(memory_space=pltpu.VMEM)
    extra = -(-sum(line.shape[0] for line in lines) * (rows // 2 + 1) // 16) * 16
    return pl.pallas_call(
        pack_kernel,
        out_shape=jax.ShapeDtypeStruct(((mirrors * rows + 2) * samples + extra, LANES), block.dtype),
        in_specs=[vmem] * (1 + len(lines)),
        out_specs=vmem,
        compiler_params=pltpu.CompilerParams(vmem_limit_bytes=VMEM_BYTES),
        cost_estimate=pl.CostEstimate(flops=0, bytes_accessed=3 * block.size, transcendentals=0),
        name="pack_influence",
    )(block, *lines)


def column_of(row):
    return jnp.transpose(jnp.broadcast_to(row, (LANES, LANES)), (1, 0))


def signs_kernel(table_ref, pokes_ref, codes_ref, words, own_signs, own_sums):
    planes = pokes_ref.shape[0]
    mirrors, rows, columns = table_ref.shape
    for line in range(codes_ref.shape[0]):
        pieces, at = [], line * LANES
        while at < (line + 1) * LANES:
            row, lane = divmod(at, columns)
            length = min(columns - lane, (line + 1) * LANES - at)
            pieces.append(table_ref[row // rows, row % rows:row % rows + 1, lane:lane + length])
            at += length
        codes_ref[line:line + 1, :] = jnp.concatenate(pieces, axis=1)
    half = LANES // 2
    own = own_signs.shape[0]
    plane = lax.broadcasted_iota(jnp.int32, pokes_ref.shape, 0)
    for bit in range(BITS):
        low = jnp.sum((pokes_ref[...] >> bit & 1) << plane, axis=0, keepdims=True)
        word = low | pltpu.roll(jnp.broadcast_to(low, (8, LANES)), half, 1)[:1] << planes
        words[bit] = column_of(word)[:half]
    count = codes_ref.shape[0] * LANES // (lax.axis_size("dir") * lax.axis_size("row"))
    first = (lax.axis_index("dir") * lax.axis_size("row") + lax.axis_index("row")) * count
    lane = lax.broadcasted_iota(jnp.int32, (8, LANES), 1)
    shift = first % LANES
    lines = [
        pltpu.roll(
            jnp.broadcast_to(
                codes_ref[pl.ds(jnp.minimum(first // LANES + n, codes_ref.shape[0] - 1), 1), :], (8, LANES)
            ),
            LANES - shift, 1,
        )
        for n in range(-(-own // LANES) + 1)
    ]
    own_column = jnp.concatenate(
        [column_of(jnp.where(lane < LANES - shift, lines[n], lines[n + 1])[:1]) for n in range(len(lines) - 1)],
        axis=0,
    )[:own]
    total = jnp.zeros((own, LANES), jnp.float32)
    for at in range(planes):
        signs = (1 - 2 * parity(own_column, pokes_ref[at:at + 1, :])).astype(jnp.float32)
        own_signs[:, at * LANES:(at + 1) * LANES] = (signs * 2.0 ** (SCALE - at)).astype(NARROW)
        total = total + signs
    own_sums[...] = jnp.broadcast_to(jnp.sum(total, axis=1, keepdims=True), own_sums.shape)


def own_side(table, pokes, own):
    own = -(-own // 32) * 32
    vmem = pl.BlockSpec(memory_space=pltpu.VMEM)
    return pl.pallas_call(
        signs_kernel,
        out_shape=[
            jax.ShapeDtypeStruct((table.size // LANES, LANES), jnp.int32),
            jax.ShapeDtypeStruct((BITS, LANES // 2, LANES), jnp.int32),
            jax.ShapeDtypeStruct((own, pokes.size), NARROW),
            jax.ShapeDtypeStruct((own, LANES), jnp.float32),
        ],
        in_specs=[vmem] * 2,
        out_specs=[vmem] * 4,
        compiler_params=pltpu.CompilerParams(vmem_limit_bytes=VMEM_BYTES),
        name="own_signs",
    )(table, pokes)


def gram_kernel(row_shape, surface_rows, codes_ref, words, own_signs, own_sums, packed_ref, gram_out, first_ref, gram_ref, semaphores):
    mirror = pl.program_id(0)
    half = LANES // 2
    own, pokes = own_signs.shape
    planes = pokes // LANES
    lines = codes_ref.shape[0] // row_shape[0]
    height = gram_ref.shape[0] // row_shape[0]

    def chunk(index, _):
        word = []
        for side in range(WINDOW // LANES):
            line = mirror * lines + index * (WINDOW // LANES) + side
            code = jnp.broadcast_to(codes_ref[pl.ds(line, 1), :], (8, LANES))
            value = None
            for bit in range(BITS):
                mask = jnp.concatenate([code << (31 - bit) >> 31] * (half // 8), axis=0)
                part = words[bit] & mask
                value = part if value is None else value ^ part
            word.append(value)
        word = jnp.concatenate(word, axis=1)
        words_of = (word, word >> planes)
        total = jnp.zeros((own, WINDOW), jnp.float32)
        for at in range(0, planes, 2):
            bits = [
                (side & (1 << plane)).astype(jnp.float32).astype(NARROW)
                for plane in (at, at + 1) for side in words_of
            ]
            total = total + jnp.dot(
                own_signs[:, at * LANES:(at + 2) * LANES], jnp.concatenate(bits, axis=0),
                preferred_element_type=jnp.float32,
            )
        sums = jnp.concatenate([own_sums[...]] * (WINDOW // LANES), axis=1)
        turned = jnp.transpose(sums - 2.0 ** (1 - SCALE) * total)
        at = pl.multiple_of(mirror * height + index * WINDOW, WINDOW)
        gram_ref[pl.ds(at, WINDOW), :] = turned.astype(jnp.bfloat16)
        return 0

    lax.fori_loop(0, height // WINDOW, chunk, 0, unroll=3)

    def send(k):
        part = pl.ds(pl.multiple_of(k * height, height), height)
        return pltpu.make_async_copy(gram_ref.at[part], gram_out.at[part], semaphores.at[k])

    send(mirror).start()
    block = lax.axis_index("row")
    for l in range(row_shape[1]):
        for k in range(row_shape[0]):
            @pl.when(mirror == k)
            def _():
                first_ref[0, l] = band_product(
                    [packed_ref], k * row_shape[1] + l, row_shape, block, surface_rows, gram_ref
                )

    @pl.when(mirror == pl.num_programs(0) - 1)
    def _():
        for k in range(row_shape[0]):
            send(k).wait()


def gram(codes, words, own_signs, own_sums, packed, row_shape, surface_rows):
    acts, (own, count) = codes.size, own_signs.shape
    mirrors, shard_rows, slots, samples = row_shape
    vmem = pl.BlockSpec(memory_space=pltpu.VMEM)
    return pl.pallas_call(
        functools.partial(gram_kernel, row_shape, surface_rows),
        grid=(mirrors,),
        out_shape=[
            jax.ShapeDtypeStruct((acts, own), jnp.bfloat16),
            jax.ShapeDtypeStruct((1, mirrors * shard_rows, samples, own), jnp.bfloat16),
        ],
        in_specs=[vmem] * 5,
        out_specs=[
            pl.BlockSpec(memory_space=pl.ANY),
            pl.BlockSpec((1, shard_rows, samples, own), lambda s: (0, s, 0, 0)),
        ],
        scratch_shapes=[pltpu.VMEM((acts, own), jnp.bfloat16), pltpu.SemaphoreType.DMA((mirrors,))],
        compiler_params=pltpu.CompilerParams(vmem_limit_bytes=VMEM_BYTES),
        cost_estimate=pl.CostEstimate(
            flops=2 * own * acts * count, bytes_accessed=2 * own * acts, transcendentals=0
        ),
        name="gram_rows",
    )(codes, words, own_signs, own_sums, packed)


def position(axis, staged):
    return lax.axis_index(axis) if staged else 0


def row_block(place, staged):
    if not staged:
        return place
    return (place ^ 7 if place in (3, 4) else place) ^ lax.axis_index("row")


def row_place(block, staged):
    if not staged:
        return block
    place = block ^ lax.axis_index("row")
    return jnp.where((place == 3) | (place == 4), place ^ 7, place)


def band_product(parts, q, row_shape, block, surface_rows, gram_ref):
    mirrors, shard_rows, slots, samples = row_shape
    groups = mirrors * shard_rows // 2
    own = gram_ref.shape[1]
    narrow = slots - LANES
    k, l = divmod(q, shard_rows)
    band = jnp.clip((block * shard_rows + l) * NAR // surface_rows - 1, 0, NAR - BAND)
    column = pl.multiple_of((k * NAR + band) * NA, 16)
    part, group = divmod(q, groups)
    source, base = (parts[0], part * (groups + 1) * samples) if len(parts) == 1 else (parts[part], 0)
    left = jnp.concatenate(
        [source[pl.ds(base + group * samples, samples), :], source[pl.ds(base + groups * samples, samples), :]],
        axis=1,
    )
    right = [gram_ref[pl.ds(column, LANES), :]]
    if group:
        right.append(jnp.zeros((group * narrow, own), jnp.bfloat16))
    right.append(gram_ref[pl.ds(column + LANES, narrow), :])
    right.append(jnp.zeros((LANES - (group + 1) * narrow, own), jnp.bfloat16))
    return jnp.dot(left, jnp.concatenate(right, axis=0), preferred_element_type=jnp.float32).astype(jnp.bfloat16)


def fetch_gram(gram_any, gram_ref, semaphores, mirrors):
    height = gram_ref.shape[0] // mirrors
    return [
        pltpu.make_async_copy(
            gram_any.at[pl.ds(k * height, height)], gram_ref.at[pl.ds(k * height, height)], semaphores.at[k]
        )
        for k in range(mirrors)
    ]


def bands_kernel(row_shape, surface_rows, first, counts, staged, gram_any, *refs):
    mirrors, shard_rows = row_shape[:2]
    sources = [ref.at[n] for ref, count in zip(refs, counts) for n in range(count)]
    out_ref, gram_ref, blocks, gram_semaphores, block_semaphores = refs[len(counts):]
    step = pl.program_id(0)
    gram_copies = fetch_gram(gram_any, gram_ref, gram_semaphores, mirrors)

    def fetch(n):
        return pltpu.make_async_copy(sources[n], blocks.at[n], block_semaphores.at[n])

    @pl.when(step == 0)
    def _():
        fetch(0).start()
        for copy in gram_copies:
            copy.start()
        for n in range(1, len(sources)):
            fetch(n).start()

    for n in range(len(sources)):
        @pl.when(step == n)
        def _():
            fetch(n).wait()
            block = row_block(first + n, staged)
            for q in range(mirrors * shard_rows):
                if n == 0 and q % shard_rows == 0:
                    gram_copies[q // shard_rows].wait()
                out_ref[0, q] = band_product([blocks.at[n]], q, row_shape, block, surface_rows, gram_ref)


def bands(gram_rows, sources, first, staged, row_shape, surface_rows):
    acts, own = gram_rows.shape
    counts = [source.shape[0] for source in sources]
    rows = row_shape[0] * row_shape[1]
    flops = 2 * own * WINDOW * row_shape[3] * rows * sum(counts)
    return pl.pallas_call(
        functools.partial(bands_kernel, row_shape, surface_rows, first, counts, staged),
        grid=(sum(counts),),
        out_shape=jax.ShapeDtypeStruct((sum(counts), rows, row_shape[3], own), jnp.bfloat16),
        in_specs=[pl.BlockSpec(memory_space=pl.ANY)] * (1 + len(sources)),
        out_specs=pl.BlockSpec((1, rows, row_shape[3], own), lambda s: (s, 0, 0, 0)),
        scratch_shapes=[
            pltpu.VMEM((acts, own), jnp.bfloat16),
            pltpu.VMEM((sum(counts),) + sources[0].shape[1:], jnp.bfloat16),
            pltpu.SemaphoreType.DMA((row_shape[0],)),
            pltpu.SemaphoreType.DMA((sum(counts),)),
        ],
        compiler_params=pltpu.CompilerParams(vmem_limit_bytes=VMEM_BYTES),
        cost_estimate=pl.CostEstimate(
            flops=flops, bytes_accessed=2 * own * WINDOW * rows * sum(counts), transcendentals=0
        ),
        name="bands",
    )(gram_rows, *sources)


def build_differences(columns, differences, mirrors, samples, pupil):
    half = pupil // 2
    slope = lax.broadcasted_iota(jnp.int32, (half, pupil), 0)
    lane = lax.broadcasted_iota(jnp.int32, (half, pupil), 1)
    at = lax.broadcasted_iota(jnp.int32, (half, mirrors * samples), 1)
    for d, lines in enumerate(columns):
        sides = []
        for side in range(2):
            hit = None
            for k in range(mirrors):
                line = jnp.broadcast_to(lines[k:k + 1], (half, pupil))
                column = jnp.sum(jnp.where(lane == slope * 2 + side, line, 0), axis=1, keepdims=True)
                here = (at == column + k * samples).astype(jnp.float32)
                hit = here if hit is None else hit + here
            sides.append(hit)
        differences[d, 0] = (sides[1] - sides[0]).astype(jnp.bfloat16)
        differences[d, 1] = (sides[1] + sides[0]).astype(jnp.bfloat16)


def decode_kernel(row_shape, surface_rows, own, staged, norm, counts, late_parts, *refs):
    mirrors, shard_rows, slots, samples = row_shape
    columns_refs, refs = refs[:counts[0]], refs[counts[0]:]
    lines_refs, refs = refs[:counts[1]], refs[counts[1]:]
    late_refs, refs = refs[:counts[2]], refs[counts[2]:]
    ready_refs, refs = refs[:counts[3]], refs[counts[3]:]
    (gram_any, out_ref, gram_ref, decoded, differences, total, packed_lines, lines, scalars, *refs) = refs
    late_blocks, refs = refs[:counts[2]], refs[counts[2]:]
    gram_semaphores, ready_semaphores, line_semaphores, late_semaphores, scalar_semaphore = refs
    group = pl.program_id(0)
    directions, pupil = differences.shape[0], 2 * differences.shape[2]
    phases = out_ref.shape[2] // pupil
    blocks = surface_rows // shard_rows
    late = len(late_parts)
    ready = blocks - late
    width = shard_rows // 2 + 1
    extra = lines.shape[1]

    @pl.when(group == 0)
    def _():
        def started(copies):
            for copy in copies:
                copy.start()
            return copies

        ends = [ref.at[n, pl.ds(ref.shape[1] - extra, extra)] for ref in lines_refs for n in range(ref.shape[0])]
        line_copies = started([
            pltpu.make_async_copy(end, packed_lines.at[n], line_semaphores.at[n]) for n, end in enumerate(ends)
        ])
        late_copies = started([
            pltpu.make_async_copy(late_refs[n], late_blocks[n], late_semaphores.at[n]) for n in range(counts[2])
        ])
        gram_copies = started(fetch_gram(gram_any, gram_ref, gram_semaphores, mirrors)) if late else []
        ready_copies = started([
            pltpu.make_async_copy(block, decoded.at[n], ready_semaphores.at[n])
            for n, block in enumerate([ref.at[m] for ref in ready_refs for m in range(ref.shape[0])])
        ])
        columns = [ref[n, :, :pupil] for ref in columns_refs for n in range(ref.shape[0])]
        build_differences(columns, differences, mirrors, samples, pupil)
        for copy in line_copies + late_copies:
            copy.wait()
        held = [packed_lines[n] for n in range(len(ends))]
        at = 0
        for part in late_parts:
            at += part
            last = late_blocks[at - 1]
            held.append(last[pl.ds(last.shape[0] - extra, extra), :])
        for n, value in enumerate(held):
            lines[n] = value.astype(jnp.float32).astype(jnp.int32)
        to_scalars = pltpu.make_async_copy(lines, scalars, scalar_semaphore.at[0])
        to_scalars.start()
        at = 0
        for n, part in enumerate(late_parts):
            parts, at = late_blocks[at:at + part], at + part
            for q in range(mirrors * shard_rows):
                if n == 0 and q % shard_rows == 0:
                    gram_copies[q // shard_rows].wait()
                decoded[ready + n, q] = band_product(
                    parts, q, row_shape, row_block(ready + n, staged), surface_rows, gram_ref
                )
        to_scalars.wait()
        for copy in ready_copies:
            copy.wait()

    for d in range(directions):
        held = d ^ position("dir", staged)
        products, factors = [], []
        for phase in range(phases):
            i = group * phases + phase
            block = row_place(2 * i // shard_rows, staged)
            sums, changes = [], []
            for k in range(mirrors):
                picked = []
                for y in range(2):
                    row = scalars[block, held * width + width - 1, k * shard_rows + (2 * phase + y) % shard_rows]
                    picked.append(decoded[row_place(row // shard_rows, staged), k * shard_rows + row % shard_rows])
                sums.append(picked[0] + picked[1])
                changes.append(picked[1] - picked[0])
            for kind, rows in enumerate((sums, changes)):
                products.append(
                    jnp.dot(
                        differences[held, kind], jnp.concatenate(rows, axis=0), preferred_element_type=jnp.float32
                    )
                )
            valid = lines[block, pl.ds(held * width + phase % (shard_rows // 2), 1), :][:, :pupil // 2]
            factors += [valid.astype(jnp.float32) * norm] * 2
        product = jnp.concatenate(products, axis=0)
        factor = jnp.concatenate(factors, axis=1)
        for tile in range(out_ref.shape[2] // LANES):
            at = tile * LANES
            value = jnp.transpose(product[at:at + LANES])[:own] * factor[:, at:at + LANES]
            total[tile, pl.ds(d, own, stride=directions), :] = value
    for tile in range(out_ref.shape[2] // LANES):
        value = total[tile].reshape(own, directions, LANES)
        out_ref[:, :, tile * LANES:(tile + 1) * LANES] = value.astype(out_ref.dtype)


def decode(columns, sources, late, ready, gram_rows, own, row_shape, surface_rows, pupil, norm, staged):
    mirrors, shard_rows, slots, samples = row_shape
    acts, padded = gram_rows.shape
    directions = sum(line.shape[0] for line in columns)
    blocks = surface_rows // shard_rows
    extra = -(-directions * (shard_rows // 2 + 1) // 16) * 16
    phases = LANES // math.gcd(pupil, LANES)
    width = surface_rows // 2 * pupil
    lanes = phases * pupil
    flops = 2 * padded * mirrors * samples * pupil * directions * surface_rows // 2
    vmem, anywhere = pl.BlockSpec(memory_space=pltpu.VMEM), pl.BlockSpec(memory_space=pl.ANY)
    parts = [part for block in late for part in block]
    counts = (len(columns), len(sources), len(parts), len(ready))
    semaphores = [mirrors, blocks, blocks, max(len(parts), 1), 1]
    return pl.pallas_call(
        functools.partial(
            decode_kernel, row_shape, surface_rows, own, staged, norm, counts, [len(block) for block in late]
        ),
        grid=(width // lanes,),
        out_shape=jax.ShapeDtypeStruct((own, directions, width), jnp.bfloat16),
        in_specs=[vmem] * counts[0] + [anywhere] * (sum(counts[1:]) + 1),
        out_specs=pl.BlockSpec((own, directions, lanes), lambda s: (0, 0, s)),
        scratch_shapes=[
            pltpu.VMEM((acts, padded), jnp.bfloat16),
            pltpu.VMEM((blocks, mirrors * shard_rows, samples, padded), jnp.bfloat16),
            pltpu.VMEM((directions, 2, pupil // 2, mirrors * samples), jnp.bfloat16),
            pltpu.VMEM((lanes // LANES, own * directions, LANES), jnp.float32),
            pltpu.VMEM((blocks, extra, LANES), jnp.bfloat16),
            pltpu.VMEM((blocks, extra, LANES), jnp.int32),
            pltpu.SMEM((blocks, extra, LANES), jnp.int32),
            *[pltpu.VMEM(part.shape, part.dtype) for part in parts],
            *[pltpu.SemaphoreType.DMA((count,)) for count in semaphores],
        ],
        compiler_params=pltpu.CompilerParams(vmem_limit_bytes=VMEM_BYTES),
        cost_estimate=pl.CostEstimate(flops=flops, bytes_accessed=2 * own * directions * width, transcendentals=0),
        name="decode",
    )(*columns, *sources, *parts, *ready, gram_rows)


def swap(block, axis, distance):
    return lax.ppermute(block, axis, [(i, i ^ distance) for i in range(lax.axis_size(axis))])


def shards(influence, foot_rows, foot_columns, actuator_codes, poke_rows, subaperture_valid):
    mirrors, shard_rows, samples, slots = influence.shape
    row_shape = (mirrors, shard_rows, slots, samples)
    directions, devices = lax.axis_size("dir"), lax.axis_size("row")
    surface_rows = shard_rows * devices
    pupil = foot_columns.shape[2]
    norm = 0.5 * poke_rows.shape[0] ** (-0.5)
    own = actuator_codes.size // (directions * devices)
    staged = devices == 8 and directions & (directions - 1) == 0
    turned = jnp.swapaxes(influence, 2, 3)
    pokes = poke_rows.reshape(-1, LANES)
    lines = small_lines(foot_rows, foot_columns, subaperture_valid)
    if not staged:
        lines = [lax.all_gather(lines, "dir")]
        packed = pack(turned, lines)
        every = lax.all_gather(packed, "row")
        gram_rows, _ = gram(*own_side(actuator_codes, pokes, own), packed, row_shape, surface_rows)
        ready = [bands(gram_rows, [every], 0, staged, row_shape, surface_rows)]
        return decode(lines, [every], [], ready, gram_rows, own, row_shape, surface_rows, pupil, norm, staged)

    lines = [lines[None]] + [swap(lines, "dir", e)[None] for e in range(1, directions)]
    sides = own_side(actuator_codes, pokes, own)
    lines, sides = lax.optimization_barrier((lines, sides))
    packed = pack(turned, lines)
    beside, across, sibling = (swap(packed, "row", distance) for distance in (2, 4, 1))
    gram_rows, first = gram(*sides, packed, row_shape, surface_rows)
    gram_rows, beside, across = lax.optimization_barrier((gram_rows, beside, across))
    half = (mirrors * shard_rows + 2) * samples // 2
    upper, lower = swap(beside[:half], "row", 4), swap(across[half:], "row", 2)
    beside_sibling, across_sibling = swap(beside, "row", 1), swap(across, "row", 1)
    sources = [source[None] for source in (sibling, beside, across)]
    ready = bands(gram_rows, sources, 1, staged, row_shape, surface_rows)
    ready, upper, lower = lax.optimization_barrier((ready, upper, lower))
    late = [[beside_sibling], [across_sibling], [upper, lower], [swap(upper, "row", 1), swap(lower, "row", 1)]]
    return decode(
        lines, [packed[None], *sources], late, [first, ready], gram_rows, own, row_shape, surface_rows, pupil, norm,
        staged,
    )


def solution(mesh):
    return jax.shard_map(
        shards,
        mesh=mesh,
        in_specs=(
            P(None, "row", None, None),
            P("dir", None, "row"),
            P("dir", None, None),
            P(),
            P(),
            P("dir", "row", None),
        ),
        out_specs=P(("dir", "row"), None, None),
        check_vma=False,
    )
```

```python
import functools
import math

import jax
import jax.numpy as jnp
import numpy as np
from jax import lax
from jax.experimental import pallas as pl
from jax.experimental.pallas import tpu as pltpu
from jax.sharding import PartitionSpec as P

NAR = 48
NA = 48
BAND = 3
BITS = 13
NARROW = jnp.float8_e5m2
LANES = 128
WINDOW = 256
VMEM_BYTES = 63 * 1024 * 1024


def parity(codes, rows):
    return lax.population_count(codes & rows) & 1


def pack_kernel(block_ref, rows_ref, columns_ref, valid_ref, packed_ref, lines_ref):
    mirrors, rows, slots, samples = block_ref.shape
    groups = mirrors * rows // 2
    lines_ref[...] = jnp.zeros(lines_ref.shape, lines_ref.dtype)
    lines_ref[mirrors:mirrors + valid_ref.shape[1], :valid_ref.shape[2]] = valid_ref[0]
    for k in range(mirrors):
        lines_ref[k:k + 1, :columns_ref.shape[2]] = columns_ref[k]
        lines_ref[mirrors + valid_ref.shape[1]:mirrors + valid_ref.shape[1] + 1, k * rows:(k + 1) * rows] = rows_ref[k]
    identity = (
        lax.broadcasted_iota(jnp.int32, (samples, samples), 0) == lax.broadcasted_iota(jnp.int32, (samples, samples), 1)
    ).astype(jnp.float32).astype(jnp.bfloat16)
    for part in range(2):
        base = part * (groups + 1) * samples
        tails = []
        for group in range(groups):
            k, l = divmod(part * groups + group, rows)
            turned = lax.dot_general(
                identity, block_ref[k, l], (((1,), (1,)), ((), ())), preferred_element_type=jnp.float32
            ).astype(jnp.bfloat16)
            packed_ref[pl.ds(base + group * samples, samples), :] = turned[:, :LANES]
            tails.append(turned[:, LANES:])
        tails.append(jnp.zeros((samples, LANES - groups * (slots - LANES)), jnp.bfloat16))
        packed_ref[pl.ds(base + groups * samples, samples), :] = jnp.concatenate(tails, axis=1)


def pack(block, foot_rows, foot_columns, valid):
    mirrors, rows, slots, samples = block.shape
    vmem = pl.BlockSpec(memory_space=pltpu.VMEM)
    count = mirrors + valid.shape[1] + 1
    return pl.pallas_call(
        pack_kernel,
        out_shape=[
            jax.ShapeDtypeStruct(((mirrors * rows + 2) * samples, LANES), block.dtype),
            jax.ShapeDtypeStruct((-(-count // 8) * 8, WINDOW), jnp.int32),
        ],
        in_specs=[vmem] * 4,
        out_specs=[vmem] * 2,
        compiler_params=pltpu.CompilerParams(vmem_limit_bytes=VMEM_BYTES),
        cost_estimate=pl.CostEstimate(flops=0, bytes_accessed=3 * block.size, transcendentals=0),
        name="pack_influence",
    )(block, jnp.swapaxes(foot_rows, 0, 1), jnp.swapaxes(foot_columns, 0, 1), valid)


def column_of(row):
    return jnp.transpose(jnp.broadcast_to(row, (LANES, LANES)), (1, 0))


def signs_kernel(table_ref, pokes_ref, codes_ref, words, own_signs, own_sums):
    planes = pokes_ref.shape[0]
    mirrors, rows, columns = table_ref.shape
    for line in range(codes_ref.shape[0]):
        pieces, at = [], line * LANES
        while at < (line + 1) * LANES:
            row, lane = divmod(at, columns)
            length = min(columns - lane, (line + 1) * LANES - at)
            pieces.append(table_ref[row // rows, row % rows:row % rows + 1, lane:lane + length])
            at += length
        codes_ref[line:line + 1, :] = jnp.concatenate(pieces, axis=1)
    half = LANES // 2
    own = own_signs.shape[0]
    plane = lax.broadcasted_iota(jnp.int32, pokes_ref.shape, 0)
    for bit in range(BITS):
        low = jnp.sum((pokes_ref[...] >> bit & 1) << plane, axis=0, keepdims=True)
        word = low | pltpu.roll(jnp.broadcast_to(low, (8, LANES)), half, 1)[:1] << planes
        words[bit] = column_of(word)[:half]
    count = codes_ref.shape[0] * LANES // (lax.axis_size("dir") * lax.axis_size("row"))
    first = (lax.axis_index("dir") * lax.axis_size("row") + lax.axis_index("row")) * count
    lane = lax.broadcasted_iota(jnp.int32, (8, LANES), 1)
    shift = first % LANES
    lines = [
        pltpu.roll(
            jnp.broadcast_to(
                codes_ref[pl.ds(jnp.minimum(first // LANES + n, codes_ref.shape[0] - 1), 1), :], (8, LANES)
            ),
            LANES - shift, 1,
        )
        for n in range(-(-own // LANES) + 1)
    ]
    own_column = jnp.concatenate(
        [column_of(jnp.where(lane < LANES - shift, lines[n], lines[n + 1])[:1]) for n in range(len(lines) - 1)],
        axis=0,
    )[:own]
    total = jnp.zeros((own, LANES), jnp.float32)
    for at in range(planes):
        signs = (1 - 2 * parity(own_column, pokes_ref[at:at + 1, :])).astype(jnp.float32)
        own_signs[:, at * LANES:(at + 1) * LANES] = signs.astype(NARROW)
        total = total + signs
    own_sums[...] = jnp.broadcast_to(jnp.sum(total, axis=1, keepdims=True), own_sums.shape)


def own_side(table, pokes, own):
    own = -(-own // 32) * 32
    vmem = pl.BlockSpec(memory_space=pltpu.VMEM)
    return pl.pallas_call(
        signs_kernel,
        out_shape=[
            jax.ShapeDtypeStruct((table.size // LANES, LANES), jnp.int32),
            jax.ShapeDtypeStruct((BITS, LANES // 2, LANES), jnp.int32),
            jax.ShapeDtypeStruct((own, pokes.size), NARROW),
            jax.ShapeDtypeStruct((own, LANES), jnp.float32),
        ],
        in_specs=[vmem] * 2,
        out_specs=[vmem] * 4,
        compiler_params=pltpu.CompilerParams(vmem_limit_bytes=VMEM_BYTES),
        name="own_signs",
    )(table, pokes)


def gram_kernel(row_shape, surface_rows, codes_ref, words, own_signs, own_sums, packed_ref, gram_out, first_ref, gram_ref, semaphores):
    mirror = pl.program_id(0)
    half = LANES // 2
    own, pokes = own_signs.shape
    planes = pokes // LANES
    lines = codes_ref.shape[0] // row_shape[0]
    height = gram_ref.shape[0] // row_shape[0]

    def chunk(index, _):
        word = []
        for side in range(WINDOW // LANES):
            line = mirror * lines + index * (WINDOW // LANES) + side
            code = jnp.broadcast_to(codes_ref[pl.ds(line, 1), :], (8, LANES))
            value = None
            for bit in range(BITS):
                mask = jnp.concatenate([code << (31 - bit) >> 31] * (half // 8), axis=0)
                part = words[bit] & mask
                value = part if value is None else value ^ part
            word.append(value)
        word = jnp.concatenate(word, axis=1)
        bits = [None] * (2 * planes)
        for byte in range(0, 2 * planes, 8):
            part = (word >> byte).astype(jnp.int8)
            for bit in range(8):
                at = byte + bit
                hit = (part & np.uint8(1 << bit).astype(np.int8)) != 0
                bits[at % planes * 2 + at // planes] = jnp.where(hit, NARROW(1.0), NARROW(0.0))
        total = jnp.dot(own_signs[...], jnp.concatenate(bits, axis=0), preferred_element_type=jnp.float32)
        sums = jnp.concatenate([own_sums[...]] * (WINDOW // LANES), axis=1)
        turned = jnp.transpose((sums - 2.0 * total).astype(jnp.bfloat16))
        at = pl.multiple_of(mirror * height + index * WINDOW, WINDOW)
        gram_ref[pl.ds(at, WINDOW), :] = turned
        return 0

    lax.fori_loop(0, height // WINDOW, chunk, 0, unroll=3)

    def send(k):
        part = pl.ds(pl.multiple_of(k * height, height), height)
        return pltpu.make_async_copy(gram_ref.at[part], gram_out.at[part], semaphores.at[k])

    send(mirror).start()
    block = lax.axis_index("row")
    for l in range(row_shape[1]):
        for k in range(row_shape[0]):
            @pl.when(mirror == k)
            def _():
                first_ref[0, l] = band_product(
                    [packed_ref], k * row_shape[1] + l, row_shape, block, surface_rows, gram_ref
                )

    @pl.when(mirror == pl.num_programs(0) - 1)
    def _():
        for k in range(row_shape[0]):
            send(k).wait()


def gram(codes, words, own_signs, own_sums, packed, row_shape, surface_rows):
    acts, (own, count) = codes.size, own_signs.shape
    mirrors, shard_rows, slots, samples = row_shape
    vmem = pl.BlockSpec(memory_space=pltpu.VMEM)
    return pl.pallas_call(
        functools.partial(gram_kernel, row_shape, surface_rows),
        grid=(mirrors,),
        out_shape=[
            jax.ShapeDtypeStruct((acts, own), jnp.bfloat16),
            jax.ShapeDtypeStruct((1, mirrors * shard_rows, samples, own), jnp.bfloat16),
        ],
        in_specs=[vmem] * 5,
        out_specs=[
            pl.BlockSpec(memory_space=pl.ANY),
            pl.BlockSpec((1, shard_rows, samples, own), lambda s: (0, s, 0, 0)),
        ],
        scratch_shapes=[pltpu.VMEM((acts, own), jnp.bfloat16), pltpu.SemaphoreType.DMA((mirrors,))],
        compiler_params=pltpu.CompilerParams(vmem_limit_bytes=VMEM_BYTES),
        cost_estimate=pl.CostEstimate(
            flops=2 * own * acts * count, bytes_accessed=2 * own * acts, transcendentals=0
        ),
        name="gram_rows",
    )(codes, words, own_signs, own_sums, packed)


def position(axis, staged):
    return lax.axis_index(axis) if staged else 0


def row_block(place, staged):
    if not staged:
        return place
    return (place ^ 7 if place in (3, 4) else place) ^ lax.axis_index("row")


def row_place(block, staged):
    if not staged:
        return block
    place = block ^ lax.axis_index("row")
    return jnp.where((place == 3) | (place == 4), place ^ 7, place)


def band_product(parts, q, row_shape, block, surface_rows, gram_ref):
    mirrors, shard_rows, slots, samples = row_shape
    groups = mirrors * shard_rows // 2
    own = gram_ref.shape[1]
    narrow = slots - LANES
    k, l = divmod(q, shard_rows)
    band = jnp.clip((block * shard_rows + l) * NAR // surface_rows - 1, 0, NAR - BAND)
    column = pl.multiple_of((k * NAR + band) * NA, 16)
    part, group = divmod(q, groups)
    source, base = (parts[0], part * (groups + 1) * samples) if len(parts) == 1 else (parts[part], 0)
    left = jnp.concatenate(
        [source[pl.ds(base + group * samples, samples), :], source[pl.ds(base + groups * samples, samples), :]],
        axis=1,
    )
    right = [gram_ref[pl.ds(column, LANES), :]]
    if group:
        right.append(jnp.zeros((group * narrow, own), jnp.bfloat16))
    right.append(gram_ref[pl.ds(column + LANES, narrow), :])
    right.append(jnp.zeros((LANES - (group + 1) * narrow, own), jnp.bfloat16))
    return jnp.dot(left, jnp.concatenate(right, axis=0), preferred_element_type=jnp.float32).astype(jnp.bfloat16)


def fetch_gram(gram_any, gram_ref, semaphores, mirrors):
    height = gram_ref.shape[0] // mirrors
    return [
        pltpu.make_async_copy(
            gram_any.at[pl.ds(k * height, height)], gram_ref.at[pl.ds(k * height, height)], semaphores.at[k]
        )
        for k in range(mirrors)
    ]


def bands_kernel(row_shape, surface_rows, first, counts, staged, gram_any, *refs):
    mirrors, shard_rows = row_shape[:2]
    sources = [ref.at[n] for ref, count in zip(refs, counts) for n in range(count)]
    out_ref, gram_ref, blocks, gram_semaphores, block_semaphores = refs[len(counts):]
    step = pl.program_id(0)
    gram_copies = fetch_gram(gram_any, gram_ref, gram_semaphores, mirrors)

    def fetch(n):
        return pltpu.make_async_copy(sources[n], blocks.at[n], block_semaphores.at[n])

    @pl.when(step == 0)
    def _():
        fetch(0).start()
        for copy in gram_copies:
            copy.start()
        for n in range(1, len(sources)):
            fetch(n).start()

    for n in range(len(sources)):
        @pl.when(step == n)
        def _():
            fetch(n).wait()
            block = row_block(first + n, staged)
            for q in range(mirrors * shard_rows):
                if n == 0 and q % shard_rows == 0:
                    gram_copies[q // shard_rows].wait()
                out_ref[0, q] = band_product([blocks.at[n]], q, row_shape, block, surface_rows, gram_ref)


def bands(gram_rows, sources, first, staged, row_shape, surface_rows):
    acts, own = gram_rows.shape
    counts = [source.shape[0] for source in sources]
    rows = row_shape[0] * row_shape[1]
    flops = 2 * own * WINDOW * row_shape[3] * rows * sum(counts)
    return pl.pallas_call(
        functools.partial(bands_kernel, row_shape, surface_rows, first, counts, staged),
        grid=(sum(counts),),
        out_shape=jax.ShapeDtypeStruct((sum(counts), rows, row_shape[3], own), jnp.bfloat16),
        in_specs=[pl.BlockSpec(memory_space=pl.ANY)] * (1 + len(sources)),
        out_specs=pl.BlockSpec((1, rows, row_shape[3], own), lambda s: (s, 0, 0, 0)),
        scratch_shapes=[
            pltpu.VMEM((acts, own), jnp.bfloat16),
            pltpu.VMEM((sum(counts),) + sources[0].shape[1:], jnp.bfloat16),
            pltpu.SemaphoreType.DMA((row_shape[0],)),
            pltpu.SemaphoreType.DMA((sum(counts),)),
        ],
        compiler_params=pltpu.CompilerParams(vmem_limit_bytes=VMEM_BYTES),
        cost_estimate=pl.CostEstimate(
            flops=flops, bytes_accessed=2 * own * WINDOW * rows * sum(counts), transcendentals=0
        ),
        name="bands",
    )(gram_rows, *sources)


def build_differences(columns, differences, mirrors, samples, pupil):
    half = pupil // 2
    slope = lax.broadcasted_iota(jnp.int32, (half, pupil), 0)
    lane = lax.broadcasted_iota(jnp.int32, (half, pupil), 1)
    at = lax.broadcasted_iota(jnp.int32, (half, mirrors * samples), 1)
    for d, lines in enumerate(columns):
        sides = []
        for side in range(2):
            hit = None
            for k in range(mirrors):
                line = jnp.broadcast_to(lines[k:k + 1], (half, pupil))
                column = jnp.sum(jnp.where(lane == slope * 2 + side, line, 0), axis=1, keepdims=True)
                here = (at == column + k * samples).astype(jnp.float32)
                hit = here if hit is None else hit + here
            sides.append(hit)
        differences[d, 0] = (sides[1] - sides[0]).astype(jnp.bfloat16)
        differences[d, 1] = (sides[1] + sides[0]).astype(jnp.bfloat16)


def decode_kernel(row_shape, surface_rows, own, staged, norm, counts, late_parts, *refs):
    mirrors, shard_rows, slots, samples = row_shape
    lines_ref, *refs = refs
    late_refs, refs = refs[:counts[0]], refs[counts[0]:]
    ready_refs, refs = refs[:counts[1]], refs[counts[1]:]
    (gram_any, out_ref, gram_ref, decoded, differences, total, foot_rows, scalars, *refs) = refs
    late_blocks, refs = refs[:counts[0]], refs[counts[0]:]
    gram_semaphores, ready_semaphores, late_semaphores, scalar_semaphore = refs
    group = pl.program_id(0)
    directions, pupil = differences.shape[0], 2 * differences.shape[2]
    phases = out_ref.shape[2] // pupil
    blocks = surface_rows // shard_rows
    late = len(late_parts)
    ready = blocks - late
    foot_line = mirrors + shard_rows // 2

    @pl.when(group == 0)
    def _():
        def started(copies):
            for copy in copies:
                copy.start()
            return copies

        for block in range(blocks):
            for d in range(directions):
                foot_rows[block, d:d + 1] = lines_ref[block, d, foot_line:foot_line + 1, :LANES]
        to_scalars = pltpu.make_async_copy(foot_rows, scalars, scalar_semaphore.at[0])
        to_scalars.start()
        late_copies = started([
            pltpu.make_async_copy(late_refs[n], late_blocks[n], late_semaphores.at[n]) for n in range(counts[0])
        ])
        gram_copies = started(fetch_gram(gram_any, gram_ref, gram_semaphores, mirrors)) if late else []
        ready_copies = started([
            pltpu.make_async_copy(block, decoded.at[n], ready_semaphores.at[n])
            for n, block in enumerate([ref.at[m] for ref in ready_refs for m in range(ref.shape[0])])
        ])
        columns = [lines_ref[0, d, :, :pupil] for d in range(directions)]
        build_differences(columns, differences, mirrors, samples, pupil)
        for copy in late_copies:
            copy.wait()
        at = 0
        for n, part in enumerate(late_parts):
            parts, at = late_blocks[at:at + part], at + part
            for q in range(mirrors * shard_rows):
                if n == 0 and q % shard_rows == 0:
                    gram_copies[q // shard_rows].wait()
                decoded[ready + n, q] = band_product(
                    parts, q, row_shape, row_block(ready + n, staged), surface_rows, gram_ref
                )
        to_scalars.wait()
        for copy in ready_copies:
            copy.wait()

    for d in range(directions):
        held = d ^ position("dir", staged)
        products, factors = [], []
        for phase in range(phases):
            i = group * phases + phase
            block = (2 * i // shard_rows) ^ position("row", staged)
            sums, changes = [], []
            for k in range(mirrors):
                picked = []
                for y in range(2):
                    row = scalars[block, held, k * shard_rows + (2 * phase + y) % shard_rows]
                    picked.append(decoded[row_place(row // shard_rows, staged), k * shard_rows + row % shard_rows])
                sums.append(picked[0] + picked[1])
                changes.append(picked[1] - picked[0])
            for kind, rows in enumerate((sums, changes)):
                products.append(
                    jnp.dot(
                        differences[held, kind], jnp.concatenate(rows, axis=0), preferred_element_type=jnp.float32
                    )
                )
            line = mirrors + phase % (shard_rows // 2)
            valid = lines_ref[block, held, line:line + 1, :pupil // 2]
            factors += [valid.astype(jnp.float32) * norm] * 2
        product = jnp.concatenate(products, axis=0)
        factor = jnp.concatenate(factors, axis=1)
        for tile in range(out_ref.shape[2] // LANES):
            at = tile * LANES
            value = jnp.transpose(product[at:at + LANES])[:own] * factor[:, at:at + LANES]
            total[tile, pl.ds(d, own, stride=directions), :] = value
    for tile in range(out_ref.shape[2] // LANES):
        value = total[tile].reshape(own, directions, LANES)
        out_ref[:, :, tile * LANES:(tile + 1) * LANES] = value.astype(out_ref.dtype)


def decode(lines, late, ready, gram_rows, own, row_shape, surface_rows, pupil, norm, staged):
    mirrors, shard_rows, slots, samples = row_shape
    acts, padded = gram_rows.shape
    blocks, directions = lines.shape[:2]
    phases = LANES // math.gcd(pupil, LANES)
    width = surface_rows // 2 * pupil
    lanes = phases * pupil
    flops = 2 * padded * mirrors * samples * pupil * directions * surface_rows // 2
    vmem, anywhere = pl.BlockSpec(memory_space=pltpu.VMEM), pl.BlockSpec(memory_space=pl.ANY)
    parts = [part for block in late for part in block]
    counts = (len(parts), len(ready))
    semaphores = [mirrors, blocks, max(len(parts), 1), 1]
    return pl.pallas_call(
        functools.partial(
            decode_kernel, row_shape, surface_rows, own, staged, norm, counts, [len(block) for block in late]
        ),
        grid=(width // lanes,),
        out_shape=jax.ShapeDtypeStruct((own, directions, width), jnp.bfloat16),
        in_specs=[vmem] + [anywhere] * (sum(counts) + 1),
        out_specs=pl.BlockSpec((own, directions, lanes), lambda s: (0, 0, s)),
        scratch_shapes=[
            pltpu.VMEM((acts, padded), jnp.bfloat16),
            pltpu.VMEM((blocks, mirrors * shard_rows, samples, padded), jnp.bfloat16),
            pltpu.VMEM((directions, 2, pupil // 2, mirrors * samples), jnp.bfloat16),
            pltpu.VMEM((lanes // LANES, own * directions, LANES), jnp.float32),
            pltpu.VMEM((blocks, -(-directions // 8) * 8, LANES), jnp.int32),
            pltpu.SMEM((blocks, -(-directions // 8) * 8, LANES), jnp.int32),
            *[pltpu.VMEM(part.shape, part.dtype) for part in parts],
            *[pltpu.SemaphoreType.DMA((count,)) for count in semaphores],
        ],
        compiler_params=pltpu.CompilerParams(vmem_limit_bytes=VMEM_BYTES),
        cost_estimate=pl.CostEstimate(flops=flops, bytes_accessed=2 * own * directions * width, transcendentals=0),
        name="decode",
    )(lines, *parts, *ready, gram_rows)


def swap(block, axis, distance):
    return lax.ppermute(block, axis, [(i, i ^ distance) for i in range(lax.axis_size(axis))])


def shards(influence, foot_rows, foot_columns, actuator_codes, poke_rows, subaperture_valid):
    mirrors, shard_rows, samples, slots = influence.shape
    row_shape = (mirrors, shard_rows, slots, samples)
    directions, devices = lax.axis_size("dir"), lax.axis_size("row")
    surface_rows = shard_rows * devices
    pupil = foot_columns.shape[2]
    norm = 0.5 * poke_rows.shape[0] ** (-0.5)
    own = actuator_codes.size // (directions * devices)
    staged = devices == 8 and directions & (directions - 1) == 0
    turned = jnp.swapaxes(influence, 2, 3)
    pokes = poke_rows.reshape(-1, LANES)
    packed, lines = pack(turned, foot_rows, foot_columns, subaperture_valid)
    if not staged:
        every = lax.all_gather(packed, "row")
        lines = lax.all_gather(lax.all_gather(lines, "dir"), "row")
        gram_rows, _ = gram(*own_side(actuator_codes, pokes, own), packed, row_shape, surface_rows)
        ready = [bands(gram_rows, [every], 0, staged, row_shape, surface_rows)]
        return decode(lines, [], ready, gram_rows, own, row_shape, surface_rows, pupil, norm, staged)

    beside, across, sibling = (swap(packed, "row", distance) for distance in (2, 4, 1))
    lines = jnp.stack([lines] + [swap(lines, "dir", e) for e in range(1, directions)])[None]
    sides = own_side(actuator_codes, pokes, own)
    lines, sides = lax.optimization_barrier((lines, sides))
    more = swap(lines, "row", 1)
    gram_rows, first = gram(*sides, packed, row_shape, surface_rows)
    gram_rows, beside, across, more = lax.optimization_barrier((gram_rows, beside, across, more))
    lines = jnp.concatenate([lines, more], axis=0)
    more = swap(lines, "row", 2)
    half = packed.shape[0] // 2
    upper, lower = swap(beside[:half], "row", 4), swap(across[half:], "row", 2)
    beside_sibling, across_sibling = swap(beside, "row", 1), swap(across, "row", 1)
    sources = [source[None] for source in (sibling, beside, across)]
    ready = bands(gram_rows, sources, 1, staged, row_shape, surface_rows)
    ready, upper, lower, more = lax.optimization_barrier((ready, upper, lower, more))
    lines = jnp.concatenate([lines, more], axis=0)
    lines = jnp.concatenate([lines, swap(lines, "row", 4)], axis=0)
    late = [[beside_sibling], [across_sibling], [upper, lower], [swap(upper, "row", 1), swap(lower, "row", 1)]]
    return decode(lines, late, [first, ready], gram_rows, own, row_shape, surface_rows, pupil, norm, staged)


def solution(mesh):
    return jax.shard_map(
        shards,
        mesh=mesh,
        in_specs=(
            P(None, "row", None, None),
            P("dir", None, "row"),
            P("dir", None, None),
            P(),
            P(),
            P("dir", "row", None),
        ),
        out_specs=P(("dir", "row"), None, None),
        check_vma=False,
    )
```

```python
import functools
import math

import jax
import jax.numpy as jnp
import numpy as np
from jax import lax
from jax.experimental import pallas as pl
from jax.experimental.pallas import tpu as pltpu
from jax.sharding import PartitionSpec as P

NAR = 48
NA = 48
BAND = 3
BITS = 13
NARROW = jnp.float8_e5m2
LANES = 128
WINDOW = 256
VMEM_BYTES = 63 * 1024 * 1024


def parity(codes, rows):
    return lax.population_count(codes & rows) & 1


def pack_kernel(block_ref, rows_ref, columns_ref, valid_ref, packed_ref, lines_ref):
    mirrors, rows, slots, samples = block_ref.shape
    groups = mirrors * rows // 2
    lines_ref[...] = jnp.zeros(lines_ref.shape, lines_ref.dtype)
    lines_ref[mirrors:mirrors + valid_ref.shape[1], :valid_ref.shape[2]] = valid_ref[0]
    for k in range(mirrors):
        lines_ref[k:k + 1, :columns_ref.shape[2]] = columns_ref[k]
        lines_ref[mirrors + valid_ref.shape[1]:mirrors + valid_ref.shape[1] + 1, k * rows:(k + 1) * rows] = rows_ref[k]
    identity = (
        lax.broadcasted_iota(jnp.int32, (samples, samples), 0) == lax.broadcasted_iota(jnp.int32, (samples, samples), 1)
    ).astype(jnp.float32).astype(jnp.bfloat16)
    for part in range(2):
        base = part * (groups + 1) * samples
        tails = []
        for group in range(groups):
            k, l = divmod(part * groups + group, rows)
            turned = lax.dot_general(
                identity, block_ref[k, l], (((1,), (1,)), ((), ())), preferred_element_type=jnp.float32
            ).astype(jnp.bfloat16)
            packed_ref[pl.ds(base + group * samples, samples), :] = turned[:, :LANES]
            tails.append(turned[:, LANES:])
        tails.append(jnp.zeros((samples, LANES - groups * (slots - LANES)), jnp.bfloat16))
        packed_ref[pl.ds(base + groups * samples, samples), :] = jnp.concatenate(tails, axis=1)


def pack(block, foot_rows, foot_columns, valid):
    mirrors, rows, slots, samples = block.shape
    vmem = pl.BlockSpec(memory_space=pltpu.VMEM)
    count = mirrors + valid.shape[1] + 1
    return pl.pallas_call(
        pack_kernel,
        out_shape=[
            jax.ShapeDtypeStruct(((mirrors * rows + 2) * samples, LANES), block.dtype),
            jax.ShapeDtypeStruct((-(-count // 8) * 8, WINDOW), jnp.int32),
        ],
        in_specs=[vmem] * 4,
        out_specs=[vmem] * 2,
        compiler_params=pltpu.CompilerParams(vmem_limit_bytes=VMEM_BYTES),
        cost_estimate=pl.CostEstimate(flops=0, bytes_accessed=3 * block.size, transcendentals=0),
        name="pack_influence",
    )(block, jnp.swapaxes(foot_rows, 0, 1), jnp.swapaxes(foot_columns, 0, 1), valid)


def column_of(row):
    return jnp.transpose(jnp.broadcast_to(row, (LANES, LANES)), (1, 0))


def signs_kernel(table_ref, pokes_ref, codes_ref, words, own_signs, own_sums):
    planes = pokes_ref.shape[0]
    mirrors, rows, columns = table_ref.shape
    for line in range(codes_ref.shape[0]):
        pieces, at = [], line * LANES
        while at < (line + 1) * LANES:
            row, lane = divmod(at, columns)
            length = min(columns - lane, (line + 1) * LANES - at)
            pieces.append(table_ref[row // rows, row % rows:row % rows + 1, lane:lane + length])
            at += length
        codes_ref[line:line + 1, :] = jnp.concatenate(pieces, axis=1)
    half = LANES // 2
    own = own_signs.shape[0]
    plane = lax.broadcasted_iota(jnp.int32, pokes_ref.shape, 0)
    for bit in range(BITS):
        low = jnp.sum((pokes_ref[...] >> bit & 1) << plane, axis=0, keepdims=True)
        word = low | pltpu.roll(jnp.broadcast_to(low, (8, LANES)), half, 1)[:1] << planes
        words[bit] = column_of(word)[:half]
    count = codes_ref.shape[0] * LANES // (lax.axis_size("dir") * lax.axis_size("row"))
    first = (lax.axis_index("dir") * lax.axis_size("row") + lax.axis_index("row")) * count
    lane = lax.broadcasted_iota(jnp.int32, (8, LANES), 1)
    shift = first % LANES
    lines = [
        pltpu.roll(
            jnp.broadcast_to(
                codes_ref[pl.ds(jnp.minimum(first // LANES + n, codes_ref.shape[0] - 1), 1), :], (8, LANES)
            ),
            LANES - shift, 1,
        )
        for n in range(-(-own // LANES) + 1)
    ]
    own_column = jnp.concatenate(
        [column_of(jnp.where(lane < LANES - shift, lines[n], lines[n + 1])[:1]) for n in range(len(lines) - 1)],
        axis=0,
    )[:own]
    total = jnp.zeros((own, LANES), jnp.float32)
    for at in range(planes):
        signs = (1 - 2 * parity(own_column, pokes_ref[at:at + 1, :])).astype(jnp.float32)
        own_signs[:, at * LANES:(at + 1) * LANES] = signs.astype(NARROW)
        total = total + signs
    own_sums[...] = jnp.broadcast_to(jnp.sum(total, axis=1, keepdims=True), own_sums.shape)


def own_side(table, pokes, own):
    own = -(-own // 32) * 32
    vmem = pl.BlockSpec(memory_space=pltpu.VMEM)
    return pl.pallas_call(
        signs_kernel,
        out_shape=[
            jax.ShapeDtypeStruct((table.size // LANES, LANES), jnp.int32),
            jax.ShapeDtypeStruct((BITS, LANES // 2, LANES), jnp.int32),
            jax.ShapeDtypeStruct((own, pokes.size), NARROW),
            jax.ShapeDtypeStruct((own, LANES), jnp.float32),
        ],
        in_specs=[vmem] * 2,
        out_specs=[vmem] * 4,
        compiler_params=pltpu.CompilerParams(vmem_limit_bytes=VMEM_BYTES),
        name="own_signs",
    )(table, pokes)


def gram_kernel(
    row_shape, surface_rows, codes_ref, words, own_signs, own_sums, packed_ref, gram_out, first_ref, gram_ref,
    even_bits, odd_bits, even_sums, odd_sums, semaphores
):
    half = LANES // 2
    own, pokes = own_signs.shape
    planes = pokes // LANES
    chunks = gram_ref.shape[0] // WINDOW
    pieces = 4
    depth = pokes // pieces

    def word_bytes(index):
        word = []
        for side in range(WINDOW // LANES):
            code = jnp.broadcast_to(codes_ref[pl.ds(index * (WINDOW // LANES) + side, 1), :], (8, LANES))
            value = None
            for bit in range(BITS):
                mask = jnp.concatenate([code << (31 - bit) >> 31] * (half // 8), axis=0)
                part = words[bit] & mask
                value = part if value is None else value ^ part
            word.append(value)
        word = jnp.concatenate(word, axis=1)
        return [(word >> byte).astype(jnp.int8) for byte in range(0, 2 * planes, 8)]

    def make_bits(parts, piece, bits_ref):
        for at in range(piece * planes // pieces, (piece + 1) * planes // pieces):
            for upper in range(2):
                plane = at + upper * planes
                hit = (parts[plane // 8] & np.uint8(1 << plane % 8).astype(np.int8)) != 0
                bits_ref[pl.ds((2 * at + upper) * half, half), :] = jnp.where(hit, NARROW(1.0), NARROW(0.0))

    def finish(index, sums_ref, side):
        lanes = slice(side * LANES, (side + 1) * LANES)
        value = (own_sums[...] - 2.0 * sums_ref[:, lanes]).astype(jnp.bfloat16)
        at = pl.multiple_of(index * WINDOW + side * LANES, LANES)
        gram_ref[pl.ds(at, LANES), :] = jnp.transpose(value)

    def product(index, bits_ref, sums_ref, next_bits, before, before_sums):
        parts = None if next_bits is None else word_bytes(index + 1)
        total = None
        for piece in range(pieces):
            part = jnp.dot(
                own_signs[:, piece * depth:(piece + 1) * depth], bits_ref[pl.ds(piece * depth, depth), :],
                preferred_element_type=jnp.float32,
            )
            total = part if total is None else total + part
            if parts is not None:
                make_bits(parts, piece, next_bits)
            if before is not None and piece % 2 == 0:
                finish(before, before_sums, piece // 2)
        sums_ref[...] = total

    parts = word_bytes(0)
    for piece in range(pieces):
        make_bits(parts, piece, even_bits)
    product(0, even_bits, even_sums, odd_bits, None, None)

    def pair(step, _):
        index = 2 * step + 1
        product(index, odd_bits, odd_sums, even_bits, index - 1, even_sums)
        product(index + 1, even_bits, even_sums, odd_bits, index, odd_sums)
        return 0

    pairs = (chunks - 2) // 2
    lax.fori_loop(0, pairs, pair, 0)
    buffers = [(even_bits, even_sums), (odd_bits, odd_sums)]
    for index in range(2 * pairs + 1, chunks):
        bits_ref, sums_ref = buffers[index % 2]
        next_bits = buffers[(index + 1) % 2][0] if index + 1 < chunks else None
        product(index, bits_ref, sums_ref, next_bits, index - 1, buffers[(index - 1) % 2][1])
    for side in range(WINDOW // LANES):
        finish(chunks - 1, buffers[(chunks - 1) % 2][1], side)

    copies = fetch_gram(gram_ref, gram_out, semaphores, row_shape[0])
    for copy in copies:
        copy.start()
    block = lax.axis_index("row")
    for q in range(row_shape[0] * row_shape[1]):
        first_ref[0, q] = band_product([packed_ref], q, row_shape, block, surface_rows, gram_ref)
    for copy in copies:
        copy.wait()


def gram(codes, words, own_signs, own_sums, packed, row_shape, surface_rows):
    acts, (own, count) = codes.size, own_signs.shape
    mirrors, shard_rows, slots, samples = row_shape
    vmem = pl.BlockSpec(memory_space=pltpu.VMEM)
    return pl.pallas_call(
        functools.partial(gram_kernel, row_shape, surface_rows),
        out_shape=[
            jax.ShapeDtypeStruct((acts, own), jnp.bfloat16),
            jax.ShapeDtypeStruct((1, mirrors * shard_rows, samples, own), jnp.bfloat16),
        ],
        in_specs=[vmem] * 5,
        out_specs=[pl.BlockSpec(memory_space=pl.ANY), vmem],
        scratch_shapes=[
            pltpu.VMEM((acts, own), jnp.bfloat16),
            pltpu.VMEM((count, WINDOW), NARROW),
            pltpu.VMEM((count, WINDOW), NARROW),
            pltpu.VMEM((own, WINDOW), jnp.float32),
            pltpu.VMEM((own, WINDOW), jnp.float32),
            pltpu.SemaphoreType.DMA((mirrors,)),
        ],
        compiler_params=pltpu.CompilerParams(vmem_limit_bytes=VMEM_BYTES),
        cost_estimate=pl.CostEstimate(
            flops=2 * own * acts * count, bytes_accessed=2 * own * acts, transcendentals=0
        ),
        name="gram_rows",
    )(codes, words, own_signs, own_sums, packed)


def position(axis, staged):
    return lax.axis_index(axis) if staged else 0


def row_block(place, staged):
    if not staged:
        return place
    row = lax.axis_index("row")
    core = row & 1
    return row ^ [0, 1, 2 << core, 4 >> core, (4 >> core) | 1, (2 << core) | 1, 6, 7][place]


def row_place(block, staged):
    if not staged:
        return block
    row = lax.axis_index("row")
    core = row & 1
    distance = block ^ row
    near = jnp.where(distance == 2 << core, 2, 3)
    far = jnp.where(distance == (4 >> core) | 1, 4, 5)
    middle = jnp.where(distance & 1 == 0, near, far)
    return jnp.where((distance >= 2) & (distance < 6), middle, distance)


def lines_place(block, staged):
    if not staged:
        return block
    distance = block ^ lax.axis_index("row")
    return (distance >> 1 & 1) * 4 + (distance >> 2) * 2 + (distance & 1)


def band_product(parts, q, row_shape, block, surface_rows, gram_ref):
    mirrors, shard_rows, slots, samples = row_shape
    groups = mirrors * shard_rows // 2
    own = gram_ref.shape[1]
    narrow = slots - LANES
    k, l = divmod(q, shard_rows)
    band = jnp.clip((block * shard_rows + l) * NAR // surface_rows - 1, 0, NAR - BAND)
    column = pl.multiple_of((k * NAR + band) * NA, 16)
    part, group = divmod(q, groups)
    source, base = (parts[0], part * (groups + 1) * samples) if len(parts) == 1 else (parts[part], 0)
    left = jnp.concatenate(
        [source[pl.ds(base + group * samples, samples), :], source[pl.ds(base + groups * samples, samples), :]],
        axis=1,
    )
    right = [gram_ref[pl.ds(column, LANES), :]]
    if group:
        right.append(jnp.zeros((group * narrow, own), jnp.bfloat16))
    right.append(gram_ref[pl.ds(column + LANES, narrow), :])
    right.append(jnp.zeros((LANES - (group + 1) * narrow, own), jnp.bfloat16))
    return jnp.dot(left, jnp.concatenate(right, axis=0), preferred_element_type=jnp.float32).astype(jnp.bfloat16)


def fetch_gram(gram_any, gram_ref, semaphores, mirrors):
    height = gram_ref.shape[0] // mirrors
    return [
        pltpu.make_async_copy(
            gram_any.at[pl.ds(k * height, height)], gram_ref.at[pl.ds(k * height, height)], semaphores.at[k]
        )
        for k in range(mirrors)
    ]


def bands_kernel(row_shape, surface_rows, first, counts, staged, gram_any, *refs):
    mirrors, shard_rows = row_shape[:2]
    sources = [ref.at[n] for ref, count in zip(refs, counts) for n in range(count)]
    out_ref, gram_ref, blocks, gram_semaphores, block_semaphores = refs[len(counts):]
    step = pl.program_id(0)
    gram_copies = fetch_gram(gram_any, gram_ref, gram_semaphores, mirrors)

    def fetch(n):
        return pltpu.make_async_copy(sources[n], blocks.at[n], block_semaphores.at[n])

    @pl.when(step == 0)
    def _():
        fetch(0).start()
        for copy in gram_copies:
            copy.start()
        for n in range(1, len(sources)):
            fetch(n).start()

    for n in range(len(sources)):
        @pl.when(step == n)
        def _():
            fetch(n).wait()
            block = row_block(first + n, staged)
            for q in range(mirrors * shard_rows):
                if n == 0 and q % shard_rows == 0:
                    gram_copies[q // shard_rows].wait()
                out_ref[0, q] = band_product([blocks.at[n]], q, row_shape, block, surface_rows, gram_ref)


def bands(gram_rows, sources, first, staged, row_shape, surface_rows):
    acts, own = gram_rows.shape
    counts = [source.shape[0] for source in sources]
    rows = row_shape[0] * row_shape[1]
    flops = 2 * own * WINDOW * row_shape[3] * rows * sum(counts)
    return pl.pallas_call(
        functools.partial(bands_kernel, row_shape, surface_rows, first, counts, staged),
        grid=(sum(counts),),
        out_shape=jax.ShapeDtypeStruct((sum(counts), rows, row_shape[3], own), jnp.bfloat16),
        in_specs=[pl.BlockSpec(memory_space=pl.ANY)] * (1 + len(sources)),
        out_specs=pl.BlockSpec((1, rows, row_shape[3], own), lambda s: (s, 0, 0, 0)),
        scratch_shapes=[
            pltpu.VMEM((acts, own), jnp.bfloat16),
            pltpu.VMEM((sum(counts),) + sources[0].shape[1:], jnp.bfloat16),
            pltpu.SemaphoreType.DMA((row_shape[0],)),
            pltpu.SemaphoreType.DMA((sum(counts),)),
        ],
        compiler_params=pltpu.CompilerParams(vmem_limit_bytes=VMEM_BYTES),
        cost_estimate=pl.CostEstimate(
            flops=flops, bytes_accessed=2 * own * WINDOW * rows * sum(counts), transcendentals=0
        ),
        name="bands",
    )(gram_rows, *sources)


def build_differences(columns, differences, mirrors, samples, pupil):
    half = pupil // 2
    slope = lax.broadcasted_iota(jnp.int32, (half, pupil), 0)
    lane = lax.broadcasted_iota(jnp.int32, (half, pupil), 1)
    at = lax.broadcasted_iota(jnp.int32, (half, mirrors * samples), 1)
    for d, lines in enumerate(columns):
        sides = []
        for side in range(2):
            hit = None
            for k in range(mirrors):
                line = jnp.broadcast_to(lines[k:k + 1], (half, pupil))
                column = jnp.sum(jnp.where(lane == slope * 2 + side, line, 0), axis=1, keepdims=True)
                here = (at == column + k * samples).astype(jnp.float32)
                hit = here if hit is None else hit + here
            sides.append(hit)
        differences[d, 0] = (sides[1] - sides[0]).astype(jnp.bfloat16)
        differences[d, 1] = (sides[1] + sides[0]).astype(jnp.bfloat16)


def decode_kernel(row_shape, surface_rows, own, staged, norm, counts, late_parts, *refs):
    mirrors, shard_rows, slots, samples = row_shape
    lines_ref, *refs = refs
    late_refs, refs = refs[:counts[0]], refs[counts[0]:]
    ready_refs, refs = refs[:counts[1]], refs[counts[1]:]
    (gram_any, out_ref, gram_ref, decoded, differences, total, foot_rows, scalars, *refs) = refs
    late_blocks, refs = refs[:counts[0]], refs[counts[0]:]
    gram_semaphores, ready_semaphores, late_semaphores, scalar_semaphore = refs
    group = pl.program_id(0)
    groups = pl.num_programs(0) - 1
    directions, pupil = differences.shape[0], 2 * differences.shape[2]
    phases = out_ref.shape[2] // pupil
    blocks = surface_rows // shard_rows
    late = len(late_parts)
    ready = blocks - late
    foot_line = mirrors + shard_rows // 2

    @pl.when(group == 0)
    def _():
        def started(copies):
            for copy in copies:
                copy.start()
            return copies

        for block in range(blocks):
            for d in range(directions):
                foot_rows[block, d:d + 1] = lines_ref[block, d, foot_line:foot_line + 1, :LANES]
        to_scalars = pltpu.make_async_copy(foot_rows, scalars, scalar_semaphore.at[0])
        to_scalars.start()
        late_copies = started([
            pltpu.make_async_copy(late_refs[n], late_blocks[n], late_semaphores.at[n]) for n in range(counts[0])
        ])
        gram_copies = started(fetch_gram(gram_any, gram_ref, gram_semaphores, mirrors)) if late else []
        ready_copies = started([
            pltpu.make_async_copy(block, decoded.at[n], ready_semaphores.at[n])
            for n, block in enumerate([ref.at[m] for ref in ready_refs for m in range(ref.shape[0])])
        ])
        columns = [lines_ref[0, d, :, :pupil] for d in range(directions)]
        build_differences(columns, differences, mirrors, samples, pupil)
        for copy in late_copies:
            copy.wait()
        at = 0
        for n, part in enumerate(late_parts):
            parts, at = late_blocks[at:at + part], at + part
            for q in range(mirrors * shard_rows):
                if n == 0 and q % shard_rows == 0:
                    gram_copies[q // shard_rows].wait()
                decoded[ready + n, q] = band_product(
                    parts, q, row_shape, row_block(ready + n, staged), surface_rows, gram_ref
                )
        to_scalars.wait()
        for copy in ready_copies:
            copy.wait()

    tiles = out_ref.shape[2] // LANES

    def relayout(slot, tile):
        value = total[slot, tile].reshape(own, directions, LANES)
        out_ref[:, :, tile * LANES:(tile + 1) * LANES] = value.astype(out_ref.dtype)

    @pl.when(group < groups)
    def _():
        slot = lax.rem(group, 2)
        waiting = []
        for d in range(directions):
            held = d ^ position("dir", staged)
            products, factors = [], []
            for phase in range(phases):
                i = group * phases + phase
                block = lines_place(2 * i // shard_rows, staged)
                sums, changes = [], []
                for k in range(mirrors):
                    picked = []
                    for y in range(2):
                        row = scalars[block, held, k * shard_rows + (2 * phase + y) % shard_rows]
                        picked.append(decoded[row_place(row // shard_rows, staged), k * shard_rows + row % shard_rows])
                    sums.append(picked[0] + picked[1])
                    changes.append(picked[1] - picked[0])
                for kind, rows in enumerate((sums, changes)):
                    products.append(
                        jnp.dot(
                            differences[held, kind], jnp.concatenate(rows, axis=0), preferred_element_type=jnp.float32
                        )
                    )
                line = mirrors + phase % (shard_rows // 2)
                valid = lines_ref[block, held, line:line + 1, :pupil // 2]
                factors += [valid.astype(jnp.float32) * norm] * 2
                for _ in range(-(-len(waiting) // (phases - phase))):
                    waiting.pop(0)()
            product = jnp.concatenate(products, axis=0)
            factor = jnp.concatenate(factors, axis=1)

            def turn(tile, d, product, factor):
                at = tile * LANES
                value = jnp.transpose(product[at:at + LANES])[:own] * factor[:, at:at + LANES]
                total[slot, tile, pl.ds(d, own, stride=directions), :] = value

            waiting = [functools.partial(turn, tile, d, product, factor) for tile in range(tiles)]
            if d < directions - 1:
                waiting += [
                    functools.partial(relayout, 1 - slot, tile)
                    for tile in range(d * tiles // (directions - 1), (d + 1) * tiles // (directions - 1))
                ]
        for last in waiting:
            last()

    @pl.when(group == groups)
    def _():
        for tile in range(tiles):
            relayout(lax.rem(group + 1, 2), tile)


def decode(lines, late, ready, gram_rows, own, row_shape, surface_rows, pupil, norm, staged):
    mirrors, shard_rows, slots, samples = row_shape
    acts, padded = gram_rows.shape
    blocks, directions = lines.shape[:2]
    phases = LANES // math.gcd(pupil, LANES)
    width = surface_rows // 2 * pupil
    lanes = phases * pupil
    flops = 2 * padded * mirrors * samples * pupil * directions * surface_rows // 2
    vmem, anywhere = pl.BlockSpec(memory_space=pltpu.VMEM), pl.BlockSpec(memory_space=pl.ANY)
    parts = [part for block in late for part in block]
    counts = (len(parts), len(ready))
    semaphores = [mirrors, blocks, max(len(parts), 1), 1]
    return pl.pallas_call(
        functools.partial(
            decode_kernel, row_shape, surface_rows, own, staged, norm, counts, [len(block) for block in late]
        ),
        grid=(width // lanes + 1,),
        out_shape=jax.ShapeDtypeStruct((own, directions, width), jnp.bfloat16),
        in_specs=[vmem] + [anywhere] * (sum(counts) + 1),
        out_specs=pl.BlockSpec((own, directions, lanes), lambda s: (0, 0, jnp.maximum(s - 1, 0))),
        scratch_shapes=[
            pltpu.VMEM((acts, padded), jnp.bfloat16),
            pltpu.VMEM((blocks, mirrors * shard_rows, samples, padded), jnp.bfloat16),
            pltpu.VMEM((directions, 2, pupil // 2, mirrors * samples), jnp.bfloat16),
            pltpu.VMEM((2, lanes // LANES, own * directions, LANES), jnp.float32),
            pltpu.VMEM((blocks, -(-directions // 8) * 8, LANES), jnp.int32),
            pltpu.SMEM((blocks, -(-directions // 8) * 8, LANES), jnp.int32),
            *[pltpu.VMEM(part.shape, part.dtype) for part in parts],
            *[pltpu.SemaphoreType.DMA((count,)) for count in semaphores],
        ],
        compiler_params=pltpu.CompilerParams(vmem_limit_bytes=VMEM_BYTES),
        cost_estimate=pl.CostEstimate(flops=flops, bytes_accessed=2 * own * directions * width, transcendentals=0),
        name="decode",
    )(lines, *parts, *ready, gram_rows)


def swap(block, axis, distance):
    return lax.ppermute(block, axis, [(i, i ^ distance) for i in range(lax.axis_size(axis))])


def turn(block, even, odd):
    return lax.ppermute(
        block, "row", [(i, i ^ (odd if i % 2 else even)) for i in range(lax.axis_size("row"))]
    )


def shards(influence, foot_rows, foot_columns, actuator_codes, poke_rows, subaperture_valid):
    mirrors, shard_rows, samples, slots = influence.shape
    row_shape = (mirrors, shard_rows, slots, samples)
    directions, devices = lax.axis_size("dir"), lax.axis_size("row")
    surface_rows = shard_rows * devices
    pupil = foot_columns.shape[2]
    norm = 0.5 * poke_rows.shape[0] ** (-0.5)
    own = actuator_codes.size // (directions * devices)
    staged = devices == 8 and directions & (directions - 1) == 0
    turned = jnp.swapaxes(influence, 2, 3)
    pokes = poke_rows.reshape(-1, LANES)
    packed, lines = pack(turned, foot_rows, foot_columns, subaperture_valid)
    if not staged:
        every = lax.all_gather(packed, "row")
        lines = lax.all_gather(lax.all_gather(lines, "dir"), "row")
        gram_rows, _ = gram(*own_side(actuator_codes, pokes, own), packed, row_shape, surface_rows)
        ready = [bands(gram_rows, [every], 0, staged, row_shape, surface_rows)]
        return decode(lines, [], ready, gram_rows, own, row_shape, surface_rows, pupil, norm, staged)

    first, second = turn(packed, 2, 4), turn(packed, 4, 2)
    sibling = swap(packed, "row", 1)
    lines = jnp.stack([lines] + [swap(lines, "dir", e) for e in range(1, directions)])[None]
    sides = own_side(actuator_codes, pokes, own)
    lines, sides = lax.optimization_barrier((lines, sides))
    lines = [lines] + [swap(lines, "row", distance) for distance in (1, 4, 5)]
    gram_rows, own_rows = gram(*sides, packed, row_shape, surface_rows)
    gram_rows, first, second, lines = lax.optimization_barrier((gram_rows, first, second, lines))
    lines = jnp.concatenate(lines, axis=0)
    diagonal = turn(first, 4, 2)
    first_sibling, second_sibling = swap(first, "row", 1), swap(second, "row", 1)
    more = swap(lines, "row", 2)
    sources = [source[None] for source in (sibling, first, second)]
    ready = bands(gram_rows, sources, 1, staged, row_shape, surface_rows)
    ready, diagonal, more = lax.optimization_barrier((ready, diagonal, more))
    lines = jnp.concatenate([lines, more], axis=0)
    late = [[block] for block in (first_sibling, second_sibling, diagonal, swap(diagonal, "row", 1))]
    return decode(lines, late, [own_rows, ready], gram_rows, own, row_shape, surface_rows, pupil, norm, staged)


def solution(mesh):
    return jax.shard_map(
        shards,
        mesh=mesh,
        in_specs=(
            P(None, "row", None, None),
            P("dir", None, "row"),
            P("dir", None, None),
            P(),
            P(),
            P("dir", "row", None),
        ),
        out_specs=P(("dir", "row"), None, None),
        check_vma=False,
    )
```

```python
import functools
import math

import jax
import jax.numpy as jnp
import numpy as np
from jax import lax
from jax.experimental import pallas as pl
from jax.experimental.pallas import tpu as pltpu
from jax.sharding import PartitionSpec as P

NAR = 48
NA = 48
BAND = 3
BITS = 13
NARROW = jnp.float8_e4m3fn
LANES = 128
WINDOW = 256
VMEM_BYTES = 63 * 1024 * 1024


def parity(codes, rows):
    return lax.population_count(codes & rows) & 1


def lines_kernel(rows_ref, columns_ref, valid_ref, lines_ref):
    mirrors, rows = rows_ref.shape[0], rows_ref.shape[2]
    lines_ref[...] = jnp.zeros(lines_ref.shape, lines_ref.dtype)
    lines_ref[mirrors:mirrors + valid_ref.shape[1], :valid_ref.shape[2]] = valid_ref[0]
    for k in range(mirrors):
        lines_ref[k:k + 1, :columns_ref.shape[2]] = columns_ref[k]
        lines_ref[mirrors + valid_ref.shape[1]:mirrors + valid_ref.shape[1] + 1, k * rows:(k + 1) * rows] = rows_ref[k]


def small_lines(foot_rows, foot_columns, valid):
    vmem = pl.BlockSpec(memory_space=pltpu.VMEM)
    count = foot_rows.shape[1] + valid.shape[1] + 1
    return pl.pallas_call(
        lines_kernel,
        out_shape=jax.ShapeDtypeStruct((-(-count // 8) * 8, WINDOW), jnp.int32),
        in_specs=[vmem] * 3,
        out_specs=vmem,
        name="small_lines",
    )(jnp.swapaxes(foot_rows, 0, 1), jnp.swapaxes(foot_columns, 0, 1), valid)


def pack_kernel(block_ref, *refs):
    lines_refs, packed_ref = refs[:-1], refs[-1]
    mirrors, rows, slots, samples = block_ref.shape
    groups = mirrors * rows // 2
    identity = (
        lax.broadcasted_iota(jnp.int32, (samples, samples), 0) == lax.broadcasted_iota(jnp.int32, (samples, samples), 1)
    ).astype(jnp.float32).astype(jnp.bfloat16)
    for part in range(2):
        base = part * (groups + 1) * samples
        tails = []
        for group in range(groups):
            k, l = divmod(part * groups + group, rows)
            turned = lax.dot_general(
                identity, block_ref[k, l], (((1,), (1,)), ((), ())), preferred_element_type=jnp.float32
            ).astype(jnp.bfloat16)
            packed_ref[pl.ds(base + group * samples, samples), :] = turned[:, :LANES]
            tails.append(turned[:, LANES:])
        tails.append(jnp.zeros((samples, LANES - groups * (slots - LANES)), jnp.bfloat16))
        packed_ref[pl.ds(base + groups * samples, samples), :] = jnp.concatenate(tails, axis=1)
    count = rows // 2 + 1
    lines = [ref[n, mirrors:mirrors + count, :LANES] for ref in lines_refs for n in range(ref.shape[0])]
    extra = packed_ref.shape[0] - 2 * (groups + 1) * samples
    lines.append(jnp.zeros((extra - count * len(lines), LANES), jnp.int32))
    packed_ref[pl.ds(packed_ref.shape[0] - extra, extra), :] = (
        jnp.concatenate(lines, axis=0).astype(jnp.float32).astype(jnp.bfloat16)
    )


def pack(block, lines):
    mirrors, rows, slots, samples = block.shape
    vmem = pl.BlockSpec(memory_space=pltpu.VMEM)
    extra = -(-sum(line.shape[0] for line in lines) * (rows // 2 + 1) // 16) * 16
    return pl.pallas_call(
        pack_kernel,
        out_shape=jax.ShapeDtypeStruct(((mirrors * rows + 2) * samples + extra, LANES), block.dtype),
        in_specs=[vmem] * (1 + len(lines)),
        out_specs=vmem,
        compiler_params=pltpu.CompilerParams(vmem_limit_bytes=VMEM_BYTES),
        cost_estimate=pl.CostEstimate(flops=0, bytes_accessed=3 * block.size, transcendentals=0),
        name="pack_influence",
    )(block, *lines)


def column_of(row):
    return jnp.transpose(jnp.broadcast_to(row, (LANES, LANES)), (1, 0))


def signs_kernel(table_ref, pokes_ref, codes_ref, words, own_signs, own_sums):
    planes = pokes_ref.shape[0]
    mirrors, rows, columns = table_ref.shape
    for line in range(codes_ref.shape[0]):
        pieces, at = [], line * LANES
        while at < (line + 1) * LANES:
            row, lane = divmod(at, columns)
            length = min(columns - lane, (line + 1) * LANES - at)
            pieces.append(table_ref[row // rows, row % rows:row % rows + 1, lane:lane + length])
            at += length
        codes_ref[line:line + 1, :] = jnp.concatenate(pieces, axis=1)
    half = LANES // 2
    own = own_signs.shape[0]
    plane = lax.broadcasted_iota(jnp.int32, pokes_ref.shape, 0)
    for bit in range(BITS):
        low = jnp.sum((pokes_ref[...] >> bit & 1) << plane, axis=0, keepdims=True)
        word = low | pltpu.roll(jnp.broadcast_to(low, (8, LANES)), half, 1)[:1] << planes
        words[bit] = column_of(word)[:half]
    count = codes_ref.shape[0] * LANES // (lax.axis_size("dir") * lax.axis_size("row"))
    first = (lax.axis_index("dir") * lax.axis_size("row") + lax.axis_index("row")) * count
    lane = lax.broadcasted_iota(jnp.int32, (8, LANES), 1)
    shift = first % LANES
    lines = [
        pltpu.roll(
            jnp.broadcast_to(
                codes_ref[pl.ds(jnp.minimum(first // LANES + n, codes_ref.shape[0] - 1), 1), :], (8, LANES)
            ),
            LANES - shift, 1,
        )
        for n in range(-(-own // LANES) + 1)
    ]
    own_column = jnp.concatenate(
        [column_of(jnp.where(lane < LANES - shift, lines[n], lines[n + 1])[:1]) for n in range(len(lines) - 1)],
        axis=0,
    )[:own]
    total = jnp.zeros((own, LANES), jnp.float32)
    for at in range(planes):
        signs = (1 - 2 * parity(own_column, pokes_ref[at:at + 1, :])).astype(jnp.float32)
        own_signs[:, at * LANES:(at + 1) * LANES] = signs.astype(NARROW)
        total = total + signs
    own_sums[...] = jnp.broadcast_to(jnp.sum(total, axis=1, keepdims=True), own_sums.shape)


def own_side(table, pokes, own):
    own = -(-own // 32) * 32
    vmem = pl.BlockSpec(memory_space=pltpu.VMEM)
    return pl.pallas_call(
        signs_kernel,
        out_shape=[
            jax.ShapeDtypeStruct((table.size // LANES, LANES), jnp.int32),
            jax.ShapeDtypeStruct((BITS, LANES // 2, LANES), jnp.int32),
            jax.ShapeDtypeStruct((own, pokes.size), NARROW),
            jax.ShapeDtypeStruct((own, LANES), jnp.float32),
        ],
        in_specs=[vmem] * 2,
        out_specs=[vmem] * 4,
        compiler_params=pltpu.CompilerParams(vmem_limit_bytes=VMEM_BYTES),
        name="own_signs",
    )(table, pokes)


def gram_kernel(row_shape, surface_rows, codes_ref, words, own_signs, own_sums, packed_ref, gram_out, first_ref, gram_ref, semaphores):
    mirror = pl.program_id(0)
    half = LANES // 2
    own, pokes = own_signs.shape
    planes = pokes // LANES
    lines = codes_ref.shape[0] // row_shape[0]
    height = gram_ref.shape[0] // row_shape[0]

    def chunk(index, _):
        word = []
        for side in range(WINDOW // LANES):
            line = mirror * lines + index * (WINDOW // LANES) + side
            code = jnp.broadcast_to(codes_ref[pl.ds(line, 1), :], (8, LANES))
            value = None
            for bit in range(BITS):
                mask = jnp.concatenate([code << (31 - bit) >> 31] * (half // 8), axis=0)
                part = words[bit] & mask
                value = part if value is None else value ^ part
            word.append(value)
        word = jnp.concatenate(word, axis=1)
        bits = [None] * (2 * planes)
        for byte in range(0, 2 * planes, 8):
            part = (word >> byte).astype(jnp.int8)
            for bit in range(8):
                at = byte + bit
                hit = (part & np.uint8(1 << bit).astype(np.int8)) != 0
                bits[at % planes * 2 + at // planes] = jnp.where(hit, NARROW(1.0), NARROW(0.0))
        total = jnp.dot(own_signs[...], jnp.concatenate(bits, axis=0), preferred_element_type=jnp.float32)
        sums = jnp.concatenate([own_sums[...]] * (WINDOW // LANES), axis=1)
        turned = jnp.transpose((sums - 2.0 * total).astype(jnp.bfloat16))
        at = pl.multiple_of(mirror * height + index * WINDOW, WINDOW)
        gram_ref[pl.ds(at, WINDOW), :] = turned
        return 0

    lax.fori_loop(0, height // WINDOW, chunk, 0, unroll=3)

    def send(k):
        part = pl.ds(pl.multiple_of(k * height, height), height)
        return pltpu.make_async_copy(gram_ref.at[part], gram_out.at[part], semaphores.at[k])

    send(mirror).start()
    block = lax.axis_index("row")
    for l in range(row_shape[1]):
        for k in range(row_shape[0]):
            @pl.when(mirror == k)
            def _():
                first_ref[0, l] = band_product(
                    [packed_ref], k * row_shape[1] + l, row_shape, block, surface_rows, gram_ref
                )

    @pl.when(mirror == pl.num_programs(0) - 1)
    def _():
        for k in range(row_shape[0]):
            send(k).wait()


def gram(codes, words, own_signs, own_sums, packed, row_shape, surface_rows):
    acts, (own, count) = codes.size, own_signs.shape
    mirrors, shard_rows, slots, samples = row_shape
    vmem = pl.BlockSpec(memory_space=pltpu.VMEM)
    return pl.pallas_call(
        functools.partial(gram_kernel, row_shape, surface_rows),
        grid=(mirrors,),
        out_shape=[
            jax.ShapeDtypeStruct((acts, own), jnp.bfloat16),
            jax.ShapeDtypeStruct((1, mirrors * shard_rows, samples, own), jnp.bfloat16),
        ],
        in_specs=[vmem] * 5,
        out_specs=[
            pl.BlockSpec(memory_space=pl.ANY),
            pl.BlockSpec((1, shard_rows, samples, own), lambda s: (0, s, 0, 0)),
        ],
        scratch_shapes=[pltpu.VMEM((acts, own), jnp.bfloat16), pltpu.SemaphoreType.DMA((mirrors,))],
        compiler_params=pltpu.CompilerParams(vmem_limit_bytes=VMEM_BYTES),
        cost_estimate=pl.CostEstimate(
            flops=2 * own * acts * count, bytes_accessed=2 * own * acts, transcendentals=0
        ),
        name="gram_rows",
    )(codes, words, own_signs, own_sums, packed)


def position(axis, staged):
    return lax.axis_index(axis) if staged else 0


def row_block(place, staged):
    if not staged:
        return place
    row = lax.axis_index("row")
    core = row & 1
    return row ^ [0, 1, 2 << core, 4 >> core, (4 >> core) | 1, (2 << core) | 1, 6, 7][place]


def row_place(block, staged):
    if not staged:
        return block
    row = lax.axis_index("row")
    core = row & 1
    distance = block ^ row
    near = jnp.where(distance == 2 << core, 2, 3)
    far = jnp.where(distance == (4 >> core) | 1, 4, 5)
    middle = jnp.where(distance & 1 == 0, near, far)
    return jnp.where((distance >= 2) & (distance < 6), middle, distance)


def band_product(parts, q, row_shape, block, surface_rows, gram_ref):
    mirrors, shard_rows, slots, samples = row_shape
    groups = mirrors * shard_rows // 2
    own = gram_ref.shape[1]
    narrow = slots - LANES
    k, l = divmod(q, shard_rows)
    band = jnp.clip((block * shard_rows + l) * NAR // surface_rows - 1, 0, NAR - BAND)
    column = pl.multiple_of((k * NAR + band) * NA, 16)
    part, group = divmod(q, groups)
    source, base = (parts[0], part * (groups + 1) * samples) if len(parts) == 1 else (parts[part], 0)
    left = jnp.concatenate(
        [source[pl.ds(base + group * samples, samples), :], source[pl.ds(base + groups * samples, samples), :]],
        axis=1,
    )
    right = [gram_ref[pl.ds(column, LANES), :]]
    if group:
        right.append(jnp.zeros((group * narrow, own), jnp.bfloat16))
    right.append(gram_ref[pl.ds(column + LANES, narrow), :])
    right.append(jnp.zeros((LANES - (group + 1) * narrow, own), jnp.bfloat16))
    return jnp.dot(left, jnp.concatenate(right, axis=0), preferred_element_type=jnp.float32).astype(jnp.bfloat16)


def fetch_gram(gram_any, gram_ref, semaphores, mirrors):
    height = gram_ref.shape[0] // mirrors
    return [
        pltpu.make_async_copy(
            gram_any.at[pl.ds(k * height, height)], gram_ref.at[pl.ds(k * height, height)], semaphores.at[k]
        )
        for k in range(mirrors)
    ]


def bands_kernel(row_shape, surface_rows, first, counts, staged, gram_any, *refs):
    mirrors, shard_rows, slots, samples = row_shape
    sources = [ref.at[n] for ref, count in zip(refs, counts) for n in range(count)]
    refs = refs[len(counts):]
    columns_ref = None
    if len(refs) == 8:
        columns_ref, out_ref, whole_ref, rest_ref, *refs = refs
    else:
        out_ref, *refs = refs
    gram_ref, blocks, gram_semaphores, block_semaphores = refs
    step = pl.program_id(0)
    gram_copies = fetch_gram(gram_any, gram_ref, gram_semaphores, mirrors)

    def fetch(n):
        return pltpu.make_async_copy(sources[n], blocks.at[n], block_semaphores.at[n])

    @pl.when(step == 0)
    def _():
        fetch(0).start()
        for copy in gram_copies:
            copy.start()
        for n in range(1, len(sources)):
            fetch(n).start()
        if columns_ref is not None:
            build_differences(columns_ref, whole_ref, rest_ref, mirrors, samples)

    for n in range(len(sources)):
        @pl.when(step == n)
        def _():
            fetch(n).wait()
            block = row_block(first + n, staged)
            for q in range(mirrors * shard_rows):
                if n == 0 and q % shard_rows == 0:
                    gram_copies[q // shard_rows].wait()
                out_ref[0, q] = band_product([blocks.at[n]], q, row_shape, block, surface_rows, gram_ref)


def bands(gram_rows, sources, first, staged, row_shape, surface_rows, columns=None, pupil=None):
    acts, own = gram_rows.shape
    mirrors, shard_rows, slots, samples = row_shape
    counts = [source.shape[0] for source in sources]
    rows = mirrors * shard_rows
    flops = 2 * own * WINDOW * samples * rows * sum(counts)
    vmem, anywhere = pl.BlockSpec(memory_space=pltpu.VMEM), pl.BlockSpec(memory_space=pl.ANY)
    out_shape = [jax.ShapeDtypeStruct((sum(counts), rows, samples, own), jnp.bfloat16)]
    out_specs = [pl.BlockSpec((1, rows, samples, own), lambda s: (s, 0, 0, 0))]
    arguments, in_specs = [gram_rows, *sources], [anywhere] * (1 + len(sources))
    if columns is not None:
        depth = mirrors * samples // WINDOW * WINDOW
        rest = 2 * (mirrors * samples - depth)
        out_shape += [
            jax.ShapeDtypeStruct((columns.shape[0], 2, pupil // 2, depth), jnp.bfloat16),
            jax.ShapeDtypeStruct((columns.shape[0], pupil, rest), jnp.bfloat16),
        ]
        out_specs += [vmem] * 2
        arguments.append(columns)
        in_specs.append(vmem)
    return pl.pallas_call(
        functools.partial(bands_kernel, row_shape, surface_rows, first, counts, staged),
        grid=(sum(counts),),
        out_shape=out_shape,
        in_specs=in_specs,
        out_specs=out_specs,
        scratch_shapes=[
            pltpu.VMEM((acts, own), jnp.bfloat16),
            pltpu.VMEM((sum(counts),) + sources[0].shape[1:], jnp.bfloat16),
            pltpu.SemaphoreType.DMA((mirrors,)),
            pltpu.SemaphoreType.DMA((sum(counts),)),
        ],
        compiler_params=pltpu.CompilerParams(vmem_limit_bytes=VMEM_BYTES),
        cost_estimate=pl.CostEstimate(
            flops=flops, bytes_accessed=2 * own * WINDOW * rows * sum(counts), transcendentals=0
        ),
        name="bands",
    )(*arguments)


def build_differences(columns_ref, whole_ref, rest_ref, mirrors, samples):
    half = whole_ref.shape[2]
    pupil, depth = 2 * half, whole_ref.shape[3]
    remainder = mirrors * samples - depth
    slope = lax.broadcasted_iota(jnp.int32, (half, pupil), 0)
    lane = lax.broadcasted_iota(jnp.int32, (half, pupil), 1)
    at = lax.broadcasted_iota(jnp.int32, (half, mirrors * samples), 1)
    for d in range(columns_ref.shape[0]):
        sides = []
        for side in range(2):
            hit = None
            for k in range(mirrors):
                line = jnp.broadcast_to(columns_ref[d, k:k + 1, :pupil], (half, pupil))
                column = jnp.sum(jnp.where(lane == slope * 2 + side, line, 0), axis=1, keepdims=True)
                here = (at == column + k * samples).astype(jnp.float32)
                hit = here if hit is None else hit + here
            sides.append(hit)
        across, down = sides[1] - sides[0], sides[1] + sides[0]
        whole_ref[d, 0] = across[:, :depth].astype(jnp.bfloat16)
        whole_ref[d, 1] = down[:, :depth].astype(jnp.bfloat16)
        blank = jnp.zeros((half, remainder), jnp.float32)
        upper = jnp.concatenate([across[:, depth:], blank], axis=1)
        lower = jnp.concatenate([blank, down[:, depth:]], axis=1)
        rest_ref[d] = jnp.concatenate([upper, lower], axis=0).astype(jnp.bfloat16)


def decode_kernel(row_shape, surface_rows, own, staged, norm, counts, late_parts, *refs):
    mirrors, shard_rows, slots, samples = row_shape
    whole_ref, rest_ref, *refs = refs
    lines_refs, refs = refs[:counts[0]], refs[counts[0]:]
    late_refs, refs = refs[:counts[1]], refs[counts[1]:]
    ready_refs, refs = refs[:counts[2]], refs[counts[2]:]
    (gram_any, out_ref, gram_ref, decoded, total, packed_lines, lines, scalars, *refs) = refs
    late_blocks, refs = refs[:counts[1]], refs[counts[1]:]
    gram_semaphores, ready_semaphores, line_semaphores, late_semaphores, scalar_semaphore = refs
    group = pl.program_id(0)
    directions, pupil = whole_ref.shape[0], 2 * whole_ref.shape[2]
    depth = whole_ref.shape[3]
    phases = out_ref.shape[2] // pupil
    blocks = surface_rows // shard_rows
    late = len(late_parts)
    ready = blocks - late
    width = shard_rows // 2 + 1
    extra = lines.shape[1]

    @pl.when(group == 0)
    def _():
        def started(copies):
            for copy in copies:
                copy.start()
            return copies

        ends = [ref.at[n, pl.ds(ref.shape[1] - extra, extra)] for ref in lines_refs for n in range(ref.shape[0])]
        line_copies = started([
            pltpu.make_async_copy(end, packed_lines.at[n], line_semaphores.at[n]) for n, end in enumerate(ends)
        ])
        late_copies = started([
            pltpu.make_async_copy(late_refs[n], late_blocks[n], late_semaphores.at[n]) for n in range(counts[1])
        ])
        gram_copies = started(fetch_gram(gram_any, gram_ref, gram_semaphores, mirrors)) if late else []
        ready_copies = started([
            pltpu.make_async_copy(block, decoded.at[n], ready_semaphores.at[n])
            for n, block in enumerate([ref.at[m] for ref in ready_refs for m in range(ref.shape[0])])
        ])
        for copy in line_copies + late_copies:
            copy.wait()
        held = [packed_lines[n] for n in range(len(ends))]
        at = 0
        for part in late_parts:
            at += part
            last = late_blocks[at - 1]
            held.append(last[pl.ds(last.shape[0] - extra, extra), :])
        for n, value in enumerate(held):
            lines[n] = value.astype(jnp.float32).astype(jnp.int32)
        to_scalars = pltpu.make_async_copy(lines, scalars, scalar_semaphore.at[0])
        to_scalars.start()
        at = 0
        for n, part in enumerate(late_parts):
            parts, at = late_blocks[at:at + part], at + part
            for q in range(mirrors * shard_rows):
                if n == 0 and q % shard_rows == 0:
                    gram_copies[q // shard_rows].wait()
                decoded[ready + n, q] = band_product(
                    parts, q, row_shape, row_block(ready + n, staged), surface_rows, gram_ref
                )
        to_scalars.wait()
        for copy in ready_copies:
            copy.wait()

    for d in range(directions):
        held = d
        products, factors = [], []
        for phase in range(phases):
            i = group * phases + phase
            block = row_place(2 * i // shard_rows, staged)
            sums, changes = [], []
            for k in range(mirrors):
                picked = []
                for y in range(2):
                    row = scalars[block, held * width + width - 1, k * shard_rows + (2 * phase + y) % shard_rows]
                    picked.append(decoded[row_place(row // shard_rows, staged), k * shard_rows + row % shard_rows])
                sums.append(picked[0] + picked[1])
                changes.append(picked[1] - picked[0])
            right = [jnp.concatenate(rows, axis=0) for rows in (sums, changes)]
            mixed = jnp.concatenate([rows[depth:] for rows in right], axis=0)
            rest = jnp.dot(rest_ref[held], mixed, preferred_element_type=jnp.float32)
            for kind, rows in enumerate(right):
                whole = jnp.dot(whole_ref[held, kind], rows[:depth], preferred_element_type=jnp.float32)
                products.append(whole + rest[kind * pupil // 2:(kind + 1) * pupil // 2])
            valid = lines[block, pl.ds(held * width + phase % (shard_rows // 2), 1), :][:, :pupil // 2]
            factors += [valid.astype(jnp.float32) * norm] * 2
        product = jnp.concatenate(products, axis=0)
        factor = jnp.concatenate(factors, axis=1)
        for tile in range(out_ref.shape[2] // LANES):
            at = tile * LANES
            value = jnp.transpose(product[at:at + LANES])[:own] * factor[:, at:at + LANES]
            total[tile, pl.ds(d, own, stride=directions), :] = value
    for tile in range(out_ref.shape[2] // LANES):
        value = total[tile].reshape(own, directions, LANES)
        out_ref[:, :, tile * LANES:(tile + 1) * LANES] = value.astype(out_ref.dtype)


def decode(differences, sources, late, ready, gram_rows, own, row_shape, surface_rows, pupil, norm, staged):
    mirrors, shard_rows, slots, samples = row_shape
    acts, padded = gram_rows.shape
    directions = differences[0].shape[0]
    blocks = surface_rows // shard_rows
    extra = -(-directions * (shard_rows // 2 + 1) // 16) * 16
    phases = LANES // math.gcd(pupil, LANES)
    width = surface_rows // 2 * pupil
    lanes = phases * pupil
    flops = 2 * padded * mirrors * samples * pupil * directions * surface_rows // 2
    vmem, anywhere = pl.BlockSpec(memory_space=pltpu.VMEM), pl.BlockSpec(memory_space=pl.ANY)
    parts = [part for block in late for part in block]
    counts = (len(sources), len(parts), len(ready))
    semaphores = [mirrors, blocks, blocks, max(len(parts), 1), 1]
    return pl.pallas_call(
        functools.partial(
            decode_kernel, row_shape, surface_rows, own, staged, norm, counts, [len(block) for block in late]
        ),
        grid=(width // lanes,),
        out_shape=jax.ShapeDtypeStruct((own, directions, width), jnp.bfloat16),
        in_specs=[vmem] * 2 + [anywhere] * (sum(counts) + 1),
        out_specs=pl.BlockSpec((own, directions, lanes), lambda s: (0, 0, s)),
        scratch_shapes=[
            pltpu.VMEM((acts, padded), jnp.bfloat16),
            pltpu.VMEM((blocks, mirrors * shard_rows, samples, padded), jnp.bfloat16),
            pltpu.VMEM((lanes // LANES, own * directions, LANES), jnp.float32),
            pltpu.VMEM((blocks, extra, LANES), jnp.bfloat16),
            pltpu.VMEM((blocks, extra, LANES), jnp.int32),
            pltpu.SMEM((blocks, extra, LANES), jnp.int32),
            *[pltpu.VMEM(part.shape, part.dtype) for part in parts],
            *[pltpu.SemaphoreType.DMA((count,)) for count in semaphores],
        ],
        compiler_params=pltpu.CompilerParams(vmem_limit_bytes=VMEM_BYTES),
        cost_estimate=pl.CostEstimate(flops=flops, bytes_accessed=2 * own * directions * width, transcendentals=0),
        name="decode",
    )(*differences, *sources, *parts, *ready, gram_rows)


def swap(block, axis, distance):
    return lax.ppermute(block, axis, [(i, i ^ distance) for i in range(lax.axis_size(axis))])


def turn(block, even, odd):
    return lax.ppermute(
        block, "row", [(i, i ^ (odd if i % 2 else even)) for i in range(lax.axis_size("row"))]
    )


def shards(influence, foot_rows, foot_columns, actuator_codes, poke_rows, subaperture_valid):
    mirrors, shard_rows, samples, slots = influence.shape
    row_shape = (mirrors, shard_rows, slots, samples)
    directions, devices = lax.axis_size("dir"), lax.axis_size("row")
    surface_rows = shard_rows * devices
    pupil = foot_columns.shape[2]
    norm = 0.5 * poke_rows.shape[0] ** (-0.5)
    own = actuator_codes.size // (directions * devices)
    staged = devices == 8 and directions & (directions - 1) == 0
    turned = jnp.swapaxes(influence, 2, 3)
    pokes = poke_rows.reshape(-1, LANES)
    lines = small_lines(foot_rows, foot_columns, subaperture_valid)
    if not staged:
        lines = lax.all_gather(lines, "dir")
        packed = pack(turned, [lines])
        every = lax.all_gather(packed, "row")
        gram_rows, _ = gram(*own_side(actuator_codes, pokes, own), packed, row_shape, surface_rows)
        ready, *differences = bands(gram_rows, [every], 0, staged, row_shape, surface_rows, lines, pupil)
        return decode(
            differences, [every], [], [ready], gram_rows, own, row_shape, surface_rows, pupil, norm, staged
        )

    lines = lax.all_to_all(jnp.broadcast_to(lines, (directions,) + lines.shape), "dir", 0, 0, tiled=True)
    packed = pack(turned, [lines])
    packed, pokes = lax.optimization_barrier((packed, pokes))
    first, second = turn(packed, 2, 4), turn(packed, 4, 2)
    sibling = swap(packed, "row", 1)
    gram_rows, own_rows = gram(*own_side(actuator_codes, pokes, own), packed, row_shape, surface_rows)
    gram_rows, first, second = lax.optimization_barrier((gram_rows, first, second))
    first_sibling, second_sibling = swap(first, "row", 1), swap(second, "row", 1)
    diagonal = turn(first, 4, 2)
    sources = [source[None] for source in (sibling, first, second)]
    near, *differences = bands(gram_rows, sources, 1, staged, row_shape, surface_rows, lines, pupil)
    near, first_sibling, second_sibling = lax.optimization_barrier((near, first_sibling, second_sibling))
    others = [first_sibling[None], second_sibling[None]]
    far, = bands(gram_rows, others, 4, staged, row_shape, surface_rows)
    far, diagonal = lax.optimization_barrier((far, diagonal))
    late = [[diagonal], [swap(diagonal, "row", 1)]]
    return decode(
        differences, [packed[None], *sources, *others], late, [own_rows, near, far], gram_rows, own, row_shape,
        surface_rows, pupil, norm, staged,
    )


def solution(mesh):
    return jax.shard_map(
        shards,
        mesh=mesh,
        in_specs=(
            P(None, "row", None, None),
            P("dir", None, "row"),
            P("dir", None, None),
            P(),
            P(),
            P("dir", "row", None),
        ),
        out_specs=P(("dir", "row"), None, None),
        check_vma=False,
    )
```

```python
import functools
import math

import jax
import jax.numpy as jnp
import numpy as np
from jax import lax
from jax.experimental import pallas as pl
from jax.experimental.pallas import tpu as pltpu
from jax.sharding import PartitionSpec as P

NAR = 48
NA = 48
BAND = 3
REACH = 2
BITS = 13
NARROW = jnp.float8_e4m3fn
LANES = 128
WINDOW = 256
VMEM_BYTES = 127 * 512 * 1024


def parity(codes, rows):
    return lax.population_count(codes & rows) & 1


def lines_kernel(rows_ref, columns_ref, valid_ref, lines_ref):
    mirrors, rows = rows_ref.shape[0], rows_ref.shape[2]
    lines_ref[...] = jnp.zeros(lines_ref.shape, lines_ref.dtype)
    lines_ref[mirrors:mirrors + valid_ref.shape[1], :valid_ref.shape[2]] = valid_ref[0]
    for k in range(mirrors):
        lines_ref[k:k + 1, :columns_ref.shape[2]] = columns_ref[k]
        lines_ref[mirrors + valid_ref.shape[1]:mirrors + valid_ref.shape[1] + 1, k * rows:(k + 1) * rows] = rows_ref[k]


def small_lines(foot_rows, foot_columns, valid):
    vmem = pl.BlockSpec(memory_space=pltpu.VMEM)
    count = foot_rows.shape[1] + valid.shape[1] + 1
    return pl.pallas_call(
        lines_kernel,
        out_shape=jax.ShapeDtypeStruct((-(-count // 8) * 8, WINDOW), jnp.int32),
        in_specs=[vmem] * 3,
        out_specs=vmem,
        name="small_lines",
    )(jnp.swapaxes(foot_rows, 0, 1), jnp.swapaxes(foot_columns, 0, 1), valid)


def pack_kernel(block_ref, *refs):
    lines_refs, packed_ref = refs[:-1], refs[-1]
    mirrors, rows, slots, samples = block_ref.shape
    groups = mirrors * rows // 2
    identity = (
        lax.broadcasted_iota(jnp.int32, (samples, samples), 0) == lax.broadcasted_iota(jnp.int32, (samples, samples), 1)
    ).astype(jnp.float32).astype(jnp.bfloat16)
    for part in range(2):
        base = part * (groups + 1) * samples
        tails = []
        for group in range(groups):
            k, l = divmod(part * groups + group, rows)
            turned = lax.dot_general(
                identity, block_ref[k, l], (((1,), (1,)), ((), ())), preferred_element_type=jnp.float32
            ).astype(jnp.bfloat16)
            packed_ref[pl.ds(base + group * samples, samples), :] = turned[:, :LANES]
            tails.append(turned[:, LANES:])
        tails.append(jnp.zeros((samples, LANES - groups * (slots - LANES)), jnp.bfloat16))
        packed_ref[pl.ds(base + groups * samples, samples), :] = jnp.concatenate(tails, axis=1)
    count = rows // 2 + 1
    lines = [ref[n, mirrors:mirrors + count, :LANES] for ref in lines_refs for n in range(ref.shape[0])]
    extra = packed_ref.shape[0] - 2 * (groups + 1) * samples
    lines.append(jnp.zeros((extra - count * len(lines), LANES), jnp.int32))
    packed_ref[pl.ds(packed_ref.shape[0] - extra, extra), :] = (
        jnp.concatenate(lines, axis=0).astype(jnp.float32).astype(jnp.bfloat16)
    )


def pack(block, lines):
    mirrors, rows, slots, samples = block.shape
    vmem = pl.BlockSpec(memory_space=pltpu.VMEM)
    extra = -(-sum(line.shape[0] for line in lines) * (rows // 2 + 1) // 16) * 16
    return pl.pallas_call(
        pack_kernel,
        out_shape=jax.ShapeDtypeStruct(((mirrors * rows + 2) * samples + extra, LANES), block.dtype),
        in_specs=[vmem] * (1 + len(lines)),
        out_specs=vmem,
        compiler_params=pltpu.CompilerParams(vmem_limit_bytes=VMEM_BYTES),
        cost_estimate=pl.CostEstimate(flops=0, bytes_accessed=3 * block.size, transcendentals=0),
        name="pack_influence",
    )(block, *lines)


def column_of(row):
    return jnp.transpose(jnp.broadcast_to(row, (LANES, LANES)), (1, 0))


def signs_kernel(table_ref, pokes_ref, codes_ref, words, own_signs, own_sums):
    planes = pokes_ref.shape[0]
    mirrors, rows, columns = table_ref.shape
    for line in range(codes_ref.shape[0]):
        pieces, at = [], line * LANES
        while at < (line + 1) * LANES:
            row, lane = divmod(at, columns)
            length = min(columns - lane, (line + 1) * LANES - at)
            pieces.append(table_ref[row // rows, row % rows:row % rows + 1, lane:lane + length])
            at += length
        codes_ref[line:line + 1, :] = jnp.concatenate(pieces, axis=1)
    half = LANES // 2
    own = own_signs.shape[0]
    plane = lax.broadcasted_iota(jnp.int32, pokes_ref.shape, 0)
    for bit in range(BITS):
        low = jnp.sum((pokes_ref[...] >> bit & 1) << plane, axis=0, keepdims=True)
        word = low | pltpu.roll(jnp.broadcast_to(low, (8, LANES)), half, 1)[:1] << planes
        words[bit] = column_of(word)[:half]
    count = codes_ref.shape[0] * LANES // (lax.axis_size("dir") * lax.axis_size("row"))
    first = (lax.axis_index("dir") * lax.axis_size("row") + lax.axis_index("row")) * count
    lane = lax.broadcasted_iota(jnp.int32, (8, LANES), 1)
    shift = first % LANES
    lines = [
        pltpu.roll(
            jnp.broadcast_to(
                codes_ref[pl.ds(jnp.minimum(first // LANES + n, codes_ref.shape[0] - 1), 1), :], (8, LANES)
            ),
            LANES - shift, 1,
        )
        for n in range(-(-own // LANES) + 1)
    ]
    own_column = jnp.concatenate(
        [column_of(jnp.where(lane < LANES - shift, lines[n], lines[n + 1])[:1]) for n in range(len(lines) - 1)],
        axis=0,
    )[:own]
    total = jnp.zeros((own, LANES), jnp.float32)
    for at in range(planes):
        signs = (1 - 2 * parity(own_column, pokes_ref[at:at + 1, :])).astype(jnp.float32)
        own_signs[:, at * LANES:(at + 1) * LANES] = signs.astype(NARROW)
        total = total + signs
    own_sums[...] = jnp.broadcast_to(jnp.sum(total, axis=1, keepdims=True), own_sums.shape)


def own_side(table, pokes, own):
    own = -(-own // 32) * 32
    vmem = pl.BlockSpec(memory_space=pltpu.VMEM)
    return pl.pallas_call(
        signs_kernel,
        out_shape=[
            jax.ShapeDtypeStruct((table.size // LANES, LANES), jnp.int32),
            jax.ShapeDtypeStruct((BITS, LANES // 2, LANES), jnp.int32),
            jax.ShapeDtypeStruct((own, pokes.size), NARROW),
            jax.ShapeDtypeStruct((own, LANES), jnp.float32),
        ],
        in_specs=[vmem] * 2,
        out_specs=[vmem] * 4,
        compiler_params=pltpu.CompilerParams(vmem_limit_bytes=VMEM_BYTES),
        name="own_signs",
    )(table, pokes)


def gram_kernel(row_shape, surface_rows, codes_ref, words, own_signs, own_sums, packed_ref, gram_out, first_ref, gram_ref, semaphores):
    mirror = pl.program_id(0)
    half = LANES // 2
    own, pokes = own_signs.shape
    planes = pokes // LANES
    lines = codes_ref.shape[0] // row_shape[0]
    height = gram_ref.shape[0] // row_shape[0]

    def chunk(index, _):
        word = []
        for side in range(WINDOW // LANES):
            line = mirror * lines + index * (WINDOW // LANES) + side
            code = jnp.broadcast_to(codes_ref[pl.ds(line, 1), :], (8, LANES))
            value = None
            for bit in range(BITS):
                mask = jnp.concatenate([code << (31 - bit) >> 31] * (half // 8), axis=0)
                part = words[bit] & mask
                value = part if value is None else value ^ part
            word.append(value)
        word = jnp.concatenate(word, axis=1)
        bits = [None] * (2 * planes)
        for byte in range(0, 2 * planes, 8):
            part = (word >> byte).astype(jnp.int8)
            for bit in range(8):
                at = byte + bit
                hit = (part & np.uint8(1 << bit).astype(np.int8)) != 0
                bits[at % planes * 2 + at // planes] = jnp.where(hit, NARROW(1.0), NARROW(0.0))
        total = jnp.dot(own_signs[...], jnp.concatenate(bits, axis=0), preferred_element_type=jnp.float32)
        sums = jnp.concatenate([own_sums[...]] * (WINDOW // LANES), axis=1)
        turned = jnp.transpose((sums - 2.0 * total).astype(jnp.bfloat16))
        at = pl.multiple_of(mirror * height + index * WINDOW, WINDOW)
        gram_ref[pl.ds(at, WINDOW), :] = turned
        return 0

    lax.fori_loop(0, height // WINDOW, chunk, 0, unroll=3)

    def send(k):
        part = pl.ds(pl.multiple_of(k * height, height), height)
        return pltpu.make_async_copy(gram_ref.at[part], gram_out.at[part], semaphores.at[k])

    send(mirror).start()
    block = lax.axis_index("row")
    for l in range(row_shape[1]):
        for k in range(row_shape[0]):
            @pl.when(mirror == k)
            def _():
                first_ref[0, l] = band_product(
                    packed_ref, k * row_shape[1] + l, row_shape, block, surface_rows,
                    gram_ref.at[pl.ds(k * height, height)], 0,
                )

    @pl.when(mirror == pl.num_programs(0) - 1)
    def _():
        for k in range(row_shape[0]):
            send(k).wait()


def gram(codes, words, own_signs, own_sums, packed, row_shape, surface_rows):
    acts, (own, count) = codes.size, own_signs.shape
    mirrors, shard_rows, slots, samples = row_shape
    vmem = pl.BlockSpec(memory_space=pltpu.VMEM)
    return pl.pallas_call(
        functools.partial(gram_kernel, row_shape, surface_rows),
        grid=(mirrors,),
        out_shape=[
            jax.ShapeDtypeStruct((acts, own), jnp.bfloat16),
            jax.ShapeDtypeStruct((1, mirrors * shard_rows, samples, own), jnp.bfloat16),
        ],
        in_specs=[vmem] * 5,
        out_specs=[
            pl.BlockSpec(memory_space=pl.ANY),
            pl.BlockSpec((1, shard_rows, samples, own), lambda s: (0, s, 0, 0)),
        ],
        scratch_shapes=[pltpu.VMEM((acts, own), jnp.bfloat16), pltpu.SemaphoreType.DMA((mirrors,))],
        compiler_params=pltpu.CompilerParams(vmem_limit_bytes=VMEM_BYTES),
        cost_estimate=pl.CostEstimate(
            flops=2 * own * acts * count, bytes_accessed=2 * own * acts, transcendentals=0
        ),
        name="gram_rows",
    )(codes, words, own_signs, own_sums, packed)


def position(axis, staged):
    return lax.axis_index(axis) if staged else 0


def row_block(place, staged):
    if not staged:
        return place
    row = lax.axis_index("row")
    core = row & 1
    return row ^ [0, 1, 2 << core, 4 >> core, (4 >> core) | 1, (2 << core) | 1, 6, 7][place]


def row_place(block, staged):
    if not staged:
        return block
    row = lax.axis_index("row")
    core = row & 1
    distance = block ^ row
    near = jnp.where(distance == 2 << core, 2, 3)
    far = jnp.where(distance == (4 >> core) | 1, 4, 5)
    middle = jnp.where(distance & 1 == 0, near, far)
    return jnp.where((distance >= 2) & (distance < 6), middle, distance)


def band_of(row, surface_rows):
    return jnp.clip(row * NAR // surface_rows - 1, 0, NAR - BAND)


def band_span(shard_rows, surface_rows):
    bands_at = np.clip(np.arange(surface_rows) * NAR // surface_rows - 1, 0, NAR - BAND).reshape(-1, shard_rows)
    return int((bands_at[:, -1] - bands_at[:, 0]).max()) + BAND


def first_band(block, shard_rows, surface_rows):
    return jnp.minimum(band_of(block * shard_rows, surface_rows), NAR - band_span(shard_rows, surface_rows))


def band_product(source, q, row_shape, block, surface_rows, gram_view, first):
    mirrors, shard_rows, slots, samples = row_shape
    groups = mirrors * shard_rows // 2
    own = gram_view.shape[1]
    narrow = slots - LANES
    band = band_of(block * shard_rows + q % shard_rows, surface_rows)
    column = pl.multiple_of((band - first) * NA, 16)
    part, group = divmod(q, groups)
    base = part * (groups + 1) * samples
    left = jnp.concatenate(
        [source[pl.ds(base + group * samples, samples), :], source[pl.ds(base + groups * samples, samples), :]],
        axis=1,
    )
    right = [gram_view[pl.ds(column, LANES), :]]
    if group:
        right.append(jnp.zeros((group * narrow, own), jnp.bfloat16))
    right.append(gram_view[pl.ds(column + LANES, narrow), :])
    right.append(jnp.zeros((LANES - (group + 1) * narrow, own), jnp.bfloat16))
    return jnp.dot(left, jnp.concatenate(right, axis=0), preferred_element_type=jnp.float32).astype(jnp.bfloat16)


def fetch_gram(gram_any, gram_ref, semaphores, n, block, row_shape, surface_rows):
    height = gram_ref.shape[2]
    first = first_band(block, row_shape[1], surface_rows)
    return [
        pltpu.make_async_copy(
            gram_any.at[pl.ds(pl.multiple_of((k * NAR + first) * NA, 16), height)], gram_ref.at[n, k],
            semaphores.at[n, k],
        )
        for k in range(row_shape[0])
    ]


def block_products(source, n, row_shape, block, surface_rows, gram_ref, gram_copies, out_ref):
    shard_rows = row_shape[1]
    for q in range(row_shape[0] * shard_rows):
        if q % shard_rows == 0:
            gram_copies[q // shard_rows].wait()
        out_ref[q] = band_product(
            source, q, row_shape, block, surface_rows, gram_ref.at[n, q // shard_rows],
            first_band(block, shard_rows, surface_rows),
        )


def bands_kernel(row_shape, surface_rows, first, counts, staged, gram_any, *refs):
    mirrors, shard_rows, slots, samples = row_shape
    sources = [ref.at[n] for ref, count in zip(refs, counts) for n in range(count)]
    refs = refs[len(counts):]
    columns_ref = None
    if len(refs) == 8:
        columns_ref, out_ref, whole_ref, rest_ref, *refs = refs
    else:
        out_ref, *refs = refs
    gram_ref, blocks, gram_semaphores, block_semaphores = refs
    step = pl.program_id(0)
    places = [row_block(first + n, staged) for n in range(len(sources))]
    gram_copies = [
        fetch_gram(gram_any, gram_ref, gram_semaphores, n, block, row_shape, surface_rows)
        for n, block in enumerate(places)
    ]

    def fetch(n):
        return pltpu.make_async_copy(sources[n], blocks.at[n], block_semaphores.at[n])

    @pl.when(step == 0)
    def _():
        for n in range(len(sources)):
            fetch(n).start()
            for copy in gram_copies[n]:
                copy.start()
        if columns_ref is not None:
            build_differences(columns_ref, whole_ref, rest_ref, mirrors, samples)

    for n in range(len(sources)):
        @pl.when(step == n)
        def _():
            fetch(n).wait()
            block_products(
                blocks.at[n], n, row_shape, places[n], surface_rows, gram_ref, gram_copies[n], out_ref.at[0]
            )


def bands(gram_rows, sources, first, staged, row_shape, surface_rows, columns=None, pupil=None):
    acts, own = gram_rows.shape
    mirrors, shard_rows, slots, samples = row_shape
    counts = [source.shape[0] for source in sources]
    rows = mirrors * shard_rows
    flops = 2 * own * WINDOW * samples * rows * sum(counts)
    vmem, anywhere = pl.BlockSpec(memory_space=pltpu.VMEM), pl.BlockSpec(memory_space=pl.ANY)
    out_shape = [jax.ShapeDtypeStruct((sum(counts), rows, samples, own), jnp.bfloat16)]
    out_specs = [pl.BlockSpec((1, rows, samples, own), lambda s: (s, 0, 0, 0))]
    arguments, in_specs = [gram_rows, *sources], [anywhere] * (1 + len(sources))
    if columns is not None:
        depth = mirrors * samples // WINDOW * WINDOW
        rest = 2 * (mirrors * samples - depth)
        out_shape += [
            jax.ShapeDtypeStruct((columns.shape[0], 2, pupil // 2, depth), jnp.bfloat16),
            jax.ShapeDtypeStruct((columns.shape[0], pupil, rest), jnp.bfloat16),
        ]
        out_specs += [vmem] * 2
        arguments.append(columns)
        in_specs.append(vmem)
    return pl.pallas_call(
        functools.partial(bands_kernel, row_shape, surface_rows, first, counts, staged),
        grid=(sum(counts),),
        out_shape=out_shape,
        in_specs=in_specs,
        out_specs=out_specs,
        scratch_shapes=[
            pltpu.VMEM((sum(counts), mirrors, band_span(shard_rows, surface_rows) * NA, own), jnp.bfloat16),
            pltpu.VMEM((sum(counts),) + sources[0].shape[1:], jnp.bfloat16),
            pltpu.SemaphoreType.DMA((sum(counts), mirrors)),
            pltpu.SemaphoreType.DMA((sum(counts),)),
        ],
        compiler_params=pltpu.CompilerParams(vmem_limit_bytes=VMEM_BYTES),
        cost_estimate=pl.CostEstimate(
            flops=flops, bytes_accessed=2 * own * WINDOW * rows * sum(counts), transcendentals=0
        ),
        name="bands",
    )(*arguments)


def build_differences(columns_ref, whole_ref, rest_ref, mirrors, samples):
    half = whole_ref.shape[2]
    pupil, depth = 2 * half, whole_ref.shape[3]
    remainder = mirrors * samples - depth
    slope = lax.broadcasted_iota(jnp.int32, (half, pupil), 0)
    lane = lax.broadcasted_iota(jnp.int32, (half, pupil), 1)
    at = lax.broadcasted_iota(jnp.int32, (half, mirrors * samples), 1)
    for d in range(columns_ref.shape[0]):
        sides = []
        for side in range(2):
            hit = None
            for k in range(mirrors):
                line = jnp.broadcast_to(columns_ref[d, k:k + 1, :pupil], (half, pupil))
                column = jnp.sum(jnp.where(lane == slope * 2 + side, line, 0), axis=1, keepdims=True)
                here = (at == column + k * samples).astype(jnp.float32)
                hit = here if hit is None else hit + here
            sides.append(hit)
        across, down = sides[1] - sides[0], sides[1] + sides[0]
        whole_ref[d, 0] = across[:, :depth].astype(jnp.bfloat16)
        whole_ref[d, 1] = down[:, :depth].astype(jnp.bfloat16)
        blank = jnp.zeros((half, remainder), jnp.float32)
        upper = jnp.concatenate([across[:, depth:], blank], axis=1)
        lower = jnp.concatenate([blank, down[:, depth:]], axis=1)
        rest_ref[d] = jnp.concatenate([upper, lower], axis=0).astype(jnp.bfloat16)


def decode_kernel(row_shape, surface_rows, own, staged, norm, counts, *refs):
    mirrors, shard_rows, slots, samples = row_shape
    whole_ref, rest_ref, *refs = refs
    lines_refs, refs = refs[:counts[0]], refs[counts[0]:]
    late_refs, refs = refs[:counts[1]], refs[counts[1]:]
    ready_refs, refs = refs[:counts[2]], refs[counts[2]:]
    (gram_any, out_ref, gram_ref, decoded, total, packed_lines, lines, scalars, *refs) = refs
    late_blocks, refs = refs[:counts[1]], refs[counts[1]:]
    gram_semaphores, ready_semaphores, line_semaphores, late_semaphores, scalar_semaphore = refs
    group = pl.program_id(0)
    directions, pupil = whole_ref.shape[0], 2 * whole_ref.shape[2]
    depth = whole_ref.shape[3]
    phases = out_ref.shape[2] // pupil
    blocks = surface_rows // shard_rows
    late = counts[1]
    ready = blocks - late
    width = shard_rows // 2 + 1
    extra = lines.shape[1]

    ready_blocks = [ref.at[n] for ref in ready_refs for n in range(ref.shape[0])]

    def last_needed(at):
        return min((2 * phases * (at + 1) - 1 + REACH) // shard_rows, blocks - 1)

    @pl.when(group == 0)
    def _():
        def started(copies):
            for copy in copies:
                copy.start()
            return copies

        ends = [ref.at[n, pl.ds(ref.shape[1] - extra, extra)] for ref in lines_refs for n in range(ref.shape[0])]
        line_copies = started([
            pltpu.make_async_copy(end, packed_lines.at[n], line_semaphores.at[n]) for n, end in enumerate(ends)
        ])
        late_copies, gram_copies = [], []
        for n in range(late):
            late_copies += started([pltpu.make_async_copy(late_refs[n], late_blocks[n], late_semaphores.at[n])])
            gram_copies.append(started(fetch_gram(
                gram_any, gram_ref, gram_semaphores, n, row_block(ready + n, staged), row_shape, surface_rows
            )))
        for block in range(blocks):
            for place, source in enumerate(ready_blocks):
                @pl.when(row_place(block, staged) == place)
                def _():
                    pltpu.make_async_copy(source, decoded.at[place], ready_semaphores.at[place]).start()
        for copy in line_copies + late_copies:
            copy.wait()
        held = [packed_lines[n] for n in range(len(ends))]
        held += [block[pl.ds(block.shape[0] - extra, extra), :] for block in late_blocks]
        for n, value in enumerate(held):
            lines[n] = value.astype(jnp.float32).astype(jnp.int32)
        to_scalars = pltpu.make_async_copy(lines, scalars, scalar_semaphore.at[0])
        to_scalars.start()
        for n in range(late):
            block_products(
                late_blocks[n], n, row_shape, row_block(ready + n, staged), surface_rows, gram_ref, gram_copies[n],
                decoded.at[ready + n],
            )
        to_scalars.wait()

    for at in range(surface_rows // 2 // phases):
        @pl.when(group == at)
        def _():
            for block in range(last_needed(at - 1) + 1 if at else 0, last_needed(at) + 1):
                place = row_place(block, staged)

                @pl.when(place < ready)
                def _():
                    pltpu.make_async_copy(ready_blocks[0], decoded.at[place], ready_semaphores.at[place]).wait()

    for d in range(directions):
        held = d ^ position("dir", staged)
        products, factors = [], []
        for phase in range(phases):
            i = group * phases + phase
            block = row_place(2 * i // shard_rows, staged)
            sums, changes = [], []
            for k in range(mirrors):
                picked = []
                for y in range(2):
                    row = scalars[block, held * width + width - 1, k * shard_rows + (2 * phase + y) % shard_rows]
                    picked.append(decoded[row_place(row // shard_rows, staged), k * shard_rows + row % shard_rows])
                sums.append(picked[0] + picked[1])
                changes.append(picked[1] - picked[0])
            right = [jnp.concatenate(rows, axis=0) for rows in (sums, changes)]
            mixed = jnp.concatenate([rows[depth:] for rows in right], axis=0)
            rest = jnp.dot(rest_ref[held], mixed, preferred_element_type=jnp.float32)
            for kind, rows in enumerate(right):
                whole = jnp.dot(whole_ref[held, kind], rows[:depth], preferred_element_type=jnp.float32)
                products.append(whole + rest[kind * pupil // 2:(kind + 1) * pupil // 2])
            valid = lines[block, pl.ds(held * width + phase % (shard_rows // 2), 1), :][:, :pupil // 2]
            factors += [valid.astype(jnp.float32) * norm] * 2
        product = jnp.concatenate(products, axis=0)
        factor = jnp.concatenate(factors, axis=1)
        for tile in range(out_ref.shape[2] // LANES):
            at = tile * LANES
            value = jnp.transpose(product[at:at + LANES])[:own] * factor[:, at:at + LANES]
            total[tile, pl.ds(d, own, stride=directions), :] = value
    for tile in range(out_ref.shape[2] // LANES):
        value = total[tile].reshape(own, directions, LANES)
        out_ref[:, :, tile * LANES:(tile + 1) * LANES] = value.astype(out_ref.dtype)


def decode(differences, sources, late, ready, gram_rows, own, row_shape, surface_rows, pupil, norm, staged):
    mirrors, shard_rows, slots, samples = row_shape
    acts, padded = gram_rows.shape
    directions = differences[0].shape[0]
    blocks = surface_rows // shard_rows
    extra = -(-directions * (shard_rows // 2 + 1) // 16) * 16
    phases = LANES // math.gcd(pupil, LANES)
    width = surface_rows // 2 * pupil
    lanes = phases * pupil
    flops = 2 * padded * mirrors * samples * pupil * directions * surface_rows // 2
    vmem, anywhere = pl.BlockSpec(memory_space=pltpu.VMEM), pl.BlockSpec(memory_space=pl.ANY)
    counts = (len(sources), len(late), len(ready))
    semaphores = [(max(len(late), 1), mirrors), (blocks,), (blocks,), (max(len(late), 1),), (1,)]
    return pl.pallas_call(
        functools.partial(decode_kernel, row_shape, surface_rows, own, staged, norm, counts),
        grid=(width // lanes,),
        out_shape=jax.ShapeDtypeStruct((own, directions, width), jnp.bfloat16),
        in_specs=[vmem] * 2 + [anywhere] * (sum(counts) + 1),
        out_specs=pl.BlockSpec((own, directions, lanes), lambda s: (0, 0, s)),
        scratch_shapes=[
            pltpu.VMEM(
                (max(len(late), 1), mirrors, band_span(shard_rows, surface_rows) * NA, padded), jnp.bfloat16
            ),
            pltpu.VMEM((blocks, mirrors * shard_rows, samples, padded), jnp.bfloat16),
            pltpu.VMEM((lanes // LANES, own * directions, LANES), jnp.float32),
            pltpu.VMEM((blocks, extra, LANES), jnp.bfloat16),
            pltpu.VMEM((blocks, extra, LANES), jnp.int32),
            pltpu.SMEM((blocks, extra, LANES), jnp.int32),
            *[pltpu.VMEM(block.shape, block.dtype) for block in late],
            *[pltpu.SemaphoreType.DMA(count) for count in semaphores],
        ],
        compiler_params=pltpu.CompilerParams(vmem_limit_bytes=VMEM_BYTES),
        cost_estimate=pl.CostEstimate(flops=flops, bytes_accessed=2 * own * directions * width, transcendentals=0),
        name="decode",
    )(*differences, *sources, *late, *ready, gram_rows)


def swap(block, axis, distance):
    return lax.ppermute(block, axis, [(i, i ^ distance) for i in range(lax.axis_size(axis))])


def turn(block, even, odd):
    return lax.ppermute(
        block, "row", [(i, i ^ (odd if i % 2 else even)) for i in range(lax.axis_size("row"))]
    )


def shards(influence, foot_rows, foot_columns, actuator_codes, poke_rows, subaperture_valid):
    mirrors, shard_rows, samples, slots = influence.shape
    row_shape = (mirrors, shard_rows, slots, samples)
    directions, devices = lax.axis_size("dir"), lax.axis_size("row")
    surface_rows = shard_rows * devices
    pupil = foot_columns.shape[2]
    norm = 0.5 * poke_rows.shape[0] ** (-0.5)
    own = actuator_codes.size // (directions * devices)
    staged = devices == 8 and directions & (directions - 1) == 0
    turned = jnp.swapaxes(influence, 2, 3)
    pokes = poke_rows.reshape(-1, LANES)
    lines = small_lines(foot_rows, foot_columns, subaperture_valid)
    if not staged:
        lines = lax.all_gather(lines, "dir")
        packed = pack(turned, [lines])
        every = lax.all_gather(packed, "row")
        gram_rows, _ = gram(*own_side(actuator_codes, pokes, own), packed, row_shape, surface_rows)
        ready, *differences = bands(gram_rows, [every], 0, staged, row_shape, surface_rows, lines, pupil)
        return decode(
            differences, [every], [], [ready], gram_rows, own, row_shape, surface_rows, pupil, norm, staged
        )

    lines = jnp.stack([lines] + [swap(lines, "dir", e) for e in range(1, directions)])
    packed = pack(turned, [lines])
    packed, pokes = lax.optimization_barrier((packed, pokes))
    first, second = turn(packed, 2, 4), turn(packed, 4, 2)
    sibling = swap(packed, "row", 1)
    gram_rows, own_rows = gram(*own_side(actuator_codes, pokes, own), packed, row_shape, surface_rows)
    gram_rows, first, second = lax.optimization_barrier((gram_rows, first, second))
    first_sibling, second_sibling = swap(first, "row", 1), swap(second, "row", 1)
    diagonal = turn(first, 4, 2)
    sources = [source[None] for source in (sibling, first, second)]
    near, *differences = bands(gram_rows, sources, 1, staged, row_shape, surface_rows, lines, pupil)
    near, first_sibling, second_sibling, diagonal = lax.optimization_barrier(
        (near, first_sibling, second_sibling, diagonal)
    )
    late = [diagonal, swap(diagonal, "row", 1)]
    others = [first_sibling[None], second_sibling[None]]
    far, = bands(gram_rows, others, 4, staged, row_shape, surface_rows)
    return decode(
        differences, [packed[None], *sources, *others], late, [own_rows, near, far], gram_rows, own, row_shape,
        surface_rows, pupil, norm, staged,
    )


def solution(mesh):
    return jax.shard_map(
        shards,
        mesh=mesh,
        in_specs=(
            P(None, "row", None, None),
            P("dir", None, "row"),
            P("dir", None, None),
            P(),
            P(),
            P("dir", "row", None),
        ),
        out_specs=P(("dir", "row"), None, None),
        check_vma=False,
    )
```

```python
import functools
import math

import jax
import jax.numpy as jnp
import numpy as np
from jax import lax
from jax.experimental import pallas as pl
from jax.experimental.pallas import tpu as pltpu
from jax.sharding import PartitionSpec as P

NAR = 48
NA = 48
BAND = 3
BITS = 13
NARROW = jnp.float8_e4m3fn
LANES = 128
WINDOW = 256
VMEM_BYTES = 127 * 512 * 1024


def parity(codes, rows):
    return lax.population_count(codes & rows) & 1


def lines_kernel(rows_ref, columns_ref, valid_ref, lines_ref):
    mirrors, rows = rows_ref.shape[0], rows_ref.shape[2]
    lines_ref[...] = jnp.zeros(lines_ref.shape, lines_ref.dtype)
    lines_ref[mirrors:mirrors + valid_ref.shape[1], :valid_ref.shape[2]] = valid_ref[0]
    for k in range(mirrors):
        lines_ref[k:k + 1, :columns_ref.shape[2]] = columns_ref[k]
        lines_ref[mirrors + valid_ref.shape[1]:mirrors + valid_ref.shape[1] + 1, k * rows:(k + 1) * rows] = rows_ref[k]


def small_lines(foot_rows, foot_columns, valid):
    vmem = pl.BlockSpec(memory_space=pltpu.VMEM)
    count = foot_rows.shape[1] + valid.shape[1] + 1
    return pl.pallas_call(
        lines_kernel,
        out_shape=jax.ShapeDtypeStruct((-(-count // 8) * 8, WINDOW), jnp.int32),
        in_specs=[vmem] * 3,
        out_specs=vmem,
        name="small_lines",
    )(jnp.swapaxes(foot_rows, 0, 1), jnp.swapaxes(foot_columns, 0, 1), valid)


def pack_kernel(block_ref, *refs):
    lines_refs, packed_ref = refs[:-1], refs[-1]
    mirrors, rows, slots, samples = block_ref.shape
    groups = mirrors * rows // 2
    identity = (
        lax.broadcasted_iota(jnp.int32, (samples, samples), 0) == lax.broadcasted_iota(jnp.int32, (samples, samples), 1)
    ).astype(jnp.float32).astype(jnp.bfloat16)
    for part in range(2):
        base = part * (groups + 1) * samples
        tails = []
        for group in range(groups):
            k, l = divmod(part * groups + group, rows)
            turned = lax.dot_general(
                identity, block_ref[k, l], (((1,), (1,)), ((), ())), preferred_element_type=jnp.float32
            ).astype(jnp.bfloat16)
            packed_ref[pl.ds(base + group * samples, samples), :] = turned[:, :LANES]
            tails.append(turned[:, LANES:])
        tails.append(jnp.zeros((samples, LANES - groups * (slots - LANES)), jnp.bfloat16))
        packed_ref[pl.ds(base + groups * samples, samples), :] = jnp.concatenate(tails, axis=1)
    count = rows // 2
    every = [ref.at[n] for ref in lines_refs for n in range(ref.shape[0])]
    feet = [ref[mirrors + count:mirrors + count + 1, :mirrors * rows] for ref in every]
    feet.append(jnp.zeros((1, LANES - mirrors * rows * len(every)), jnp.int32))
    lines = [ref[mirrors:mirrors + count, :LANES] for ref in every] + [jnp.concatenate(feet, axis=1)]
    extra = packed_ref.shape[0] - 2 * (groups + 1) * samples
    lines.append(jnp.zeros((extra - count * len(every) - 1, LANES), jnp.int32))
    packed_ref[pl.ds(packed_ref.shape[0] - extra, extra), :] = (
        jnp.concatenate(lines, axis=0).astype(jnp.float32).astype(jnp.bfloat16)
    )


def extra_rows(directions, rows):
    return -(-(directions * (rows // 2) + 1) // 16) * 16


def pack(block, lines):
    mirrors, rows, slots, samples = block.shape
    vmem = pl.BlockSpec(memory_space=pltpu.VMEM)
    extra = extra_rows(sum(line.shape[0] for line in lines), rows)
    return pl.pallas_call(
        pack_kernel,
        out_shape=jax.ShapeDtypeStruct(((mirrors * rows + 2) * samples + extra, LANES), block.dtype),
        in_specs=[vmem] * (1 + len(lines)),
        out_specs=vmem,
        compiler_params=pltpu.CompilerParams(vmem_limit_bytes=VMEM_BYTES),
        cost_estimate=pl.CostEstimate(flops=0, bytes_accessed=3 * block.size, transcendentals=0),
        name="pack_influence",
    )(block, *lines)


def column_of(row):
    return jnp.transpose(jnp.broadcast_to(row, (LANES, LANES)), (1, 0))


def own_side_of(table_ref, pokes_ref, codes_ref, words, own_signs, own_sums):
    planes = pokes_ref.shape[0]
    mirrors, rows, columns = table_ref.shape
    for line in range(codes_ref.shape[0]):
        pieces, at = [], line * LANES
        while at < (line + 1) * LANES:
            row, lane = divmod(at, columns)
            length = min(columns - lane, (line + 1) * LANES - at)
            pieces.append(table_ref[row // rows, row % rows:row % rows + 1, lane:lane + length])
            at += length
        codes_ref[line:line + 1, :] = jnp.concatenate(pieces, axis=1)
    half = LANES // 2
    own = own_signs.shape[0]
    plane = lax.broadcasted_iota(jnp.int32, pokes_ref.shape, 0)
    for bit in range(BITS):
        low = jnp.sum((pokes_ref[...] >> bit & 1) << plane, axis=0, keepdims=True)
        word = low | pltpu.roll(jnp.broadcast_to(low, (8, LANES)), half, 1)[:1] << planes
        words[bit] = column_of(word)[:half]
    count = codes_ref.shape[0] * LANES // (lax.axis_size("dir") * lax.axis_size("row"))
    first = (lax.axis_index("dir") * lax.axis_size("row") + lax.axis_index("row")) * count
    lane = lax.broadcasted_iota(jnp.int32, (8, LANES), 1)
    shift = first % LANES
    lines = [
        pltpu.roll(
            jnp.broadcast_to(
                codes_ref[pl.ds(jnp.minimum(first // LANES + n, codes_ref.shape[0] - 1), 1), :], (8, LANES)
            ),
            LANES - shift, 1,
        )
        for n in range(-(-own // LANES) + 1)
    ]
    own_column = jnp.concatenate(
        [column_of(jnp.where(lane < LANES - shift, lines[n], lines[n + 1])[:1]) for n in range(len(lines) - 1)],
        axis=0,
    )[:own]
    total = jnp.zeros((own, LANES), jnp.float32)
    for at in range(planes):
        signs = (1 - 2 * parity(own_column, pokes_ref[at:at + 1, :])).astype(jnp.float32)
        own_signs[:, at * LANES:(at + 1) * LANES] = signs.astype(NARROW)
        total = total + signs
    own_sums[...] = jnp.broadcast_to(jnp.sum(total, axis=1, keepdims=True), own_sums.shape)


def gram_kernel(
    row_shape, surface_rows, table_ref, pokes_ref, packed_ref, gram_out, first_ref, gram_ref, codes_ref, words,
    own_signs, own_sums, semaphores
):
    mirror = pl.program_id(0)
    half = LANES // 2
    own, pokes = own_signs.shape
    planes = pokes // LANES
    lines = codes_ref.shape[0] // row_shape[0]
    height = gram_ref.shape[0] // row_shape[0]

    @pl.when(mirror == 0)
    def _():
        own_side_of(table_ref, pokes_ref, codes_ref, words, own_signs, own_sums)

    def chunk(index, _):
        word = []
        for side in range(WINDOW // LANES):
            line = mirror * lines + index * (WINDOW // LANES) + side
            code = jnp.broadcast_to(codes_ref[pl.ds(line, 1), :], (8, LANES))
            value = None
            for bit in range(BITS):
                mask = jnp.concatenate([code << (31 - bit) >> 31] * (half // 8), axis=0)
                part = words[bit] & mask
                value = part if value is None else value ^ part
            word.append(value)
        word = jnp.concatenate(word, axis=1)
        bits = [None] * (2 * planes)
        for byte in range(0, 2 * planes, 8):
            part = (word >> byte).astype(jnp.int8)
            for bit in range(8):
                at = byte + bit
                hit = (part & np.uint8(1 << bit).astype(np.int8)) != 0
                bits[at % planes * 2 + at // planes] = jnp.where(hit, NARROW(1.0), NARROW(0.0))
        total = jnp.dot(own_signs[...], jnp.concatenate(bits, axis=0), preferred_element_type=jnp.float32)
        sums = jnp.concatenate([own_sums[...]] * (WINDOW // LANES), axis=1)
        turned = jnp.transpose((sums - 2.0 * total).astype(jnp.bfloat16))
        at = pl.multiple_of(mirror * height + index * WINDOW, WINDOW)
        gram_ref[pl.ds(at, WINDOW), :] = turned
        return 0

    lax.fori_loop(0, height // WINDOW, chunk, 0, unroll=3)

    def send(k):
        part = pl.ds(pl.multiple_of(k * height, height), height)
        return pltpu.make_async_copy(gram_ref.at[part], gram_out.at[part], semaphores.at[k])

    send(mirror).start()
    block = lax.axis_index("row")
    for l in range(row_shape[1]):
        for k in range(row_shape[0]):
            @pl.when(mirror == k)
            def _():
                first_ref[0, l] = band_product(
                    [packed_ref], k * row_shape[1] + l, row_shape, block, surface_rows, gram_ref
                )

    @pl.when(mirror == pl.num_programs(0) - 1)
    def _():
        for k in range(row_shape[0]):
            send(k).wait()


def gram(table, pokes, packed, own, row_shape, surface_rows):
    own = -(-own // 32) * 32
    acts, count = table.size, pokes.size
    mirrors, shard_rows, slots, samples = row_shape
    vmem = pl.BlockSpec(memory_space=pltpu.VMEM)
    return pl.pallas_call(
        functools.partial(gram_kernel, row_shape, surface_rows),
        grid=(mirrors,),
        out_shape=[
            jax.ShapeDtypeStruct((acts, own), jnp.bfloat16),
            jax.ShapeDtypeStruct((1, mirrors * shard_rows, samples, own), jnp.bfloat16),
        ],
        in_specs=[vmem] * 3,
        out_specs=[
            pl.BlockSpec(memory_space=pl.ANY),
            pl.BlockSpec((1, shard_rows, samples, own), lambda s: (0, s, 0, 0)),
        ],
        scratch_shapes=[
            pltpu.VMEM((acts, own), jnp.bfloat16),
            pltpu.VMEM((acts // LANES, LANES), jnp.int32),
            pltpu.VMEM((BITS, LANES // 2, LANES), jnp.int32),
            pltpu.VMEM((own, count), NARROW),
            pltpu.VMEM((own, LANES), jnp.float32),
            pltpu.SemaphoreType.DMA((mirrors,)),
        ],
        compiler_params=pltpu.CompilerParams(vmem_limit_bytes=VMEM_BYTES),
        cost_estimate=pl.CostEstimate(
            flops=2 * own * acts * count, bytes_accessed=2 * own * acts, transcendentals=0
        ),
        name="gram_rows",
    )(table, pokes, packed)


def position(axis, staged):
    return lax.axis_index(axis) if staged else 0


def row_block(place, staged):
    if not staged:
        return place
    row = lax.axis_index("row")
    core = row & 1
    return row ^ [0, 1, 2 << core, 4 >> core, (4 >> core) | 1, (2 << core) | 1, 6, 7][place]


def row_place(block, staged):
    if not staged:
        return block
    row = lax.axis_index("row")
    core = row & 1
    distance = block ^ row
    near = jnp.where(distance == 2 << core, 2, 3)
    far = jnp.where(distance == (4 >> core) | 1, 4, 5)
    middle = jnp.where(distance & 1 == 0, near, far)
    return jnp.where((distance >= 2) & (distance < 6), middle, distance)


def band_product(parts, q, row_shape, block, surface_rows, gram_ref):
    mirrors, shard_rows, slots, samples = row_shape
    groups = mirrors * shard_rows // 2
    own = gram_ref.shape[1]
    narrow = slots - LANES
    k, l = divmod(q, shard_rows)
    band = jnp.clip((block * shard_rows + l) * NAR // surface_rows - 1, 0, NAR - BAND)
    column = pl.multiple_of((k * NAR + band) * NA, 16)
    part, group = divmod(q, groups)
    source, base = (parts[0], part * (groups + 1) * samples) if len(parts) == 1 else (parts[part], 0)
    left = jnp.concatenate(
        [source[pl.ds(base + group * samples, samples), :], source[pl.ds(base + groups * samples, samples), :]],
        axis=1,
    )
    right = [gram_ref[pl.ds(column, LANES), :]]
    if group:
        right.append(jnp.zeros((group * narrow, own), jnp.bfloat16))
    right.append(gram_ref[pl.ds(column + LANES, narrow), :])
    right.append(jnp.zeros((LANES - (group + 1) * narrow, own), jnp.bfloat16))
    return jnp.dot(left, jnp.concatenate(right, axis=0), preferred_element_type=jnp.float32).astype(jnp.bfloat16)


def fetch_gram(gram_any, gram_ref, semaphores, mirrors):
    height = gram_ref.shape[0] // mirrors
    return [
        pltpu.make_async_copy(
            gram_any.at[pl.ds(k * height, height)], gram_ref.at[pl.ds(k * height, height)], semaphores.at[k]
        )
        for k in range(mirrors)
    ]


def bands_kernel(row_shape, surface_rows, first, counts, staged, gram_any, *refs):
    mirrors, shard_rows, slots, samples = row_shape
    sources = [ref.at[n] for ref, count in zip(refs, counts) for n in range(count)]
    refs = refs[len(counts):]
    columns_ref = None
    if len(refs) == 8:
        columns_ref, out_ref, whole_ref, rest_ref, *refs = refs
    else:
        out_ref, *refs = refs
    gram_ref, blocks, gram_semaphores, block_semaphores = refs
    step = pl.program_id(0)
    gram_copies = fetch_gram(gram_any, gram_ref, gram_semaphores, mirrors)

    def fetch(n):
        return pltpu.make_async_copy(sources[n], blocks.at[n], block_semaphores.at[n])

    @pl.when(step == 0)
    def _():
        fetch(0).start()
        for copy in gram_copies:
            copy.start()
        for n in range(1, len(sources)):
            fetch(n).start()
        if columns_ref is not None:
            build_differences(columns_ref, whole_ref, rest_ref, mirrors, samples)

    for n in range(len(sources)):
        @pl.when(step == n)
        def _():
            fetch(n).wait()
            block = row_block(first + n, staged)
            for q in range(mirrors * shard_rows):
                if n == 0 and q % shard_rows == 0:
                    gram_copies[q // shard_rows].wait()
                out_ref[0, q] = band_product([blocks.at[n]], q, row_shape, block, surface_rows, gram_ref)


def bands(gram_rows, sources, first, staged, row_shape, surface_rows, columns=None, pupil=None):
    acts, own = gram_rows.shape
    mirrors, shard_rows, slots, samples = row_shape
    counts = [source.shape[0] for source in sources]
    rows = mirrors * shard_rows
    flops = 2 * own * WINDOW * samples * rows * sum(counts)
    vmem, anywhere = pl.BlockSpec(memory_space=pltpu.VMEM), pl.BlockSpec(memory_space=pl.ANY)
    out_shape = [jax.ShapeDtypeStruct((sum(counts), rows, samples, own), jnp.bfloat16)]
    out_specs = [pl.BlockSpec((1, rows, samples, own), lambda s: (s, 0, 0, 0))]
    arguments, in_specs = [gram_rows, *sources], [anywhere] * (1 + len(sources))
    if columns is not None:
        depth = mirrors * samples // WINDOW * WINDOW
        rest = 2 * (mirrors * samples - depth)
        out_shape += [
            jax.ShapeDtypeStruct((columns.shape[0], 2, pupil // 2, depth), jnp.bfloat16),
            jax.ShapeDtypeStruct((columns.shape[0], pupil, rest), jnp.bfloat16),
        ]
        out_specs += [vmem] * 2
        arguments.append(columns)
        in_specs.append(vmem)
    return pl.pallas_call(
        functools.partial(bands_kernel, row_shape, surface_rows, first, counts, staged),
        grid=(sum(counts),),
        out_shape=out_shape,
        in_specs=in_specs,
        out_specs=out_specs,
        scratch_shapes=[
            pltpu.VMEM((acts, own), jnp.bfloat16),
            pltpu.VMEM((sum(counts),) + sources[0].shape[1:], jnp.bfloat16),
            pltpu.SemaphoreType.DMA((mirrors,)),
            pltpu.SemaphoreType.DMA((sum(counts),)),
        ],
        compiler_params=pltpu.CompilerParams(vmem_limit_bytes=VMEM_BYTES),
        cost_estimate=pl.CostEstimate(
            flops=flops, bytes_accessed=2 * own * WINDOW * rows * sum(counts), transcendentals=0
        ),
        name="bands",
    )(*arguments)


def build_differences(columns_ref, whole_ref, rest_ref, mirrors, samples):
    half = whole_ref.shape[2]
    pupil, depth = 2 * half, whole_ref.shape[3]
    remainder = mirrors * samples - depth
    slope = lax.broadcasted_iota(jnp.int32, (half, pupil), 0)
    lane = lax.broadcasted_iota(jnp.int32, (half, pupil), 1)
    at = lax.broadcasted_iota(jnp.int32, (half, mirrors * samples), 1)
    for d in range(columns_ref.shape[0]):
        sides = []
        for side in range(2):
            hit = None
            for k in range(mirrors):
                line = jnp.broadcast_to(columns_ref[d, k:k + 1, :pupil], (half, pupil))
                column = jnp.sum(jnp.where(lane == slope * 2 + side, line, 0), axis=1, keepdims=True)
                here = (at == column + k * samples).astype(jnp.float32)
                hit = here if hit is None else hit + here
            sides.append(hit)
        across, down = sides[1] - sides[0], sides[1] + sides[0]
        whole_ref[d, 0] = across[:, :depth].astype(jnp.bfloat16)
        whole_ref[d, 1] = down[:, :depth].astype(jnp.bfloat16)
        blank = jnp.zeros((half, remainder), jnp.float32)
        upper = jnp.concatenate([across[:, depth:], blank], axis=1)
        lower = jnp.concatenate([blank, down[:, depth:]], axis=1)
        rest_ref[d] = jnp.concatenate([upper, lower], axis=0).astype(jnp.bfloat16)


def decode_kernel(row_shape, surface_rows, own, staged, norm, counts, late_parts, *refs):
    mirrors, shard_rows, slots, samples = row_shape
    whole_ref, rest_ref, *refs = refs
    lines_refs, refs = refs[:counts[0]], refs[counts[0]:]
    late_refs, refs = refs[:counts[1]], refs[counts[1]:]
    ready_refs, refs = refs[:counts[2]], refs[counts[2]:]
    (gram_any, out_ref, gram_ref, decoded, total, packed_lines, lines, foot_rows, scalars, *refs) = refs
    late_blocks, refs = refs[:counts[1]], refs[counts[1]:]
    gram_semaphores, ready_semaphores, line_semaphores, late_semaphores, scalar_semaphore = refs
    group = pl.program_id(0)
    directions, pupil = whole_ref.shape[0], 2 * whole_ref.shape[2]
    depth = whole_ref.shape[3]
    phases = out_ref.shape[2] // pupil
    blocks = surface_rows // shard_rows
    late = len(late_parts)
    ready = blocks - late
    count = shard_rows // 2
    rows = mirrors * shard_rows
    extra = lines.shape[1]

    @pl.when(group == 0)
    def _():
        def started(copies):
            for copy in copies:
                copy.start()
            return copies

        ends = [ref.at[n, pl.ds(ref.shape[1] - extra, extra)] for ref in lines_refs for n in range(ref.shape[0])]
        line_copies = started([
            pltpu.make_async_copy(end, packed_lines.at[n], line_semaphores.at[n]) for n, end in enumerate(ends)
        ])
        late_copies = started([
            pltpu.make_async_copy(late_refs[n], late_blocks[n], late_semaphores.at[n]) for n in range(counts[1])
        ])
        gram_copies = started(fetch_gram(gram_any, gram_ref, gram_semaphores, mirrors)) if late else []
        ready_copies = started([
            pltpu.make_async_copy(block, decoded.at[pl.ds(n * rows, rows)], ready_semaphores.at[n])
            for n, block in enumerate([ref.at[m] for ref in ready_refs for m in range(ref.shape[0])])
        ])
        for copy in line_copies + late_copies:
            copy.wait()
        held = [packed_lines[n] for n in range(len(ends))]
        at = 0
        for part in late_parts:
            at += part
            last = late_blocks[at - 1]
            held.append(last[pl.ds(last.shape[0] - extra, extra), :])
        for n, value in enumerate(held):
            lines[n] = value.astype(jnp.float32).astype(jnp.int32)
        feet = jnp.concatenate([lines[n, directions * count:directions * count + 1] for n in range(blocks)], axis=0)
        foot_rows[...] = row_place(feet // shard_rows, staged) * rows + feet % shard_rows
        to_scalars = pltpu.make_async_copy(foot_rows, scalars, scalar_semaphore.at[0])
        to_scalars.start()
        at = 0
        for n, part in enumerate(late_parts):
            parts, at = late_blocks[at:at + part], at + part
            for q in range(mirrors * shard_rows):
                if n == 0 and q % shard_rows == 0:
                    gram_copies[q // shard_rows].wait()
                decoded[(ready + n) * rows + q] = band_product(
                    parts, q, row_shape, row_block(ready + n, staged), surface_rows, gram_ref
                )
        to_scalars.wait()
        for copy in ready_copies:
            copy.wait()

    for d in range(directions):
        held = d ^ position("dir", staged)
        products, factors = [], []
        for phase in range(phases):
            i = group * phases + phase
            block = row_place(2 * i // shard_rows, staged)
            sums, changes = [], []
            for k in range(mirrors):
                picked = []
                for y in range(2):
                    row = k * shard_rows + (2 * phase + y) % shard_rows
                    picked.append(decoded[scalars[block, held * rows + row] + k * shard_rows])
                sums.append(picked[0] + picked[1])
                changes.append(picked[1] - picked[0])
            right = [jnp.concatenate(part, axis=0) for part in (sums, changes)]
            mixed = jnp.concatenate([part[depth:] for part in right], axis=0)
            rest = jnp.dot(rest_ref[held], mixed, preferred_element_type=jnp.float32)
            for kind, part in enumerate(right):
                whole = jnp.dot(whole_ref[held, kind], part[:depth], preferred_element_type=jnp.float32)
                products.append(whole + rest[kind * pupil // 2:(kind + 1) * pupil // 2])
            valid = lines[block, pl.ds(held * count + phase % count, 1), :][:, :pupil // 2]
            factors += [valid.astype(jnp.float32) * norm] * 2
        product = jnp.concatenate(products, axis=0)
        factor = jnp.concatenate(factors, axis=1)
        for tile in range(out_ref.shape[2] // LANES):
            at = tile * LANES
            value = jnp.transpose(product[at:at + LANES])[:own] * factor[:, at:at + LANES]
            total[tile, pl.ds(d, own, stride=directions), :] = value
    for tile in range(out_ref.shape[2] // LANES):
        value = total[tile].reshape(own, directions, LANES)
        out_ref[:, :, tile * LANES:(tile + 1) * LANES] = value.astype(out_ref.dtype)


def decode(differences, sources, late, ready, gram_rows, own, row_shape, surface_rows, pupil, norm, staged):
    mirrors, shard_rows, slots, samples = row_shape
    acts, padded = gram_rows.shape
    directions = differences[0].shape[0]
    blocks = surface_rows // shard_rows
    extra = extra_rows(directions, shard_rows)
    phases = LANES // math.gcd(pupil, LANES)
    width = surface_rows // 2 * pupil
    lanes = phases * pupil
    flops = 2 * padded * mirrors * samples * pupil * directions * surface_rows // 2
    vmem, anywhere = pl.BlockSpec(memory_space=pltpu.VMEM), pl.BlockSpec(memory_space=pl.ANY)
    parts = [part for block in late for part in block]
    counts = (len(sources), len(parts), len(ready))
    semaphores = [mirrors, blocks, blocks, max(len(parts), 1), 1]
    return pl.pallas_call(
        functools.partial(
            decode_kernel, row_shape, surface_rows, own, staged, norm, counts, [len(block) for block in late]
        ),
        grid=(width // lanes,),
        out_shape=jax.ShapeDtypeStruct((own, directions, width), jnp.bfloat16),
        in_specs=[vmem] * 2 + [anywhere] * (sum(counts) + 1),
        out_specs=pl.BlockSpec((own, directions, lanes), lambda s: (0, 0, s)),
        scratch_shapes=[
            pltpu.VMEM((acts, padded), jnp.bfloat16),
            pltpu.VMEM((blocks * mirrors * shard_rows, samples, padded), jnp.bfloat16),
            pltpu.VMEM((lanes // LANES, own * directions, LANES), jnp.float32),
            pltpu.VMEM((blocks, extra, LANES), jnp.bfloat16),
            pltpu.VMEM((blocks, extra, LANES), jnp.int32),
            pltpu.VMEM((blocks, LANES), jnp.int32),
            pltpu.SMEM((blocks, LANES), jnp.int32),
            *[pltpu.VMEM(part.shape, part.dtype) for part in parts],
            *[pltpu.SemaphoreType.DMA((count,)) for count in semaphores],
        ],
        compiler_params=pltpu.CompilerParams(vmem_limit_bytes=VMEM_BYTES),
        cost_estimate=pl.CostEstimate(flops=flops, bytes_accessed=2 * own * directions * width, transcendentals=0),
        name="decode",
    )(*differences, *sources, *parts, *ready, gram_rows)


def swap(block, axis, distance):
    return lax.ppermute(block, axis, [(i, i ^ distance) for i in range(lax.axis_size(axis))])


def turn(block, even, odd):
    return lax.ppermute(
        block, "row", [(i, i ^ (odd if i % 2 else even)) for i in range(lax.axis_size("row"))]
    )


def shards(influence, foot_rows, foot_columns, actuator_codes, poke_rows, subaperture_valid):
    mirrors, shard_rows, samples, slots = influence.shape
    row_shape = (mirrors, shard_rows, slots, samples)
    directions, devices = lax.axis_size("dir"), lax.axis_size("row")
    surface_rows = shard_rows * devices
    pupil = foot_columns.shape[2]
    norm = 0.5 * poke_rows.shape[0] ** (-0.5)
    own = actuator_codes.size // (directions * devices)
    staged = devices == 8 and directions & (directions - 1) == 0
    turned = jnp.swapaxes(influence, 2, 3)
    pokes = poke_rows.reshape(-1, LANES)
    lines = small_lines(foot_rows, foot_columns, subaperture_valid)
    if not staged:
        lines = lax.all_gather(lines, "dir")
        packed = pack(turned, [lines])
        every = lax.all_gather(packed, "row")
        gram_rows, _ = gram(actuator_codes, pokes, packed, own, row_shape, surface_rows)
        ready, *differences = bands(gram_rows, [every], 0, staged, row_shape, surface_rows, lines, pupil)
        return decode(
            differences, [every], [], [ready], gram_rows, own, row_shape, surface_rows, pupil, norm, staged
        )

    lines = [lines[None]] + [swap(lines, "dir", e)[None] for e in range(1, directions)]
    packed = pack(turned, lines)
    first, second = turn(packed, 2, 4), turn(packed, 4, 2)
    sibling = swap(packed, "row", 1)
    gram_rows, own_rows = gram(actuator_codes, pokes, packed, own, row_shape, surface_rows)
    gram_rows, first, second = lax.optimization_barrier((gram_rows, first, second))
    diagonal = turn(first, 4, 2)
    first_sibling, second_sibling = swap(first, "row", 1), swap(second, "row", 1)
    sources = [source[None] for source in (sibling, first, second)]
    lines = jnp.concatenate(lines, axis=0)
    near, *differences = bands(gram_rows, sources, 1, staged, row_shape, surface_rows, lines, pupil)
    near, diagonal = lax.optimization_barrier((near, diagonal))
    late = [[block] for block in (first_sibling, second_sibling, diagonal, swap(diagonal, "row", 1))]
    return decode(
        differences, [packed[None], *sources], late, [own_rows, near], gram_rows, own, row_shape, surface_rows, pupil,
        norm, staged,
    )


def solution(mesh):
    return jax.shard_map(
        shards,
        mesh=mesh,
        in_specs=(
            P(None, "row", None, None),
            P("dir", None, "row"),
            P("dir", None, None),
            P(),
            P(),
            P("dir", "row", None),
        ),
        out_specs=P(("dir", "row"), None, None),
        check_vma=False,
    )
```

```python
import functools
import math

import jax
import jax.numpy as jnp
import numpy as np
from jax import lax
from jax.experimental import pallas as pl
from jax.experimental.pallas import tpu as pltpu
from jax.sharding import PartitionSpec as P

NAR = 48
NA = 48
BAND = 3
BITS = 13
NARROW = jnp.float8_e4m3fn
LANES = 128
WINDOW = 256
VMEM_BYTES = 127 * 512 * 1024


def parity(codes, rows):
    return lax.population_count(codes & rows) & 1


def lines_kernel(rows_ref, columns_ref, valid_ref, lines_ref):
    mirrors, rows = rows_ref.shape[0], rows_ref.shape[2]
    lines_ref[...] = jnp.zeros(lines_ref.shape, lines_ref.dtype)
    lines_ref[mirrors:mirrors + valid_ref.shape[1], :valid_ref.shape[2]] = valid_ref[0]
    for k in range(mirrors):
        lines_ref[k:k + 1, :columns_ref.shape[2]] = columns_ref[k]
        lines_ref[mirrors + valid_ref.shape[1]:mirrors + valid_ref.shape[1] + 1, k * rows:(k + 1) * rows] = rows_ref[k]


def small_lines(foot_rows, foot_columns, valid):
    vmem = pl.BlockSpec(memory_space=pltpu.VMEM)
    count = foot_rows.shape[1] + valid.shape[1] + 1
    return pl.pallas_call(
        lines_kernel,
        out_shape=jax.ShapeDtypeStruct((-(-count // 8) * 8, WINDOW), jnp.int32),
        in_specs=[vmem] * 3,
        out_specs=vmem,
        name="small_lines",
    )(jnp.swapaxes(foot_rows, 0, 1), jnp.swapaxes(foot_columns, 0, 1), valid)


def narrow_places(q, slots, samples):
    narrow = slots - LANES
    whole = LANES // narrow
    if q < whole:
        return [(0, samples, 0, q * narrow)]
    half = samples // 2
    lane = (q - whole) * narrow
    return [(0, half, samples, lane), (half, half, samples, LANES // 2 + lane)]


def pack_kernel(block_ref, *refs):
    lines_refs, packed_ref = refs[:-1], refs[-1]
    mirrors, rows, slots, samples = block_ref.shape
    identity = (
        lax.broadcasted_iota(jnp.int32, (samples, samples), 0) == lax.broadcasted_iota(jnp.int32, (samples, samples), 1)
    ).astype(jnp.float32).astype(jnp.bfloat16)
    wide = mirrors * rows * samples
    tails = {}
    for q in range(mirrors * rows):
        turned = lax.dot_general(
            identity, block_ref[q // rows, q % rows], (((1,), (1,)), ((), ())), preferred_element_type=jnp.float32
        ).astype(jnp.bfloat16)
        packed_ref[pl.ds(q * samples, samples), :] = turned[:, :LANES]
        for start, length, row, lane in narrow_places(q, slots, samples):
            tails.setdefault((row, length), {})[lane] = turned[start:start + length, LANES:]
    for (row, length), pieces in tails.items():
        packed_ref[pl.ds(wide + row, length), :] = jnp.concatenate([pieces[lane] for lane in sorted(pieces)], axis=1)
    count = rows // 2
    every = [ref.at[n] for ref in lines_refs for n in range(ref.shape[0])]
    feet = [ref[mirrors + count:mirrors + count + 1, :mirrors * rows] for ref in every]
    feet.append(jnp.zeros((1, LANES - mirrors * rows * len(every)), jnp.int32))
    lines = [ref[mirrors:mirrors + count, :LANES] for ref in every] + [jnp.concatenate(feet, axis=1)]
    extra = packed_ref.shape[0] - mirrors * rows * samples * slots // LANES
    lines.append(jnp.zeros((extra - count * len(every) - 1, LANES), jnp.int32))
    packed_ref[pl.ds(packed_ref.shape[0] - extra, extra), :] = (
        jnp.concatenate(lines, axis=0).astype(jnp.float32).astype(jnp.bfloat16)
    )


def extra_rows(directions, rows):
    return -(-(directions * (rows // 2) + 1) // 16) * 16


def pack(block, lines):
    mirrors, rows, slots, samples = block.shape
    vmem = pl.BlockSpec(memory_space=pltpu.VMEM)
    extra = extra_rows(sum(line.shape[0] for line in lines), rows)
    return pl.pallas_call(
        pack_kernel,
        out_shape=jax.ShapeDtypeStruct((mirrors * rows * samples * slots // LANES + extra, LANES), block.dtype),
        in_specs=[vmem] * (1 + len(lines)),
        out_specs=vmem,
        compiler_params=pltpu.CompilerParams(vmem_limit_bytes=VMEM_BYTES),
        cost_estimate=pl.CostEstimate(flops=0, bytes_accessed=3 * block.size, transcendentals=0),
        name="pack_influence",
    )(block, *lines)


def column_of(row):
    return jnp.transpose(jnp.broadcast_to(row, (LANES, LANES)), (1, 0))


def own_side_of(table_ref, pokes_ref, codes_ref, words, own_signs, own_sums):
    planes = pokes_ref.shape[0]
    mirrors, rows, columns = table_ref.shape
    for line in range(codes_ref.shape[0]):
        pieces, at = [], line * LANES
        while at < (line + 1) * LANES:
            row, lane = divmod(at, columns)
            length = min(columns - lane, (line + 1) * LANES - at)
            pieces.append(table_ref[row // rows, row % rows:row % rows + 1, lane:lane + length])
            at += length
        codes_ref[line:line + 1, :] = jnp.concatenate(pieces, axis=1)
    half = LANES // 2
    own = own_signs.shape[0]
    plane = lax.broadcasted_iota(jnp.int32, pokes_ref.shape, 0)
    for bit in range(BITS):
        low = jnp.sum((pokes_ref[...] >> bit & 1) << plane, axis=0, keepdims=True)
        word = low | pltpu.roll(jnp.broadcast_to(low, (8, LANES)), half, 1)[:1] << planes
        words[bit] = column_of(word)[:half]
    count = codes_ref.shape[0] * LANES // (lax.axis_size("dir") * lax.axis_size("row"))
    first = (lax.axis_index("dir") * lax.axis_size("row") + lax.axis_index("row")) * count
    lane = lax.broadcasted_iota(jnp.int32, (8, LANES), 1)
    shift = first % LANES
    lines = [
        pltpu.roll(
            jnp.broadcast_to(
                codes_ref[pl.ds(jnp.minimum(first // LANES + n, codes_ref.shape[0] - 1), 1), :], (8, LANES)
            ),
            LANES - shift, 1,
        )
        for n in range(-(-own // LANES) + 1)
    ]
    own_column = jnp.concatenate(
        [column_of(jnp.where(lane < LANES - shift, lines[n], lines[n + 1])[:1]) for n in range(len(lines) - 1)],
        axis=0,
    )[:own]
    total = jnp.zeros((own, LANES), jnp.float32)
    for at in range(planes):
        signs = (1 - 2 * parity(own_column, pokes_ref[at:at + 1, :])).astype(jnp.float32)
        own_signs[:, at * LANES:(at + 1) * LANES] = signs.astype(NARROW)
        total = total + signs
    own_sums[...] = jnp.broadcast_to(jnp.sum(total, axis=1, keepdims=True), own_sums.shape)


def gram_kernel(
    row_shape, surface_rows, table_ref, pokes_ref, packed_ref, gram_out, first_ref, gram_ref, codes_ref, words,
    own_signs, own_sums, semaphores
):
    mirror = pl.program_id(0)
    half = LANES // 2
    own, pokes = own_signs.shape
    planes = pokes // LANES
    lines = codes_ref.shape[0] // row_shape[0]
    height = gram_ref.shape[0] // row_shape[0]

    @pl.when(mirror == 0)
    def _():
        own_side_of(table_ref, pokes_ref, codes_ref, words, own_signs, own_sums)

    def chunk(index, _):
        word = []
        for side in range(WINDOW // LANES):
            line = mirror * lines + index * (WINDOW // LANES) + side
            code = jnp.broadcast_to(codes_ref[pl.ds(line, 1), :], (8, LANES))
            value = None
            for bit in range(BITS):
                mask = jnp.concatenate([code << (31 - bit) >> 31] * (half // 8), axis=0)
                part = words[bit] & mask
                value = part if value is None else value ^ part
            word.append(value)
        word = jnp.concatenate(word, axis=1)
        bits = [None] * (2 * planes)
        for byte in range(0, 2 * planes, 8):
            part = (word >> byte).astype(jnp.int8)
            for bit in range(8):
                at = byte + bit
                hit = (part & np.uint8(1 << bit).astype(np.int8)) != 0
                bits[at % planes * 2 + at // planes] = jnp.where(hit, NARROW(1.0), NARROW(0.0))
        total = jnp.dot(own_signs[...], jnp.concatenate(bits, axis=0), preferred_element_type=jnp.float32)
        sums = jnp.concatenate([own_sums[...]] * (WINDOW // LANES), axis=1)
        turned = jnp.transpose((sums - 2.0 * total).astype(jnp.bfloat16))
        at = pl.multiple_of(mirror * height + index * WINDOW, WINDOW)
        gram_ref[pl.ds(at, WINDOW), :] = turned
        return 0

    lax.fori_loop(0, height // WINDOW, chunk, 0, unroll=3)

    def send(k):
        part = pl.ds(pl.multiple_of(k * height, height), height)
        return pltpu.make_async_copy(gram_ref.at[part], gram_out.at[part], semaphores.at[k])

    send(mirror).start()
    block = lax.axis_index("row")
    for l in range(row_shape[1]):
        for k in range(row_shape[0]):
            @pl.when(mirror == k)
            def _():
                first_ref[0, l] = band_product(
                    packed_ref, k * row_shape[1] + l, row_shape, block, surface_rows, gram_ref
                )

    @pl.when(mirror == pl.num_programs(0) - 1)
    def _():
        for k in range(row_shape[0]):
            send(k).wait()


def gram(table, pokes, packed, own, row_shape, surface_rows):
    own = -(-own // 32) * 32
    acts, count = table.size, pokes.size
    mirrors, shard_rows, slots, samples = row_shape
    vmem = pl.BlockSpec(memory_space=pltpu.VMEM)
    return pl.pallas_call(
        functools.partial(gram_kernel, row_shape, surface_rows),
        grid=(mirrors,),
        out_shape=[
            jax.ShapeDtypeStruct((acts, own), jnp.bfloat16),
            jax.ShapeDtypeStruct((1, mirrors * shard_rows, samples, own), jnp.bfloat16),
        ],
        in_specs=[vmem] * 3,
        out_specs=[
            pl.BlockSpec(memory_space=pl.ANY),
            pl.BlockSpec((1, shard_rows, samples, own), lambda s: (0, s, 0, 0)),
        ],
        scratch_shapes=[
            pltpu.VMEM((acts, own), jnp.bfloat16),
            pltpu.VMEM((acts // LANES, LANES), jnp.int32),
            pltpu.VMEM((BITS, LANES // 2, LANES), jnp.int32),
            pltpu.VMEM((own, count), NARROW),
            pltpu.VMEM((own, LANES), jnp.float32),
            pltpu.SemaphoreType.DMA((mirrors,)),
        ],
        compiler_params=pltpu.CompilerParams(vmem_limit_bytes=VMEM_BYTES),
        cost_estimate=pl.CostEstimate(
            flops=2 * own * acts * count, bytes_accessed=2 * own * acts, transcendentals=0
        ),
        name="gram_rows",
    )(table, pokes, packed)


def position(axis, staged):
    return lax.axis_index(axis) if staged else 0


def row_block(place, staged):
    if not staged:
        return place
    row = lax.axis_index("row")
    core = row & 1
    return row ^ [0, 1, 2 << core, 4 >> core, (4 >> core) | 1, (2 << core) | 1, 6, 7][place]


def row_place(block, staged):
    if not staged:
        return block
    row = lax.axis_index("row")
    core = row & 1
    distance = block ^ row
    near = jnp.where(distance == 2 << core, 2, 3)
    far = jnp.where(distance == (4 >> core) | 1, 4, 5)
    middle = jnp.where(distance & 1 == 0, near, far)
    return jnp.where((distance >= 2) & (distance < 6), middle, distance)


def band_product(source, q, row_shape, block, surface_rows, gram_ref):
    mirrors, shard_rows, slots, samples = row_shape
    own = gram_ref.shape[1]
    narrow = slots - LANES
    k, l = divmod(q, shard_rows)
    band = jnp.clip((block * shard_rows + l) * NAR // surface_rows - 1, 0, NAR - BAND)
    column = pl.multiple_of((k * NAR + band) * NA, 16)
    wide = mirrors * shard_rows * samples
    products = []
    for start, length, row, lane in narrow_places(q, slots, samples):
        left = jnp.concatenate(
            [source[pl.ds(q * samples + start, length), :], source[pl.ds(wide + row, length), :]], axis=1
        )
        right = [gram_ref[pl.ds(column, LANES), :]]
        if lane:
            right.append(jnp.zeros((lane, own), jnp.bfloat16))
        right.append(gram_ref[pl.ds(column + LANES, narrow), :])
        if lane + narrow < LANES:
            right.append(jnp.zeros((LANES - lane - narrow, own), jnp.bfloat16))
        products.append(
            jnp.dot(left, jnp.concatenate(right, axis=0), preferred_element_type=jnp.float32).astype(jnp.bfloat16)
        )
    return jnp.concatenate(products, axis=0)


def fetch_gram(gram_any, gram_ref, semaphores, mirrors):
    height = gram_ref.shape[0] // mirrors
    return [
        pltpu.make_async_copy(
            gram_any.at[pl.ds(k * height, height)], gram_ref.at[pl.ds(k * height, height)], semaphores.at[k]
        )
        for k in range(mirrors)
    ]


def bands_kernel(row_shape, surface_rows, first, counts, staged, gram_any, *refs):
    mirrors, shard_rows, slots, samples = row_shape
    sources = [ref.at[n] for ref, count in zip(refs, counts) for n in range(count)]
    refs = refs[len(counts):]
    *columns_refs, out_ref, whole_ref, rest_ref, gram_ref, blocks, gram_semaphores, block_semaphores = refs
    step = pl.program_id(0)
    gram_copies = fetch_gram(gram_any, gram_ref, gram_semaphores, mirrors)

    def fetch(n):
        return pltpu.make_async_copy(sources[n], blocks.at[n], block_semaphores.at[n])

    @pl.when(step == 0)
    def _():
        fetch(0).start()
        for copy in gram_copies:
            copy.start()
        for n in range(1, len(sources)):
            fetch(n).start()
        columns = [ref.at[n] for ref in columns_refs for n in range(ref.shape[0])]
        build_differences(columns, whole_ref, rest_ref, mirrors, samples)

    for n in range(len(sources)):
        @pl.when(step == n)
        def _():
            fetch(n).wait()
            block = row_block(first + n, staged)
            for q in range(mirrors * shard_rows):
                if n == 0 and q % shard_rows == 0:
                    gram_copies[q // shard_rows].wait()
                out_ref[0, q] = band_product(blocks.at[n], q, row_shape, block, surface_rows, gram_ref)


def bands(gram_rows, sources, first, staged, row_shape, surface_rows, columns, pupil):
    acts, own = gram_rows.shape
    mirrors, shard_rows, slots, samples = row_shape
    counts = [source.shape[0] for source in sources]
    rows = mirrors * shard_rows
    flops = 2 * own * WINDOW * samples * rows * sum(counts)
    vmem, anywhere = pl.BlockSpec(memory_space=pltpu.VMEM), pl.BlockSpec(memory_space=pl.ANY)
    out_shape = [jax.ShapeDtypeStruct((sum(counts), rows, samples, own), jnp.bfloat16)]
    out_specs = [pl.BlockSpec((1, rows, samples, own), lambda s: (s, 0, 0, 0))]
    arguments, in_specs = [gram_rows, *sources], [anywhere] * (1 + len(sources))
    directions = sum(lines.shape[0] for lines in columns)
    depth = mirrors * samples // WINDOW * WINDOW
    rest = 2 * (mirrors * samples - depth)
    out_shape += [
        jax.ShapeDtypeStruct((directions, 2, pupil // 2, depth), jnp.bfloat16),
        jax.ShapeDtypeStruct((directions, pupil, rest), jnp.bfloat16),
    ]
    out_specs += [vmem] * 2
    arguments += columns
    in_specs += [vmem] * len(columns)
    return pl.pallas_call(
        functools.partial(bands_kernel, row_shape, surface_rows, first, counts, staged),
        grid=(sum(counts),),
        out_shape=out_shape,
        in_specs=in_specs,
        out_specs=out_specs,
        scratch_shapes=[
            pltpu.VMEM((acts, own), jnp.bfloat16),
            pltpu.VMEM((sum(counts),) + sources[0].shape[1:], jnp.bfloat16),
            pltpu.SemaphoreType.DMA((mirrors,)),
            pltpu.SemaphoreType.DMA((sum(counts),)),
        ],
        compiler_params=pltpu.CompilerParams(vmem_limit_bytes=VMEM_BYTES),
        cost_estimate=pl.CostEstimate(
            flops=flops, bytes_accessed=2 * own * WINDOW * rows * sum(counts), transcendentals=0
        ),
        name="bands",
    )(*arguments)


def build_differences(columns, whole_ref, rest_ref, mirrors, samples):
    half = whole_ref.shape[2]
    pupil, depth = 2 * half, whole_ref.shape[3]
    remainder = mirrors * samples - depth
    slope = lax.broadcasted_iota(jnp.int32, (half, pupil), 0)
    lane = lax.broadcasted_iota(jnp.int32, (half, pupil), 1)
    at = lax.broadcasted_iota(jnp.int32, (half, mirrors * samples), 1)
    for d, columns_ref in enumerate(columns):
        sides = []
        for side in range(2):
            hit = None
            for k in range(mirrors):
                line = jnp.broadcast_to(columns_ref[k:k + 1, :pupil], (half, pupil))
                column = jnp.sum(jnp.where(lane == slope * 2 + side, line, 0), axis=1, keepdims=True)
                here = (at == column + k * samples).astype(jnp.float32)
                hit = here if hit is None else hit + here
            sides.append(hit)
        across, down = sides[1] - sides[0], sides[1] + sides[0]
        whole_ref[d, 0] = across[:, :depth].astype(jnp.bfloat16)
        whole_ref[d, 1] = down[:, :depth].astype(jnp.bfloat16)
        blank = jnp.zeros((half, remainder), jnp.float32)
        upper = jnp.concatenate([across[:, depth:], blank], axis=1)
        lower = jnp.concatenate([blank, down[:, depth:]], axis=1)
        rest_ref[d] = jnp.concatenate([upper, lower], axis=0).astype(jnp.bfloat16)


def decode_kernel(row_shape, surface_rows, own, staged, norm, counts, late_parts, *refs):
    mirrors, shard_rows, slots, samples = row_shape
    whole_ref, rest_ref, *refs = refs
    lines_refs, refs = refs[:counts[0]], refs[counts[0]:]
    late_refs, refs = refs[:counts[1]], refs[counts[1]:]
    ready_refs, refs = refs[:counts[2]], refs[counts[2]:]
    (gram_any, out_ref, gram_ref, decoded, total, packed_lines, lines, foot_rows, scalars, *refs) = refs
    late_blocks, refs = refs[:counts[1]], refs[counts[1]:]
    gram_semaphores, ready_semaphores, line_semaphores, late_semaphores, scalar_semaphore = refs
    group = pl.program_id(0)
    directions, pupil = whole_ref.shape[0], 2 * whole_ref.shape[2]
    depth = whole_ref.shape[3]
    phases = out_ref.shape[2] // pupil
    blocks = surface_rows // shard_rows
    late = len(late_parts)
    ready = blocks - late
    count = shard_rows // 2
    rows = mirrors * shard_rows
    extra = lines.shape[1]

    @pl.when(group == 0)
    def _():
        def started(copies):
            for copy in copies:
                copy.start()
            return copies

        ends = [ref.at[n, pl.ds(ref.shape[1] - extra, extra)] for ref in lines_refs for n in range(ref.shape[0])]
        line_copies = started([
            pltpu.make_async_copy(end, packed_lines.at[n], line_semaphores.at[n]) for n, end in enumerate(ends)
        ])
        late_copies = started([
            pltpu.make_async_copy(late_refs[n], late_blocks[n], late_semaphores.at[n]) for n in range(counts[1])
        ])
        gram_copies = started(fetch_gram(gram_any, gram_ref, gram_semaphores, mirrors)) if late else []
        ready_copies = started([
            pltpu.make_async_copy(block, decoded.at[pl.ds(n * rows, rows)], ready_semaphores.at[n])
            for n, block in enumerate([ref.at[m] for ref in ready_refs for m in range(ref.shape[0])])
        ])
        for copy in line_copies + late_copies:
            copy.wait()
        held = [packed_lines[n] for n in range(len(ends))]
        at = 0
        for part in late_parts:
            at += part
            last = late_blocks[at - 1]
            held.append(last[pl.ds(last.shape[0] - extra, extra), :])
        for n, value in enumerate(held):
            lines[n] = value.astype(jnp.float32).astype(jnp.int32)
        feet = jnp.concatenate([lines[n, directions * count:directions * count + 1] for n in range(blocks)], axis=0)
        foot_rows[...] = row_place(feet // shard_rows, staged) * rows + feet % shard_rows
        to_scalars = pltpu.make_async_copy(foot_rows, scalars, scalar_semaphore.at[0])
        to_scalars.start()
        at = 0
        for n, part in enumerate(late_parts):
            source, at = late_blocks[at], at + part
            for q in range(mirrors * shard_rows):
                if n == 0 and q % shard_rows == 0:
                    gram_copies[q // shard_rows].wait()
                decoded[(ready + n) * rows + q] = band_product(
                    source, q, row_shape, row_block(ready + n, staged), surface_rows, gram_ref
                )
        to_scalars.wait()
        for copy in ready_copies:
            copy.wait()

    for d in range(directions):
        held = d ^ position("dir", staged)
        products, factors = [], []
        for phase in range(phases):
            i = group * phases + phase
            block = row_place(2 * i // shard_rows, staged)
            sums, changes = [], []
            for k in range(mirrors):
                picked = []
                for y in range(2):
                    row = k * shard_rows + (2 * phase + y) % shard_rows
                    picked.append(decoded[scalars[block, held * rows + row] + k * shard_rows])
                sums.append(picked[0] + picked[1])
                changes.append(picked[1] - picked[0])
            right = [jnp.concatenate(part, axis=0) for part in (sums, changes)]
            mixed = jnp.concatenate([part[depth:] for part in right], axis=0)
            rest = jnp.dot(rest_ref[held], mixed, preferred_element_type=jnp.float32)
            for kind, part in enumerate(right):
                whole = jnp.dot(whole_ref[held, kind], part[:depth], preferred_element_type=jnp.float32)
                products.append(whole + rest[kind * pupil // 2:(kind + 1) * pupil // 2])
            valid = lines[block, pl.ds(held * count + phase % count, 1), :][:, :pupil // 2]
            factors += [valid.astype(jnp.float32)] * 2
        product = jnp.concatenate(products, axis=0)
        factor = jnp.concatenate(factors, axis=1)
        for tile in range(out_ref.shape[2] // LANES):
            at = tile * LANES
            value = jnp.transpose((product[at:at + LANES] * norm).astype(jnp.bfloat16))
            value = value.astype(jnp.float32)[:own] * factor[:, at:at + LANES]
            total[tile, pl.ds(d, own, stride=directions), :] = value
    for tile in range(out_ref.shape[2] // LANES):
        value = total[tile].reshape(own, directions, LANES)
        out_ref[:, :, tile * LANES:(tile + 1) * LANES] = value.astype(out_ref.dtype)


def decode(differences, sources, late, ready, gram_rows, own, row_shape, surface_rows, pupil, norm, staged):
    mirrors, shard_rows, slots, samples = row_shape
    acts, padded = gram_rows.shape
    directions = differences[0].shape[0]
    blocks = surface_rows // shard_rows
    extra = extra_rows(directions, shard_rows)
    phases = LANES // math.gcd(pupil, LANES)
    width = surface_rows // 2 * pupil
    lanes = phases * pupil
    flops = 2 * padded * mirrors * samples * pupil * directions * surface_rows // 2
    vmem, anywhere = pl.BlockSpec(memory_space=pltpu.VMEM), pl.BlockSpec(memory_space=pl.ANY)
    parts = [part for block in late for part in block]
    counts = (len(sources), len(parts), len(ready))
    semaphores = [mirrors, blocks, blocks, max(len(parts), 1), 1]
    return pl.pallas_call(
        functools.partial(
            decode_kernel, row_shape, surface_rows, own, staged, norm, counts, [len(block) for block in late]
        ),
        grid=(width // lanes,),
        out_shape=jax.ShapeDtypeStruct((own, directions, width), jnp.bfloat16),
        in_specs=[vmem] * 2 + [anywhere] * (sum(counts) + 1),
        out_specs=pl.BlockSpec((own, directions, lanes), lambda s: (0, 0, s)),
        scratch_shapes=[
            pltpu.VMEM((acts, padded), jnp.bfloat16),
            pltpu.VMEM((blocks * mirrors * shard_rows, samples, padded), jnp.bfloat16),
            pltpu.VMEM((lanes // LANES, own * directions, LANES), jnp.float32),
            pltpu.VMEM((blocks, extra, LANES), jnp.bfloat16),
            pltpu.VMEM((blocks, extra, LANES), jnp.int32),
            pltpu.VMEM((blocks, LANES), jnp.int32),
            pltpu.SMEM((blocks, LANES), jnp.int32),
            *[pltpu.VMEM(part.shape, part.dtype) for part in parts],
            *[pltpu.SemaphoreType.DMA((count,)) for count in semaphores],
        ],
        compiler_params=pltpu.CompilerParams(vmem_limit_bytes=VMEM_BYTES),
        cost_estimate=pl.CostEstimate(flops=flops, bytes_accessed=2 * own * directions * width, transcendentals=0),
        name="decode",
    )(*differences, *sources, *parts, *ready, gram_rows)


def swap(block, axis, distance):
    return lax.ppermute(block, axis, [(i, i ^ distance) for i in range(lax.axis_size(axis))])


def turn(block, even, odd):
    return lax.ppermute(
        block, "row", [(i, i ^ (odd if i % 2 else even)) for i in range(lax.axis_size("row"))]
    )


def shards(influence, foot_rows, foot_columns, actuator_codes, poke_rows, subaperture_valid):
    mirrors, shard_rows, samples, slots = influence.shape
    row_shape = (mirrors, shard_rows, slots, samples)
    directions, devices = lax.axis_size("dir"), lax.axis_size("row")
    surface_rows = shard_rows * devices
    pupil = foot_columns.shape[2]
    norm = 0.5 * poke_rows.shape[0] ** (-0.5)
    own = actuator_codes.size // (directions * devices)
    staged = devices == 8 and directions & (directions - 1) == 0
    turned = jnp.swapaxes(influence, 2, 3)
    pokes = poke_rows.reshape(-1, LANES)
    lines = small_lines(foot_rows, foot_columns, subaperture_valid)
    if not staged:
        lines = lax.all_gather(lines, "dir")
        packed = pack(turned, [lines])
        every = lax.all_gather(packed, "row")
        gram_rows, _ = gram(actuator_codes, pokes, packed, own, row_shape, surface_rows)
        ready, *differences = bands(gram_rows, [every], 0, staged, row_shape, surface_rows, [lines], pupil)
        return decode(
            differences, [every], [], [ready], gram_rows, own, row_shape, surface_rows, pupil, norm, staged
        )

    lines = [lines[None]] + [swap(lines, "dir", e)[None] for e in range(1, directions)]
    packed = pack(turned, lines)
    first, second = turn(packed, 2, 4), turn(packed, 4, 2)
    sibling = swap(packed, "row", 1)
    gram_rows, own_rows = gram(actuator_codes, pokes, packed, own, row_shape, surface_rows)
    gram_rows, first, second = lax.optimization_barrier((gram_rows, first, second))
    diagonal = turn(first, 4, 2)
    first_sibling, second_sibling = swap(first, "row", 1), swap(second, "row", 1)
    sources = [source[None] for source in (sibling, first, second)]
    near, *differences = bands(gram_rows, sources, 1, staged, row_shape, surface_rows, lines, pupil)
    near, diagonal = lax.optimization_barrier((near, diagonal))
    late = [[block] for block in (first_sibling, second_sibling, diagonal, swap(diagonal, "row", 1))]
    return decode(
        differences, [packed[None], *sources], late, [own_rows, near], gram_rows, own, row_shape, surface_rows, pupil,
        norm, staged,
    )


def solution(mesh):
    return jax.shard_map(
        shards,
        mesh=mesh,
        in_specs=(
            P(None, "row", None, None),
            P("dir", None, "row"),
            P("dir", None, None),
            P(),
            P(),
            P("dir", "row", None),
        ),
        out_specs=P(("dir", "row"), None, None),
        check_vma=False,
    )
```

```python
import functools
import math

import jax
import jax.numpy as jnp
import numpy as np
from jax import lax
from jax.experimental import pallas as pl
from jax.experimental.pallas import tpu as pltpu
from jax.sharding import PartitionSpec as P

NAR = 48
NA = 48
BAND = 3
REACH = 2
BITS = 13
NARROW = jnp.float8_e4m3fn
LANES = 128
WINDOW = 256
VMEM_BYTES = 127 * 512 * 1024


def parity(codes, rows):
    return lax.population_count(codes & rows) & 1


def lines_kernel(rows_ref, columns_ref, valid_ref, lines_ref):
    mirrors, rows = rows_ref.shape[0], rows_ref.shape[2]
    lines_ref[...] = jnp.zeros(lines_ref.shape, lines_ref.dtype)
    lines_ref[mirrors:mirrors + valid_ref.shape[1], :valid_ref.shape[2]] = valid_ref[0]
    for k in range(mirrors):
        lines_ref[k:k + 1, :columns_ref.shape[2]] = columns_ref[k]
        lines_ref[mirrors + valid_ref.shape[1]:mirrors + valid_ref.shape[1] + 1, k * rows:(k + 1) * rows] = rows_ref[k]


def small_lines(foot_rows, foot_columns, valid):
    vmem = pl.BlockSpec(memory_space=pltpu.VMEM)
    count = foot_rows.shape[1] + valid.shape[1] + 1
    return pl.pallas_call(
        lines_kernel,
        out_shape=jax.ShapeDtypeStruct((-(-count // 8) * 8, WINDOW), jnp.int32),
        in_specs=[vmem] * 3,
        out_specs=vmem,
        name="small_lines",
    )(jnp.swapaxes(foot_rows, 0, 1), jnp.swapaxes(foot_columns, 0, 1), valid)


def narrow_places(q, slots, samples):
    narrow = slots - LANES
    whole = LANES // narrow
    if q < whole:
        return [(0, samples, 0, q * narrow)]
    half = samples // 2
    lane = (q - whole) * narrow
    return [(0, half, samples, lane), (half, half, samples, LANES // 2 + lane)]


def pack_kernel(block_ref, *refs):
    lines_refs, packed_ref = refs[:-1], refs[-1]
    mirrors, rows, slots, samples = block_ref.shape
    identity = (
        lax.broadcasted_iota(jnp.int32, (samples, samples), 0) == lax.broadcasted_iota(jnp.int32, (samples, samples), 1)
    ).astype(jnp.float32).astype(jnp.bfloat16)
    wide = mirrors * rows * samples
    tails = {}
    for q in range(mirrors * rows):
        turned = lax.dot_general(
            identity, block_ref[q // rows, q % rows], (((1,), (1,)), ((), ())), preferred_element_type=jnp.float32
        ).astype(jnp.bfloat16)
        packed_ref[pl.ds(q * samples, samples), :] = turned[:, :LANES]
        for start, length, row, lane in narrow_places(q, slots, samples):
            tails.setdefault((row, length), {})[lane] = turned[start:start + length, LANES:]
    for (row, length), pieces in tails.items():
        packed_ref[pl.ds(wide + row, length), :] = jnp.concatenate([pieces[lane] for lane in sorted(pieces)], axis=1)
    count = rows // 2
    every = [ref.at[n] for ref in lines_refs for n in range(ref.shape[0])]
    feet = [ref[mirrors + count:mirrors + count + 1, :mirrors * rows] for ref in every]
    feet.append(jnp.zeros((1, LANES - mirrors * rows * len(every)), jnp.int32))
    lines = [ref[mirrors:mirrors + count, :LANES] for ref in every] + [jnp.concatenate(feet, axis=1)]
    extra = packed_ref.shape[0] - mirrors * rows * samples * slots // LANES
    lines.append(jnp.zeros((extra - count * len(every) - 1, LANES), jnp.int32))
    packed_ref[pl.ds(packed_ref.shape[0] - extra, extra), :] = (
        jnp.concatenate(lines, axis=0).astype(jnp.float32).astype(jnp.bfloat16)
    )


def extra_rows(directions, rows):
    return -(-(directions * (rows // 2) + 1) // 16) * 16


def pack(block, lines):
    mirrors, rows, slots, samples = block.shape
    vmem = pl.BlockSpec(memory_space=pltpu.VMEM)
    extra = extra_rows(sum(line.shape[0] for line in lines), rows)
    return pl.pallas_call(
        pack_kernel,
        out_shape=jax.ShapeDtypeStruct((mirrors * rows * samples * slots // LANES + extra, LANES), block.dtype),
        in_specs=[vmem] * (1 + len(lines)),
        out_specs=vmem,
        compiler_params=pltpu.CompilerParams(vmem_limit_bytes=VMEM_BYTES),
        cost_estimate=pl.CostEstimate(flops=0, bytes_accessed=3 * block.size, transcendentals=0),
        name="pack_influence",
    )(block, *lines)


def column_of(row):
    return jnp.transpose(jnp.broadcast_to(row, (LANES, LANES)), (1, 0))


def own_side_of(table_ref, pokes_ref, codes_ref, words, own_signs, own_sums):
    planes = pokes_ref.shape[0]
    mirrors, rows, columns = table_ref.shape
    for line in range(codes_ref.shape[0]):
        pieces, at = [], line * LANES
        while at < (line + 1) * LANES:
            row, lane = divmod(at, columns)
            length = min(columns - lane, (line + 1) * LANES - at)
            pieces.append(table_ref[row // rows, row % rows:row % rows + 1, lane:lane + length])
            at += length
        codes_ref[line:line + 1, :] = jnp.concatenate(pieces, axis=1)
    half = LANES // 2
    own = own_signs.shape[0]
    plane = lax.broadcasted_iota(jnp.int32, pokes_ref.shape, 0)
    for bit in range(BITS):
        low = jnp.sum((pokes_ref[...] >> bit & 1) << plane, axis=0, keepdims=True)
        word = low | pltpu.roll(jnp.broadcast_to(low, (8, LANES)), half, 1)[:1] << planes
        words[bit] = column_of(word)[:half]
    count = codes_ref.shape[0] * LANES // (lax.axis_size("dir") * lax.axis_size("row"))
    first = (lax.axis_index("dir") * lax.axis_size("row") + lax.axis_index("row")) * count
    lane = lax.broadcasted_iota(jnp.int32, (8, LANES), 1)
    shift = first % LANES
    lines = [
        pltpu.roll(
            jnp.broadcast_to(
                codes_ref[pl.ds(jnp.minimum(first // LANES + n, codes_ref.shape[0] - 1), 1), :], (8, LANES)
            ),
            LANES - shift, 1,
        )
        for n in range(-(-own // LANES) + 1)
    ]
    own_column = jnp.concatenate(
        [column_of(jnp.where(lane < LANES - shift, lines[n], lines[n + 1])[:1]) for n in range(len(lines) - 1)],
        axis=0,
    )[:own]
    total = jnp.zeros((own, LANES), jnp.float32)
    for at in range(planes):
        signs = (1 - 2 * parity(own_column, pokes_ref[at:at + 1, :])).astype(jnp.float32)
        own_signs[:, at * LANES:(at + 1) * LANES] = signs.astype(NARROW)
        total = total + signs
    own_sums[...] = jnp.broadcast_to(jnp.sum(total, axis=1, keepdims=True), own_sums.shape)


def gram_kernel(
    row_shape, surface_rows, table_ref, pokes_ref, packed_ref, gram_out, first_ref, gram_ref, codes_ref, words,
    own_signs, own_sums, semaphores
):
    mirror = pl.program_id(0)
    half = LANES // 2
    own, pokes = own_signs.shape
    planes = pokes // LANES
    lines = codes_ref.shape[0] // row_shape[0]
    height = gram_ref.shape[0] // row_shape[0]

    @pl.when(mirror == 0)
    def _():
        own_side_of(table_ref, pokes_ref, codes_ref, words, own_signs, own_sums)

    def chunk(index, _):
        word = []
        for side in range(WINDOW // LANES):
            line = mirror * lines + index * (WINDOW // LANES) + side
            code = jnp.broadcast_to(codes_ref[pl.ds(line, 1), :], (8, LANES))
            value = None
            for bit in range(BITS):
                mask = jnp.concatenate([code << (31 - bit) >> 31] * (half // 8), axis=0)
                part = words[bit] & mask
                value = part if value is None else value ^ part
            word.append(value)
        word = jnp.concatenate(word, axis=1)
        bits = [None] * (2 * planes)
        for byte in range(0, 2 * planes, 8):
            part = (word >> byte).astype(jnp.int8)
            for bit in range(8):
                at = byte + bit
                hit = (part & np.uint8(1 << bit).astype(np.int8)) != 0
                bits[at % planes * 2 + at // planes] = jnp.where(hit, NARROW(1.0), NARROW(0.0))
        total = jnp.dot(own_signs[...], jnp.concatenate(bits, axis=0), preferred_element_type=jnp.float32)
        sums = jnp.concatenate([own_sums[...]] * (WINDOW // LANES), axis=1)
        turned = jnp.transpose((sums - 2.0 * total).astype(jnp.bfloat16))
        at = pl.multiple_of(mirror * height + index * WINDOW, WINDOW)
        gram_ref[pl.ds(at, WINDOW), :] = turned
        return 0

    lax.fori_loop(0, height // WINDOW, chunk, 0, unroll=3)

    def send(k):
        part = pl.ds(pl.multiple_of(k * height, height), height)
        return pltpu.make_async_copy(gram_ref.at[part], gram_out.at[part], semaphores.at[k])

    send(mirror).start()
    block = lax.axis_index("row")
    for l in range(row_shape[1]):
        for k in range(row_shape[0]):
            @pl.when(mirror == k)
            def _():
                first_ref[0, l] = band_product(
                    packed_ref, k * row_shape[1] + l, row_shape, block, surface_rows, gram_ref
                )

    @pl.when(mirror == pl.num_programs(0) - 1)
    def _():
        for k in range(row_shape[0]):
            send(k).wait()


def gram(table, pokes, packed, own, row_shape, surface_rows):
    own = -(-own // 32) * 32
    acts, count = table.size, pokes.size
    mirrors, shard_rows, slots, samples = row_shape
    vmem = pl.BlockSpec(memory_space=pltpu.VMEM)
    return pl.pallas_call(
        functools.partial(gram_kernel, row_shape, surface_rows),
        grid=(mirrors,),
        out_shape=[
            jax.ShapeDtypeStruct((acts, own), jnp.bfloat16),
            jax.ShapeDtypeStruct((1, mirrors * shard_rows, samples, own), jnp.bfloat16),
        ],
        in_specs=[vmem] * 3,
        out_specs=[
            pl.BlockSpec(memory_space=pl.ANY),
            pl.BlockSpec((1, shard_rows, samples, own), lambda s: (0, s, 0, 0)),
        ],
        scratch_shapes=[
            pltpu.VMEM((acts, own), jnp.bfloat16),
            pltpu.VMEM((acts // LANES, LANES), jnp.int32),
            pltpu.VMEM((BITS, LANES // 2, LANES), jnp.int32),
            pltpu.VMEM((own, count), NARROW),
            pltpu.VMEM((own, LANES), jnp.float32),
            pltpu.SemaphoreType.DMA((mirrors,)),
        ],
        compiler_params=pltpu.CompilerParams(vmem_limit_bytes=VMEM_BYTES),
        cost_estimate=pl.CostEstimate(
            flops=2 * own * acts * count, bytes_accessed=2 * own * acts, transcendentals=0
        ),
        name="gram_rows",
    )(table, pokes, packed)


def position(axis, staged):
    return lax.axis_index(axis) if staged else 0


def row_block(place, staged):
    if not staged:
        return place
    row = lax.axis_index("row")
    core = row & 1
    return row ^ [0, 1, 2 << core, 4 >> core, (4 >> core) | 1, (2 << core) | 1, 6, 7][place]


def row_place(block, staged):
    if not staged:
        return block
    row = lax.axis_index("row")
    core = row & 1
    distance = block ^ row
    near = jnp.where(distance == 2 << core, 2, 3)
    far = jnp.where(distance == (4 >> core) | 1, 4, 5)
    middle = jnp.where(distance & 1 == 0, near, far)
    return jnp.where((distance >= 2) & (distance < 6), middle, distance)


def band_product(source, q, row_shape, block, surface_rows, gram_ref):
    mirrors, shard_rows, slots, samples = row_shape
    own = gram_ref.shape[1]
    narrow = slots - LANES
    k, l = divmod(q, shard_rows)
    band = jnp.clip((block * shard_rows + l) * NAR // surface_rows - 1, 0, NAR - BAND)
    column = pl.multiple_of((k * NAR + band) * NA, 16)
    wide = mirrors * shard_rows * samples
    products = []
    for start, length, row, lane in narrow_places(q, slots, samples):
        left = jnp.concatenate(
            [source[pl.ds(q * samples + start, length), :], source[pl.ds(wide + row, length), :]], axis=1
        )
        right = [gram_ref[pl.ds(column, LANES), :]]
        if lane:
            right.append(jnp.zeros((lane, own), jnp.bfloat16))
        right.append(gram_ref[pl.ds(column + LANES, narrow), :])
        if lane + narrow < LANES:
            right.append(jnp.zeros((LANES - lane - narrow, own), jnp.bfloat16))
        products.append(
            jnp.dot(left, jnp.concatenate(right, axis=0), preferred_element_type=jnp.float32).astype(jnp.bfloat16)
        )
    return jnp.concatenate(products, axis=0)


def fetch_gram(gram_any, gram_ref, semaphores, mirrors):
    height = gram_ref.shape[0] // mirrors
    return [
        pltpu.make_async_copy(
            gram_any.at[pl.ds(k * height, height)], gram_ref.at[pl.ds(k * height, height)], semaphores.at[k]
        )
        for k in range(mirrors)
    ]


def bands_kernel(row_shape, surface_rows, first, counts, staged, gram_any, *refs):
    mirrors, shard_rows, slots, samples = row_shape
    sources = [ref.at[n] for ref, count in zip(refs, counts) for n in range(count)]
    refs = refs[len(counts):]
    *refs, gram_ref, blocks, gram_semaphores, block_semaphores = refs
    if len(refs) > 1:
        *columns_refs, out_ref, whole_ref, rest_ref = refs
    else:
        columns_refs, out_ref = [], refs[0]
    step = pl.program_id(0)
    gram_copies = fetch_gram(gram_any, gram_ref, gram_semaphores, mirrors)

    def fetch(n):
        return pltpu.make_async_copy(sources[n], blocks.at[n], block_semaphores.at[n])

    @pl.when(step == 0)
    def _():
        fetch(0).start()
        for copy in gram_copies:
            copy.start()
        for n in range(1, len(sources)):
            fetch(n).start()
        columns = [ref.at[n] for ref in columns_refs for n in range(ref.shape[0])]
        if columns:
            build_differences(columns, whole_ref, rest_ref, mirrors, samples)

    for n in range(len(sources)):
        @pl.when(step == n)
        def _():
            fetch(n).wait()
            block = row_block(first + n, staged)
            for q in range(mirrors * shard_rows):
                if n == 0 and q % shard_rows == 0:
                    gram_copies[q // shard_rows].wait()
                out_ref[0, q] = band_product(blocks.at[n], q, row_shape, block, surface_rows, gram_ref)


def bands(gram_rows, sources, first, staged, row_shape, surface_rows, columns, pupil):
    acts, own = gram_rows.shape
    mirrors, shard_rows, slots, samples = row_shape
    counts = [source.shape[0] for source in sources]
    rows = mirrors * shard_rows
    flops = 2 * own * WINDOW * samples * rows * sum(counts)
    vmem, anywhere = pl.BlockSpec(memory_space=pltpu.VMEM), pl.BlockSpec(memory_space=pl.ANY)
    out_shape = [jax.ShapeDtypeStruct((sum(counts), rows, samples, own), jnp.bfloat16)]
    out_specs = [pl.BlockSpec((1, rows, samples, own), lambda s: (s, 0, 0, 0))]
    arguments, in_specs = [gram_rows, *sources], [anywhere] * (1 + len(sources))
    directions = sum(lines.shape[0] for lines in columns)
    depth = mirrors * samples // WINDOW * WINDOW
    rest = 2 * (mirrors * samples - depth)
    if columns:
        out_shape += [
            jax.ShapeDtypeStruct((directions, 2, pupil // 2, depth), jnp.bfloat16),
            jax.ShapeDtypeStruct((directions, pupil, rest), jnp.bfloat16),
        ]
        out_specs += [vmem] * 2
    arguments += columns
    in_specs += [vmem] * len(columns)
    return pl.pallas_call(
        functools.partial(bands_kernel, row_shape, surface_rows, first, counts, staged),
        grid=(sum(counts),),
        out_shape=out_shape,
        in_specs=in_specs,
        out_specs=out_specs,
        scratch_shapes=[
            pltpu.VMEM((acts, own), jnp.bfloat16),
            pltpu.VMEM((sum(counts),) + sources[0].shape[1:], jnp.bfloat16),
            pltpu.SemaphoreType.DMA((mirrors,)),
            pltpu.SemaphoreType.DMA((sum(counts),)),
        ],
        compiler_params=pltpu.CompilerParams(vmem_limit_bytes=VMEM_BYTES),
        cost_estimate=pl.CostEstimate(
            flops=flops, bytes_accessed=2 * own * WINDOW * rows * sum(counts), transcendentals=0
        ),
        name="bands",
    )(*arguments)


def build_differences(columns, whole_ref, rest_ref, mirrors, samples):
    half = whole_ref.shape[2]
    pupil, depth = 2 * half, whole_ref.shape[3]
    remainder = mirrors * samples - depth
    pick = lax.broadcasted_iota(jnp.int32, (pupil, pupil), 0)
    lane = lax.broadcasted_iota(jnp.int32, (pupil, pupil), 1)
    pick = (lane == pick % half * 2 + pick // half).astype(jnp.float32).astype(jnp.bfloat16)
    lines = jnp.concatenate([ref[:, :pupil] for ref in columns], axis=0)
    height = columns[0].shape[0]
    turned = lax.dot_general(
        pick, lines.astype(jnp.float32).astype(jnp.bfloat16), (((1,), (1,)), ((), ())),
        preferred_element_type=jnp.float32,
    ).astype(jnp.int32)
    at = lax.broadcasted_iota(jnp.int32, (half, mirrors * samples), 1)
    for d in range(len(columns)):
        sides = []
        for side in range(2):
            wanted = None
            for k in range(mirrors):
                column = turned[side * half:(side + 1) * half, d * height + k:d * height + k + 1] + k * samples
                wanted = column if wanted is None else jnp.where(at < k * samples, wanted, column)
            sides.append((at == wanted).astype(jnp.float32))
        across, down = sides[1] - sides[0], sides[1] + sides[0]
        whole_ref[d, 0] = across[:, :depth].astype(jnp.bfloat16)
        whole_ref[d, 1] = down[:, :depth].astype(jnp.bfloat16)
        blank = jnp.zeros((half, remainder), jnp.float32)
        upper = jnp.concatenate([across[:, depth:], blank], axis=1)
        lower = jnp.concatenate([blank, down[:, depth:]], axis=1)
        rest_ref[d] = jnp.concatenate([upper, lower], axis=0).astype(jnp.bfloat16)


def decode_kernel(row_shape, surface_rows, own, staged, norm, counts, late_parts, *refs):
    mirrors, shard_rows, slots, samples = row_shape
    whole_ref, rest_ref, *refs = refs
    lines_refs, refs = refs[:counts[0]], refs[counts[0]:]
    late_refs, refs = refs[:counts[1]], refs[counts[1]:]
    ready_refs, refs = refs[:counts[2]], refs[counts[2]:]
    (gram_any, out_ref, gram_ref, decoded, total, packed_lines, lines, foot_rows, scalars, *refs) = refs
    late_blocks, refs = refs[:counts[1]], refs[counts[1]:]
    gram_semaphores, ready_semaphores, line_semaphores, late_semaphores, scalar_semaphore = refs
    group = pl.program_id(0)
    directions, pupil = whole_ref.shape[0], 2 * whole_ref.shape[2]
    depth = whole_ref.shape[3]
    phases = out_ref.shape[2] // pupil
    blocks = surface_rows // shard_rows
    late = len(late_parts)
    ready = blocks - late
    count = shard_rows // 2
    rows = mirrors * shard_rows
    extra = lines.shape[1]

    ready_blocks = [ref.at[m] for ref in ready_refs for m in range(ref.shape[0])]

    @pl.when(group == 0)
    def _():
        def started(copies):
            for copy in copies:
                copy.start()
            return copies

        ends = [ref.at[n, pl.ds(ref.shape[1] - extra, extra)] for ref in lines_refs for n in range(ref.shape[0])]
        line_copies = started([
            pltpu.make_async_copy(end, packed_lines.at[n], line_semaphores.at[n]) for n, end in enumerate(ends)
        ])
        late_copies = started([
            pltpu.make_async_copy(late_refs[n], late_blocks[n], late_semaphores.at[n]) for n in range(counts[1])
        ])
        gram_copies = started(fetch_gram(gram_any, gram_ref, gram_semaphores, mirrors)) if late else []
        started([
            pltpu.make_async_copy(block, decoded.at[pl.ds(n * rows, rows)], ready_semaphores.at[n])
            for n, block in enumerate(ready_blocks)
        ])
        for copy in line_copies + late_copies:
            copy.wait()
        held = [packed_lines[n] for n in range(len(ends))]
        at = 0
        for part in late_parts:
            at += part
            last = late_blocks[at - 1]
            held.append(last[pl.ds(last.shape[0] - extra, extra), :])
        for n, value in enumerate(held):
            lines[n] = value.astype(jnp.float32).astype(jnp.int32)
        feet = jnp.concatenate([lines[n, directions * count:directions * count + 1] for n in range(blocks)], axis=0)
        foot_rows[...] = row_place(feet // shard_rows, staged) * rows + feet % shard_rows
        to_scalars = pltpu.make_async_copy(foot_rows, scalars, scalar_semaphore.at[0])
        to_scalars.start()
        at = 0
        for n, part in enumerate(late_parts):
            source, at = late_blocks[at], at + part
            for q in range(mirrors * shard_rows):
                if n == 0 and q % shard_rows == 0:
                    gram_copies[q // shard_rows].wait()
                decoded[(ready + n) * rows + q] = band_product(
                    source, q, row_shape, row_block(ready + n, staged), surface_rows, gram_ref
                )
        to_scalars.wait()

    def last_needed(at):
        return min((2 * phases * (at + 1) - 1 + REACH) // shard_rows, blocks - 1)

    for at in range(surface_rows // 2 // phases):
        @pl.when(group == at)
        def _():
            for block in range(last_needed(at - 1) + 1 if at else 0, last_needed(at) + 1):
                place = row_place(block, staged)

                @pl.when(place < ready)
                def _():
                    pltpu.make_async_copy(
                        ready_blocks[0], decoded.at[pl.ds(place * rows, rows)], ready_semaphores.at[place]
                    ).wait()

    for d in range(directions):
        held = d ^ position("dir", staged)
        products, factors = [], []
        for phase in range(phases):
            i = group * phases + phase
            block = row_place(2 * i // shard_rows, staged)
            sums, changes = [], []
            for k in range(mirrors):
                picked = []
                for y in range(2):
                    row = k * shard_rows + (2 * phase + y) % shard_rows
                    picked.append(decoded[scalars[block, held * rows + row] + k * shard_rows])
                sums.append(picked[0] + picked[1])
                changes.append(picked[1] - picked[0])
            right = [jnp.concatenate(part, axis=0) for part in (sums, changes)]
            mixed = jnp.concatenate([part[depth:] for part in right], axis=0)
            rest = jnp.dot(rest_ref[held], mixed, preferred_element_type=jnp.float32)
            for kind, part in enumerate(right):
                whole = jnp.dot(whole_ref[held, kind], part[:depth], preferred_element_type=jnp.float32)
                products.append(whole + rest[kind * pupil // 2:(kind + 1) * pupil // 2])
            valid = lines[block, pl.ds(held * count + phase % count, 1), :][:, :pupil // 2]
            factors += [valid.astype(jnp.float32)] * 2
        product = jnp.concatenate(products, axis=0)
        factor = jnp.concatenate(factors, axis=1)
        for tile in range(out_ref.shape[2] // LANES):
            at = tile * LANES
            value = jnp.transpose((product[at:at + LANES] * norm).astype(jnp.bfloat16))
            value = value.astype(jnp.float32)[:own] * factor[:, at:at + LANES]
            total[tile, pl.ds(d, own, stride=directions), :] = value
    for tile in range(out_ref.shape[2] // LANES):
        value = total[tile].reshape(own, directions, LANES)
        out_ref[:, :, tile * LANES:(tile + 1) * LANES] = value.astype(out_ref.dtype)


def decode(differences, sources, late, ready, gram_rows, own, row_shape, surface_rows, pupil, norm, staged):
    mirrors, shard_rows, slots, samples = row_shape
    acts, padded = gram_rows.shape
    directions = differences[0].shape[0]
    blocks = surface_rows // shard_rows
    extra = extra_rows(directions, shard_rows)
    phases = LANES // math.gcd(pupil, LANES)
    width = surface_rows // 2 * pupil
    lanes = phases * pupil
    flops = 2 * padded * mirrors * samples * pupil * directions * surface_rows // 2
    vmem, anywhere = pl.BlockSpec(memory_space=pltpu.VMEM), pl.BlockSpec(memory_space=pl.ANY)
    parts = [part for block in late for part in block]
    counts = (len(sources), len(parts), len(ready))
    semaphores = [mirrors, blocks, blocks, max(len(parts), 1), 1]
    return pl.pallas_call(
        functools.partial(
            decode_kernel, row_shape, surface_rows, own, staged, norm, counts, [len(block) for block in late]
        ),
        grid=(width // lanes,),
        out_shape=jax.ShapeDtypeStruct((own, directions, width), jnp.bfloat16),
        in_specs=[vmem] * 2 + [anywhere] * (sum(counts) + 1),
        out_specs=pl.BlockSpec((own, directions, lanes), lambda s: (0, 0, s)),
        scratch_shapes=[
            pltpu.VMEM((acts, padded), jnp.bfloat16),
            pltpu.VMEM((blocks * mirrors * shard_rows, samples, padded), jnp.bfloat16),
            pltpu.VMEM((lanes // LANES, own * directions, LANES), jnp.float32),
            pltpu.VMEM((blocks, extra, LANES), jnp.bfloat16),
            pltpu.VMEM((blocks, extra, LANES), jnp.int32),
            pltpu.VMEM((blocks, LANES), jnp.int32),
            pltpu.SMEM((blocks, LANES), jnp.int32),
            *[pltpu.VMEM(part.shape, part.dtype) for part in parts],
            *[pltpu.SemaphoreType.DMA((count,)) for count in semaphores],
        ],
        compiler_params=pltpu.CompilerParams(vmem_limit_bytes=VMEM_BYTES),
        cost_estimate=pl.CostEstimate(flops=flops, bytes_accessed=2 * own * directions * width, transcendentals=0),
        name="decode",
    )(*differences, *sources, *parts, *ready, gram_rows)


def swap(block, axis, distance):
    return lax.ppermute(block, axis, [(i, i ^ distance) for i in range(lax.axis_size(axis))])


def turn(block, even, odd):
    return lax.ppermute(
        block, "row", [(i, i ^ (odd if i % 2 else even)) for i in range(lax.axis_size("row"))]
    )


def shards(influence, foot_rows, foot_columns, actuator_codes, poke_rows, subaperture_valid):
    mirrors, shard_rows, samples, slots = influence.shape
    row_shape = (mirrors, shard_rows, slots, samples)
    directions, devices = lax.axis_size("dir"), lax.axis_size("row")
    surface_rows = shard_rows * devices
    pupil = foot_columns.shape[2]
    norm = 0.5 * poke_rows.shape[0] ** (-0.5)
    own = actuator_codes.size // (directions * devices)
    staged = devices == 8 and directions & (directions - 1) == 0
    turned = jnp.swapaxes(influence, 2, 3)
    pokes = poke_rows.reshape(-1, LANES)
    lines = small_lines(foot_rows, foot_columns, subaperture_valid)
    if not staged:
        lines = lax.all_gather(lines, "dir")
        packed = pack(turned, [lines])
        every = lax.all_gather(packed, "row")
        gram_rows, _ = gram(actuator_codes, pokes, packed, own, row_shape, surface_rows)
        ready, *differences = bands(gram_rows, [every], 0, staged, row_shape, surface_rows, [lines], pupil)
        return decode(
            differences, [every], [], [ready], gram_rows, own, row_shape, surface_rows, pupil, norm, staged
        )

    lines = [lines[None]] + [swap(lines, "dir", e)[None] for e in range(1, directions)]
    packed = pack(turned, lines)
    first, second = turn(packed, 2, 4), turn(packed, 4, 2)
    sibling = swap(packed, "row", 1)
    gram_rows, own_rows = gram(actuator_codes, pokes, packed, own, row_shape, surface_rows)
    gram_rows, first, second = lax.optimization_barrier((gram_rows, first, second))
    diagonal = turn(first, 4, 2)
    first_sibling, second_sibling = swap(first, "row", 1), swap(second, "row", 1)
    sources = [source[None] for source in (sibling, first, second)]
    near, *differences = bands(gram_rows, sources, 1, staged, row_shape, surface_rows, lines, pupil)
    near, first_sibling, second_sibling = lax.optimization_barrier((near, first_sibling, second_sibling))
    others = [first_sibling[None], second_sibling[None]]
    far, = bands(gram_rows, others, 4, staged, row_shape, surface_rows, [], pupil)
    far, diagonal = lax.optimization_barrier((far, diagonal))
    late = [[diagonal], [swap(diagonal, "row", 1)]]
    return decode(
        differences, [packed[None], *sources, *others], late, [own_rows, near, far], gram_rows, own, row_shape,
        surface_rows, pupil, norm, staged,
    )


def solution(mesh):
    return jax.shard_map(
        shards,
        mesh=mesh,
        in_specs=(
            P(None, "row", None, None),
            P("dir", None, "row"),
            P("dir", None, None),
            P(),
            P(),
            P("dir", "row", None),
        ),
        out_specs=P(("dir", "row"), None, None),
        check_vma=False,
    )
```

```python
import functools
import math

import jax
import jax.numpy as jnp
import numpy as np
from jax import lax
from jax.experimental import pallas as pl
from jax.experimental.pallas import tpu as pltpu
from jax.sharding import PartitionSpec as P

NAR = 48
NA = 48
BAND = 3
REACH = 2
BITS = 13
NARROW = jnp.float8_e4m3fn
LANES = 128
WINDOW = 256
VMEM_BYTES = 127 * 512 * 1024


def parity(codes, rows):
    return lax.population_count(codes & rows) & 1


def lines_kernel(rows_ref, columns_ref, valid_ref, lines_ref):
    mirrors, rows = rows_ref.shape[0], rows_ref.shape[2]
    lines_ref[...] = jnp.zeros(lines_ref.shape, lines_ref.dtype)
    lines_ref[mirrors:mirrors + valid_ref.shape[1], :valid_ref.shape[2]] = valid_ref[0]
    for k in range(mirrors):
        lines_ref[k:k + 1, :columns_ref.shape[2]] = columns_ref[k]
        lines_ref[mirrors + valid_ref.shape[1]:mirrors + valid_ref.shape[1] + 1, k * rows:(k + 1) * rows] = rows_ref[k]


def small_lines(foot_rows, foot_columns, valid):
    vmem = pl.BlockSpec(memory_space=pltpu.VMEM)
    count = foot_rows.shape[1] + valid.shape[1] + 1
    return pl.pallas_call(
        lines_kernel,
        out_shape=jax.ShapeDtypeStruct((-(-count // 8) * 8, WINDOW), jnp.int32),
        in_specs=[vmem] * 3,
        out_specs=vmem,
        name="small_lines",
    )(jnp.swapaxes(foot_rows, 0, 1), jnp.swapaxes(foot_columns, 0, 1), valid)


def narrow_places(q, slots, samples):
    narrow = slots - LANES
    whole = LANES // narrow
    if q < whole:
        return [(0, samples, 0, q * narrow)]
    half = samples // 2
    lane = (q - whole) * narrow
    return [(0, half, samples, lane), (half, half, samples, LANES // 2 + lane)]


def pack_kernel(block_ref, *refs):
    lines_refs, packed_ref = refs[:-1], refs[-1]
    mirrors, rows, slots, samples = block_ref.shape
    identity = (
        lax.broadcasted_iota(jnp.int32, (samples, samples), 0) == lax.broadcasted_iota(jnp.int32, (samples, samples), 1)
    ).astype(jnp.float32).astype(jnp.bfloat16)
    wide = mirrors * rows * samples
    tails = {}
    for q in range(mirrors * rows):
        turned = lax.dot_general(
            identity, block_ref[q // rows, q % rows], (((1,), (1,)), ((), ())), preferred_element_type=jnp.float32
        ).astype(jnp.bfloat16)
        packed_ref[pl.ds(q * samples, samples), :] = turned[:, :LANES]
        for start, length, row, lane in narrow_places(q, slots, samples):
            tails.setdefault((row, length), {})[lane] = turned[start:start + length, LANES:]
    for (row, length), pieces in tails.items():
        packed_ref[pl.ds(wide + row, length), :] = jnp.concatenate([pieces[lane] for lane in sorted(pieces)], axis=1)
    count = rows // 2
    every = [ref.at[n] for ref in lines_refs for n in range(ref.shape[0])]
    feet = [ref[mirrors + count:mirrors + count + 1, :mirrors * rows] for ref in every]
    feet.append(jnp.zeros((1, LANES - mirrors * rows * len(every)), jnp.int32))
    lines = [ref[mirrors:mirrors + count, :LANES] for ref in every] + [jnp.concatenate(feet, axis=1)]
    extra = packed_ref.shape[0] - mirrors * rows * samples * slots // LANES
    lines.append(jnp.zeros((extra - count * len(every) - 1, LANES), jnp.int32))
    packed_ref[pl.ds(packed_ref.shape[0] - extra, extra), :] = (
        jnp.concatenate(lines, axis=0).astype(jnp.float32).astype(jnp.bfloat16)
    )


def extra_rows(directions, rows):
    return -(-(directions * (rows // 2) + 1) // 16) * 16


def pack(block, lines):
    mirrors, rows, slots, samples = block.shape
    vmem = pl.BlockSpec(memory_space=pltpu.VMEM)
    extra = extra_rows(sum(line.shape[0] for line in lines), rows)
    return pl.pallas_call(
        pack_kernel,
        out_shape=jax.ShapeDtypeStruct((mirrors * rows * samples * slots // LANES + extra, LANES), block.dtype),
        in_specs=[vmem] * (1 + len(lines)),
        out_specs=vmem,
        compiler_params=pltpu.CompilerParams(vmem_limit_bytes=VMEM_BYTES),
        cost_estimate=pl.CostEstimate(flops=0, bytes_accessed=3 * block.size, transcendentals=0),
        name="pack_influence",
    )(block, *lines)


def column_of(row):
    return jnp.transpose(jnp.broadcast_to(row, (LANES, LANES)), (1, 0))


def own_side_of(table_ref, pokes_ref, codes_ref, words, own_signs, own_sums):
    planes = pokes_ref.shape[0]
    mirrors, rows, columns = table_ref.shape
    for line in range(codes_ref.shape[0]):
        pieces, at = [], line * LANES
        while at < (line + 1) * LANES:
            row, lane = divmod(at, columns)
            length = min(columns - lane, (line + 1) * LANES - at)
            pieces.append(table_ref[row // rows, row % rows:row % rows + 1, lane:lane + length])
            at += length
        codes_ref[line:line + 1, :] = jnp.concatenate(pieces, axis=1)
    half = LANES // 2
    own = own_signs.shape[0]
    plane = lax.broadcasted_iota(jnp.int32, pokes_ref.shape, 0)
    for bit in range(BITS):
        low = jnp.sum((pokes_ref[...] >> bit & 1) << plane, axis=0, keepdims=True)
        word = low | pltpu.roll(jnp.broadcast_to(low, (8, LANES)), half, 1)[:1] << planes
        words[bit] = column_of(word)[:half]
    count = codes_ref.shape[0] * LANES // (lax.axis_size("dir") * lax.axis_size("row"))
    first = (lax.axis_index("dir") * lax.axis_size("row") + lax.axis_index("row")) * count
    lane = lax.broadcasted_iota(jnp.int32, (8, LANES), 1)
    shift = first % LANES
    lines = [
        pltpu.roll(
            jnp.broadcast_to(
                codes_ref[pl.ds(jnp.minimum(first // LANES + n, codes_ref.shape[0] - 1), 1), :], (8, LANES)
            ),
            LANES - shift, 1,
        )
        for n in range(-(-own // LANES) + 1)
    ]
    own_column = jnp.concatenate(
        [column_of(jnp.where(lane < LANES - shift, lines[n], lines[n + 1])[:1]) for n in range(len(lines) - 1)],
        axis=0,
    )[:own]
    total = jnp.zeros((own, LANES), jnp.float32)
    for at in range(planes):
        signs = (1 - 2 * parity(own_column, pokes_ref[at:at + 1, :])).astype(jnp.float32)
        own_signs[:, at * LANES:(at + 1) * LANES] = signs.astype(NARROW)
        total = total + signs
    own_sums[...] = jnp.broadcast_to(jnp.sum(total, axis=1, keepdims=True), own_sums.shape)


def gram_kernel(
    row_shape, surface_rows, table_ref, pokes_ref, packed_ref, gram_out, first_ref, gram_ref, codes_ref, words,
    own_signs, own_sums, semaphores
):
    mirror = pl.program_id(0)
    half = LANES // 2
    own, pokes = own_signs.shape
    planes = pokes // LANES
    lines = codes_ref.shape[0] // row_shape[0]
    height = gram_ref.shape[0] // row_shape[0]

    @pl.when(mirror == 0)
    def _():
        own_side_of(table_ref, pokes_ref, codes_ref, words, own_signs, own_sums)

    def chunk(index, _):
        word = []
        for side in range(WINDOW // LANES):
            line = mirror * lines + index * (WINDOW // LANES) + side
            code = jnp.broadcast_to(codes_ref[pl.ds(line, 1), :], (8, LANES))
            value = None
            for bit in range(BITS):
                mask = jnp.concatenate([code << (31 - bit) >> 31] * (half // 8), axis=0)
                part = words[bit] & mask
                value = part if value is None else value ^ part
            word.append(value)
        word = jnp.concatenate(word, axis=1)
        bits = [None] * (2 * planes)
        for byte in range(0, 2 * planes, 8):
            part = (word >> byte).astype(jnp.int8)
            for bit in range(8):
                at = byte + bit
                hit = (part & np.uint8(1 << bit).astype(np.int8)) != 0
                bits[at % planes * 2 + at // planes] = jnp.where(hit, NARROW(1.0), NARROW(0.0))
        total = jnp.dot(own_signs[...], jnp.concatenate(bits, axis=0), preferred_element_type=jnp.float32)
        sums = jnp.concatenate([own_sums[...]] * (WINDOW // LANES), axis=1)
        turned = jnp.transpose((sums - 2.0 * total).astype(jnp.bfloat16))
        at = pl.multiple_of(mirror * height + index * WINDOW, WINDOW)
        gram_ref[pl.ds(at, WINDOW), :] = turned
        return 0

    lax.fori_loop(0, height // WINDOW, chunk, 0, unroll=3)

    def send(k):
        part = pl.ds(pl.multiple_of(k * height, height), height)
        return pltpu.make_async_copy(gram_ref.at[part], gram_out.at[part], semaphores.at[k])

    send(mirror).start()
    block = lax.axis_index("row")
    for l in range(row_shape[1]):
        for k in range(row_shape[0]):
            @pl.when(mirror == k)
            def _():
                first_ref[0, l] = band_product(
                    packed_ref, k * row_shape[1] + l, row_shape, block, surface_rows, gram_ref
                )

    @pl.when(mirror == pl.num_programs(0) - 1)
    def _():
        for k in range(row_shape[0]):
            send(k).wait()


def gram(table, pokes, packed, own, row_shape, surface_rows):
    own = -(-own // 32) * 32
    acts, count = table.size, pokes.size
    mirrors, shard_rows, slots, samples = row_shape
    vmem = pl.BlockSpec(memory_space=pltpu.VMEM)
    return pl.pallas_call(
        functools.partial(gram_kernel, row_shape, surface_rows),
        grid=(mirrors,),
        out_shape=[
            jax.ShapeDtypeStruct((acts, own), jnp.bfloat16),
            jax.ShapeDtypeStruct((1, mirrors * shard_rows, samples, own), jnp.bfloat16),
        ],
        in_specs=[vmem] * 3,
        out_specs=[
            pl.BlockSpec(memory_space=pl.ANY),
            pl.BlockSpec((1, shard_rows, samples, own), lambda s: (0, s, 0, 0)),
        ],
        scratch_shapes=[
            pltpu.VMEM((acts, own), jnp.bfloat16),
            pltpu.VMEM((acts // LANES, LANES), jnp.int32),
            pltpu.VMEM((BITS, LANES // 2, LANES), jnp.int32),
            pltpu.VMEM((own, count), NARROW),
            pltpu.VMEM((own, LANES), jnp.float32),
            pltpu.SemaphoreType.DMA((mirrors,)),
        ],
        compiler_params=pltpu.CompilerParams(vmem_limit_bytes=VMEM_BYTES),
        cost_estimate=pl.CostEstimate(
            flops=2 * own * acts * count, bytes_accessed=2 * own * acts, transcendentals=0
        ),
        name="gram_rows",
    )(table, pokes, packed)


def position(axis, staged):
    return lax.axis_index(axis) if staged else 0


def row_block(place, staged):
    if not staged:
        return place
    row = lax.axis_index("row")
    core = row & 1
    return row ^ [0, 1, 2 << core, 4 >> core, (4 >> core) | 1, (2 << core) | 1, 6, 7][place]


def row_place(block, staged):
    if not staged:
        return block
    row = lax.axis_index("row")
    core = row & 1
    distance = block ^ row
    near = jnp.where(distance == 2 << core, 2, 3)
    far = jnp.where(distance == (4 >> core) | 1, 4, 5)
    middle = jnp.where(distance & 1 == 0, near, far)
    return jnp.where((distance >= 2) & (distance < 6), middle, distance)


def band_product(source, q, row_shape, block, surface_rows, gram_ref):
    mirrors, shard_rows, slots, samples = row_shape
    own = gram_ref.shape[1]
    narrow = slots - LANES
    k, l = divmod(q, shard_rows)
    band = jnp.clip((block * shard_rows + l) * NAR // surface_rows - 1, 0, NAR - BAND)
    column = pl.multiple_of((k * NAR + band) * NA, 16)
    wide = mirrors * shard_rows * samples
    products = []
    for start, length, row, lane in narrow_places(q, slots, samples):
        left = jnp.concatenate(
            [source[pl.ds(q * samples + start, length), :], source[pl.ds(wide + row, length), :]], axis=1
        )
        right = [gram_ref[pl.ds(column, LANES), :]]
        if lane:
            right.append(jnp.zeros((lane, own), jnp.bfloat16))
        right.append(gram_ref[pl.ds(column + LANES, narrow), :])
        if lane + narrow < LANES:
            right.append(jnp.zeros((LANES - lane - narrow, own), jnp.bfloat16))
        products.append(
            jnp.dot(left, jnp.concatenate(right, axis=0), preferred_element_type=jnp.float32).astype(jnp.bfloat16)
        )
    return jnp.concatenate(products, axis=0)


def fetch_gram(gram_any, gram_ref, semaphores, mirrors):
    height = gram_ref.shape[0] // mirrors
    return [
        pltpu.make_async_copy(
            gram_any.at[pl.ds(k * height, height)], gram_ref.at[pl.ds(k * height, height)], semaphores.at[k]
        )
        for k in range(mirrors)
    ]


def bands_kernel(row_shape, surface_rows, first, counts, staged, gram_any, *refs):
    mirrors, shard_rows, slots, samples = row_shape
    sources = [ref.at[n] for ref, count in zip(refs, counts) for n in range(count)]
    refs = refs[len(counts):]
    *refs, gram_ref, blocks, gram_semaphores, block_semaphores = refs
    if len(refs) > 1:
        *columns_refs, out_ref, whole_ref, rest_ref = refs
    else:
        columns_refs, out_ref = [], refs[0]
    step = pl.program_id(0)
    gram_copies = fetch_gram(gram_any, gram_ref, gram_semaphores, mirrors)

    def fetch(n):
        return pltpu.make_async_copy(sources[n], blocks.at[n], block_semaphores.at[n])

    @pl.when(step == 0)
    def _():
        fetch(0).start()
        for copy in gram_copies:
            copy.start()
        for n in range(1, len(sources)):
            fetch(n).start()
        columns = [ref.at[n] for ref in columns_refs for n in range(ref.shape[0])]
        if columns:
            build_differences(columns, whole_ref, rest_ref, mirrors, samples)

    for n in range(len(sources)):
        @pl.when(step == n)
        def _():
            fetch(n).wait()
            block = row_block(first + n, staged)
            for q in range(mirrors * shard_rows):
                if n == 0 and q % shard_rows == 0:
                    gram_copies[q // shard_rows].wait()
                out_ref[0, q] = band_product(blocks.at[n], q, row_shape, block, surface_rows, gram_ref)


def bands(gram_rows, sources, first, staged, row_shape, surface_rows, columns, pupil):
    acts, own = gram_rows.shape
    mirrors, shard_rows, slots, samples = row_shape
    counts = [source.shape[0] for source in sources]
    rows = mirrors * shard_rows
    flops = 2 * own * WINDOW * samples * rows * sum(counts)
    vmem, anywhere = pl.BlockSpec(memory_space=pltpu.VMEM), pl.BlockSpec(memory_space=pl.ANY)
    out_shape = [jax.ShapeDtypeStruct((sum(counts), rows, samples, own), jnp.bfloat16)]
    out_specs = [pl.BlockSpec((1, rows, samples, own), lambda s: (s, 0, 0, 0))]
    arguments, in_specs = [gram_rows, *sources], [anywhere] * (1 + len(sources))
    directions = sum(lines.shape[0] for lines in columns)
    depth = mirrors * samples // WINDOW * WINDOW
    rest = 2 * (mirrors * samples - depth)
    if columns:
        out_shape += [
            jax.ShapeDtypeStruct((directions, 2, pupil // 2, depth), jnp.bfloat16),
            jax.ShapeDtypeStruct((directions, pupil, rest), jnp.bfloat16),
        ]
        out_specs += [vmem] * 2
    arguments += columns
    in_specs += [vmem] * len(columns)
    return pl.pallas_call(
        functools.partial(bands_kernel, row_shape, surface_rows, first, counts, staged),
        grid=(sum(counts),),
        out_shape=out_shape,
        in_specs=in_specs,
        out_specs=out_specs,
        scratch_shapes=[
            pltpu.VMEM((acts, own), jnp.bfloat16),
            pltpu.VMEM((sum(counts),) + sources[0].shape[1:], jnp.bfloat16),
            pltpu.SemaphoreType.DMA((mirrors,)),
            pltpu.SemaphoreType.DMA((sum(counts),)),
        ],
        compiler_params=pltpu.CompilerParams(vmem_limit_bytes=VMEM_BYTES),
        cost_estimate=pl.CostEstimate(
            flops=flops, bytes_accessed=2 * own * WINDOW * rows * sum(counts), transcendentals=0
        ),
        name="bands",
    )(*arguments)


def build_differences(columns, whole_ref, rest_ref, mirrors, samples):
    half = whole_ref.shape[2]
    pupil, depth = 2 * half, whole_ref.shape[3]
    remainder = mirrors * samples - depth
    pick = lax.broadcasted_iota(jnp.int32, (pupil, pupil), 0)
    lane = lax.broadcasted_iota(jnp.int32, (pupil, pupil), 1)
    pick = (lane == pick % half * 2 + pick // half).astype(jnp.float32).astype(jnp.bfloat16)
    lines = jnp.concatenate([ref[:, :pupil] for ref in columns], axis=0)
    height = columns[0].shape[0]
    turned = lax.dot_general(
        pick, lines.astype(jnp.float32).astype(jnp.bfloat16), (((1,), (1,)), ((), ())),
        preferred_element_type=jnp.float32,
    ).astype(jnp.int32)
    at = lax.broadcasted_iota(jnp.int32, (half, mirrors * samples), 1)
    for d in range(len(columns)):
        sides = []
        for side in range(2):
            wanted = None
            for k in range(mirrors):
                column = turned[side * half:(side + 1) * half, d * height + k:d * height + k + 1] + k * samples
                wanted = column if wanted is None else jnp.where(at < k * samples, wanted, column)
            sides.append((at == wanted).astype(jnp.float32))
        across, down = sides[1] - sides[0], sides[1] + sides[0]
        whole_ref[d, 0] = across[:, :depth].astype(jnp.bfloat16)
        whole_ref[d, 1] = down[:, :depth].astype(jnp.bfloat16)
        blank = jnp.zeros((half, remainder), jnp.float32)
        upper = jnp.concatenate([across[:, depth:], blank], axis=1)
        lower = jnp.concatenate([blank, down[:, depth:]], axis=1)
        rest_ref[d] = jnp.concatenate([upper, lower], axis=0).astype(jnp.bfloat16)


def decode_kernel(row_shape, surface_rows, own, staged, norm, counts, late_parts, *refs):
    mirrors, shard_rows, slots, samples = row_shape
    whole_ref, rest_ref, *refs = refs
    lines_refs, refs = refs[:counts[0]], refs[counts[0]:]
    late_refs, refs = refs[:counts[1]], refs[counts[1]:]
    ready_refs, refs = refs[:counts[2]], refs[counts[2]:]
    (gram_any, out_ref, gram_ref, decoded, total, packed_lines, lines, foot_rows, scalars, *refs) = refs
    late_blocks, refs = refs[:counts[1]], refs[counts[1]:]
    gram_semaphores, ready_semaphores, line_semaphores, late_semaphores, scalar_semaphore = refs
    group = pl.program_id(0)
    directions, pupil = whole_ref.shape[0], 2 * whole_ref.shape[2]
    depth = whole_ref.shape[3]
    phases = out_ref.shape[2] // pupil
    blocks = surface_rows // shard_rows
    late = len(late_parts)
    ready = blocks - late
    count = shard_rows // 2
    rows = mirrors * shard_rows
    extra = lines.shape[1]

    ready_blocks = [ref.at[m] for ref in ready_refs for m in range(ref.shape[0])]

    @pl.when(group == 0)
    def _():
        def started(copies):
            for copy in copies:
                copy.start()
            return copies

        ends = [ref.at[n, pl.ds(ref.shape[1] - extra, extra)] for ref in lines_refs for n in range(ref.shape[0])]
        line_copies = started([
            pltpu.make_async_copy(end, packed_lines.at[n], line_semaphores.at[n]) for n, end in enumerate(ends)
        ])
        late_copies = started([
            pltpu.make_async_copy(late_refs[n], late_blocks[n], late_semaphores.at[n]) for n in range(counts[1])
        ])
        gram_copies = started(fetch_gram(gram_any, gram_ref, gram_semaphores, mirrors)) if late else []
        started([
            pltpu.make_async_copy(block, decoded.at[pl.ds(n * rows, rows)], ready_semaphores.at[n])
            for n, block in enumerate(ready_blocks)
        ])
        for copy in line_copies + late_copies:
            copy.wait()
        held = [packed_lines[n] for n in range(len(ends))]
        at = 0
        for part in late_parts:
            at += part
            last = late_blocks[at - 1]
            held.append(last[pl.ds(last.shape[0] - extra, extra), :])
        for n, value in enumerate(held):
            lines[n] = value.astype(jnp.float32).astype(jnp.int32)
        feet = jnp.concatenate([lines[n, directions * count:directions * count + 1] for n in range(blocks)], axis=0)
        foot_rows[...] = row_place(feet // shard_rows, staged) * rows + feet % shard_rows
        to_scalars = pltpu.make_async_copy(foot_rows, scalars, scalar_semaphore.at[0])
        to_scalars.start()
        at = 0
        for n, part in enumerate(late_parts):
            source, at = late_blocks[at], at + part
            for q in range(mirrors * shard_rows):
                if n == 0 and q % shard_rows == 0:
                    gram_copies[q // shard_rows].wait()
                decoded[(ready + n) * rows + q] = band_product(
                    source, q, row_shape, row_block(ready + n, staged), surface_rows, gram_ref
                )
        to_scalars.wait()

    def last_needed(at):
        return min((2 * phases * (at + 1) - 1 + REACH) // shard_rows, blocks - 1)

    for at in range(surface_rows // 2 // phases):
        @pl.when(group == at)
        def _():
            for block in range(last_needed(at - 1) + 1 if at else 0, last_needed(at) + 1):
                place = row_place(block, staged)

                @pl.when(place < ready)
                def _():
                    pltpu.make_async_copy(
                        ready_blocks[0], decoded.at[pl.ds(place * rows, rows)], ready_semaphores.at[place]
                    ).wait()

    for d in range(directions):
        held = d ^ position("dir", staged)
        products, factors = [], []
        for phase in range(phases):
            i = group * phases + phase
            block = row_place(2 * i // shard_rows, staged)
            sums, changes = [], []
            for k in range(mirrors):
                picked = []
                for y in range(2):
                    row = k * shard_rows + (2 * phase + y) % shard_rows
                    picked.append(decoded[scalars[block, held * rows + row] + k * shard_rows])
                sums.append(picked[0] + picked[1])
                changes.append(picked[1] - picked[0])
            right = [jnp.concatenate(part, axis=0) for part in (sums, changes)]
            mixed = jnp.concatenate([part[depth:] for part in right], axis=0)
            rest = jnp.dot(rest_ref[held], mixed, preferred_element_type=jnp.float32)
            for kind, part in enumerate(right):
                whole = jnp.dot(whole_ref[held, kind], part[:depth], preferred_element_type=jnp.float32)
                products.append(whole + rest[kind * pupil // 2:(kind + 1) * pupil // 2])
            valid = lines[block, pl.ds(held * count + phase % count, 1), :][:, :pupil // 2]
            factors += [valid.astype(jnp.float32)] * 2
        product = jnp.concatenate(products, axis=0)
        factor = jnp.concatenate(factors, axis=1)
        for tile in range(out_ref.shape[2] // LANES):
            at = tile * LANES
            value = jnp.transpose((product[at:at + LANES] * norm).astype(jnp.bfloat16))
            value = value.astype(jnp.float32)[:own] * factor[:, at:at + LANES]
            total[tile, pl.ds(d, own, stride=directions), :] = value
    for tile in range(out_ref.shape[2] // LANES):
        value = total[tile].astype(out_ref.dtype).reshape(own, directions, LANES)
        out_ref[:, :, tile * LANES:(tile + 1) * LANES] = value


def decode(differences, sources, late, ready, gram_rows, own, row_shape, surface_rows, pupil, norm, staged):
    mirrors, shard_rows, slots, samples = row_shape
    acts, padded = gram_rows.shape
    directions = differences[0].shape[0]
    blocks = surface_rows // shard_rows
    extra = extra_rows(directions, shard_rows)
    phases = LANES // math.gcd(pupil, LANES)
    width = surface_rows // 2 * pupil
    lanes = phases * pupil
    flops = 2 * padded * mirrors * samples * pupil * directions * surface_rows // 2
    vmem, anywhere = pl.BlockSpec(memory_space=pltpu.VMEM), pl.BlockSpec(memory_space=pl.ANY)
    parts = [part for block in late for part in block]
    counts = (len(sources), len(parts), len(ready))
    semaphores = [mirrors, blocks, blocks, max(len(parts), 1), 1]
    return pl.pallas_call(
        functools.partial(
            decode_kernel, row_shape, surface_rows, own, staged, norm, counts, [len(block) for block in late]
        ),
        grid=(width // lanes,),
        out_shape=jax.ShapeDtypeStruct((own, directions, width), jnp.bfloat16),
        in_specs=[vmem] * 2 + [anywhere] * (sum(counts) + 1),
        out_specs=pl.BlockSpec((own, directions, lanes), lambda s: (0, 0, s)),
        scratch_shapes=[
            pltpu.VMEM((acts, padded), jnp.bfloat16),
            pltpu.VMEM((blocks * mirrors * shard_rows, samples, padded), jnp.bfloat16),
            pltpu.VMEM((lanes // LANES, own * directions, LANES), jnp.float32),
            pltpu.VMEM((blocks, extra, LANES), jnp.bfloat16),
            pltpu.VMEM((blocks, extra, LANES), jnp.int32),
            pltpu.VMEM((blocks, LANES), jnp.int32),
            pltpu.SMEM((blocks, LANES), jnp.int32),
            *[pltpu.VMEM(part.shape, part.dtype) for part in parts],
            *[pltpu.SemaphoreType.DMA((count,)) for count in semaphores],
        ],
        compiler_params=pltpu.CompilerParams(vmem_limit_bytes=VMEM_BYTES),
        cost_estimate=pl.CostEstimate(flops=flops, bytes_accessed=2 * own * directions * width, transcendentals=0),
        name="decode",
    )(*differences, *sources, *parts, *ready, gram_rows)


def swap(block, axis, distance):
    return lax.ppermute(block, axis, [(i, i ^ distance) for i in range(lax.axis_size(axis))])


def turn(block, even, odd):
    return lax.ppermute(
        block, "row", [(i, i ^ (odd if i % 2 else even)) for i in range(lax.axis_size("row"))]
    )


def shards(influence, foot_rows, foot_columns, actuator_codes, poke_rows, subaperture_valid):
    mirrors, shard_rows, samples, slots = influence.shape
    row_shape = (mirrors, shard_rows, slots, samples)
    directions, devices = lax.axis_size("dir"), lax.axis_size("row")
    surface_rows = shard_rows * devices
    pupil = foot_columns.shape[2]
    norm = 0.5 * poke_rows.shape[0] ** (-0.5)
    own = actuator_codes.size // (directions * devices)
    staged = devices == 8 and directions & (directions - 1) == 0
    turned = jnp.swapaxes(influence, 2, 3)
    pokes = poke_rows.reshape(-1, LANES)
    lines = small_lines(foot_rows, foot_columns, subaperture_valid)
    if not staged:
        lines = lax.all_gather(lines, "dir")
        packed = pack(turned, [lines])
        every = lax.all_gather(packed, "row")
        gram_rows, _ = gram(actuator_codes, pokes, packed, own, row_shape, surface_rows)
        ready, *differences = bands(gram_rows, [every], 0, staged, row_shape, surface_rows, [lines], pupil)
        return decode(
            differences, [every], [], [ready], gram_rows, own, row_shape, surface_rows, pupil, norm, staged
        )

    lines = [lines[None]] + [swap(lines, "dir", e)[None] for e in range(1, directions)]
    packed = pack(turned, lines)
    first, second = turn(packed, 2, 4), turn(packed, 4, 2)
    sibling = swap(packed, "row", 1)
    gram_rows, own_rows = gram(actuator_codes, pokes, packed, own, row_shape, surface_rows)
    gram_rows, first, second = lax.optimization_barrier((gram_rows, first, second))
    diagonal = turn(first, 4, 2)
    first_sibling, second_sibling = swap(first, "row", 1), swap(second, "row", 1)
    sources = [source[None] for source in (sibling, first, second)]
    near, *differences = bands(gram_rows, sources, 1, staged, row_shape, surface_rows, lines, pupil)
    near, diagonal = lax.optimization_barrier((near, diagonal))
    late = [[block] for block in (first_sibling, second_sibling, diagonal, swap(diagonal, "row", 1))]
    return decode(
        differences, [packed[None], *sources], late, [own_rows, near], gram_rows, own, row_shape, surface_rows, pupil,
        norm, staged,
    )


def solution(mesh):
    return jax.shard_map(
        shards,
        mesh=mesh,
        in_specs=(
            P(None, "row", None, None),
            P("dir", None, "row"),
            P("dir", None, None),
            P(),
            P(),
            P("dir", "row", None),
        ),
        out_specs=P(("dir", "row"), None, None),
        check_vma=False,
    )
```

```python
import functools
import math

import jax
import jax.numpy as jnp
import numpy as np
from jax import lax
from jax.experimental import pallas as pl
from jax.experimental.pallas import tpu as pltpu
from jax.sharding import PartitionSpec as P

NAR = 48
NA = 48
BAND = 3
REACH = 2
BITS = 13
NARROW = jnp.float8_e4m3fn
LANES = 128
WINDOW = 256
VMEM_BYTES = 127 * 512 * 1024


def parity(codes, rows):
    return lax.population_count(codes & rows) & 1


def narrow_places(q, slots, samples):
    narrow = slots - LANES
    whole = LANES // narrow
    if q < whole:
        return [(0, samples, 0, q * narrow)]
    half = samples // 2
    lane = (q - whole) * narrow
    return [(0, half, samples, lane), (half, half, samples, LANES // 2 + lane)]


def pack_kernel(block_ref, rows_ref, columns_ref, valid_ref, packed_ref, lines_ref):
    mirrors, rows, slots, samples = block_ref.shape
    foot_line = mirrors + valid_ref.shape[1]
    lines_ref[...] = jnp.zeros(lines_ref.shape, lines_ref.dtype)
    lines_ref[mirrors:foot_line, :valid_ref.shape[2]] = valid_ref[0]
    for k in range(mirrors):
        lines_ref[k:k + 1, :columns_ref.shape[2]] = columns_ref[k]
        lines_ref[foot_line:foot_line + 1, k * rows:(k + 1) * rows] = rows_ref[k]
    identity = (
        lax.broadcasted_iota(jnp.int32, (samples, samples), 0) == lax.broadcasted_iota(jnp.int32, (samples, samples), 1)
    ).astype(jnp.float32).astype(jnp.bfloat16)
    wide = mirrors * rows * samples
    tails = {}
    for q in range(mirrors * rows):
        turned = lax.dot_general(
            identity, block_ref[q // rows, q % rows], (((1,), (1,)), ((), ())), preferred_element_type=jnp.float32
        ).astype(jnp.bfloat16)
        packed_ref[pl.ds(q * samples, samples), :] = turned[:, :LANES]
        for start, length, row, lane in narrow_places(q, slots, samples):
            tails.setdefault((row, length), {})[lane] = turned[start:start + length, LANES:]
    for (row, length), pieces in tails.items():
        packed_ref[pl.ds(wide + row, length), :] = jnp.concatenate([pieces[lane] for lane in sorted(pieces)], axis=1)


def pack(block, foot_rows, foot_columns, valid):
    mirrors, rows, slots, samples = block.shape
    vmem = pl.BlockSpec(memory_space=pltpu.VMEM)
    height = mirrors + valid.shape[1] + 1
    return pl.pallas_call(
        pack_kernel,
        out_shape=[
            jax.ShapeDtypeStruct((mirrors * rows * samples * slots // LANES, LANES), block.dtype),
            jax.ShapeDtypeStruct((-(-height // 8) * 8, WINDOW), jnp.int32),
        ],
        in_specs=[vmem] * 4,
        out_specs=[vmem] * 2,
        compiler_params=pltpu.CompilerParams(vmem_limit_bytes=VMEM_BYTES),
        cost_estimate=pl.CostEstimate(flops=0, bytes_accessed=3 * block.size, transcendentals=0),
        name="pack_influence",
    )(block, jnp.swapaxes(foot_rows, 0, 1), jnp.swapaxes(foot_columns, 0, 1), valid)


def column_of(row):
    return jnp.transpose(jnp.broadcast_to(row, (LANES, LANES)), (1, 0))


def own_side_of(table_ref, pokes_ref, codes_ref, words, own_signs, own_sums):
    planes = pokes_ref.shape[0]
    mirrors, rows, columns = table_ref.shape
    for line in range(codes_ref.shape[0]):
        pieces, at = [], line * LANES
        while at < (line + 1) * LANES:
            row, lane = divmod(at, columns)
            length = min(columns - lane, (line + 1) * LANES - at)
            pieces.append(table_ref[row // rows, row % rows:row % rows + 1, lane:lane + length])
            at += length
        codes_ref[line:line + 1, :] = jnp.concatenate(pieces, axis=1)
    half = LANES // 2
    own = own_signs.shape[0]
    plane = lax.broadcasted_iota(jnp.int32, pokes_ref.shape, 0)
    for bit in range(BITS):
        low = jnp.sum((pokes_ref[...] >> bit & 1) << plane, axis=0, keepdims=True)
        word = low | pltpu.roll(jnp.broadcast_to(low, (8, LANES)), half, 1)[:1] << planes
        words[bit] = column_of(word)[:half]
    count = codes_ref.shape[0] * LANES // (lax.axis_size("dir") * lax.axis_size("row"))
    first = (lax.axis_index("dir") * lax.axis_size("row") + lax.axis_index("row")) * count
    lane = lax.broadcasted_iota(jnp.int32, (8, LANES), 1)
    shift = first % LANES
    lines = [
        pltpu.roll(
            jnp.broadcast_to(
                codes_ref[pl.ds(jnp.minimum(first // LANES + n, codes_ref.shape[0] - 1), 1), :], (8, LANES)
            ),
            LANES - shift, 1,
        )
        for n in range(-(-own // LANES) + 1)
    ]
    own_column = jnp.concatenate(
        [column_of(jnp.where(lane < LANES - shift, lines[n], lines[n + 1])[:1]) for n in range(len(lines) - 1)],
        axis=0,
    )[:own]
    total = jnp.zeros((own, LANES), jnp.float32)
    for at in range(planes):
        signs = (1 - 2 * parity(own_column, pokes_ref[at:at + 1, :])).astype(jnp.float32)
        own_signs[:, at * LANES:(at + 1) * LANES] = signs.astype(NARROW)
        total = total + signs
    own_sums[...] = jnp.broadcast_to(jnp.sum(total, axis=1, keepdims=True), own_sums.shape)


def gram_kernel(
    row_shape, surface_rows, table_ref, pokes_ref, packed_ref, gram_out, first_ref, gram_ref, codes_ref, words,
    own_signs, own_sums, semaphores
):
    mirror = pl.program_id(0)
    half = LANES // 2
    own, pokes = own_signs.shape
    planes = pokes // LANES
    lines = codes_ref.shape[0] // row_shape[0]
    height = gram_ref.shape[0] // row_shape[0]

    @pl.when(mirror == 0)
    def _():
        own_side_of(table_ref, pokes_ref, codes_ref, words, own_signs, own_sums)

    def chunk(index, _):
        word = []
        for side in range(WINDOW // LANES):
            line = mirror * lines + index * (WINDOW // LANES) + side
            code = jnp.broadcast_to(codes_ref[pl.ds(line, 1), :], (8, LANES))
            value = None
            for bit in range(BITS):
                mask = jnp.concatenate([code << (31 - bit) >> 31] * (half // 8), axis=0)
                part = words[bit] & mask
                value = part if value is None else value ^ part
            word.append(value)
        word = jnp.concatenate(word, axis=1)
        bits = [None] * (2 * planes)
        for byte in range(0, 2 * planes, 8):
            part = (word >> byte).astype(jnp.int8)
            for bit in range(8):
                at = byte + bit
                hit = (part & np.uint8(1 << bit).astype(np.int8)) != 0
                bits[at % planes * 2 + at // planes] = jnp.where(hit, NARROW(1.0), NARROW(0.0))
        total = jnp.dot(own_signs[...], jnp.concatenate(bits, axis=0), preferred_element_type=jnp.float32)
        sums = jnp.concatenate([own_sums[...]] * (WINDOW // LANES), axis=1)
        turned = jnp.transpose((sums - 2.0 * total).astype(jnp.bfloat16))
        at = pl.multiple_of(mirror * height + index * WINDOW, WINDOW)
        gram_ref[pl.ds(at, WINDOW), :] = turned
        return 0

    lax.fori_loop(0, height // WINDOW, chunk, 0, unroll=3)

    def send(k):
        part = pl.ds(pl.multiple_of(k * height, height), height)
        return pltpu.make_async_copy(gram_ref.at[part], gram_out.at[part], semaphores.at[k])

    send(mirror).start()
    block = lax.axis_index("row")
    for l in range(row_shape[1]):
        for k in range(row_shape[0]):
            @pl.when(mirror == k)
            def _():
                first_ref[0, l] = band_product(
                    packed_ref, k * row_shape[1] + l, row_shape, block, surface_rows, gram_ref
                )

    @pl.when(mirror == pl.num_programs(0) - 1)
    def _():
        for k in range(row_shape[0]):
            send(k).wait()


def gram(table, pokes, packed, own, row_shape, surface_rows):
    own = -(-own // 32) * 32
    acts, count = table.size, pokes.size
    mirrors, shard_rows, slots, samples = row_shape
    vmem = pl.BlockSpec(memory_space=pltpu.VMEM)
    return pl.pallas_call(
        functools.partial(gram_kernel, row_shape, surface_rows),
        grid=(mirrors,),
        out_shape=[
            jax.ShapeDtypeStruct((acts, own), jnp.bfloat16),
            jax.ShapeDtypeStruct((1, mirrors * shard_rows, samples, own), jnp.bfloat16),
        ],
        in_specs=[vmem] * 3,
        out_specs=[
            pl.BlockSpec(memory_space=pl.ANY),
            pl.BlockSpec((1, shard_rows, samples, own), lambda s: (0, s, 0, 0)),
        ],
        scratch_shapes=[
            pltpu.VMEM((acts, own), jnp.bfloat16),
            pltpu.VMEM((acts // LANES, LANES), jnp.int32),
            pltpu.VMEM((BITS, LANES // 2, LANES), jnp.int32),
            pltpu.VMEM((own, count), NARROW),
            pltpu.VMEM((own, LANES), jnp.float32),
            pltpu.SemaphoreType.DMA((mirrors,)),
        ],
        compiler_params=pltpu.CompilerParams(vmem_limit_bytes=VMEM_BYTES),
        cost_estimate=pl.CostEstimate(
            flops=2 * own * acts * count, bytes_accessed=2 * own * acts, transcendentals=0
        ),
        name="gram_rows",
    )(table, pokes, packed)


def position(axis, staged):
    return lax.axis_index(axis) if staged else 0


def row_block(place, staged):
    if not staged:
        return place
    row = lax.axis_index("row")
    core = row & 1
    return row ^ [0, 1, 2 << core, 4 >> core, (4 >> core) | 1, (2 << core) | 1, 6, 7][place]


def row_place(block, staged):
    if not staged:
        return block
    row = lax.axis_index("row")
    core = row & 1
    distance = block ^ row
    near = jnp.where(distance == 2 << core, 2, 3)
    far = jnp.where(distance == (4 >> core) | 1, 4, 5)
    middle = jnp.where(distance & 1 == 0, near, far)
    return jnp.where((distance >= 2) & (distance < 6), middle, distance)


def band_product(source, q, row_shape, block, surface_rows, gram_ref):
    mirrors, shard_rows, slots, samples = row_shape
    own = gram_ref.shape[1]
    narrow = slots - LANES
    k, l = divmod(q, shard_rows)
    band = jnp.clip((block * shard_rows + l) * NAR // surface_rows - 1, 0, NAR - BAND)
    column = pl.multiple_of((k * NAR + band) * NA, 16)
    wide = mirrors * shard_rows * samples
    products = []
    for start, length, row, lane in narrow_places(q, slots, samples):
        left = jnp.concatenate(
            [source[pl.ds(q * samples + start, length), :], source[pl.ds(wide + row, length), :]], axis=1
        )
        right = [gram_ref[pl.ds(column, LANES), :]]
        if lane:
            right.append(jnp.zeros((lane, own), jnp.bfloat16))
        right.append(gram_ref[pl.ds(column + LANES, narrow), :])
        if lane + narrow < LANES:
            right.append(jnp.zeros((LANES - lane - narrow, own), jnp.bfloat16))
        products.append(
            jnp.dot(left, jnp.concatenate(right, axis=0), preferred_element_type=jnp.float32).astype(jnp.bfloat16)
        )
    return jnp.concatenate(products, axis=0)


def fetch_gram(gram_any, gram_ref, semaphores, mirrors):
    height = gram_ref.shape[0] // mirrors
    return [
        pltpu.make_async_copy(
            gram_any.at[pl.ds(k * height, height)], gram_ref.at[pl.ds(k * height, height)], semaphores.at[k]
        )
        for k in range(mirrors)
    ]


def bands_kernel(row_shape, surface_rows, first, counts, staged, gram_any, *refs):
    mirrors, shard_rows, slots, samples = row_shape
    sources = [ref.at[n] for ref, count in zip(refs, counts) for n in range(count)]
    refs = refs[len(counts):]
    *refs, gram_ref, blocks, gram_semaphores, block_semaphores = refs
    if len(refs) > 1:
        *columns_refs, out_ref, whole_ref, rest_ref = refs
    else:
        columns_refs, out_ref = [], refs[0]
    step = pl.program_id(0)
    gram_copies = fetch_gram(gram_any, gram_ref, gram_semaphores, mirrors)

    def fetch(n):
        return pltpu.make_async_copy(sources[n], blocks.at[n], block_semaphores.at[n])

    @pl.when(step == 0)
    def _():
        fetch(0).start()
        for copy in gram_copies:
            copy.start()
        for n in range(1, len(sources)):
            fetch(n).start()
        columns = [ref.at[n] for ref in columns_refs for n in range(ref.shape[0])]
        if columns:
            build_differences(columns, whole_ref, rest_ref, mirrors, samples)

    for n in range(len(sources)):
        @pl.when(step == n)
        def _():
            fetch(n).wait()
            block = row_block(first + n, staged)
            for q in range(mirrors * shard_rows):
                if n == 0 and q % shard_rows == 0:
                    gram_copies[q // shard_rows].wait()
                out_ref[0, q] = band_product(blocks.at[n], q, row_shape, block, surface_rows, gram_ref)


def bands(gram_rows, sources, first, staged, row_shape, surface_rows, columns, pupil):
    acts, own = gram_rows.shape
    mirrors, shard_rows, slots, samples = row_shape
    counts = [source.shape[0] for source in sources]
    rows = mirrors * shard_rows
    flops = 2 * own * WINDOW * samples * rows * sum(counts)
    vmem, anywhere = pl.BlockSpec(memory_space=pltpu.VMEM), pl.BlockSpec(memory_space=pl.ANY)
    out_shape = [jax.ShapeDtypeStruct((sum(counts), rows, samples, own), jnp.bfloat16)]
    out_specs = [pl.BlockSpec((1, rows, samples, own), lambda s: (s, 0, 0, 0))]
    arguments, in_specs = [gram_rows, *sources], [anywhere] * (1 + len(sources))
    directions = sum(lines.shape[0] for lines in columns)
    depth = mirrors * samples // WINDOW * WINDOW
    rest = 2 * (mirrors * samples - depth)
    if columns:
        out_shape += [
            jax.ShapeDtypeStruct((directions, 2, pupil // 2, depth), jnp.bfloat16),
            jax.ShapeDtypeStruct((directions, pupil, rest), jnp.bfloat16),
        ]
        out_specs += [vmem] * 2
    arguments += columns
    in_specs += [vmem] * len(columns)
    return pl.pallas_call(
        functools.partial(bands_kernel, row_shape, surface_rows, first, counts, staged),
        grid=(sum(counts),),
        out_shape=out_shape,
        in_specs=in_specs,
        out_specs=out_specs,
        scratch_shapes=[
            pltpu.VMEM((acts, own), jnp.bfloat16),
            pltpu.VMEM((sum(counts),) + sources[0].shape[1:], jnp.bfloat16),
            pltpu.SemaphoreType.DMA((mirrors,)),
            pltpu.SemaphoreType.DMA((sum(counts),)),
        ],
        compiler_params=pltpu.CompilerParams(vmem_limit_bytes=VMEM_BYTES),
        cost_estimate=pl.CostEstimate(
            flops=flops, bytes_accessed=2 * own * WINDOW * rows * sum(counts), transcendentals=0
        ),
        name="bands",
    )(*arguments)


def build_differences(columns, whole_ref, rest_ref, mirrors, samples):
    half = whole_ref.shape[2]
    pupil, depth = 2 * half, whole_ref.shape[3]
    remainder = mirrors * samples - depth
    pick = lax.broadcasted_iota(jnp.int32, (pupil, pupil), 0)
    lane = lax.broadcasted_iota(jnp.int32, (pupil, pupil), 1)
    pick = (lane == pick % half * 2 + pick // half).astype(jnp.float32).astype(jnp.bfloat16)
    lines = jnp.concatenate([ref[:, :pupil] for ref in columns], axis=0)
    height = columns[0].shape[0]
    turned = lax.dot_general(
        pick, lines.astype(jnp.float32).astype(jnp.bfloat16), (((1,), (1,)), ((), ())),
        preferred_element_type=jnp.float32,
    ).astype(jnp.int32)
    at = lax.broadcasted_iota(jnp.int32, (half, mirrors * samples), 1)
    for d in range(len(columns)):
        sides = []
        for side in range(2):
            wanted = None
            for k in range(mirrors):
                column = turned[side * half:(side + 1) * half, d * height + k:d * height + k + 1] + k * samples
                wanted = column if wanted is None else jnp.where(at < k * samples, wanted, column)
            sides.append((at == wanted).astype(jnp.float32))
        across, down = sides[1] - sides[0], sides[1] + sides[0]
        whole_ref[d, 0] = across[:, :depth].astype(jnp.bfloat16)
        whole_ref[d, 1] = down[:, :depth].astype(jnp.bfloat16)
        blank = jnp.zeros((half, remainder), jnp.float32)
        upper = jnp.concatenate([across[:, depth:], blank], axis=1)
        lower = jnp.concatenate([blank, down[:, depth:]], axis=1)
        rest_ref[d] = jnp.concatenate([upper, lower], axis=0).astype(jnp.bfloat16)


def decode_kernel(row_shape, surface_rows, own, staged, norm, counts, late, places, *refs):
    mirrors, shard_rows, slots, samples = row_shape
    whole_ref, rest_ref, *refs = refs
    lines_refs, refs = refs[:counts[0]], refs[counts[0]:]
    late_refs, refs = refs[:counts[1]], refs[counts[1]:]
    ready_refs, refs = refs[:counts[2]], refs[counts[2]:]
    (gram_any, out_ref, gram_ref, decoded, total, lines, foot_rows, scalars, *refs) = refs
    late_blocks, refs = refs[:counts[1]], refs[counts[1]:]
    gram_semaphores, ready_semaphores, late_semaphores, scalar_semaphore = refs
    group = pl.program_id(0)
    directions, pupil = whole_ref.shape[0], 2 * whole_ref.shape[2]
    depth = whole_ref.shape[3]
    phases = out_ref.shape[2] // pupil
    blocks = surface_rows // shard_rows
    ready = blocks - late
    count = shard_rows // 2
    rows = mirrors * shard_rows
    foot_line = mirrors + count

    @pl.when(group == 0)
    def _():
        def started(copies):
            for copy in copies:
                copy.start()
            return copies

        late_copies = started([
            pltpu.make_async_copy(late_refs[n], late_blocks[n], late_semaphores.at[n]) for n in range(counts[1])
        ])
        gram_copies = started(fetch_gram(gram_any, gram_ref, gram_semaphores, mirrors)) if late else []
        ready_copies = started([
            pltpu.make_async_copy(block, decoded.at[pl.ds(n * rows, rows)], ready_semaphores.at[n])
            for n, block in enumerate([ref.at[m] for ref in ready_refs for m in range(ref.shape[0])])
        ])
        held = [ref.at[n] for ref in lines_refs for n in range(ref.shape[0])]
        feet = [None] * blocks
        for place, ref in zip(places, held):
            for d in range(directions):
                lines[place, d * count:(d + 1) * count] = ref[d, mirrors:foot_line, :LANES]
            pieces = [ref[d, foot_line:foot_line + 1, :rows] for d in range(directions)]
            pieces.append(jnp.zeros((1, LANES - rows * directions), jnp.int32))
            feet[place] = jnp.concatenate(pieces, axis=1)
        feet = jnp.concatenate(feet, axis=0)
        foot_rows[...] = row_place(feet // shard_rows, staged) * rows + feet % shard_rows
        to_scalars = pltpu.make_async_copy(foot_rows, scalars, scalar_semaphore.at[0])
        to_scalars.start()
        for copy in late_copies:
            copy.wait()
        for n in range(late):
            source = late_blocks[n]
            for q in range(mirrors * shard_rows):
                if n == 0 and q % shard_rows == 0:
                    gram_copies[q // shard_rows].wait()
                decoded[(ready + n) * rows + q] = band_product(
                    source, q, row_shape, row_block(ready + n, staged), surface_rows, gram_ref
                )
        to_scalars.wait()
        for copy in ready_copies:
            copy.wait()

    for d in range(directions):
        held = d ^ position("dir", staged)
        products, factors = [], []
        for phase in range(phases):
            i = group * phases + phase
            block = row_place(2 * i // shard_rows, staged)
            sums, changes = [], []
            for k in range(mirrors):
                picked = []
                for y in range(2):
                    row = k * shard_rows + (2 * phase + y) % shard_rows
                    picked.append(decoded[scalars[block, held * rows + row] + k * shard_rows])
                sums.append(picked[0] + picked[1])
                changes.append(picked[1] - picked[0])
            right = [jnp.concatenate(part, axis=0) for part in (sums, changes)]
            mixed = jnp.concatenate([part[depth:] for part in right], axis=0)
            rest = jnp.dot(rest_ref[held], mixed, preferred_element_type=jnp.float32)
            for kind, part in enumerate(right):
                whole = jnp.dot(whole_ref[held, kind], part[:depth], preferred_element_type=jnp.float32)
                products.append(whole + rest[kind * pupil // 2:(kind + 1) * pupil // 2])
            valid = lines[block, pl.ds(held * count + phase % count, 1), :][:, :pupil // 2]
            factors += [valid.astype(jnp.float32)] * 2
        product = jnp.concatenate(products, axis=0)
        factor = jnp.concatenate(factors, axis=1)
        for tile in range(out_ref.shape[2] // LANES):
            at = tile * LANES
            value = jnp.transpose((product[at:at + LANES] * norm).astype(jnp.bfloat16))
            value = value.astype(jnp.float32)[:own] * factor[:, at:at + LANES]
            total[tile, pl.ds(d, own, stride=directions), :] = value
    for tile in range(out_ref.shape[2] // LANES):
        value = total[tile].reshape(own, directions, LANES)
        out_ref[:, :, tile * LANES:(tile + 1) * LANES] = value.astype(out_ref.dtype)


def decode(differences, lines, places, late, ready, gram_rows, own, row_shape, surface_rows, pupil, norm, staged):
    mirrors, shard_rows, slots, samples = row_shape
    acts, padded = gram_rows.shape
    directions = differences[0].shape[0]
    blocks = surface_rows // shard_rows
    phases = LANES // math.gcd(pupil, LANES)
    width = surface_rows // 2 * pupil
    lanes = phases * pupil
    flops = 2 * padded * mirrors * samples * pupil * directions * surface_rows // 2
    vmem, anywhere = pl.BlockSpec(memory_space=pltpu.VMEM), pl.BlockSpec(memory_space=pl.ANY)
    counts = (len(lines), len(late), len(ready))
    semaphores = [mirrors, blocks, max(len(late), 1), 1]
    held = -(-directions * (shard_rows // 2) // 8) * 8
    return pl.pallas_call(
        functools.partial(
            decode_kernel, row_shape, surface_rows, own, staged, norm, counts, len(late), places
        ),
        grid=(width // lanes,),
        out_shape=jax.ShapeDtypeStruct((own, directions, width), jnp.bfloat16),
        in_specs=[vmem] * (2 + len(lines)) + [anywhere] * (len(late) + len(ready) + 1),
        out_specs=pl.BlockSpec((own, directions, lanes), lambda s: (0, 0, s)),
        scratch_shapes=[
            pltpu.VMEM((acts, padded), jnp.bfloat16),
            pltpu.VMEM((blocks * mirrors * shard_rows, samples, padded), jnp.bfloat16),
            pltpu.VMEM((lanes // LANES, own * directions, LANES), jnp.float32),
            pltpu.VMEM((blocks, held, LANES), jnp.int32),
            pltpu.VMEM((blocks, LANES), jnp.int32),
            pltpu.SMEM((blocks, LANES), jnp.int32),
            *[pltpu.VMEM(block.shape, block.dtype) for block in late],
            *[pltpu.SemaphoreType.DMA((count,)) for count in semaphores],
        ],
        compiler_params=pltpu.CompilerParams(vmem_limit_bytes=VMEM_BYTES),
        cost_estimate=pl.CostEstimate(flops=flops, bytes_accessed=2 * own * directions * width, transcendentals=0),
        name="decode",
    )(*differences, *lines, *late, *ready, gram_rows)


def swap(block, axis, distance):
    return lax.ppermute(block, axis, [(i, i ^ distance) for i in range(lax.axis_size(axis))])


def turn(block, even, odd):
    return lax.ppermute(
        block, "row", [(i, i ^ (odd if i % 2 else even)) for i in range(lax.axis_size("row"))]
    )


def shards(influence, foot_rows, foot_columns, actuator_codes, poke_rows, subaperture_valid):
    mirrors, shard_rows, samples, slots = influence.shape
    row_shape = (mirrors, shard_rows, slots, samples)
    directions, devices = lax.axis_size("dir"), lax.axis_size("row")
    surface_rows = shard_rows * devices
    pupil = foot_columns.shape[2]
    norm = 0.5 * poke_rows.shape[0] ** (-0.5)
    own = actuator_codes.size // (directions * devices)
    staged = devices == 8 and directions & (directions - 1) == 0
    turned = jnp.swapaxes(influence, 2, 3)
    pokes = poke_rows.reshape(-1, LANES)
    packed, lines = pack(turned, foot_rows, foot_columns, subaperture_valid)
    if not staged:
        every = lax.all_gather(packed, "row")
        lines = lax.all_gather(lax.all_gather(lines, "dir"), "row")
        gram_rows, _ = gram(actuator_codes, pokes, packed, own, row_shape, surface_rows)
        ready, *differences = bands(gram_rows, [every], 0, staged, row_shape, surface_rows, [lines[0]], pupil)
        return decode(
            differences, [lines], list(range(devices)), [], [ready], gram_rows, own, row_shape, surface_rows, pupil,
            norm, staged,
        )

    lines = [lines[None]] + [swap(lines, "dir", e)[None] for e in range(1, directions)]
    first, second = turn(packed, 2, 4), turn(packed, 4, 2)
    sibling = swap(packed, "row", 1)
    held = jnp.concatenate(lines, axis=0)[None]
    gram_rows, own_rows = gram(actuator_codes, pokes, packed, own, row_shape, surface_rows)
    gram_rows, first, second, held = lax.optimization_barrier((gram_rows, first, second, held))
    diagonal = turn(first, 4, 2)
    first_sibling = swap(first, "row", 1)
    mine = [held, turn(held, 2, 4), turn(held, 4, 2), swap(held, "row", 6)]
    sources = [source[None] for source in (sibling, first, second)]
    near, *differences = bands(gram_rows, sources, 1, staged, row_shape, surface_rows, lines, pupil)
    near, second = lax.optimization_barrier((near, second))
    second_sibling = swap(second, "row", 1)
    mine = jnp.concatenate(mine, axis=0)
    near, diagonal, mine = lax.optimization_barrier((near, diagonal, mine))
    theirs = swap(mine, "row", 1)
    late = [first_sibling, second_sibling, diagonal, swap(diagonal, "row", 1)]
    return decode(
        differences, [mine, theirs], [0, 2, 3, 6, 1, 4, 5, 7], late, [own_rows, near], gram_rows, own, row_shape,
        surface_rows, pupil, norm, staged,
    )


def solution(mesh):
    return jax.shard_map(
        shards,
        mesh=mesh,
        in_specs=(
            P(None, "row", None, None),
            P("dir", None, "row"),
            P("dir", None, None),
            P(),
            P(),
            P("dir", "row", None),
        ),
        out_specs=P(("dir", "row"), None, None),
        check_vma=False,
    )
```

```python
import functools
import math

import jax
import jax.numpy as jnp
import numpy as np
from jax import lax
from jax.experimental import pallas as pl
from jax.experimental.pallas import tpu as pltpu
from jax.sharding import PartitionSpec as P

NAR = 48
NA = 48
BAND = 3
REACH = 2
BITS = 13
NARROW = jnp.float8_e4m3fn
LANES = 128
WINDOW = 256
VMEM_BYTES = 127 * 512 * 1024


def parity(codes, rows):
    return lax.population_count(codes & rows) & 1


def narrow_places(q, slots, samples):
    narrow = slots - LANES
    whole = LANES // narrow
    if q < whole:
        return [(0, samples, 0, q * narrow)]
    half = samples // 2
    lane = (q - whole) * narrow
    return [(0, half, samples, lane), (half, half, samples, LANES // 2 + lane)]


def pack_kernel(block_ref, rows_ref, columns_ref, valid_ref, packed_ref, lines_ref):
    mirrors, rows, slots, samples = block_ref.shape
    foot_line = mirrors + valid_ref.shape[1]
    lines_ref[...] = jnp.zeros(lines_ref.shape, lines_ref.dtype)
    lines_ref[mirrors:foot_line, :valid_ref.shape[2]] = valid_ref[0]
    for k in range(mirrors):
        lines_ref[k:k + 1, :columns_ref.shape[2]] = columns_ref[k]
        lines_ref[foot_line:foot_line + 1, k * rows:(k + 1) * rows] = rows_ref[k]
    identity = (
        lax.broadcasted_iota(jnp.int32, (samples, samples), 0) == lax.broadcasted_iota(jnp.int32, (samples, samples), 1)
    ).astype(jnp.float32).astype(jnp.bfloat16)
    wide = mirrors * rows * samples
    tails = {}
    for q in range(mirrors * rows):
        turned = lax.dot_general(
            identity, block_ref[q // rows, q % rows], (((1,), (1,)), ((), ())), preferred_element_type=jnp.float32
        ).astype(jnp.bfloat16)
        packed_ref[pl.ds(q * samples, samples), :] = turned[:, :LANES]
        for start, length, row, lane in narrow_places(q, slots, samples):
            tails.setdefault((row, length), {})[lane] = turned[start:start + length, LANES:]
    for (row, length), pieces in tails.items():
        packed_ref[pl.ds(wide + row, length), :] = jnp.concatenate([pieces[lane] for lane in sorted(pieces)], axis=1)


def pack(block, foot_rows, foot_columns, valid):
    mirrors, rows, slots, samples = block.shape
    vmem = pl.BlockSpec(memory_space=pltpu.VMEM)
    height = mirrors + valid.shape[1] + 1
    return pl.pallas_call(
        pack_kernel,
        out_shape=[
            jax.ShapeDtypeStruct((mirrors * rows * samples * slots // LANES, LANES), block.dtype),
            jax.ShapeDtypeStruct((-(-height // 8) * 8, WINDOW), jnp.int32),
        ],
        in_specs=[vmem] * 4,
        out_specs=[vmem] * 2,
        compiler_params=pltpu.CompilerParams(vmem_limit_bytes=VMEM_BYTES),
        cost_estimate=pl.CostEstimate(flops=0, bytes_accessed=3 * block.size, transcendentals=0),
        name="pack_influence",
    )(block, jnp.swapaxes(foot_rows, 0, 1), jnp.swapaxes(foot_columns, 0, 1), valid)


def column_of(row):
    return jnp.transpose(jnp.broadcast_to(row, (LANES, LANES)), (1, 0))


def own_side_of(table_ref, pokes_ref, codes_ref, words, own_signs, own_sums):
    planes = pokes_ref.shape[0]
    mirrors, rows, columns = table_ref.shape
    for line in range(codes_ref.shape[0]):
        pieces, at = [], line * LANES
        while at < (line + 1) * LANES:
            row, lane = divmod(at, columns)
            length = min(columns - lane, (line + 1) * LANES - at)
            pieces.append(table_ref[row // rows, row % rows:row % rows + 1, lane:lane + length])
            at += length
        codes_ref[line:line + 1, :] = jnp.concatenate(pieces, axis=1)
    half = LANES // 2
    own = own_signs.shape[0]
    plane = lax.broadcasted_iota(jnp.int32, pokes_ref.shape, 0)
    for bit in range(BITS):
        low = jnp.sum((pokes_ref[...] >> bit & 1) << plane, axis=0, keepdims=True)
        word = low | pltpu.roll(jnp.broadcast_to(low, (8, LANES)), half, 1)[:1] << planes
        words[bit] = column_of(word)[:half]
    count = codes_ref.shape[0] * LANES // (lax.axis_size("dir") * lax.axis_size("row"))
    first = (lax.axis_index("dir") * lax.axis_size("row") + lax.axis_index("row")) * count
    lane = lax.broadcasted_iota(jnp.int32, (8, LANES), 1)
    shift = first % LANES
    lines = [
        pltpu.roll(
            jnp.broadcast_to(
                codes_ref[pl.ds(jnp.minimum(first // LANES + n, codes_ref.shape[0] - 1), 1), :], (8, LANES)
            ),
            LANES - shift, 1,
        )
        for n in range(-(-own // LANES) + 1)
    ]
    own_column = jnp.concatenate(
        [column_of(jnp.where(lane < LANES - shift, lines[n], lines[n + 1])[:1]) for n in range(len(lines) - 1)],
        axis=0,
    )[:own]
    total = jnp.zeros((own, LANES), jnp.float32)
    for at in range(planes):
        signs = (1 - 2 * parity(own_column, pokes_ref[at:at + 1, :])).astype(jnp.float32)
        own_signs[:, at * LANES:(at + 1) * LANES] = signs.astype(NARROW)
        total = total + signs
    own_sums[...] = jnp.broadcast_to(jnp.sum(total, axis=1, keepdims=True), own_sums.shape)


def gram_kernel(
    row_shape, surface_rows, table_ref, pokes_ref, packed_ref, gram_out, first_ref, gram_ref, codes_ref, words,
    own_signs, own_sums, semaphores
):
    mirror = pl.program_id(0)
    half = LANES // 2
    own, pokes = own_signs.shape
    planes = pokes // LANES
    lines = codes_ref.shape[0] // row_shape[0]
    height = gram_ref.shape[0] // row_shape[0]

    @pl.when(mirror == 0)
    def _():
        own_side_of(table_ref, pokes_ref, codes_ref, words, own_signs, own_sums)

    def chunk(index, _):
        word = []
        for side in range(WINDOW // LANES):
            line = mirror * lines + index * (WINDOW // LANES) + side
            code = jnp.broadcast_to(codes_ref[pl.ds(line, 1), :], (8, LANES))
            value = None
            for bit in range(BITS):
                mask = jnp.concatenate([code << (31 - bit) >> 31] * (half // 8), axis=0)
                part = words[bit] & mask
                value = part if value is None else value ^ part
            word.append(value)
        word = jnp.concatenate(word, axis=1)
        bits = [None] * (2 * planes)
        for byte in range(0, 2 * planes, 8):
            part = (word >> byte).astype(jnp.int8)
            for bit in range(8):
                at = byte + bit
                hit = (part & np.uint8(1 << bit).astype(np.int8)) != 0
                bits[at % planes * 2 + at // planes] = jnp.where(hit, NARROW(1.0), NARROW(0.0))
        total = jnp.dot(own_signs[...], jnp.concatenate(bits, axis=0), preferred_element_type=jnp.float32)
        sums = jnp.concatenate([own_sums[...]] * (WINDOW // LANES), axis=1)
        turned = jnp.transpose((sums - 2.0 * total).astype(jnp.bfloat16))
        at = pl.multiple_of(mirror * height + index * WINDOW, WINDOW)
        gram_ref[pl.ds(at, WINDOW), :] = turned
        return 0

    lax.fori_loop(0, height // WINDOW, chunk, 0, unroll=3)

    def send(k):
        part = pl.ds(pl.multiple_of(k * height, height), height)
        return pltpu.make_async_copy(gram_ref.at[part], gram_out.at[part], semaphores.at[k])

    send(mirror).start()
    block = lax.axis_index("row")
    for l in range(row_shape[1]):
        for k in range(row_shape[0]):
            @pl.when(mirror == k)
            def _():
                first_ref[0, l] = band_product(
                    packed_ref, k * row_shape[1] + l, row_shape, block, surface_rows, gram_ref
                )

    @pl.when(mirror == pl.num_programs(0) - 1)
    def _():
        for k in range(row_shape[0]):
            send(k).wait()


def gram(table, pokes, packed, own, row_shape, surface_rows):
    own = -(-own // 32) * 32
    acts, count = table.size, pokes.size
    mirrors, shard_rows, slots, samples = row_shape
    vmem = pl.BlockSpec(memory_space=pltpu.VMEM)
    return pl.pallas_call(
        functools.partial(gram_kernel, row_shape, surface_rows),
        grid=(mirrors,),
        out_shape=[
            jax.ShapeDtypeStruct((acts, own), jnp.bfloat16),
            jax.ShapeDtypeStruct((1, mirrors * shard_rows, samples, own), jnp.bfloat16),
        ],
        in_specs=[vmem] * 3,
        out_specs=[
            pl.BlockSpec(memory_space=pl.ANY),
            pl.BlockSpec((1, shard_rows, samples, own), lambda s: (0, s, 0, 0)),
        ],
        scratch_shapes=[
            pltpu.VMEM((acts, own), jnp.bfloat16),
            pltpu.VMEM((acts // LANES, LANES), jnp.int32),
            pltpu.VMEM((BITS, LANES // 2, LANES), jnp.int32),
            pltpu.VMEM((own, count), NARROW),
            pltpu.VMEM((own, LANES), jnp.float32),
            pltpu.SemaphoreType.DMA((mirrors,)),
        ],
        compiler_params=pltpu.CompilerParams(vmem_limit_bytes=VMEM_BYTES),
        cost_estimate=pl.CostEstimate(
            flops=2 * own * acts * count, bytes_accessed=2 * own * acts, transcendentals=0
        ),
        name="gram_rows",
    )(table, pokes, packed)


def position(axis, staged):
    return lax.axis_index(axis) if staged else 0


def row_block(place, staged):
    if not staged:
        return place
    row = lax.axis_index("row")
    core = row & 1
    return row ^ [0, 1, 2 << core, 4 >> core, (4 >> core) | 1, (2 << core) | 1, 6, 7][place]


def row_place(block, staged):
    if not staged:
        return block
    row = lax.axis_index("row")
    core = row & 1
    distance = block ^ row
    near = jnp.where(distance == 2 << core, 2, 3)
    far = jnp.where(distance == (4 >> core) | 1, 4, 5)
    middle = jnp.where(distance & 1 == 0, near, far)
    return jnp.where((distance >= 2) & (distance < 6), middle, distance)


def band_product(source, q, row_shape, block, surface_rows, gram_ref):
    mirrors, shard_rows, slots, samples = row_shape
    own = gram_ref.shape[1]
    narrow = slots - LANES
    k, l = divmod(q, shard_rows)
    band = jnp.clip((block * shard_rows + l) * NAR // surface_rows - 1, 0, NAR - BAND)
    column = pl.multiple_of((k * NAR + band) * NA, 16)
    wide = mirrors * shard_rows * samples
    products = []
    for start, length, row, lane in narrow_places(q, slots, samples):
        left = jnp.concatenate(
            [source[pl.ds(q * samples + start, length), :], source[pl.ds(wide + row, length), :]], axis=1
        )
        right = [gram_ref[pl.ds(column, LANES), :]]
        if lane:
            right.append(jnp.zeros((lane, own), jnp.bfloat16))
        right.append(gram_ref[pl.ds(column + LANES, narrow), :])
        if lane + narrow < LANES:
            right.append(jnp.zeros((LANES - lane - narrow, own), jnp.bfloat16))
        products.append(
            jnp.dot(left, jnp.concatenate(right, axis=0), preferred_element_type=jnp.float32).astype(jnp.bfloat16)
        )
    return jnp.concatenate(products, axis=0)


def fetch_gram(gram_any, gram_ref, semaphores, mirrors):
    height = gram_ref.shape[0] // mirrors
    return [
        pltpu.make_async_copy(
            gram_any.at[pl.ds(k * height, height)], gram_ref.at[pl.ds(k * height, height)], semaphores.at[k]
        )
        for k in range(mirrors)
    ]


def bands_kernel(row_shape, surface_rows, first, counts, staged, gram_any, *refs):
    mirrors, shard_rows, slots, samples = row_shape
    sources = [ref.at[n] for ref, count in zip(refs, counts) for n in range(count)]
    refs = refs[len(counts):]
    *refs, gram_ref, blocks, gram_semaphores, block_semaphores = refs
    if len(refs) > 1:
        *columns_refs, out_ref, whole_ref, rest_ref = refs
    else:
        columns_refs, out_ref = [], refs[0]
    step = pl.program_id(0)
    gram_copies = fetch_gram(gram_any, gram_ref, gram_semaphores, mirrors)

    def fetch(n):
        return pltpu.make_async_copy(sources[n], blocks.at[n], block_semaphores.at[n])

    @pl.when(step == 0)
    def _():
        fetch(0).start()
        for copy in gram_copies:
            copy.start()
        for n in range(1, len(sources)):
            fetch(n).start()
        columns = [ref.at[n] for ref in columns_refs for n in range(ref.shape[0])]
        if columns:
            build_differences(columns, whole_ref, rest_ref, mirrors, samples)

    for n in range(len(sources)):
        @pl.when(step == n)
        def _():
            fetch(n).wait()
            block = row_block(first + n, staged)
            for q in range(mirrors * shard_rows):
                if n == 0 and q % shard_rows == 0:
                    gram_copies[q // shard_rows].wait()
                out_ref[0, q] = band_product(blocks.at[n], q, row_shape, block, surface_rows, gram_ref)


def bands(gram_rows, sources, first, staged, row_shape, surface_rows, columns, pupil):
    acts, own = gram_rows.shape
    mirrors, shard_rows, slots, samples = row_shape
    counts = [source.shape[0] for source in sources]
    rows = mirrors * shard_rows
    flops = 2 * own * WINDOW * samples * rows * sum(counts)
    vmem, anywhere = pl.BlockSpec(memory_space=pltpu.VMEM), pl.BlockSpec(memory_space=pl.ANY)
    out_shape = [jax.ShapeDtypeStruct((sum(counts), rows, samples, own), jnp.bfloat16)]
    out_specs = [pl.BlockSpec((1, rows, samples, own), lambda s: (s, 0, 0, 0))]
    arguments, in_specs = [gram_rows, *sources], [anywhere] * (1 + len(sources))
    directions = sum(lines.shape[0] for lines in columns)
    depth = mirrors * samples // WINDOW * WINDOW
    rest = 2 * (mirrors * samples - depth)
    if columns:
        out_shape += [
            jax.ShapeDtypeStruct((directions, 2, pupil // 2, depth), jnp.bfloat16),
            jax.ShapeDtypeStruct((directions, pupil, rest), jnp.bfloat16),
        ]
        out_specs += [vmem] * 2
    arguments += columns
    in_specs += [vmem] * len(columns)
    return pl.pallas_call(
        functools.partial(bands_kernel, row_shape, surface_rows, first, counts, staged),
        grid=(sum(counts),),
        out_shape=out_shape,
        in_specs=in_specs,
        out_specs=out_specs,
        scratch_shapes=[
            pltpu.VMEM((acts, own), jnp.bfloat16),
            pltpu.VMEM((sum(counts),) + sources[0].shape[1:], jnp.bfloat16),
            pltpu.SemaphoreType.DMA((mirrors,)),
            pltpu.SemaphoreType.DMA((sum(counts),)),
        ],
        compiler_params=pltpu.CompilerParams(vmem_limit_bytes=VMEM_BYTES),
        cost_estimate=pl.CostEstimate(
            flops=flops, bytes_accessed=2 * own * WINDOW * rows * sum(counts), transcendentals=0
        ),
        name="bands",
    )(*arguments)


def build_differences(columns, whole_ref, rest_ref, mirrors, samples):
    half = whole_ref.shape[2]
    pupil, depth = 2 * half, whole_ref.shape[3]
    remainder = mirrors * samples - depth
    pick = lax.broadcasted_iota(jnp.int32, (pupil, pupil), 0)
    lane = lax.broadcasted_iota(jnp.int32, (pupil, pupil), 1)
    pick = (lane == pick % half * 2 + pick // half).astype(jnp.float32).astype(jnp.bfloat16)
    lines = jnp.concatenate([ref[:, :pupil] for ref in columns], axis=0)
    height = columns[0].shape[0]
    turned = lax.dot_general(
        pick, lines.astype(jnp.float32).astype(jnp.bfloat16), (((1,), (1,)), ((), ())),
        preferred_element_type=jnp.float32,
    ).astype(jnp.int32)
    at = lax.broadcasted_iota(jnp.int32, (half, mirrors * samples), 1)
    for d in range(len(columns)):
        sides = []
        for side in range(2):
            wanted = None
            for k in range(mirrors):
                column = turned[side * half:(side + 1) * half, d * height + k:d * height + k + 1] + k * samples
                wanted = column if wanted is None else jnp.where(at < k * samples, wanted, column)
            sides.append((at == wanted).astype(jnp.float32))
        across, down = sides[1] - sides[0], sides[1] + sides[0]
        whole_ref[d, 0] = across[:, :depth].astype(jnp.bfloat16)
        whole_ref[d, 1] = down[:, :depth].astype(jnp.bfloat16)
        blank = jnp.zeros((half, remainder), jnp.float32)
        upper = jnp.concatenate([across[:, depth:], blank], axis=1)
        lower = jnp.concatenate([blank, down[:, depth:]], axis=1)
        rest_ref[d] = jnp.concatenate([upper, lower], axis=0).astype(jnp.bfloat16)


def decode_kernel(row_shape, surface_rows, own, staged, norm, counts, late, places, *refs):
    mirrors, shard_rows, slots, samples = row_shape
    whole_ref, rest_ref, *refs = refs
    lines_refs, refs = refs[:counts[0]], refs[counts[0]:]
    late_refs, refs = refs[:counts[1]], refs[counts[1]:]
    ready_refs, refs = refs[:counts[2]], refs[counts[2]:]
    (gram_any, out_ref, gram_ref, decoded, total, lines, foot_rows, scalars, *refs) = refs
    late_blocks, refs = refs[:counts[1]], refs[counts[1]:]
    gram_semaphores, ready_semaphores, late_semaphores, scalar_semaphore = refs
    group = pl.program_id(0)
    directions, pupil = whole_ref.shape[0], 2 * whole_ref.shape[2]
    depth = whole_ref.shape[3]
    phases = out_ref.shape[2] // pupil
    blocks = surface_rows // shard_rows
    ready = blocks - late
    count = shard_rows // 2
    rows = mirrors * shard_rows
    foot_line = mirrors + count

    @pl.when(group == 0)
    def _():
        def started(copies):
            for copy in copies:
                copy.start()
            return copies

        late_copies = started([
            pltpu.make_async_copy(late_refs[n], late_blocks[n], late_semaphores.at[n]) for n in range(counts[1])
        ])
        gram_copies = started(fetch_gram(gram_any, gram_ref, gram_semaphores, mirrors)) if late else []
        ready_copies = started([
            pltpu.make_async_copy(block, decoded.at[pl.ds(n * rows, rows)], ready_semaphores.at[n])
            for n, block in enumerate([ref.at[m] for ref in ready_refs for m in range(ref.shape[0])])
        ])
        held = [ref.at[n] for ref in lines_refs for n in range(ref.shape[0])]
        feet = [None] * blocks
        for place, ref in zip(places, held):
            for d in range(directions):
                lines[place, d * count:(d + 1) * count] = ref[d, mirrors:foot_line, :LANES]
            pieces = [ref[d, foot_line:foot_line + 1, :rows] for d in range(directions)]
            pieces.append(jnp.zeros((1, LANES - rows * directions), jnp.int32))
            feet[place] = jnp.concatenate(pieces, axis=1)
        feet = jnp.concatenate(feet, axis=0)
        foot_rows[...] = row_place(feet // shard_rows, staged) * rows + feet % shard_rows
        to_scalars = pltpu.make_async_copy(foot_rows, scalars, scalar_semaphore.at[0])
        to_scalars.start()
        for copy in late_copies:
            copy.wait()
        for n in range(late):
            source = late_blocks[n]
            for q in range(mirrors * shard_rows):
                if n == 0 and q % shard_rows == 0:
                    gram_copies[q // shard_rows].wait()
                decoded[(ready + n) * rows + q] = band_product(
                    source, q, row_shape, row_block(ready + n, staged), surface_rows, gram_ref
                )
        to_scalars.wait()
        for copy in ready_copies:
            copy.wait()

    for d in range(directions):
        held = d ^ position("dir", staged)
        products, factors = [], []
        for phase in range(phases):
            i = group * phases + phase
            block = row_place(2 * i // shard_rows, staged)
            sums, changes = [], []
            for k in range(mirrors):
                picked = []
                for y in range(2):
                    row = k * shard_rows + (2 * phase + y) % shard_rows
                    picked.append(decoded[scalars[block, held * rows + row] + k * shard_rows])
                sums.append(picked[0] + picked[1])
                changes.append(picked[1] - picked[0])
            right = [jnp.concatenate(part, axis=0) for part in (sums, changes)]
            mixed = jnp.concatenate([part[depth:] for part in right], axis=0)
            rest = jnp.dot(rest_ref[held], mixed, preferred_element_type=jnp.float32)
            for kind, part in enumerate(right):
                whole = jnp.dot(whole_ref[held, kind], part[:depth], preferred_element_type=jnp.float32)
                products.append(whole + rest[kind * pupil // 2:(kind + 1) * pupil // 2])
            valid = lines[block, pl.ds(held * count + phase % count, 1), :][:, :pupil // 2]
            factors += [valid.astype(jnp.float32)] * 2
        product = jnp.concatenate(products, axis=0)
        factor = jnp.concatenate(factors, axis=1)
        for tile in range(out_ref.shape[2] // LANES):
            at = tile * LANES
            value = jnp.transpose((product[at:at + LANES] * norm).astype(jnp.bfloat16))
            value = value.astype(jnp.float32)[:own] * factor[:, at:at + LANES]
            total[tile, pl.ds(d, own, stride=directions), :] = value
    for tile in range(out_ref.shape[2] // LANES):
        value = total[tile].reshape(own, directions, LANES)
        out_ref[:, :, tile * LANES:(tile + 1) * LANES] = value.astype(out_ref.dtype)


def decode(differences, lines, places, late, ready, gram_rows, own, row_shape, surface_rows, pupil, norm, staged):
    mirrors, shard_rows, slots, samples = row_shape
    acts, padded = gram_rows.shape
    directions = differences[0].shape[0]
    blocks = surface_rows // shard_rows
    phases = LANES // math.gcd(pupil, LANES)
    width = surface_rows // 2 * pupil
    lanes = phases * pupil
    flops = 2 * padded * mirrors * samples * pupil * directions * surface_rows // 2
    vmem, anywhere = pl.BlockSpec(memory_space=pltpu.VMEM), pl.BlockSpec(memory_space=pl.ANY)
    counts = (len(lines), len(late), len(ready))
    semaphores = [mirrors, blocks, max(len(late), 1), 1]
    held = -(-directions * (shard_rows // 2) // 8) * 8
    return pl.pallas_call(
        functools.partial(
            decode_kernel, row_shape, surface_rows, own, staged, norm, counts, len(late), places
        ),
        grid=(width // lanes,),
        out_shape=jax.ShapeDtypeStruct((own, directions, width), jnp.bfloat16),
        in_specs=[vmem] * (2 + len(lines)) + [anywhere] * (len(late) + len(ready) + 1),
        out_specs=pl.BlockSpec((own, directions, lanes), lambda s: (0, 0, s)),
        scratch_shapes=[
            pltpu.VMEM((acts, padded), jnp.bfloat16),
            pltpu.VMEM((blocks * mirrors * shard_rows, samples, padded), jnp.bfloat16),
            pltpu.VMEM((lanes // LANES, own * directions, LANES), jnp.float32),
            pltpu.VMEM((blocks, held, LANES), jnp.int32),
            pltpu.VMEM((blocks, LANES), jnp.int32),
            pltpu.SMEM((blocks, LANES), jnp.int32),
            *[pltpu.VMEM(block.shape, block.dtype) for block in late],
            *[pltpu.SemaphoreType.DMA((count,)) for count in semaphores],
        ],
        compiler_params=pltpu.CompilerParams(vmem_limit_bytes=VMEM_BYTES),
        cost_estimate=pl.CostEstimate(flops=flops, bytes_accessed=2 * own * directions * width, transcendentals=0),
        name="decode",
    )(*differences, *lines, *late, *ready, gram_rows)


def swap(block, axis, distance):
    return lax.ppermute(block, axis, [(i, i ^ distance) for i in range(lax.axis_size(axis))])


def turn(block, even, odd):
    return lax.ppermute(
        block, "row", [(i, i ^ (odd if i % 2 else even)) for i in range(lax.axis_size("row"))]
    )


def shards(influence, foot_rows, foot_columns, actuator_codes, poke_rows, subaperture_valid):
    mirrors, shard_rows, samples, slots = influence.shape
    row_shape = (mirrors, shard_rows, slots, samples)
    directions, devices = lax.axis_size("dir"), lax.axis_size("row")
    surface_rows = shard_rows * devices
    pupil = foot_columns.shape[2]
    norm = 0.5 * poke_rows.shape[0] ** (-0.5)
    own = actuator_codes.size // (directions * devices)
    staged = devices == 8 and directions > 1 and directions & (directions - 1) == 0
    turned = jnp.swapaxes(influence, 2, 3)
    pokes = poke_rows.reshape(-1, LANES)
    packed, lines = pack(turned, foot_rows, foot_columns, subaperture_valid)
    if not staged:
        every = lax.all_gather(packed, "row")
        lines = lax.all_gather(lax.all_gather(lines, "dir"), "row")
        gram_rows, _ = gram(actuator_codes, pokes, packed, own, row_shape, surface_rows)
        ready, *differences = bands(gram_rows, [every], 0, staged, row_shape, surface_rows, [lines[0]], pupil)
        return decode(
            differences, [lines], list(range(devices)), [], [ready], gram_rows, own, row_shape, surface_rows, pupil,
            norm, staged,
        )

    first, second = turn(packed, 2, 4), turn(packed, 4, 2)
    sibling = swap(packed, "row", 1)
    lines, distance = [jnp.stack([lines, swap(lines, "dir", 1)])], 2
    lines[0], pokes = lax.optimization_barrier((lines[0], pokes))
    while distance < directions:
        lines.append(swap(jnp.concatenate(lines, axis=0), "dir", distance))
        distance *= 2
    held = jnp.concatenate(lines, axis=0)[None]
    gram_rows, own_rows = gram(actuator_codes, pokes, packed, own, row_shape, surface_rows)
    gram_rows, first, second, held = lax.optimization_barrier((gram_rows, first, second, held))
    diagonal = turn(first, 4, 2)
    first_sibling = swap(first, "row", 1)
    mine = [held, turn(held, 2, 4), turn(held, 4, 2), swap(held, "row", 6)]
    sources = [source[None] for source in (sibling, first, second)]
    near, *differences = bands(gram_rows, sources, 1, staged, row_shape, surface_rows, lines, pupil)
    near, second = lax.optimization_barrier((near, second))
    second_sibling = swap(second, "row", 1)
    mine = jnp.concatenate(mine, axis=0)
    near, diagonal, mine = lax.optimization_barrier((near, diagonal, mine))
    theirs = swap(mine, "row", 1)
    late = [first_sibling, second_sibling, diagonal, swap(diagonal, "row", 1)]
    return decode(
        differences, [mine, theirs], [0, 2, 3, 6, 1, 4, 5, 7], late, [own_rows, near], gram_rows, own, row_shape,
        surface_rows, pupil, norm, staged,
    )


def solution(mesh):
    return jax.shard_map(
        shards,
        mesh=mesh,
        in_specs=(
            P(None, "row", None, None),
            P("dir", None, "row"),
            P("dir", None, None),
            P(),
            P(),
            P("dir", "row", None),
        ),
        out_specs=P(("dir", "row"), None, None),
        check_vma=False,
    )
```

```python
import functools
import math

import jax
import jax.numpy as jnp
import numpy as np
from jax import lax
from jax.experimental import pallas as pl
from jax.experimental.pallas import tpu as pltpu
from jax.sharding import PartitionSpec as P

NAR = 48
NA = 48
BAND = 3
REACH = 2
BITS = 13
NARROW = jnp.float8_e4m3fn
LANES = 128
WINDOW = 256
VMEM_BYTES = 127 * 512 * 1024


def parity(codes, rows):
    return lax.population_count(codes & rows) & 1


def narrow_places(q, slots, samples):
    narrow = slots - LANES
    whole = LANES // narrow
    if q < whole:
        return [(0, samples, 0, q * narrow)]
    half = samples // 2
    lane = (q - whole) * narrow
    return [(0, half, samples, lane), (half, half, samples, LANES // 2 + lane)]


def pack_kernel(block_ref, rows_ref, columns_ref, valid_ref, packed_ref, lines_ref):
    mirrors, rows, slots, samples = block_ref.shape
    foot_line = mirrors + valid_ref.shape[1]
    lines_ref[...] = jnp.zeros(lines_ref.shape, lines_ref.dtype)
    lines_ref[mirrors:foot_line, :valid_ref.shape[2]] = valid_ref[0]
    for k in range(mirrors):
        lines_ref[k:k + 1, :columns_ref.shape[2]] = columns_ref[k]
        lines_ref[foot_line:foot_line + 1, k * rows:(k + 1) * rows] = rows_ref[k]
    identity = (
        lax.broadcasted_iota(jnp.int32, (samples, samples), 0) == lax.broadcasted_iota(jnp.int32, (samples, samples), 1)
    ).astype(jnp.float32).astype(jnp.bfloat16)
    wide = mirrors * rows * samples
    tails = {}
    for q in range(mirrors * rows):
        turned = lax.dot_general(
            identity, block_ref[q // rows, q % rows], (((1,), (1,)), ((), ())), preferred_element_type=jnp.float32
        ).astype(jnp.bfloat16)
        packed_ref[pl.ds(q * samples, samples), :] = turned[:, :LANES]
        for start, length, row, lane in narrow_places(q, slots, samples):
            tails.setdefault((row, length), {})[lane] = turned[start:start + length, LANES:]
    for (row, length), pieces in tails.items():
        packed_ref[pl.ds(wide + row, length), :] = jnp.concatenate([pieces[lane] for lane in sorted(pieces)], axis=1)


def pack(block, foot_rows, foot_columns, valid):
    mirrors, rows, slots, samples = block.shape
    vmem = pl.BlockSpec(memory_space=pltpu.VMEM)
    height = mirrors + valid.shape[1] + 1
    return pl.pallas_call(
        pack_kernel,
        out_shape=[
            jax.ShapeDtypeStruct((mirrors * rows * samples * slots // LANES, LANES), block.dtype),
            jax.ShapeDtypeStruct((-(-height // 8) * 8, WINDOW), jnp.int32),
        ],
        in_specs=[vmem] * 4,
        out_specs=[vmem] * 2,
        compiler_params=pltpu.CompilerParams(vmem_limit_bytes=VMEM_BYTES),
        cost_estimate=pl.CostEstimate(flops=0, bytes_accessed=3 * block.size, transcendentals=0),
        name="pack_influence",
    )(block, jnp.swapaxes(foot_rows, 0, 1), jnp.swapaxes(foot_columns, 0, 1), valid)


def column_of(row):
    return jnp.transpose(jnp.broadcast_to(row, (LANES, LANES)), (1, 0))


def own_side_of(table_ref, pokes_ref, codes_ref, words, own_signs, own_sums):
    planes = pokes_ref.shape[0]
    mirrors, rows, columns = table_ref.shape
    for line in range(codes_ref.shape[0]):
        pieces, at = [], line * LANES
        while at < (line + 1) * LANES:
            row, lane = divmod(at, columns)
            length = min(columns - lane, (line + 1) * LANES - at)
            pieces.append(table_ref[row // rows, row % rows:row % rows + 1, lane:lane + length])
            at += length
        codes_ref[line:line + 1, :] = jnp.concatenate(pieces, axis=1)
    half = LANES // 2
    own = own_signs.shape[0]
    plane = lax.broadcasted_iota(jnp.int32, pokes_ref.shape, 0)
    for bit in range(BITS):
        low = jnp.sum((pokes_ref[...] >> bit & 1) << plane, axis=0, keepdims=True)
        word = low | pltpu.roll(jnp.broadcast_to(low, (8, LANES)), half, 1)[:1] << planes
        words[bit] = column_of(word)[:half]
    count = codes_ref.shape[0] * LANES // (lax.axis_size("dir") * lax.axis_size("row"))
    first = (lax.axis_index("dir") * lax.axis_size("row") + lax.axis_index("row")) * count
    lane = lax.broadcasted_iota(jnp.int32, (8, LANES), 1)
    shift = first % LANES
    lines = [
        pltpu.roll(
            jnp.broadcast_to(
                codes_ref[pl.ds(jnp.minimum(first // LANES + n, codes_ref.shape[0] - 1), 1), :], (8, LANES)
            ),
            LANES - shift, 1,
        )
        for n in range(-(-own // LANES) + 1)
    ]
    own_column = jnp.concatenate(
        [column_of(jnp.where(lane < LANES - shift, lines[n], lines[n + 1])[:1]) for n in range(len(lines) - 1)],
        axis=0,
    )[:own]
    total = jnp.zeros((own, LANES), jnp.float32)
    for at in range(planes):
        signs = (1 - 2 * parity(own_column, pokes_ref[at:at + 1, :])).astype(jnp.float32)
        own_signs[:, at * LANES:(at + 1) * LANES] = signs.astype(NARROW)
        total = total + signs
    own_sums[...] = jnp.broadcast_to(jnp.sum(total, axis=1, keepdims=True), own_sums.shape)


def gram_kernel(
    row_shape, surface_rows, table_ref, pokes_ref, packed_ref, gram_out, first_ref, gram_ref, codes_ref, words,
    own_signs, own_sums, semaphores
):
    mirror = pl.program_id(0)
    half = LANES // 2
    own, pokes = own_signs.shape
    planes = pokes // LANES
    lines = codes_ref.shape[0] // row_shape[0]
    height = gram_ref.shape[0] // row_shape[0]

    @pl.when(mirror == 0)
    def _():
        own_side_of(table_ref, pokes_ref, codes_ref, words, own_signs, own_sums)

    def chunk(index, _):
        word = []
        for side in range(WINDOW // LANES):
            line = mirror * lines + index * (WINDOW // LANES) + side
            code = jnp.broadcast_to(codes_ref[pl.ds(line, 1), :], (8, LANES))
            value = None
            for bit in range(BITS):
                mask = jnp.concatenate([code << (31 - bit) >> 31] * (half // 8), axis=0)
                part = words[bit] & mask
                value = part if value is None else value ^ part
            word.append(value)
        word = jnp.concatenate(word, axis=1)
        bits = [None] * (2 * planes)
        for byte in range(0, 2 * planes, 8):
            part = (word >> byte).astype(jnp.int8)
            for bit in range(8):
                at = byte + bit
                hit = (part & np.uint8(1 << bit).astype(np.int8)) != 0
                bits[at % planes * 2 + at // planes] = jnp.where(hit, NARROW(1.0), NARROW(0.0))
        total = jnp.dot(own_signs[...], jnp.concatenate(bits, axis=0), preferred_element_type=jnp.float32)
        sums = jnp.concatenate([own_sums[...]] * (WINDOW // LANES), axis=1)
        turned = jnp.transpose((sums - 2.0 * total).astype(jnp.bfloat16))
        at = pl.multiple_of(mirror * height + index * WINDOW, WINDOW)
        gram_ref[pl.ds(at, WINDOW), :] = turned
        return 0

    lax.fori_loop(0, height // WINDOW, chunk, 0, unroll=3)

    def send(k):
        part = pl.ds(pl.multiple_of(k * height, height), height)
        return pltpu.make_async_copy(gram_ref.at[part], gram_out.at[part], semaphores.at[k])

    send(mirror).start()
    block = lax.axis_index("row")
    for l in range(row_shape[1]):
        for k in range(row_shape[0]):
            @pl.when(mirror == k)
            def _():
                first_ref[0, l] = band_product(
                    packed_ref, k * row_shape[1] + l, row_shape, block, surface_rows, gram_ref
                )

    @pl.when(mirror == pl.num_programs(0) - 1)
    def _():
        for k in range(row_shape[0]):
            send(k).wait()


def gram(table, pokes, packed, own, row_shape, surface_rows):
    own = -(-own // 32) * 32
    acts, count = table.size, pokes.size
    mirrors, shard_rows, slots, samples = row_shape
    vmem = pl.BlockSpec(memory_space=pltpu.VMEM)
    return pl.pallas_call(
        functools.partial(gram_kernel, row_shape, surface_rows),
        grid=(mirrors,),
        out_shape=[
            jax.ShapeDtypeStruct((acts, own), jnp.bfloat16),
            jax.ShapeDtypeStruct((1, mirrors * shard_rows, samples, own), jnp.bfloat16),
        ],
        in_specs=[vmem] * 3,
        out_specs=[
            pl.BlockSpec(memory_space=pl.ANY),
            pl.BlockSpec((1, shard_rows, samples, own), lambda s: (0, s, 0, 0)),
        ],
        scratch_shapes=[
            pltpu.VMEM((acts, own), jnp.bfloat16),
            pltpu.VMEM((acts // LANES, LANES), jnp.int32),
            pltpu.VMEM((BITS, LANES // 2, LANES), jnp.int32),
            pltpu.VMEM((own, count), NARROW),
            pltpu.VMEM((own, LANES), jnp.float32),
            pltpu.SemaphoreType.DMA((mirrors,)),
        ],
        compiler_params=pltpu.CompilerParams(vmem_limit_bytes=VMEM_BYTES),
        cost_estimate=pl.CostEstimate(
            flops=2 * own * acts * count, bytes_accessed=2 * own * acts, transcendentals=0
        ),
        name="gram_rows",
    )(table, pokes, packed)


def position(axis, staged):
    return lax.axis_index(axis) if staged else 0


def row_block(place, staged):
    if not staged:
        return place
    row = lax.axis_index("row")
    core = row & 1
    return row ^ [0, 1, 2 << core, 4 >> core, (4 >> core) | 1, (2 << core) | 1, 6, 7][place]


def row_place(block, staged):
    if not staged:
        return block
    row = lax.axis_index("row")
    core = row & 1
    distance = block ^ row
    near = jnp.where(distance == 2 << core, 2, 3)
    far = jnp.where(distance == (4 >> core) | 1, 4, 5)
    middle = jnp.where(distance & 1 == 0, near, far)
    return jnp.where((distance >= 2) & (distance < 6), middle, distance)


def band_product(source, q, row_shape, block, surface_rows, gram_ref):
    mirrors, shard_rows, slots, samples = row_shape
    own = gram_ref.shape[1]
    narrow = slots - LANES
    k, l = divmod(q, shard_rows)
    band = jnp.clip((block * shard_rows + l) * NAR // surface_rows - 1, 0, NAR - BAND)
    column = pl.multiple_of((k * NAR + band) * NA, 16)
    wide = mirrors * shard_rows * samples
    products = []
    for start, length, row, lane in narrow_places(q, slots, samples):
        left = jnp.concatenate(
            [source[pl.ds(q * samples + start, length), :], source[pl.ds(wide + row, length), :]], axis=1
        )
        right = [gram_ref[pl.ds(column, LANES), :]]
        if lane:
            right.append(jnp.zeros((lane, own), jnp.bfloat16))
        right.append(gram_ref[pl.ds(column + LANES, narrow), :])
        if lane + narrow < LANES:
            right.append(jnp.zeros((LANES - lane - narrow, own), jnp.bfloat16))
        products.append(
            jnp.dot(left, jnp.concatenate(right, axis=0), preferred_element_type=jnp.float32).astype(jnp.bfloat16)
        )
    return jnp.concatenate(products, axis=0)


def fetch_gram(gram_any, gram_ref, semaphores, mirrors):
    height = gram_ref.shape[0] // mirrors
    return [
        pltpu.make_async_copy(
            gram_any.at[pl.ds(k * height, height)], gram_ref.at[pl.ds(k * height, height)], semaphores.at[k]
        )
        for k in range(mirrors)
    ]


def bands_kernel(row_shape, surface_rows, first, counts, staged, gram_any, *refs):
    mirrors, shard_rows, slots, samples = row_shape
    sources = [ref.at[n] for ref, count in zip(refs, counts) for n in range(count)]
    refs = refs[len(counts):]
    *refs, gram_ref, blocks, gram_semaphores, block_semaphores = refs
    out_ref, = refs
    step = pl.program_id(0)
    gram_copies = fetch_gram(gram_any, gram_ref, gram_semaphores, mirrors)

    def fetch(n):
        return pltpu.make_async_copy(sources[n], blocks.at[n], block_semaphores.at[n])

    @pl.when(step == 0)
    def _():
        fetch(0).start()
        for copy in gram_copies:
            copy.start()
        for n in range(1, len(sources)):
            fetch(n).start()

    for n in range(len(sources)):
        @pl.when(step == n)
        def _():
            fetch(n).wait()
            block = row_block(first + n, staged)
            for q in range(mirrors * shard_rows):
                if n == 0 and q % shard_rows == 0:
                    gram_copies[q // shard_rows].wait()
                out_ref[0, q] = band_product(blocks.at[n], q, row_shape, block, surface_rows, gram_ref)


def bands(gram_rows, sources, first, staged, row_shape, surface_rows):
    acts, own = gram_rows.shape
    mirrors, shard_rows, slots, samples = row_shape
    counts = [source.shape[0] for source in sources]
    rows = mirrors * shard_rows
    flops = 2 * own * WINDOW * samples * rows * sum(counts)
    vmem, anywhere = pl.BlockSpec(memory_space=pltpu.VMEM), pl.BlockSpec(memory_space=pl.ANY)
    out_shape = [jax.ShapeDtypeStruct((sum(counts), rows, samples, own), jnp.bfloat16)]
    out_specs = [pl.BlockSpec((1, rows, samples, own), lambda s: (s, 0, 0, 0))]
    arguments, in_specs = [gram_rows, *sources], [anywhere] * (1 + len(sources))
    return pl.pallas_call(
        functools.partial(bands_kernel, row_shape, surface_rows, first, counts, staged),
        grid=(sum(counts),),
        out_shape=out_shape,
        in_specs=in_specs,
        out_specs=out_specs,
        scratch_shapes=[
            pltpu.VMEM((acts, own), jnp.bfloat16),
            pltpu.VMEM((sum(counts),) + sources[0].shape[1:], jnp.bfloat16),
            pltpu.SemaphoreType.DMA((mirrors,)),
            pltpu.SemaphoreType.DMA((sum(counts),)),
        ],
        compiler_params=pltpu.CompilerParams(vmem_limit_bytes=VMEM_BYTES),
        cost_estimate=pl.CostEstimate(
            flops=flops, bytes_accessed=2 * own * WINDOW * rows * sum(counts), transcendentals=0
        ),
        name="bands",
    )(*arguments)


def build_differences(columns, whole_ref, rest_ref, mirrors, samples):
    half = whole_ref.shape[2]
    pupil, depth = 2 * half, whole_ref.shape[3]
    remainder = mirrors * samples - depth
    pick = lax.broadcasted_iota(jnp.int32, (pupil, pupil), 0)
    lane = lax.broadcasted_iota(jnp.int32, (pupil, pupil), 1)
    pick = (lane == pick % half * 2 + pick // half).astype(jnp.float32).astype(jnp.bfloat16)
    lines = jnp.concatenate([ref[:, :pupil] for ref in columns], axis=0)
    height = columns[0].shape[0]
    turned = lax.dot_general(
        pick, lines.astype(jnp.float32).astype(jnp.bfloat16), (((1,), (1,)), ((), ())),
        preferred_element_type=jnp.float32,
    ).astype(jnp.int32)
    at = lax.broadcasted_iota(jnp.int32, (half, mirrors * samples), 1)
    for d in range(len(columns)):
        sides = []
        for side in range(2):
            wanted = None
            for k in range(mirrors):
                column = turned[side * half:(side + 1) * half, d * height + k:d * height + k + 1] + k * samples
                wanted = column if wanted is None else jnp.where(at < k * samples, wanted, column)
            sides.append((at == wanted).astype(jnp.float32))
        across, down = sides[1] - sides[0], sides[1] + sides[0]
        whole_ref[d, 0] = across[:, :depth].astype(jnp.bfloat16)
        whole_ref[d, 1] = down[:, :depth].astype(jnp.bfloat16)
        blank = jnp.zeros((half, remainder), jnp.float32)
        upper = jnp.concatenate([across[:, depth:], blank], axis=1)
        lower = jnp.concatenate([blank, down[:, depth:]], axis=1)
        rest_ref[d] = jnp.concatenate([upper, lower], axis=0).astype(jnp.bfloat16)


def decode_kernel(row_shape, surface_rows, own, staged, norm, counts, late, places, *refs):
    mirrors, shard_rows, slots, samples = row_shape
    columns_refs, refs = refs[:counts[3]], refs[counts[3]:]
    lines_refs, refs = refs[:counts[0]], refs[counts[0]:]
    late_refs, refs = refs[:counts[1]], refs[counts[1]:]
    ready_refs, refs = refs[:counts[2]], refs[counts[2]:]
    (gram_any, out_ref, gram_ref, decoded, whole_ref, rest_ref, total, lines, foot_rows, scalars, *refs) = refs
    late_blocks, refs = refs[:counts[1]], refs[counts[1]:]
    gram_semaphores, ready_semaphores, late_semaphores, scalar_semaphore = refs
    group = pl.program_id(0)
    directions, pupil = whole_ref.shape[0], 2 * whole_ref.shape[2]
    depth = whole_ref.shape[3]
    phases = out_ref.shape[2] // pupil
    blocks = surface_rows // shard_rows
    ready = blocks - late
    count = shard_rows // 2
    rows = mirrors * shard_rows
    foot_line = mirrors + count

    @pl.when(group == 0)
    def _():
        def started(copies):
            for copy in copies:
                copy.start()
            return copies

        late_copies = started([
            pltpu.make_async_copy(late_refs[n], late_blocks[n], late_semaphores.at[n]) for n in range(counts[1])
        ])
        gram_copies = started(fetch_gram(gram_any, gram_ref, gram_semaphores, mirrors)) if late else []
        ready_copies = started([
            pltpu.make_async_copy(block, decoded.at[pl.ds(n * rows, rows)], ready_semaphores.at[n])
            for n, block in enumerate([ref.at[m] for ref in ready_refs for m in range(ref.shape[0])])
        ])
        held = [ref.at[n] for ref in lines_refs for n in range(ref.shape[0])]
        feet = [None] * blocks
        for place, ref in zip(places, held):
            for d in range(directions):
                lines[place, d * count:(d + 1) * count] = ref[d, mirrors:foot_line, :LANES]
            pieces = [ref[d, foot_line:foot_line + 1, :rows] for d in range(directions)]
            pieces.append(jnp.zeros((1, LANES - rows * directions), jnp.int32))
            feet[place] = jnp.concatenate(pieces, axis=1)
        feet = jnp.concatenate(feet, axis=0)
        foot_rows[...] = row_place(feet // shard_rows, staged) * rows + feet % shard_rows
        to_scalars = pltpu.make_async_copy(foot_rows, scalars, scalar_semaphore.at[0])
        to_scalars.start()
        columns = [ref.at[n] for ref in columns_refs for n in range(ref.shape[0])]
        build_differences(columns, whole_ref, rest_ref, mirrors, samples)
        for copy in late_copies:
            copy.wait()
        for n in range(late):
            source = late_blocks[n]
            for q in range(mirrors * shard_rows):
                if n == 0 and q % shard_rows == 0:
                    gram_copies[q // shard_rows].wait()
                decoded[(ready + n) * rows + q] = band_product(
                    source, q, row_shape, row_block(ready + n, staged), surface_rows, gram_ref
                )
        to_scalars.wait()
        for copy in ready_copies:
            copy.wait()

    for d in range(directions):
        held = d ^ position("dir", staged)
        products, factors = [], []
        for phase in range(phases):
            i = group * phases + phase
            block = row_place(2 * i // shard_rows, staged)
            sums, changes = [], []
            for k in range(mirrors):
                picked = []
                for y in range(2):
                    row = k * shard_rows + (2 * phase + y) % shard_rows
                    picked.append(decoded[scalars[block, held * rows + row] + k * shard_rows])
                sums.append(picked[0] + picked[1])
                changes.append(picked[1] - picked[0])
            right = [jnp.concatenate(part, axis=0) for part in (sums, changes)]
            mixed = jnp.concatenate([part[depth:] for part in right], axis=0)
            rest = jnp.dot(rest_ref[held], mixed, preferred_element_type=jnp.float32)
            for kind, part in enumerate(right):
                whole = jnp.dot(whole_ref[held, kind], part[:depth], preferred_element_type=jnp.float32)
                products.append(whole + rest[kind * pupil // 2:(kind + 1) * pupil // 2])
            valid = lines[block, pl.ds(held * count + phase % count, 1), :][:, :pupil // 2]
            factors += [valid.astype(jnp.float32)] * 2
        product = jnp.concatenate(products, axis=0)
        factor = jnp.concatenate(factors, axis=1)
        for tile in range(out_ref.shape[2] // LANES):
            at = tile * LANES
            value = jnp.transpose((product[at:at + LANES] * norm).astype(jnp.bfloat16))
            value = value.astype(jnp.float32)[:own] * factor[:, at:at + LANES]
            total[tile, pl.ds(d, own, stride=directions), :] = value
    for tile in range(out_ref.shape[2] // LANES):
        value = total[tile].reshape(own, directions, LANES)
        out_ref[:, :, tile * LANES:(tile + 1) * LANES] = value.astype(out_ref.dtype)


def decode(columns, lines, places, late, ready, gram_rows, own, row_shape, surface_rows, pupil, norm, staged):
    mirrors, shard_rows, slots, samples = row_shape
    acts, padded = gram_rows.shape
    directions = sum(line.shape[0] for line in columns)
    depth = mirrors * samples // WINDOW * WINDOW
    blocks = surface_rows // shard_rows
    phases = LANES // math.gcd(pupil, LANES)
    width = surface_rows // 2 * pupil
    lanes = phases * pupil
    flops = 2 * padded * mirrors * samples * pupil * directions * surface_rows // 2
    vmem, anywhere = pl.BlockSpec(memory_space=pltpu.VMEM), pl.BlockSpec(memory_space=pl.ANY)
    counts = (len(lines), len(late), len(ready), len(columns))
    semaphores = [mirrors, blocks, max(len(late), 1), 1]
    held = -(-directions * (shard_rows // 2) // 8) * 8
    return pl.pallas_call(
        functools.partial(
            decode_kernel, row_shape, surface_rows, own, staged, norm, counts, len(late), places
        ),
        grid=(width // lanes,),
        out_shape=jax.ShapeDtypeStruct((own, directions, width), jnp.bfloat16),
        in_specs=[vmem] * (len(columns) + len(lines)) + [anywhere] * (len(late) + len(ready) + 1),
        out_specs=pl.BlockSpec((own, directions, lanes), lambda s: (0, 0, s)),
        scratch_shapes=[
            pltpu.VMEM((acts, padded), jnp.bfloat16),
            pltpu.VMEM((blocks * mirrors * shard_rows, samples, padded), jnp.bfloat16),
            pltpu.VMEM((directions, 2, pupil // 2, depth), jnp.bfloat16),
            pltpu.VMEM((directions, pupil, 2 * (mirrors * samples - depth)), jnp.bfloat16),
            pltpu.VMEM((lanes // LANES, own * directions, LANES), jnp.float32),
            pltpu.VMEM((blocks, held, LANES), jnp.int32),
            pltpu.VMEM((blocks, LANES), jnp.int32),
            pltpu.SMEM((blocks, LANES), jnp.int32),
            *[pltpu.VMEM(block.shape, block.dtype) for block in late],
            *[pltpu.SemaphoreType.DMA((count,)) for count in semaphores],
        ],
        compiler_params=pltpu.CompilerParams(vmem_limit_bytes=VMEM_BYTES),
        cost_estimate=pl.CostEstimate(flops=flops, bytes_accessed=2 * own * directions * width, transcendentals=0),
        name="decode",
    )(*columns, *lines, *late, *ready, gram_rows)


def swap(block, axis, distance):
    return lax.ppermute(block, axis, [(i, i ^ distance) for i in range(lax.axis_size(axis))])


def turn(block, even, odd):
    return lax.ppermute(
        block, "row", [(i, i ^ (odd if i % 2 else even)) for i in range(lax.axis_size("row"))]
    )


def shards(influence, foot_rows, foot_columns, actuator_codes, poke_rows, subaperture_valid):
    mirrors, shard_rows, samples, slots = influence.shape
    row_shape = (mirrors, shard_rows, slots, samples)
    directions, devices = lax.axis_size("dir"), lax.axis_size("row")
    surface_rows = shard_rows * devices
    pupil = foot_columns.shape[2]
    norm = 0.5 * poke_rows.shape[0] ** (-0.5)
    own = actuator_codes.size // (directions * devices)
    staged = devices == 8 and directions > 1 and directions & (directions - 1) == 0
    turned = jnp.swapaxes(influence, 2, 3)
    pokes = poke_rows.reshape(-1, LANES)
    packed, lines = pack(turned, foot_rows, foot_columns, subaperture_valid)
    if not staged:
        every = lax.all_gather(packed, "row")
        lines = lax.all_gather(lax.all_gather(lines, "dir"), "row")
        gram_rows, _ = gram(actuator_codes, pokes, packed, own, row_shape, surface_rows)
        ready, = bands(gram_rows, [every], 0, staged, row_shape, surface_rows)
        return decode(
            [lines[0]], [lines], list(range(devices)), [], [ready], gram_rows, own, row_shape, surface_rows, pupil,
            norm, staged,
        )

    first, second = turn(packed, 2, 4), turn(packed, 4, 2)
    sibling = swap(packed, "row", 1)
    lines, distance = [jnp.stack([lines, swap(lines, "dir", 1)])], 2
    lines[0], pokes = lax.optimization_barrier((lines[0], pokes))
    while distance < directions:
        lines.append(swap(jnp.concatenate(lines, axis=0), "dir", distance))
        distance *= 2
    held = jnp.concatenate(lines, axis=0)[None, :, :, :LANES]
    gram_rows, own_rows = gram(actuator_codes, pokes, packed, own, row_shape, surface_rows)
    gram_rows, first, second, held = lax.optimization_barrier((gram_rows, first, second, held))
    diagonal = turn(first, 4, 2)
    first_sibling = swap(first, "row", 1)
    mine = [held, turn(held, 2, 4), turn(held, 4, 2), swap(held, "row", 6)]
    sources = [source[None] for source in (sibling, first, second)]
    near, = bands(gram_rows, sources, 1, staged, row_shape, surface_rows)
    near, second = lax.optimization_barrier((near, second))
    second_sibling = swap(second, "row", 1)
    mine = jnp.concatenate(mine, axis=0)
    near, diagonal, mine = lax.optimization_barrier((near, diagonal, mine))
    theirs = swap(mine, "row", 1)
    late = [first_sibling, second_sibling, diagonal, swap(diagonal, "row", 1)]
    return decode(
        lines, [mine, theirs], [0, 2, 3, 6, 1, 4, 5, 7], late, [own_rows, near], gram_rows, own, row_shape,
        surface_rows, pupil, norm, staged,
    )


def solution(mesh):
    return jax.shard_map(
        shards,
        mesh=mesh,
        in_specs=(
            P(None, "row", None, None),
            P("dir", None, "row"),
            P("dir", None, None),
            P(),
            P(),
            P("dir", "row", None),
        ),
        out_specs=P(("dir", "row"), None, None),
        check_vma=False,
    )
```

```python
import functools
import math

import jax
import jax.numpy as jnp
import numpy as np
from jax import lax
from jax.experimental import pallas as pl
from jax.experimental.pallas import tpu as pltpu
from jax.sharding import PartitionSpec as P

NAR = 48
NA = 48
BAND = 3
REACH = 2
BITS = 13
NARROW = jnp.float8_e4m3fn
LANES = 128
WINDOW = 256
VMEM_BYTES = 127 * 512 * 1024


def parity(codes, rows):
    return lax.population_count(codes & rows) & 1


def narrow_places(q, slots, samples):
    narrow = slots - LANES
    whole = LANES // narrow
    if q < whole:
        return [(0, samples, 0, q * narrow)]
    half = samples // 2
    lane = (q - whole) * narrow
    return [(0, half, samples, lane), (half, half, samples, LANES // 2 + lane)]


def pack_kernel(block_ref, rows_ref, columns_ref, valid_ref, packed_ref, lines_ref):
    mirrors, rows, slots, samples = block_ref.shape
    foot_line = mirrors + valid_ref.shape[1]
    lines_ref[...] = jnp.zeros(lines_ref.shape, lines_ref.dtype)
    lines_ref[mirrors:foot_line, :valid_ref.shape[2]] = valid_ref[0]
    for k in range(mirrors):
        lines_ref[k:k + 1, :columns_ref.shape[2]] = columns_ref[k]
        lines_ref[foot_line:foot_line + 1, k * rows:(k + 1) * rows] = rows_ref[k]
    identity = (
        lax.broadcasted_iota(jnp.int32, (samples, samples), 0) == lax.broadcasted_iota(jnp.int32, (samples, samples), 1)
    ).astype(jnp.float32).astype(jnp.bfloat16)
    wide = mirrors * rows * samples
    tails = {}
    for q in range(mirrors * rows):
        turned = lax.dot_general(
            identity, block_ref[q // rows, q % rows], (((1,), (1,)), ((), ())), preferred_element_type=jnp.float32
        ).astype(jnp.bfloat16)
        packed_ref[pl.ds(q * samples, samples), :] = turned[:, :LANES]
        for start, length, row, lane in narrow_places(q, slots, samples):
            tails.setdefault((row, length), {})[lane] = turned[start:start + length, LANES:]
    for (row, length), pieces in tails.items():
        packed_ref[pl.ds(wide + row, length), :] = jnp.concatenate([pieces[lane] for lane in sorted(pieces)], axis=1)


def pack(block, foot_rows, foot_columns, valid):
    mirrors, rows, slots, samples = block.shape
    vmem = pl.BlockSpec(memory_space=pltpu.VMEM)
    height = mirrors + valid.shape[1] + 1
    return pl.pallas_call(
        pack_kernel,
        out_shape=[
            jax.ShapeDtypeStruct((mirrors * rows * samples * slots // LANES, LANES), block.dtype),
            jax.ShapeDtypeStruct((-(-height // 8) * 8, WINDOW), jnp.int32),
        ],
        in_specs=[vmem] * 4,
        out_specs=[vmem] * 2,
        compiler_params=pltpu.CompilerParams(vmem_limit_bytes=VMEM_BYTES),
        cost_estimate=pl.CostEstimate(flops=0, bytes_accessed=3 * block.size, transcendentals=0),
        name="pack_influence",
    )(block, jnp.swapaxes(foot_rows, 0, 1), jnp.swapaxes(foot_columns, 0, 1), valid)


def column_of(row):
    return jnp.transpose(jnp.broadcast_to(row, (LANES, LANES)), (1, 0))


def own_side_of(table_ref, pokes_ref, codes_ref, words, own_signs, own_sums):
    planes = pokes_ref.shape[0]
    mirrors, rows, columns = table_ref.shape
    for line in range(codes_ref.shape[0]):
        pieces, at = [], line * LANES
        while at < (line + 1) * LANES:
            row, lane = divmod(at, columns)
            length = min(columns - lane, (line + 1) * LANES - at)
            pieces.append(table_ref[row // rows, row % rows:row % rows + 1, lane:lane + length])
            at += length
        codes_ref[line:line + 1, :] = jnp.concatenate(pieces, axis=1)
    half = LANES // 2
    own = own_signs.shape[0]
    plane = lax.broadcasted_iota(jnp.int32, pokes_ref.shape, 0)
    for bit in range(BITS):
        low = jnp.sum((pokes_ref[...] >> bit & 1) << plane, axis=0, keepdims=True)
        word = low | pltpu.roll(jnp.broadcast_to(low, (8, LANES)), half, 1)[:1] << planes
        words[bit] = column_of(word)[:half]
    count = codes_ref.shape[0] * LANES // (lax.axis_size("dir") * lax.axis_size("row"))
    first = (lax.axis_index("dir") * lax.axis_size("row") + lax.axis_index("row")) * count
    lane = lax.broadcasted_iota(jnp.int32, (8, LANES), 1)
    shift = first % LANES
    lines = [
        pltpu.roll(
            jnp.broadcast_to(
                codes_ref[pl.ds(jnp.minimum(first // LANES + n, codes_ref.shape[0] - 1), 1), :], (8, LANES)
            ),
            LANES - shift, 1,
        )
        for n in range(-(-own // LANES) + 1)
    ]
    own_column = jnp.concatenate(
        [column_of(jnp.where(lane < LANES - shift, lines[n], lines[n + 1])[:1]) for n in range(len(lines) - 1)],
        axis=0,
    )[:own]
    total = jnp.zeros((own, LANES), jnp.float32)
    for at in range(planes):
        signs = (1 - 2 * parity(own_column, pokes_ref[at:at + 1, :])).astype(jnp.float32)
        own_signs[:, at * LANES:(at + 1) * LANES] = signs.astype(NARROW)
        total = total + signs
    own_sums[...] = jnp.broadcast_to(jnp.sum(total, axis=1, keepdims=True), own_sums.shape)


def gram_kernel(
    row_shape, surface_rows, table_ref, pokes_ref, packed_ref, gram_out, first_ref, gram_ref, codes_ref, words,
    own_signs, own_sums, semaphores
):
    mirror = pl.program_id(0)
    half = LANES // 2
    own, pokes = own_signs.shape
    planes = pokes // LANES
    lines = codes_ref.shape[0] // row_shape[0]
    height = gram_ref.shape[0] // row_shape[0]

    @pl.when(mirror == 0)
    def _():
        own_side_of(table_ref, pokes_ref, codes_ref, words, own_signs, own_sums)

    def chunk(index, _):
        word = []
        for side in range(WINDOW // LANES):
            line = mirror * lines + index * (WINDOW // LANES) + side
            code = jnp.broadcast_to(codes_ref[pl.ds(line, 1), :], (8, LANES))
            value = None
            for bit in range(BITS):
                mask = jnp.concatenate([code << (31 - bit) >> 31] * (half // 8), axis=0)
                part = words[bit] & mask
                value = part if value is None else value ^ part
            word.append(value)
        word = jnp.concatenate(word, axis=1)
        bits = [None] * (2 * planes)
        for byte in range(0, 2 * planes, 8):
            part = (word >> byte).astype(jnp.int8)
            for bit in range(8):
                at = byte + bit
                hit = (part & np.uint8(1 << bit).astype(np.int8)) != 0
                bits[at % planes * 2 + at // planes] = jnp.where(hit, NARROW(1.0), NARROW(0.0))
        total = jnp.dot(own_signs[...], jnp.concatenate(bits, axis=0), preferred_element_type=jnp.float32)
        sums = jnp.concatenate([own_sums[...]] * (WINDOW // LANES), axis=1)
        turned = jnp.transpose((sums - 2.0 * total).astype(jnp.bfloat16))
        at = pl.multiple_of(mirror * height + index * WINDOW, WINDOW)
        gram_ref[pl.ds(at, WINDOW), :] = turned
        return 0

    lax.fori_loop(0, height // WINDOW, chunk, 0, unroll=3)

    def send(k):
        part = pl.ds(pl.multiple_of(k * height, height), height)
        return pltpu.make_async_copy(gram_ref.at[part], gram_out.at[part], semaphores.at[k])

    send(mirror).start()
    block = lax.axis_index("row")
    for l in range(row_shape[1]):
        for k in range(row_shape[0]):
            @pl.when(mirror == k)
            def _():
                first_ref[0, l] = band_product(
                    packed_ref, k * row_shape[1] + l, row_shape, block, surface_rows, gram_ref
                )

    @pl.when(mirror == pl.num_programs(0) - 1)
    def _():
        for k in range(row_shape[0]):
            send(k).wait()


def gram(table, pokes, packed, own, row_shape, surface_rows):
    own = -(-own // 32) * 32
    acts, count = table.size, pokes.size
    mirrors, shard_rows, slots, samples = row_shape
    vmem = pl.BlockSpec(memory_space=pltpu.VMEM)
    return pl.pallas_call(
        functools.partial(gram_kernel, row_shape, surface_rows),
        grid=(mirrors,),
        out_shape=[
            jax.ShapeDtypeStruct((acts, own), jnp.bfloat16),
            jax.ShapeDtypeStruct((1, mirrors * shard_rows, samples, own), jnp.bfloat16),
        ],
        in_specs=[vmem] * 3,
        out_specs=[
            pl.BlockSpec(memory_space=pl.ANY),
            pl.BlockSpec((1, shard_rows, samples, own), lambda s: (0, s, 0, 0)),
        ],
        scratch_shapes=[
            pltpu.VMEM((acts, own), jnp.bfloat16),
            pltpu.VMEM((acts // LANES, LANES), jnp.int32),
            pltpu.VMEM((BITS, LANES // 2, LANES), jnp.int32),
            pltpu.VMEM((own, count), NARROW),
            pltpu.VMEM((own, LANES), jnp.float32),
            pltpu.SemaphoreType.DMA((mirrors,)),
        ],
        compiler_params=pltpu.CompilerParams(vmem_limit_bytes=VMEM_BYTES),
        cost_estimate=pl.CostEstimate(
            flops=2 * own * acts * count, bytes_accessed=2 * own * acts, transcendentals=0
        ),
        name="gram_rows",
    )(table, pokes, packed)


def position(axis, staged):
    return lax.axis_index(axis) if staged else 0


def row_block(place, staged):
    if not staged:
        return place
    row = lax.axis_index("row")
    core = row & 1
    return row ^ [0, 1, 2 << core, 4 >> core, (4 >> core) | 1, (2 << core) | 1, 6, 7][place]


def row_place(block, staged):
    if not staged:
        return block
    row = lax.axis_index("row")
    core = row & 1
    distance = block ^ row
    near = jnp.where(distance == 2 << core, 2, 3)
    far = jnp.where(distance == (4 >> core) | 1, 4, 5)
    middle = jnp.where(distance & 1 == 0, near, far)
    return jnp.where((distance >= 2) & (distance < 6), middle, distance)


def band_product(source, q, row_shape, block, surface_rows, gram_ref):
    mirrors, shard_rows, slots, samples = row_shape
    own = gram_ref.shape[1]
    narrow = slots - LANES
    k, l = divmod(q, shard_rows)
    band = jnp.clip((block * shard_rows + l) * NAR // surface_rows - 1, 0, NAR - BAND)
    column = pl.multiple_of((k * NAR + band) * NA, 16)
    wide = mirrors * shard_rows * samples
    products = []
    for start, length, row, lane in narrow_places(q, slots, samples):
        left = jnp.concatenate(
            [source[pl.ds(q * samples + start, length), :], source[pl.ds(wide + row, length), :]], axis=1
        )
        right = [gram_ref[pl.ds(column, LANES), :]]
        if lane:
            right.append(jnp.zeros((lane, own), jnp.bfloat16))
        right.append(gram_ref[pl.ds(column + LANES, narrow), :])
        if lane + narrow < LANES:
            right.append(jnp.zeros((LANES - lane - narrow, own), jnp.bfloat16))
        products.append(
            jnp.dot(left, jnp.concatenate(right, axis=0), preferred_element_type=jnp.float32).astype(jnp.bfloat16)
        )
    return jnp.concatenate(products, axis=0)


def fetch_gram(gram_any, gram_ref, semaphores, mirrors):
    height = gram_ref.shape[0] // mirrors
    return [
        pltpu.make_async_copy(
            gram_any.at[pl.ds(k * height, height)], gram_ref.at[pl.ds(k * height, height)], semaphores.at[k]
        )
        for k in range(mirrors)
    ]


def bands_kernel(row_shape, surface_rows, first, counts, staged, gram_any, *refs):
    mirrors, shard_rows, slots, samples = row_shape
    sources = [ref.at[n] for ref, count in zip(refs, counts) for n in range(count)]
    refs = refs[len(counts):]
    *refs, gram_ref, blocks, gram_semaphores, block_semaphores = refs
    out_ref, = refs
    step = pl.program_id(0)
    gram_copies = fetch_gram(gram_any, gram_ref, gram_semaphores, mirrors)

    def fetch(n):
        return pltpu.make_async_copy(sources[n], blocks.at[n], block_semaphores.at[n])

    @pl.when(step == 0)
    def _():
        fetch(0).start()
        for copy in gram_copies:
            copy.start()
        for n in range(1, len(sources)):
            fetch(n).start()

    for n in range(len(sources)):
        @pl.when(step == n)
        def _():
            fetch(n).wait()
            block = row_block(first + n, staged)
            for q in range(mirrors * shard_rows):
                if n == 0 and q % shard_rows == 0:
                    gram_copies[q // shard_rows].wait()
                out_ref[0, q] = band_product(blocks.at[n], q, row_shape, block, surface_rows, gram_ref)


def bands(gram_rows, sources, first, staged, row_shape, surface_rows):
    acts, own = gram_rows.shape
    mirrors, shard_rows, slots, samples = row_shape
    counts = [source.shape[0] for source in sources]
    rows = mirrors * shard_rows
    flops = 2 * own * WINDOW * samples * rows * sum(counts)
    vmem, anywhere = pl.BlockSpec(memory_space=pltpu.VMEM), pl.BlockSpec(memory_space=pl.ANY)
    out_shape = [jax.ShapeDtypeStruct((sum(counts), rows, samples, own), jnp.bfloat16)]
    out_specs = [pl.BlockSpec((1, rows, samples, own), lambda s: (s, 0, 0, 0))]
    arguments, in_specs = [gram_rows, *sources], [anywhere] * (1 + len(sources))
    return pl.pallas_call(
        functools.partial(bands_kernel, row_shape, surface_rows, first, counts, staged),
        grid=(sum(counts),),
        out_shape=out_shape,
        in_specs=in_specs,
        out_specs=out_specs,
        scratch_shapes=[
            pltpu.VMEM((acts, own), jnp.bfloat16),
            pltpu.VMEM((sum(counts),) + sources[0].shape[1:], jnp.bfloat16),
            pltpu.SemaphoreType.DMA((mirrors,)),
            pltpu.SemaphoreType.DMA((sum(counts),)),
        ],
        compiler_params=pltpu.CompilerParams(vmem_limit_bytes=VMEM_BYTES),
        cost_estimate=pl.CostEstimate(
            flops=flops, bytes_accessed=2 * own * WINDOW * rows * sum(counts), transcendentals=0
        ),
        name="bands",
    )(*arguments)


def build_differences(columns, whole_ref, rest_ref, mirrors, samples):
    half = whole_ref.shape[2]
    pupil, depth = 2 * half, whole_ref.shape[3]
    remainder = mirrors * samples - depth
    pick = lax.broadcasted_iota(jnp.int32, (pupil, pupil), 0)
    lane = lax.broadcasted_iota(jnp.int32, (pupil, pupil), 1)
    pick = (lane == pick % half * 2 + pick // half).astype(jnp.float32).astype(jnp.bfloat16)
    lines = jnp.concatenate([ref[:, :pupil] for ref in columns], axis=0)
    height = columns[0].shape[0]
    turned = lax.dot_general(
        pick, lines.astype(jnp.float32).astype(jnp.bfloat16), (((1,), (1,)), ((), ())),
        preferred_element_type=jnp.float32,
    ).astype(jnp.int32)
    at = lax.broadcasted_iota(jnp.int32, (half, mirrors * samples), 1)
    for d in range(len(columns)):
        sides = []
        for side in range(2):
            wanted = None
            for k in range(mirrors):
                column = turned[side * half:(side + 1) * half, d * height + k:d * height + k + 1] + k * samples
                wanted = column if wanted is None else jnp.where(at < k * samples, wanted, column)
            sides.append((at == wanted).astype(jnp.float32))
        across, down = sides[1] - sides[0], sides[1] + sides[0]
        whole_ref[d, 0] = across[:, :depth].astype(jnp.bfloat16)
        whole_ref[d, 1] = down[:, :depth].astype(jnp.bfloat16)
        blank = jnp.zeros((half, remainder), jnp.float32)
        upper = jnp.concatenate([across[:, depth:], blank], axis=1)
        lower = jnp.concatenate([blank, down[:, depth:]], axis=1)
        rest_ref[d] = jnp.concatenate([upper, lower], axis=0).astype(jnp.bfloat16)


def decode_kernel(row_shape, surface_rows, own, staged, norm, counts, late, places, *refs):
    mirrors, shard_rows, slots, samples = row_shape
    columns_refs, refs = refs[:counts[3]], refs[counts[3]:]
    lines_refs, refs = refs[:counts[0]], refs[counts[0]:]
    late_refs, refs = refs[:counts[1]], refs[counts[1]:]
    ready_refs, refs = refs[:counts[2]], refs[counts[2]:]
    (gram_any, out_ref, gram_ref, decoded, whole_ref, rest_ref, total, lines, foot_rows, scalars, *refs) = refs
    late_blocks, refs = refs[:counts[1]], refs[counts[1]:]
    gram_semaphores, ready_semaphores, late_semaphores, scalar_semaphore = refs
    group = pl.program_id(0)
    directions, pupil = whole_ref.shape[0], 2 * whole_ref.shape[2]
    depth = whole_ref.shape[3]
    phases = out_ref.shape[2] // pupil
    blocks = surface_rows // shard_rows
    ready = blocks - late
    count = shard_rows // 2
    rows = mirrors * shard_rows
    foot_line = mirrors + count

    @pl.when(group == 0)
    def _():
        def started(copies):
            for copy in copies:
                copy.start()
            return copies

        late_copies = started([
            pltpu.make_async_copy(late_refs[n], late_blocks[n], late_semaphores.at[n]) for n in range(counts[1])
        ])
        gram_copies = started(fetch_gram(gram_any, gram_ref, gram_semaphores, mirrors)) if late else []
        ready_copies = started([
            pltpu.make_async_copy(block, decoded.at[pl.ds(n * rows, rows)], ready_semaphores.at[n])
            for n, block in enumerate([ref.at[m] for ref in ready_refs for m in range(ref.shape[0])])
        ])
        held = [ref.at[n] for ref in lines_refs for n in range(ref.shape[0])]
        feet = [None] * blocks
        for place, ref in zip(places, held):
            for d in range(directions):
                lines[place, d * count:(d + 1) * count] = ref[d, mirrors:foot_line, :LANES]
            pieces = [ref[d, foot_line:foot_line + 1, :rows] for d in range(directions)]
            pieces.append(jnp.zeros((1, LANES - rows * directions), jnp.int32))
            feet[place] = jnp.concatenate(pieces, axis=1)
        feet = jnp.concatenate(feet, axis=0)
        foot_rows[...] = row_place(feet // shard_rows, staged) * rows + feet % shard_rows
        to_scalars = pltpu.make_async_copy(foot_rows, scalars, scalar_semaphore.at[0])
        to_scalars.start()
        columns = [ref.at[n] for ref in columns_refs for n in range(ref.shape[0])]
        build_differences(columns, whole_ref, rest_ref, mirrors, samples)
        for copy in late_copies:
            copy.wait()
        for n in range(late):
            source = late_blocks[n]
            for q in range(mirrors * shard_rows):
                if n == 0 and q % shard_rows == 0:
                    gram_copies[q // shard_rows].wait()
                decoded[(ready + n) * rows + q] = band_product(
                    source, q, row_shape, row_block(ready + n, staged), surface_rows, gram_ref
                )
        to_scalars.wait()
        for copy in ready_copies:
            copy.wait()

    for d in range(directions):
        held = d ^ position("dir", staged)
        products, factors = [], []
        for phase in range(phases):
            i = group * phases + phase
            block = row_place(2 * i // shard_rows, staged)
            sums, changes = [], []
            for k in range(mirrors):
                picked = []
                for y in range(2):
                    row = k * shard_rows + (2 * phase + y) % shard_rows
                    picked.append(decoded[scalars[block, held * rows + row] + k * shard_rows])
                sums.append(picked[0] + picked[1])
                changes.append(picked[1] - picked[0])
            right = [jnp.concatenate(part, axis=0) for part in (sums, changes)]
            mixed = jnp.concatenate([part[depth:] for part in right], axis=0)
            rest = jnp.dot(rest_ref[held], mixed, preferred_element_type=jnp.float32)
            for kind, part in enumerate(right):
                whole = jnp.dot(whole_ref[held, kind], part[:depth], preferred_element_type=jnp.float32)
                products.append(whole + rest[kind * pupil // 2:(kind + 1) * pupil // 2])
            valid = lines[block, pl.ds(held * count + phase % count, 1), :][:, :pupil // 2]
            factors += [valid.astype(jnp.float32)] * 2
        product = jnp.concatenate(products, axis=0)
        factor = jnp.concatenate(factors, axis=1)
        for tile in range(out_ref.shape[2] // LANES):
            at = tile * LANES
            value = jnp.transpose((product[at:at + LANES] * norm).astype(jnp.bfloat16))
            value = value.astype(jnp.float32)[:own] * factor[:, at:at + LANES]
            total[tile, pl.ds(d, own, stride=directions), :] = value
    for tile in range(out_ref.shape[2] // LANES):
        value = total[tile].reshape(own, directions, LANES)
        out_ref[:, :, tile * LANES:(tile + 1) * LANES] = value.astype(out_ref.dtype)


def decode(columns, lines, places, late, ready, gram_rows, own, row_shape, surface_rows, pupil, norm, staged):
    mirrors, shard_rows, slots, samples = row_shape
    acts, padded = gram_rows.shape
    directions = sum(line.shape[0] for line in columns)
    depth = mirrors * samples // WINDOW * WINDOW
    blocks = surface_rows // shard_rows
    phases = LANES // math.gcd(pupil, LANES)
    width = surface_rows // 2 * pupil
    lanes = phases * pupil
    flops = 2 * padded * mirrors * samples * pupil * directions * surface_rows // 2
    vmem, anywhere = pl.BlockSpec(memory_space=pltpu.VMEM), pl.BlockSpec(memory_space=pl.ANY)
    counts = (len(lines), len(late), len(ready), len(columns))
    semaphores = [mirrors, blocks, max(len(late), 1), 1]
    held = -(-directions * (shard_rows // 2) // 8) * 8
    return pl.pallas_call(
        functools.partial(
            decode_kernel, row_shape, surface_rows, own, staged, norm, counts, len(late), places
        ),
        grid=(width // lanes,),
        out_shape=jax.ShapeDtypeStruct((own, directions, width), jnp.bfloat16),
        in_specs=[vmem] * (len(columns) + len(lines)) + [anywhere] * (len(late) + len(ready) + 1),
        out_specs=pl.BlockSpec((own, directions, lanes), lambda s: (0, 0, s)),
        scratch_shapes=[
            pltpu.VMEM((acts, padded), jnp.bfloat16),
            pltpu.VMEM((blocks * mirrors * shard_rows, samples, padded), jnp.bfloat16),
            pltpu.VMEM((directions, 2, pupil // 2, depth), jnp.bfloat16),
            pltpu.VMEM((directions, pupil, 2 * (mirrors * samples - depth)), jnp.bfloat16),
            pltpu.VMEM((lanes // LANES, own * directions, LANES), jnp.float32),
            pltpu.VMEM((blocks, held, LANES), jnp.int32),
            pltpu.VMEM((blocks, LANES), jnp.int32),
            pltpu.SMEM((blocks, LANES), jnp.int32),
            *[pltpu.VMEM(block.shape, block.dtype) for block in late],
            *[pltpu.SemaphoreType.DMA((count,)) for count in semaphores],
        ],
        compiler_params=pltpu.CompilerParams(vmem_limit_bytes=VMEM_BYTES),
        cost_estimate=pl.CostEstimate(flops=flops, bytes_accessed=2 * own * directions * width, transcendentals=0),
        name="decode",
    )(*columns, *lines, *late, *ready, gram_rows)


def swap(block, axis, distance):
    return lax.ppermute(block, axis, [(i, i ^ distance) for i in range(lax.axis_size(axis))])


def turn(block, even, odd):
    return lax.ppermute(
        block, "row", [(i, i ^ (odd if i % 2 else even)) for i in range(lax.axis_size("row"))]
    )


def shards(influence, foot_rows, foot_columns, actuator_codes, poke_rows, subaperture_valid):
    mirrors, shard_rows, samples, slots = influence.shape
    row_shape = (mirrors, shard_rows, slots, samples)
    directions, devices = lax.axis_size("dir"), lax.axis_size("row")
    surface_rows = shard_rows * devices
    pupil = foot_columns.shape[2]
    norm = 0.5 * poke_rows.shape[0] ** (-0.5)
    own = actuator_codes.size // (directions * devices)
    staged = devices == 8 and directions > 1 and directions & (directions - 1) == 0
    turned = jnp.swapaxes(influence, 2, 3)
    pokes = poke_rows.reshape(-1, LANES)
    packed, lines = pack(turned, foot_rows, foot_columns, subaperture_valid)
    if not staged:
        every = lax.all_gather(packed, "row")
        lines = lax.all_gather(lax.all_gather(lines, "dir"), "row")
        gram_rows, _ = gram(actuator_codes, pokes, packed, own, row_shape, surface_rows)
        ready, = bands(gram_rows, [every], 0, staged, row_shape, surface_rows)
        return decode(
            [lines[0]], [lines], list(range(devices)), [], [ready], gram_rows, own, row_shape, surface_rows, pupil,
            norm, staged,
        )

    first, second = turn(packed, 2, 4), turn(packed, 4, 2)
    lines, distance = [jnp.stack([lines, swap(lines, "dir", 1)])], 2
    lines[0], pokes, again = lax.optimization_barrier((lines[0], pokes, packed))
    sibling = swap(again, "row", 1)
    while distance < directions:
        lines.append(swap(jnp.concatenate(lines, axis=0), "dir", distance))
        distance *= 2
    held = jnp.concatenate(lines, axis=0)[None, :, :, :LANES]
    gram_rows, own_rows = gram(actuator_codes, pokes, packed, own, row_shape, surface_rows)
    gram_rows, first, second, held = lax.optimization_barrier((gram_rows, first, second, held))
    diagonal = turn(first, 4, 2)
    first_sibling, second_sibling = swap(first, "row", 1), swap(second, "row", 1)
    mine = jnp.concatenate([held, turn(held, 2, 4)], axis=0)
    sources = [source[None] for source in (sibling, first, second)]
    near, = bands(gram_rows, sources, 1, staged, row_shape, surface_rows)
    near, mine, first_sibling, second_sibling = lax.optimization_barrier(
        (near, mine, first_sibling, second_sibling)
    )
    mine = jnp.concatenate([mine, turn(mine, 4, 2)], axis=0)
    near, diagonal, mine = lax.optimization_barrier((near, diagonal, mine))
    theirs = swap(mine, "row", 1)
    late = [first_sibling, second_sibling, diagonal, swap(diagonal, "row", 1)]
    return decode(
        lines, [mine, theirs], [0, 2, 3, 6, 1, 4, 5, 7], late, [own_rows, near], gram_rows, own, row_shape,
        surface_rows, pupil, norm, staged,
    )


def solution(mesh):
    return jax.shard_map(
        shards,
        mesh=mesh,
        in_specs=(
            P(None, "row", None, None),
            P("dir", None, "row"),
            P("dir", None, None),
            P(),
            P(),
            P("dir", "row", None),
        ),
        out_specs=P(("dir", "row"), None, None),
        check_vma=False,
    )
```

```python
import functools
import math

import jax
import jax.numpy as jnp
import numpy as np
from jax import lax
from jax.experimental import pallas as pl
from jax.experimental.pallas import tpu as pltpu
from jax.sharding import PartitionSpec as P

NAR = 48
NA = 48
BAND = 3
REACH = 2
BITS = 13
NARROW = jnp.float8_e4m3fn
LANES = 128
WINDOW = 256
VMEM_BYTES = 127 * 512 * 1024


def parity(codes, rows):
    return lax.population_count(codes & rows) & 1


def narrow_places(q, slots, samples):
    narrow = slots - LANES
    whole = LANES // narrow
    if q < whole:
        return [(0, samples, 0, q * narrow)]
    half = samples // 2
    lane = (q - whole) * narrow
    return [(0, half, samples, lane), (half, half, samples, LANES // 2 + lane)]


def pack_kernel(block_ref, rows_ref, columns_ref, valid_ref, packed_ref, lines_ref):
    mirrors, rows, slots, samples = block_ref.shape
    foot_line = mirrors + valid_ref.shape[1]
    lines_ref[...] = jnp.zeros(lines_ref.shape, lines_ref.dtype)
    lines_ref[mirrors:foot_line, :valid_ref.shape[2]] = valid_ref[0]
    for k in range(mirrors):
        lines_ref[k:k + 1, :columns_ref.shape[2]] = columns_ref[k]
        lines_ref[foot_line:foot_line + 1, k * rows:(k + 1) * rows] = rows_ref[k]
    identity = (
        lax.broadcasted_iota(jnp.int32, (samples, samples), 0) == lax.broadcasted_iota(jnp.int32, (samples, samples), 1)
    ).astype(jnp.float32).astype(jnp.bfloat16)
    wide = mirrors * rows * samples
    tails = {}
    for q in range(mirrors * rows):
        turned = lax.dot_general(
            identity, block_ref[q // rows, q % rows], (((1,), (1,)), ((), ())), preferred_element_type=jnp.float32
        ).astype(jnp.bfloat16)
        packed_ref[pl.ds(q * samples, samples), :] = turned[:, :LANES]
        for start, length, row, lane in narrow_places(q, slots, samples):
            tails.setdefault((row, length), {})[lane] = turned[start:start + length, LANES:]
    for (row, length), pieces in tails.items():
        packed_ref[pl.ds(wide + row, length), :] = jnp.concatenate([pieces[lane] for lane in sorted(pieces)], axis=1)


def pack(block, foot_rows, foot_columns, valid):
    mirrors, rows, slots, samples = block.shape
    vmem = pl.BlockSpec(memory_space=pltpu.VMEM)
    height = mirrors + valid.shape[1] + 1
    return pl.pallas_call(
        pack_kernel,
        out_shape=[
            jax.ShapeDtypeStruct((mirrors * rows * samples * slots // LANES, LANES), block.dtype),
            jax.ShapeDtypeStruct((-(-height // 8) * 8, WINDOW), jnp.int32),
        ],
        in_specs=[vmem] * 4,
        out_specs=[vmem] * 2,
        compiler_params=pltpu.CompilerParams(vmem_limit_bytes=VMEM_BYTES),
        cost_estimate=pl.CostEstimate(flops=0, bytes_accessed=3 * block.size, transcendentals=0),
        name="pack_influence",
    )(block, jnp.swapaxes(foot_rows, 0, 1), jnp.swapaxes(foot_columns, 0, 1), valid)


def column_of(row):
    return jnp.transpose(jnp.broadcast_to(row, (LANES, LANES)), (1, 0))


def own_side_of(table_ref, pokes_ref, codes_ref, words, own_signs, own_sums):
    planes = pokes_ref.shape[0]
    mirrors, rows, columns = table_ref.shape
    for line in range(codes_ref.shape[0]):
        pieces, at = [], line * LANES
        while at < (line + 1) * LANES:
            row, lane = divmod(at, columns)
            length = min(columns - lane, (line + 1) * LANES - at)
            pieces.append(table_ref[row // rows, row % rows:row % rows + 1, lane:lane + length])
            at += length
        codes_ref[line:line + 1, :] = jnp.concatenate(pieces, axis=1)
    half = LANES // 2
    own = own_signs.shape[0]
    plane = lax.broadcasted_iota(jnp.int32, pokes_ref.shape, 0)
    for bit in range(BITS):
        low = jnp.sum((pokes_ref[...] >> bit & 1) << plane, axis=0, keepdims=True)
        word = low | pltpu.roll(jnp.broadcast_to(low, (8, LANES)), half, 1)[:1] << planes
        words[bit] = column_of(word)[:half]
    count = codes_ref.shape[0] * LANES // (lax.axis_size("dir") * lax.axis_size("row"))
    first = (lax.axis_index("dir") * lax.axis_size("row") + lax.axis_index("row")) * count
    lane = lax.broadcasted_iota(jnp.int32, (8, LANES), 1)
    shift = first % LANES
    lines = [
        pltpu.roll(
            jnp.broadcast_to(
                codes_ref[pl.ds(jnp.minimum(first // LANES + n, codes_ref.shape[0] - 1), 1), :], (8, LANES)
            ),
            LANES - shift, 1,
        )
        for n in range(-(-own // LANES) + 1)
    ]
    own_column = jnp.concatenate(
        [column_of(jnp.where(lane < LANES - shift, lines[n], lines[n + 1])[:1]) for n in range(len(lines) - 1)],
        axis=0,
    )[:own]
    total = jnp.zeros((own, LANES), jnp.float32)
    for at in range(planes):
        signs = (1 - 2 * parity(own_column, pokes_ref[at:at + 1, :])).astype(jnp.float32)
        own_signs[:, at * LANES:(at + 1) * LANES] = signs.astype(NARROW)
        total = total + signs
    own_sums[...] = jnp.broadcast_to(jnp.sum(total, axis=1, keepdims=True), own_sums.shape)


def gram_kernel(
    row_shape, surface_rows, table_ref, pokes_ref, packed_ref, gram_out, first_ref, gram_ref, codes_ref, words,
    own_signs, own_sums, semaphores
):
    mirror = pl.program_id(0)
    half = LANES // 2
    own, pokes = own_signs.shape
    planes = pokes // LANES
    lines = codes_ref.shape[0] // row_shape[0]
    height = gram_ref.shape[0] // row_shape[0]

    @pl.when(mirror == 0)
    def _():
        own_side_of(table_ref, pokes_ref, codes_ref, words, own_signs, own_sums)

    def chunk(index, _):
        word = []
        for side in range(WINDOW // LANES):
            line = mirror * lines + index * (WINDOW // LANES) + side
            code = jnp.broadcast_to(codes_ref[pl.ds(line, 1), :], (8, LANES))
            value = None
            for bit in range(BITS):
                mask = jnp.concatenate([code << (31 - bit) >> 31] * (half // 8), axis=0)
                part = words[bit] & mask
                value = part if value is None else value ^ part
            word.append(value)
        word = jnp.concatenate(word, axis=1)
        bits = [None] * (2 * planes)
        for byte in range(0, 2 * planes, 8):
            part = (word >> byte).astype(jnp.int8)
            for bit in range(8):
                at = byte + bit
                hit = (part & np.uint8(1 << bit).astype(np.int8)) != 0
                bits[at % planes * 2 + at // planes] = jnp.where(hit, NARROW(1.0), NARROW(0.0))
        total = jnp.dot(own_signs[...], jnp.concatenate(bits, axis=0), preferred_element_type=jnp.float32)
        sums = jnp.concatenate([own_sums[...]] * (WINDOW // LANES), axis=1)
        turned = jnp.transpose((sums - 2.0 * total).astype(jnp.bfloat16))
        at = pl.multiple_of(mirror * height + index * WINDOW, WINDOW)
        gram_ref[pl.ds(at, WINDOW), :] = turned
        return 0

    lax.fori_loop(0, height // WINDOW, chunk, 0, unroll=3)

    def send(k):
        part = pl.ds(pl.multiple_of(k * height, height), height)
        return pltpu.make_async_copy(gram_ref.at[part], gram_out.at[part], semaphores.at[k])

    send(mirror).start()
    block = lax.axis_index("row")
    for l in range(row_shape[1]):
        for k in range(row_shape[0]):
            @pl.when(mirror == k)
            def _():
                first_ref[0, l] = band_product(
                    packed_ref, k * row_shape[1] + l, row_shape, block, surface_rows, gram_ref
                )

    @pl.when(mirror == pl.num_programs(0) - 1)
    def _():
        for k in range(row_shape[0]):
            send(k).wait()


def gram(table, pokes, packed, own, row_shape, surface_rows):
    own = -(-own // 32) * 32
    acts, count = table.size, pokes.size
    mirrors, shard_rows, slots, samples = row_shape
    vmem = pl.BlockSpec(memory_space=pltpu.VMEM)
    return pl.pallas_call(
        functools.partial(gram_kernel, row_shape, surface_rows),
        grid=(mirrors,),
        out_shape=[
            jax.ShapeDtypeStruct((acts, own), jnp.bfloat16),
            jax.ShapeDtypeStruct((1, mirrors * shard_rows, samples, own), jnp.bfloat16),
        ],
        in_specs=[vmem] * 3,
        out_specs=[
            pl.BlockSpec(memory_space=pl.ANY),
            pl.BlockSpec((1, shard_rows, samples, own), lambda s: (0, s, 0, 0)),
        ],
        scratch_shapes=[
            pltpu.VMEM((acts, own), jnp.bfloat16),
            pltpu.VMEM((acts // LANES, LANES), jnp.int32),
            pltpu.VMEM((BITS, LANES // 2, LANES), jnp.int32),
            pltpu.VMEM((own, count), NARROW),
            pltpu.VMEM((own, LANES), jnp.float32),
            pltpu.SemaphoreType.DMA((mirrors,)),
        ],
        compiler_params=pltpu.CompilerParams(vmem_limit_bytes=VMEM_BYTES),
        cost_estimate=pl.CostEstimate(
            flops=2 * own * acts * count, bytes_accessed=2 * own * acts, transcendentals=0
        ),
        name="gram_rows",
    )(table, pokes, packed)


def position(axis, staged):
    return lax.axis_index(axis) if staged else 0


def row_block(place, staged):
    if not staged:
        return place
    row = lax.axis_index("row")
    core = row & 1
    return row ^ [0, 1, 2 << core, 4 >> core, (4 >> core) | 1, (2 << core) | 1, 6, 7][place]


def row_place(block, staged):
    if not staged:
        return block
    row = lax.axis_index("row")
    core = row & 1
    distance = block ^ row
    near = jnp.where(distance == 2 << core, 2, 3)
    far = jnp.where(distance == (4 >> core) | 1, 4, 5)
    middle = jnp.where(distance & 1 == 0, near, far)
    return jnp.where((distance >= 2) & (distance < 6), middle, distance)


def band_product(source, q, row_shape, block, surface_rows, gram_ref):
    mirrors, shard_rows, slots, samples = row_shape
    own = gram_ref.shape[1]
    narrow = slots - LANES
    k, l = divmod(q, shard_rows)
    band = jnp.clip((block * shard_rows + l) * NAR // surface_rows - 1, 0, NAR - BAND)
    column = pl.multiple_of((k * NAR + band) * NA, 16)
    wide = mirrors * shard_rows * samples
    products = []
    for start, length, row, lane in narrow_places(q, slots, samples):
        left = jnp.concatenate(
            [source[pl.ds(q * samples + start, length), :], source[pl.ds(wide + row, length), :]], axis=1
        )
        right = [gram_ref[pl.ds(column, LANES), :]]
        if lane:
            right.append(jnp.zeros((lane, own), jnp.bfloat16))
        right.append(gram_ref[pl.ds(column + LANES, narrow), :])
        if lane + narrow < LANES:
            right.append(jnp.zeros((LANES - lane - narrow, own), jnp.bfloat16))
        products.append(
            jnp.dot(left, jnp.concatenate(right, axis=0), preferred_element_type=jnp.float32).astype(jnp.bfloat16)
        )
    return jnp.concatenate(products, axis=0)


def fetch_gram(gram_any, gram_ref, semaphores, mirrors):
    height = gram_ref.shape[0] // mirrors
    return [
        pltpu.make_async_copy(
            gram_any.at[pl.ds(k * height, height)], gram_ref.at[pl.ds(k * height, height)], semaphores.at[k]
        )
        for k in range(mirrors)
    ]


def bands_kernel(row_shape, surface_rows, first, counts, staged, gram_any, *refs):
    mirrors, shard_rows, slots, samples = row_shape
    sources = [ref.at[n] for ref, count in zip(refs, counts) for n in range(count)]
    refs = refs[len(counts):]
    *refs, gram_ref, blocks, gram_semaphores, block_semaphores = refs
    out_ref, = refs
    step = pl.program_id(0)
    gram_copies = fetch_gram(gram_any, gram_ref, gram_semaphores, mirrors)

    def fetch(n):
        return pltpu.make_async_copy(sources[n], blocks.at[n], block_semaphores.at[n])

    @pl.when(step == 0)
    def _():
        fetch(0).start()
        for copy in gram_copies:
            copy.start()
        for n in range(1, len(sources)):
            fetch(n).start()

    for n in range(len(sources)):
        @pl.when(step == n)
        def _():
            fetch(n).wait()
            block = row_block(first + n, staged)
            for q in range(mirrors * shard_rows):
                if n == 0 and q % shard_rows == 0:
                    gram_copies[q // shard_rows].wait()
                out_ref[0, q] = band_product(blocks.at[n], q, row_shape, block, surface_rows, gram_ref)


def bands(gram_rows, sources, first, staged, row_shape, surface_rows):
    acts, own = gram_rows.shape
    mirrors, shard_rows, slots, samples = row_shape
    counts = [source.shape[0] for source in sources]
    rows = mirrors * shard_rows
    flops = 2 * own * WINDOW * samples * rows * sum(counts)
    vmem, anywhere = pl.BlockSpec(memory_space=pltpu.VMEM), pl.BlockSpec(memory_space=pl.ANY)
    out_shape = [jax.ShapeDtypeStruct((sum(counts), rows, samples, own), jnp.bfloat16)]
    out_specs = [pl.BlockSpec((1, rows, samples, own), lambda s: (s, 0, 0, 0))]
    arguments, in_specs = [gram_rows, *sources], [anywhere] * (1 + len(sources))
    return pl.pallas_call(
        functools.partial(bands_kernel, row_shape, surface_rows, first, counts, staged),
        grid=(sum(counts),),
        out_shape=out_shape,
        in_specs=in_specs,
        out_specs=out_specs,
        scratch_shapes=[
            pltpu.VMEM((acts, own), jnp.bfloat16),
            pltpu.VMEM((sum(counts),) + sources[0].shape[1:], jnp.bfloat16),
            pltpu.SemaphoreType.DMA((mirrors,)),
            pltpu.SemaphoreType.DMA((sum(counts),)),
        ],
        compiler_params=pltpu.CompilerParams(vmem_limit_bytes=VMEM_BYTES),
        cost_estimate=pl.CostEstimate(
            flops=flops, bytes_accessed=2 * own * WINDOW * rows * sum(counts), transcendentals=0
        ),
        name="bands",
    )(*arguments)


def build_differences(columns, whole_ref, rest_ref, mirrors, samples):
    half = whole_ref.shape[2]
    pupil, depth = 2 * half, whole_ref.shape[3]
    remainder = mirrors * samples - depth
    pick = lax.broadcasted_iota(jnp.int32, (pupil, pupil), 0)
    lane = lax.broadcasted_iota(jnp.int32, (pupil, pupil), 1)
    pick = (lane == pick % half * 2 + pick // half).astype(jnp.float32).astype(jnp.bfloat16)
    lines = jnp.concatenate([ref[:, :pupil] for ref in columns], axis=0)
    height = columns[0].shape[0]
    turned = lax.dot_general(
        pick, lines.astype(jnp.float32).astype(jnp.bfloat16), (((1,), (1,)), ((), ())),
        preferred_element_type=jnp.float32,
    ).astype(jnp.int32)
    at = lax.broadcasted_iota(jnp.int32, (half, mirrors * samples), 1)
    for d in range(len(columns)):
        sides = []
        for side in range(2):
            wanted = None
            for k in range(mirrors):
                column = turned[side * half:(side + 1) * half, d * height + k:d * height + k + 1] + k * samples
                wanted = column if wanted is None else jnp.where(at < k * samples, wanted, column)
            sides.append((at == wanted).astype(jnp.float32))
        across, down = sides[1] - sides[0], sides[1] + sides[0]
        whole_ref[d, 0] = across[:, :depth].astype(jnp.bfloat16)
        whole_ref[d, 1] = down[:, :depth].astype(jnp.bfloat16)
        blank = jnp.zeros((half, remainder), jnp.float32)
        upper = jnp.concatenate([across[:, depth:], blank], axis=1)
        lower = jnp.concatenate([blank, down[:, depth:]], axis=1)
        rest_ref[d] = jnp.concatenate([upper, lower], axis=0).astype(jnp.bfloat16)


def decode_kernel(row_shape, surface_rows, own, staged, norm, counts, late, places, *refs):
    mirrors, shard_rows, slots, samples = row_shape
    columns_refs, refs = refs[:counts[3]], refs[counts[3]:]
    lines_refs, refs = refs[:counts[0]], refs[counts[0]:]
    late_refs, refs = refs[:counts[1]], refs[counts[1]:]
    ready_refs, refs = refs[:counts[2]], refs[counts[2]:]
    (gram_any, out_ref, gram_ref, decoded, whole_ref, rest_ref, total, lines, foot_rows, scalars, *refs) = refs
    late_blocks, refs = refs[:counts[1]], refs[counts[1]:]
    gram_semaphores, ready_semaphores, late_semaphores, scalar_semaphore = refs
    group = pl.program_id(0)
    directions, pupil = whole_ref.shape[0], 2 * whole_ref.shape[2]
    depth = whole_ref.shape[3]
    phases = out_ref.shape[2] // pupil
    blocks = surface_rows // shard_rows
    ready = blocks - late
    count = shard_rows // 2
    rows = mirrors * shard_rows
    foot_line = mirrors + count

    @pl.when(group == 0)
    def _():
        def started(copies):
            for copy in copies:
                copy.start()
            return copies

        late_copies = started([
            pltpu.make_async_copy(late_refs[n], late_blocks[n], late_semaphores.at[n]) for n in range(counts[1])
        ])
        gram_copies = started(fetch_gram(gram_any, gram_ref, gram_semaphores, mirrors)) if late else []
        ready_copies = started([
            pltpu.make_async_copy(block, decoded.at[pl.ds(n * rows, rows)], ready_semaphores.at[n])
            for n, block in enumerate([ref.at[m] for ref in ready_refs for m in range(ref.shape[0])])
        ])
        held = [ref.at[n] for ref in lines_refs for n in range(ref.shape[0])]
        feet = [None] * blocks
        for place, ref in zip(places, held):
            for d in range(directions):
                lines[place, d * count:(d + 1) * count] = ref[d, mirrors:foot_line, :LANES]
            pieces = [ref[d, foot_line:foot_line + 1, :rows] for d in range(directions)]
            pieces.append(jnp.zeros((1, LANES - rows * directions), jnp.int32))
            feet[place] = jnp.concatenate(pieces, axis=1)
        feet = jnp.concatenate(feet, axis=0)
        foot_rows[...] = row_place(feet // shard_rows, staged) * rows + feet % shard_rows
        to_scalars = pltpu.make_async_copy(foot_rows, scalars, scalar_semaphore.at[0])
        to_scalars.start()
        columns = [ref.at[n] for ref in columns_refs for n in range(ref.shape[0])]
        build_differences(columns, whole_ref, rest_ref, mirrors, samples)
        for copy in late_copies:
            copy.wait()
        for n in range(late):
            source = late_blocks[n]
            for q in range(mirrors * shard_rows):
                if n == 0 and q % shard_rows == 0:
                    gram_copies[q // shard_rows].wait()
                decoded[(ready + n) * rows + q] = band_product(
                    source, q, row_shape, row_block(ready + n, staged), surface_rows, gram_ref
                )
        to_scalars.wait()
        for copy in ready_copies:
            copy.wait()

    for d in range(directions):
        held = d ^ position("dir", staged)
        products, factors = [], []
        for phase in range(phases):
            i = group * phases + phase
            block = row_place(2 * i // shard_rows, staged)
            sums, changes = [], []
            for k in range(mirrors):
                picked = []
                for y in range(2):
                    row = k * shard_rows + (2 * phase + y) % shard_rows
                    picked.append(decoded[scalars[block, held * rows + row] + k * shard_rows])
                sums.append(picked[0] + picked[1])
                changes.append(picked[1] - picked[0])
            right = [jnp.concatenate(part, axis=0) for part in (sums, changes)]
            mixed = jnp.concatenate([part[depth:] for part in right], axis=0)
            rest = jnp.dot(rest_ref[held], mixed, preferred_element_type=jnp.float32)
            for kind, part in enumerate(right):
                whole = jnp.dot(whole_ref[held, kind], part[:depth], preferred_element_type=jnp.float32)
                products.append(whole + rest[kind * pupil // 2:(kind + 1) * pupil // 2])
            valid = lines[block, pl.ds(held * count + phase % count, 1), :][:, :pupil // 2]
            factors += [valid.astype(jnp.float32)] * 2
        product = jnp.concatenate(products, axis=0)
        factor = jnp.concatenate(factors, axis=1)
        for tile in range(out_ref.shape[2] // LANES):
            at = tile * LANES
            value = jnp.transpose((product[at:at + LANES] * norm).astype(jnp.bfloat16))
            value = value.astype(jnp.float32)[:own] * factor[:, at:at + LANES]
            total[tile, pl.ds(d, own, stride=directions), :] = value
    for tile in range(out_ref.shape[2] // LANES):
        value = total[tile].reshape(own, directions, LANES)
        out_ref[:, :, tile * LANES:(tile + 1) * LANES] = value.astype(out_ref.dtype)


def decode(columns, lines, places, late, ready, gram_rows, own, row_shape, surface_rows, pupil, norm, staged):
    mirrors, shard_rows, slots, samples = row_shape
    acts, padded = gram_rows.shape
    directions = sum(line.shape[0] for line in columns)
    depth = mirrors * samples // WINDOW * WINDOW
    blocks = surface_rows // shard_rows
    phases = LANES // math.gcd(pupil, LANES)
    width = surface_rows // 2 * pupil
    lanes = phases * pupil
    flops = 2 * padded * mirrors * samples * pupil * directions * surface_rows // 2
    vmem, anywhere = pl.BlockSpec(memory_space=pltpu.VMEM), pl.BlockSpec(memory_space=pl.ANY)
    counts = (len(lines), len(late), len(ready), len(columns))
    semaphores = [mirrors, blocks, max(len(late), 1), 1]
    held = -(-directions * (shard_rows // 2) // 8) * 8
    return pl.pallas_call(
        functools.partial(
            decode_kernel, row_shape, surface_rows, own, staged, norm, counts, len(late), places
        ),
        grid=(width // lanes,),
        out_shape=jax.ShapeDtypeStruct((own, directions, width), jnp.bfloat16),
        in_specs=[vmem] * (len(columns) + len(lines)) + [anywhere] * (len(late) + len(ready) + 1),
        out_specs=pl.BlockSpec((own, directions, lanes), lambda s: (0, 0, s)),
        scratch_shapes=[
            pltpu.VMEM((acts, padded), jnp.bfloat16),
            pltpu.VMEM((blocks * mirrors * shard_rows, samples, padded), jnp.bfloat16),
            pltpu.VMEM((directions, 2, pupil // 2, depth), jnp.bfloat16),
            pltpu.VMEM((directions, pupil, 2 * (mirrors * samples - depth)), jnp.bfloat16),
            pltpu.VMEM((lanes // LANES, own * directions, LANES), jnp.float32),
            pltpu.VMEM((blocks, held, LANES), jnp.int32),
            pltpu.VMEM((blocks, LANES), jnp.int32),
            pltpu.SMEM((blocks, LANES), jnp.int32),
            *[pltpu.VMEM(block.shape, block.dtype) for block in late],
            *[pltpu.SemaphoreType.DMA((count,)) for count in semaphores],
        ],
        compiler_params=pltpu.CompilerParams(vmem_limit_bytes=VMEM_BYTES),
        cost_estimate=pl.CostEstimate(flops=flops, bytes_accessed=2 * own * directions * width, transcendentals=0),
        name="decode",
    )(*columns, *lines, *late, *ready, gram_rows)


def swap(block, axis, distance):
    return lax.ppermute(block, axis, [(i, i ^ distance) for i in range(lax.axis_size(axis))])


def turn(block, even, odd):
    return lax.ppermute(
        block, "row", [(i, i ^ (odd if i % 2 else even)) for i in range(lax.axis_size("row"))]
    )


def shards(influence, foot_rows, foot_columns, actuator_codes, poke_rows, subaperture_valid):
    mirrors, shard_rows, samples, slots = influence.shape
    row_shape = (mirrors, shard_rows, slots, samples)
    directions, devices = lax.axis_size("dir"), lax.axis_size("row")
    surface_rows = shard_rows * devices
    pupil = foot_columns.shape[2]
    norm = 0.5 * poke_rows.shape[0] ** (-0.5)
    own = actuator_codes.size // (directions * devices)
    staged = devices == 8 and directions > 1 and directions & (directions - 1) == 0
    turned = jnp.swapaxes(influence, 2, 3)
    pokes = poke_rows.reshape(-1, LANES)
    packed, lines = pack(turned, foot_rows, foot_columns, subaperture_valid)
    if not staged:
        every = lax.all_gather(packed, "row")
        lines = lax.all_gather(lax.all_gather(lines, "dir"), "row")
        gram_rows, _ = gram(actuator_codes, pokes, packed, own, row_shape, surface_rows)
        ready, = bands(gram_rows, [every], 0, staged, row_shape, surface_rows)
        return decode(
            [lines[0]], [lines], list(range(devices)), [], [ready], gram_rows, own, row_shape, surface_rows, pupil,
            norm, staged,
        )

    first, second = turn(packed, 2, 4), turn(packed, 4, 2)
    sibling = swap(packed, "row", 1)
    lines, distance = [jnp.stack([lines, swap(lines, "dir", 1)])], 2
    lines[0], pokes = lax.optimization_barrier((lines[0], pokes))
    while distance < directions:
        lines.append(swap(jnp.concatenate(lines, axis=0), "dir", distance))
        distance *= 2
    held = jnp.concatenate(lines, axis=0)[None, :, :, :LANES]
    gram_rows, own_rows = gram(actuator_codes, pokes, packed, own, row_shape, surface_rows)
    gram_rows, first, second, held = lax.optimization_barrier((gram_rows, first, second, held))
    diagonal = turn(first, 4, 2)
    first_sibling, second_sibling = swap(first, "row", 1), swap(second, "row", 1)
    mine = jnp.concatenate([held, turn(held, 2, 4)], axis=0)
    sources = [source[None] for source in (sibling, first, second)]
    near, = bands(gram_rows, sources, 1, staged, row_shape, surface_rows)
    near, mine, first_sibling, second_sibling = lax.optimization_barrier(
        (near, mine, first_sibling, second_sibling)
    )
    mine = jnp.concatenate([mine, turn(mine, 4, 2)], axis=0)
    near, diagonal, mine = lax.optimization_barrier((near, diagonal, mine))
    theirs = swap(mine, "row", 1)
    late = [first_sibling, second_sibling, diagonal, swap(diagonal, "row", 1)]
    return decode(
        lines, [mine, theirs], [0, 2, 3, 6, 1, 4, 5, 7], late, [own_rows, near], gram_rows, own, row_shape,
        surface_rows, pupil, norm, staged,
    )


def solution(mesh):
    return jax.shard_map(
        shards,
        mesh=mesh,
        in_specs=(
            P(None, "row", None, None),
            P("dir", None, "row"),
            P("dir", None, None),
            P(),
            P(),
            P("dir", "row", None),
        ),
        out_specs=P(("dir", "row"), None, None),
        check_vma=False,
    )
```

```python
import functools
import math

import jax
import jax.numpy as jnp
import numpy as np
from jax import lax
from jax.experimental import pallas as pl
from jax.experimental.pallas import tpu as pltpu
from jax.sharding import PartitionSpec as P

NAR = 48
NA = 48
BAND = 3
REACH = 2
BITS = 13
NARROW = jnp.float8_e4m3fn
LANES = 128
WINDOW = 256
VMEM_BYTES = 127 * 512 * 1024


def parity(codes, rows):
    return lax.population_count(codes & rows) & 1


def narrow_places(q, slots, samples):
    narrow = slots - LANES
    whole = LANES // narrow
    if q < whole:
        return [(0, samples, 0, q * narrow)]
    half = samples // 2
    lane = (q - whole) * narrow
    return [(0, half, samples, lane), (half, half, samples, LANES // 2 + lane)]


def pack_kernel(block_ref, rows_ref, columns_ref, valid_ref, packed_ref, lines_ref):
    mirrors, rows, slots, samples = block_ref.shape
    foot_line = mirrors + valid_ref.shape[1]
    lines_ref[...] = jnp.zeros(lines_ref.shape, lines_ref.dtype)
    lines_ref[mirrors:foot_line, :valid_ref.shape[2]] = valid_ref[0]
    for k in range(mirrors):
        lines_ref[k:k + 1, :columns_ref.shape[2]] = columns_ref[k]
        lines_ref[foot_line:foot_line + 1, k * rows:(k + 1) * rows] = rows_ref[k]
    identity = (
        lax.broadcasted_iota(jnp.int32, (samples, samples), 0) == lax.broadcasted_iota(jnp.int32, (samples, samples), 1)
    ).astype(jnp.float32).astype(jnp.bfloat16)
    wide = mirrors * rows * samples
    tails = {}
    for q in range(mirrors * rows):
        turned = lax.dot_general(
            identity, block_ref[q // rows, q % rows], (((1,), (1,)), ((), ())), preferred_element_type=jnp.float32
        ).astype(jnp.bfloat16)
        packed_ref[pl.ds(q * samples, samples), :] = turned[:, :LANES]
        for start, length, row, lane in narrow_places(q, slots, samples):
            tails.setdefault((row, length), {})[lane] = turned[start:start + length, LANES:]
    for (row, length), pieces in tails.items():
        packed_ref[pl.ds(wide + row, length), :] = jnp.concatenate([pieces[lane] for lane in sorted(pieces)], axis=1)


def pack(block, foot_rows, foot_columns, valid):
    mirrors, rows, slots, samples = block.shape
    vmem = pl.BlockSpec(memory_space=pltpu.VMEM)
    height = mirrors + valid.shape[1] + 1
    return pl.pallas_call(
        pack_kernel,
        out_shape=[
            jax.ShapeDtypeStruct((mirrors * rows * samples * slots // LANES, LANES), block.dtype),
            jax.ShapeDtypeStruct((-(-height // 8) * 8, WINDOW), jnp.int32),
        ],
        in_specs=[vmem] * 4,
        out_specs=[vmem] * 2,
        compiler_params=pltpu.CompilerParams(vmem_limit_bytes=VMEM_BYTES),
        cost_estimate=pl.CostEstimate(flops=0, bytes_accessed=3 * block.size, transcendentals=0),
        name="pack_influence",
    )(block, jnp.swapaxes(foot_rows, 0, 1), jnp.swapaxes(foot_columns, 0, 1), valid)


def column_of(row):
    return jnp.transpose(jnp.broadcast_to(row, (LANES, LANES)), (1, 0))


def own_side_of(table_ref, pokes_ref, codes_ref, words, own_signs, own_sums):
    planes = pokes_ref.shape[0]
    mirrors, rows, columns = table_ref.shape
    for line in range(codes_ref.shape[0]):
        pieces, at = [], line * LANES
        while at < (line + 1) * LANES:
            row, lane = divmod(at, columns)
            length = min(columns - lane, (line + 1) * LANES - at)
            pieces.append(table_ref[row // rows, row % rows:row % rows + 1, lane:lane + length])
            at += length
        codes_ref[line:line + 1, :] = jnp.concatenate(pieces, axis=1)
    half = LANES // 2
    own = own_signs.shape[0]
    plane = lax.broadcasted_iota(jnp.int32, pokes_ref.shape, 0)
    for bit in range(BITS):
        low = jnp.sum((pokes_ref[...] >> bit & 1) << plane, axis=0, keepdims=True)
        word = low | pltpu.roll(jnp.broadcast_to(low, (8, LANES)), half, 1)[:1] << planes
        words[bit] = column_of(word)[:half]
    count = codes_ref.shape[0] * LANES // (lax.axis_size("dir") * lax.axis_size("row"))
    first = (lax.axis_index("dir") * lax.axis_size("row") + lax.axis_index("row")) * count
    lane = lax.broadcasted_iota(jnp.int32, (8, LANES), 1)
    shift = first % LANES
    lines = [
        pltpu.roll(
            jnp.broadcast_to(
                codes_ref[pl.ds(jnp.minimum(first // LANES + n, codes_ref.shape[0] - 1), 1), :], (8, LANES)
            ),
            LANES - shift, 1,
        )
        for n in range(-(-own // LANES) + 1)
    ]
    own_column = jnp.concatenate(
        [column_of(jnp.where(lane < LANES - shift, lines[n], lines[n + 1])[:1]) for n in range(len(lines) - 1)],
        axis=0,
    )[:own]
    total = jnp.zeros((own, LANES), jnp.float32)
    for at in range(planes):
        signs = (1 - 2 * parity(own_column, pokes_ref[at:at + 1, :])).astype(jnp.float32)
        own_signs[:, at * LANES:(at + 1) * LANES] = signs.astype(NARROW)
        total = total + signs
    own_sums[...] = jnp.broadcast_to(jnp.sum(total, axis=1, keepdims=True), own_sums.shape)


def gram_kernel(
    row_shape, surface_rows, table_ref, pokes_ref, packed_ref, gram_out, first_ref, gram_ref, codes_ref, words,
    own_signs, own_sums, semaphores
):
    mirror = pl.program_id(0)
    half = LANES // 2
    own, pokes = own_signs.shape
    planes = pokes // LANES
    lines = codes_ref.shape[0] // row_shape[0]
    height = gram_ref.shape[0] // row_shape[0]

    @pl.when(mirror == 0)
    def _():
        own_side_of(table_ref, pokes_ref, codes_ref, words, own_signs, own_sums)

    def chunk(index, _):
        word = []
        for side in range(WINDOW // LANES):
            line = mirror * lines + index * (WINDOW // LANES) + side
            code = jnp.broadcast_to(codes_ref[pl.ds(line, 1), :], (8, LANES))
            value = None
            for bit in range(BITS):
                mask = jnp.concatenate([code << (31 - bit) >> 31] * (half // 8), axis=0)
                part = words[bit] & mask
                value = part if value is None else value ^ part
            word.append(value)
        word = jnp.concatenate(word, axis=1)
        bits = [None] * (2 * planes)
        for byte in range(0, 2 * planes, 8):
            part = (word >> byte).astype(jnp.int8)
            for bit in range(8):
                at = byte + bit
                hit = (part & np.uint8(1 << bit).astype(np.int8)) != 0
                bits[at % planes * 2 + at // planes] = jnp.where(hit, NARROW(1.0), NARROW(0.0))
        total = jnp.dot(own_signs[...], jnp.concatenate(bits, axis=0), preferred_element_type=jnp.float32)
        sums = jnp.concatenate([own_sums[...]] * (WINDOW // LANES), axis=1)
        turned = jnp.transpose((sums - 2.0 * total).astype(jnp.bfloat16))
        at = pl.multiple_of(mirror * height + index * WINDOW, WINDOW)
        gram_ref[pl.ds(at, WINDOW), :] = turned
        return 0

    lax.fori_loop(0, height // WINDOW, chunk, 0, unroll=3)

    def send(k):
        part = pl.ds(pl.multiple_of(k * height, height), height)
        return pltpu.make_async_copy(gram_ref.at[part], gram_out.at[part], semaphores.at[k])

    send(mirror).start()
    block = lax.axis_index("row")
    for l in range(row_shape[1]):
        for k in range(row_shape[0]):
            @pl.when(mirror == k)
            def _():
                first_ref[0, l] = band_product(
                    packed_ref, k * row_shape[1] + l, row_shape, block, surface_rows, gram_ref
                )

    @pl.when(mirror == pl.num_programs(0) - 1)
    def _():
        for k in range(row_shape[0]):
            send(k).wait()


def gram(table, pokes, packed, own, row_shape, surface_rows):
    own = -(-own // 32) * 32
    acts, count = table.size, pokes.size
    mirrors, shard_rows, slots, samples = row_shape
    vmem = pl.BlockSpec(memory_space=pltpu.VMEM)
    return pl.pallas_call(
        functools.partial(gram_kernel, row_shape, surface_rows),
        grid=(mirrors,),
        out_shape=[
            jax.ShapeDtypeStruct((acts, own), jnp.bfloat16),
            jax.ShapeDtypeStruct((1, mirrors * shard_rows, samples, own), jnp.bfloat16),
        ],
        in_specs=[vmem] * 3,
        out_specs=[
            pl.BlockSpec(memory_space=pl.ANY),
            pl.BlockSpec((1, shard_rows, samples, own), lambda s: (0, s, 0, 0)),
        ],
        scratch_shapes=[
            pltpu.VMEM((acts, own), jnp.bfloat16),
            pltpu.VMEM((acts // LANES, LANES), jnp.int32),
            pltpu.VMEM((BITS, LANES // 2, LANES), jnp.int32),
            pltpu.VMEM((own, count), NARROW),
            pltpu.VMEM((own, LANES), jnp.float32),
            pltpu.SemaphoreType.DMA((mirrors,)),
        ],
        compiler_params=pltpu.CompilerParams(vmem_limit_bytes=VMEM_BYTES),
        cost_estimate=pl.CostEstimate(
            flops=2 * own * acts * count, bytes_accessed=2 * own * acts, transcendentals=0
        ),
        name="gram_rows",
    )(table, pokes, packed)


def position(axis, staged):
    return lax.axis_index(axis) if staged else 0


def row_block(place, staged):
    if not staged:
        return place
    row = lax.axis_index("row")
    core = row & 1
    return row ^ [0, 1, 2 << core, 4 >> core, (4 >> core) | 1, (2 << core) | 1, 6, 7][place]


def row_place(block, staged):
    if not staged:
        return block
    row = lax.axis_index("row")
    core = row & 1
    distance = block ^ row
    near = jnp.where(distance == 2 << core, 2, 3)
    far = jnp.where(distance == (4 >> core) | 1, 4, 5)
    middle = jnp.where(distance & 1 == 0, near, far)
    return jnp.where((distance >= 2) & (distance < 6), middle, distance)


def band_product(source, q, row_shape, block, surface_rows, gram_ref):
    mirrors, shard_rows, slots, samples = row_shape
    own = gram_ref.shape[1]
    narrow = slots - LANES
    k, l = divmod(q, shard_rows)
    band = jnp.clip((block * shard_rows + l) * NAR // surface_rows - 1, 0, NAR - BAND)
    column = pl.multiple_of((k * NAR + band) * NA, 16)
    wide = mirrors * shard_rows * samples
    products = []
    for start, length, row, lane in narrow_places(q, slots, samples):
        left = jnp.concatenate(
            [source[pl.ds(q * samples + start, length), :], source[pl.ds(wide + row, length), :]], axis=1
        )
        right = [gram_ref[pl.ds(column, LANES), :]]
        if lane:
            right.append(jnp.zeros((lane, own), jnp.bfloat16))
        right.append(gram_ref[pl.ds(column + LANES, narrow), :])
        if lane + narrow < LANES:
            right.append(jnp.zeros((LANES - lane - narrow, own), jnp.bfloat16))
        products.append(
            jnp.dot(left, jnp.concatenate(right, axis=0), preferred_element_type=jnp.float32).astype(jnp.bfloat16)
        )
    return jnp.concatenate(products, axis=0)


def fetch_gram(gram_any, gram_ref, semaphores, mirrors):
    height = gram_ref.shape[0] // mirrors
    return [
        pltpu.make_async_copy(
            gram_any.at[pl.ds(k * height, height)], gram_ref.at[pl.ds(k * height, height)], semaphores.at[k]
        )
        for k in range(mirrors)
    ]


def bands_kernel(row_shape, surface_rows, first, counts, staged, gram_any, *refs):
    mirrors, shard_rows, slots, samples = row_shape
    sources = [ref.at[n] for ref, count in zip(refs, counts) for n in range(count)]
    refs = refs[len(counts):]
    *refs, gram_ref, blocks, gram_semaphores, block_semaphores = refs
    out_ref, = refs
    step = pl.program_id(0)
    gram_copies = fetch_gram(gram_any, gram_ref, gram_semaphores, mirrors)

    def fetch(n):
        return pltpu.make_async_copy(sources[n], blocks.at[n], block_semaphores.at[n])

    @pl.when(step == 0)
    def _():
        fetch(0).start()
        for copy in gram_copies:
            copy.start()
        for n in range(1, len(sources)):
            fetch(n).start()

    for n in range(len(sources)):
        @pl.when(step == n)
        def _():
            fetch(n).wait()
            block = row_block(first + n, staged)
            for q in range(mirrors * shard_rows):
                if n == 0 and q % shard_rows == 0:
                    gram_copies[q // shard_rows].wait()
                out_ref[0, q] = band_product(blocks.at[n], q, row_shape, block, surface_rows, gram_ref)


def bands(gram_rows, sources, first, staged, row_shape, surface_rows):
    acts, own = gram_rows.shape
    mirrors, shard_rows, slots, samples = row_shape
    counts = [source.shape[0] for source in sources]
    rows = mirrors * shard_rows
    flops = 2 * own * WINDOW * samples * rows * sum(counts)
    vmem, anywhere = pl.BlockSpec(memory_space=pltpu.VMEM), pl.BlockSpec(memory_space=pl.ANY)
    out_shape = [jax.ShapeDtypeStruct((sum(counts), rows, samples, own), jnp.bfloat16)]
    out_specs = [pl.BlockSpec((1, rows, samples, own), lambda s: (s, 0, 0, 0))]
    arguments, in_specs = [gram_rows, *sources], [anywhere] * (1 + len(sources))
    return pl.pallas_call(
        functools.partial(bands_kernel, row_shape, surface_rows, first, counts, staged),
        grid=(sum(counts),),
        out_shape=out_shape,
        in_specs=in_specs,
        out_specs=out_specs,
        scratch_shapes=[
            pltpu.VMEM((acts, own), jnp.bfloat16),
            pltpu.VMEM((sum(counts),) + sources[0].shape[1:], jnp.bfloat16),
            pltpu.SemaphoreType.DMA((mirrors,)),
            pltpu.SemaphoreType.DMA((sum(counts),)),
        ],
        compiler_params=pltpu.CompilerParams(vmem_limit_bytes=VMEM_BYTES),
        cost_estimate=pl.CostEstimate(
            flops=flops, bytes_accessed=2 * own * WINDOW * rows * sum(counts), transcendentals=0
        ),
        name="bands",
    )(*arguments)


def build_differences(columns, whole_ref, rest_ref, mirrors, samples):
    half = whole_ref.shape[2]
    pupil, depth = 2 * half, whole_ref.shape[3]
    remainder = mirrors * samples - depth
    pick = lax.broadcasted_iota(jnp.int32, (pupil, pupil), 0)
    lane = lax.broadcasted_iota(jnp.int32, (pupil, pupil), 1)
    pick = (lane == pick % half * 2 + pick // half).astype(jnp.float32).astype(jnp.bfloat16)
    lines = jnp.concatenate([ref[:, :pupil] for ref in columns], axis=0)
    height = columns[0].shape[0]
    turned = lax.dot_general(
        pick, lines.astype(jnp.float32).astype(jnp.bfloat16), (((1,), (1,)), ((), ())),
        preferred_element_type=jnp.float32,
    ).astype(jnp.int32)
    at = lax.broadcasted_iota(jnp.int32, (half, mirrors * samples), 1)
    for d in range(len(columns)):
        sides = []
        for side in range(2):
            wanted = None
            for k in range(mirrors):
                column = turned[side * half:(side + 1) * half, d * height + k:d * height + k + 1] + k * samples
                wanted = column if wanted is None else jnp.where(at < k * samples, wanted, column)
            sides.append((at == wanted).astype(jnp.float32))
        across, down = sides[1] - sides[0], sides[1] + sides[0]
        whole_ref[d, 0] = across[:, :depth].astype(jnp.bfloat16)
        whole_ref[d, 1] = down[:, :depth].astype(jnp.bfloat16)
        blank = jnp.zeros((half, remainder), jnp.float32)
        upper = jnp.concatenate([across[:, depth:], blank], axis=1)
        lower = jnp.concatenate([blank, down[:, depth:]], axis=1)
        rest_ref[d] = jnp.concatenate([upper, lower], axis=0).astype(jnp.bfloat16)


def decode_kernel(row_shape, surface_rows, own, staged, norm, counts, late, places, *refs):
    mirrors, shard_rows, slots, samples = row_shape
    columns_refs, refs = refs[:counts[3]], refs[counts[3]:]
    lines_refs, refs = refs[:counts[0]], refs[counts[0]:]
    late_refs, refs = refs[:counts[1]], refs[counts[1]:]
    ready_refs, refs = refs[:counts[2]], refs[counts[2]:]
    (gram_any, out_ref, gram_ref, decoded, whole_ref, rest_ref, total, lines, foot_rows, scalars, *refs) = refs
    late_blocks, refs = refs[:counts[1]], refs[counts[1]:]
    gram_semaphores, ready_semaphores, late_semaphores, scalar_semaphore = refs
    group = pl.program_id(0)
    directions, pupil = whole_ref.shape[0], 2 * whole_ref.shape[2]
    depth = whole_ref.shape[3]
    phases = out_ref.shape[2] // pupil
    blocks = surface_rows // shard_rows
    ready = blocks - late
    count = shard_rows // 2
    rows = mirrors * shard_rows
    foot_line = mirrors + count

    @pl.when(group == 0)
    def _():
        def started(copies):
            for copy in copies:
                copy.start()
            return copies

        late_copies = started([
            pltpu.make_async_copy(late_refs[n], late_blocks[n], late_semaphores.at[n]) for n in range(counts[1])
        ])
        gram_copies = started(fetch_gram(gram_any, gram_ref, gram_semaphores, mirrors)) if late else []
        ready_copies = started([
            pltpu.make_async_copy(block, decoded.at[pl.ds(n * rows, rows)], ready_semaphores.at[n])
            for n, block in enumerate([ref.at[m] for ref in ready_refs for m in range(ref.shape[0])])
        ])
        held = [ref.at[n] for ref in lines_refs for n in range(ref.shape[0])]
        feet = [None] * blocks
        for place, ref in zip(places, held):
            for d in range(directions):
                lines[place, d * count:(d + 1) * count] = ref[d, mirrors:foot_line, :LANES]
            pieces = [ref[d, foot_line:foot_line + 1, :rows] for d in range(directions)]
            pieces.append(jnp.zeros((1, LANES - rows * directions), jnp.int32))
            feet[place] = jnp.concatenate(pieces, axis=1)
        feet = jnp.concatenate(feet, axis=0)
        foot_rows[...] = row_place(feet // shard_rows, staged) * rows + feet % shard_rows
        to_scalars = pltpu.make_async_copy(foot_rows, scalars, scalar_semaphore.at[0])
        to_scalars.start()
        columns = [ref.at[n] for ref in columns_refs for n in range(ref.shape[0])]
        build_differences(columns, whole_ref, rest_ref, mirrors, samples)
        for copy in late_copies:
            copy.wait()
        for n in range(late):
            source = late_blocks[n]
            for q in range(mirrors * shard_rows):
                if n == 0 and q % shard_rows == 0:
                    gram_copies[q // shard_rows].wait()
                decoded[(ready + n) * rows + q] = band_product(
                    source, q, row_shape, row_block(ready + n, staged), surface_rows, gram_ref
                )
        to_scalars.wait()
        for copy in ready_copies:
            copy.wait()

    for d in range(directions):
        held = d ^ position("dir", staged)
        products, factors = [], []
        for phase in range(phases):
            i = group * phases + phase
            block = row_place(2 * i // shard_rows, staged)
            sums, changes = [], []
            for k in range(mirrors):
                picked = []
                for y in range(2):
                    row = k * shard_rows + (2 * phase + y) % shard_rows
                    picked.append(decoded[scalars[block, held * rows + row] + k * shard_rows])
                sums.append(picked[0] + picked[1])
                changes.append(picked[1] - picked[0])
            right = [jnp.concatenate(part, axis=0) for part in (sums, changes)]
            mixed = jnp.concatenate([part[depth:] for part in right], axis=0)
            rest = jnp.dot(rest_ref[held], mixed, preferred_element_type=jnp.float32)
            for kind, part in enumerate(right):
                whole = jnp.dot(whole_ref[held, kind], part[:depth], preferred_element_type=jnp.float32)
                products.append(whole + rest[kind * pupil // 2:(kind + 1) * pupil // 2])
            valid = lines[block, pl.ds(held * count + phase % count, 1), :][:, :pupil // 2]
            factors += [valid.astype(jnp.float32)] * 2
        product = jnp.concatenate(products, axis=0)
        factor = jnp.concatenate(factors, axis=1)
        for tile in range(out_ref.shape[2] // LANES):
            at = tile * LANES
            value = jnp.transpose((product[at:at + LANES] * norm).astype(jnp.bfloat16))
            value = value.astype(jnp.float32)[:own] * factor[:, at:at + LANES]
            total[tile, pl.ds(d, own, stride=directions), :] = value
    for tile in range(out_ref.shape[2] // LANES):
        value = total[tile].reshape(own, directions, LANES)
        out_ref[:, :, tile * LANES:(tile + 1) * LANES] = value.astype(out_ref.dtype)


def decode(columns, lines, places, late, ready, gram_rows, own, row_shape, surface_rows, pupil, norm, staged):
    mirrors, shard_rows, slots, samples = row_shape
    acts, padded = gram_rows.shape
    directions = sum(line.shape[0] for line in columns)
    depth = mirrors * samples // WINDOW * WINDOW
    blocks = surface_rows // shard_rows
    phases = LANES // math.gcd(pupil, LANES)
    width = surface_rows // 2 * pupil
    lanes = phases * pupil
    flops = 2 * padded * mirrors * samples * pupil * directions * surface_rows // 2
    vmem, anywhere = pl.BlockSpec(memory_space=pltpu.VMEM), pl.BlockSpec(memory_space=pl.ANY)
    counts = (len(lines), len(late), len(ready), len(columns))
    semaphores = [mirrors, blocks, max(len(late), 1), 1]
    held = -(-directions * (shard_rows // 2) // 8) * 8
    return pl.pallas_call(
        functools.partial(
            decode_kernel, row_shape, surface_rows, own, staged, norm, counts, len(late), places
        ),
        grid=(width // lanes,),
        out_shape=jax.ShapeDtypeStruct((own, directions, width), jnp.bfloat16),
        in_specs=[vmem] * (len(columns) + len(lines)) + [anywhere] * (len(late) + len(ready) + 1),
        out_specs=pl.BlockSpec((own, directions, lanes), lambda s: (0, 0, s)),
        scratch_shapes=[
            pltpu.VMEM((acts, padded), jnp.bfloat16),
            pltpu.VMEM((blocks * mirrors * shard_rows, samples, padded), jnp.bfloat16),
            pltpu.VMEM((directions, 2, pupil // 2, depth), jnp.bfloat16),
            pltpu.VMEM((directions, pupil, 2 * (mirrors * samples - depth)), jnp.bfloat16),
            pltpu.VMEM((lanes // LANES, own * directions, LANES), jnp.float32),
            pltpu.VMEM((blocks, held, LANES), jnp.int32),
            pltpu.VMEM((blocks, LANES), jnp.int32),
            pltpu.SMEM((blocks, LANES), jnp.int32),
            *[pltpu.VMEM(block.shape, block.dtype) for block in late],
            *[pltpu.SemaphoreType.DMA((count,)) for count in semaphores],
        ],
        compiler_params=pltpu.CompilerParams(vmem_limit_bytes=VMEM_BYTES),
        cost_estimate=pl.CostEstimate(flops=flops, bytes_accessed=2 * own * directions * width, transcendentals=0),
        name="decode",
    )(*columns, *lines, *late, *ready, gram_rows)


def swap(block, axis, distance):
    return lax.ppermute(block, axis, [(i, i ^ distance) for i in range(lax.axis_size(axis))])


def turn(block, even, odd):
    return lax.ppermute(
        block, "row", [(i, i ^ (odd if i % 2 else even)) for i in range(lax.axis_size("row"))]
    )


def shards(influence, foot_rows, foot_columns, actuator_codes, poke_rows, subaperture_valid):
    mirrors, shard_rows, samples, slots = influence.shape
    row_shape = (mirrors, shard_rows, slots, samples)
    directions, devices = lax.axis_size("dir"), lax.axis_size("row")
    surface_rows = shard_rows * devices
    pupil = foot_columns.shape[2]
    norm = 0.5 * poke_rows.shape[0] ** (-0.5)
    own = actuator_codes.size // (directions * devices)
    staged = devices == 8 and directions > 1 and directions & (directions - 1) == 0
    turned = jnp.swapaxes(influence, 2, 3)
    pokes = poke_rows.reshape(-1, LANES)
    packed, lines = pack(turned, foot_rows, foot_columns, subaperture_valid)
    if not staged:
        every = lax.all_gather(packed, "row")
        lines = lax.all_gather(lax.all_gather(lines, "dir"), "row")
        gram_rows, _ = gram(actuator_codes, pokes, packed, own, row_shape, surface_rows)
        ready, = bands(gram_rows, [every], 0, staged, row_shape, surface_rows)
        return decode(
            [lines[0]], [lines], list(range(devices)), [], [ready], gram_rows, own, row_shape, surface_rows, pupil,
            norm, staged,
        )

    first, second = turn(packed, 2, 4), turn(packed, 4, 2)
    sibling = swap(packed, "row", 1)
    lines, distance = [jnp.stack([lines, swap(lines, "dir", 1)])], 2
    lines[0], pokes = lax.optimization_barrier((lines[0], pokes))
    while distance < directions:
        lines.append(swap(jnp.concatenate(lines, axis=0), "dir", distance))
        distance *= 2
    held = jnp.concatenate(lines, axis=0)[None, :, :, :LANES]
    gram_rows, own_rows = gram(actuator_codes, pokes, packed, own, row_shape, surface_rows)
    gram_rows, first, second, held = lax.optimization_barrier((gram_rows, first, second, held))
    diagonal = turn(first, 4, 2)
    mine = [held, turn(held, 2, 4), turn(held, 4, 2), swap(held, "row", 6)]
    sources = [source[None] for source in (sibling, first, second)]
    near, = bands(gram_rows, sources, 1, staged, row_shape, surface_rows)
    near, first, second = lax.optimization_barrier((near, first, second))
    first_sibling, second_sibling = swap(first, "row", 1), swap(second, "row", 1)
    mine = jnp.concatenate(mine, axis=0)
    near, diagonal, mine = lax.optimization_barrier((near, diagonal, mine))
    theirs = swap(mine, "row", 1)
    late = [first_sibling, second_sibling, diagonal, swap(diagonal, "row", 1)]
    return decode(
        lines, [mine, theirs], [0, 2, 3, 6, 1, 4, 5, 7], late, [own_rows, near], gram_rows, own, row_shape,
        surface_rows, pupil, norm, staged,
    )


def solution(mesh):
    return jax.shard_map(
        shards,
        mesh=mesh,
        in_specs=(
            P(None, "row", None, None),
            P("dir", None, "row"),
            P("dir", None, None),
            P(),
            P(),
            P("dir", "row", None),
        ),
        out_specs=P(("dir", "row"), None, None),
        check_vma=False,
    )
```

```python
import functools
import math

import jax
import jax.numpy as jnp
import numpy as np
from jax import lax
from jax.experimental import pallas as pl
from jax.experimental.pallas import tpu as pltpu
from jax.sharding import PartitionSpec as P

NAR = 48
NA = 48
BAND = 3
REACH = 2
BITS = 13
NARROW = jnp.float8_e4m3fn
LANES = 128
WINDOW = 256
VMEM_BYTES = 127 * 512 * 1024


def parity(codes, rows):
    return lax.population_count(codes & rows) & 1


def narrow_places(q, slots, samples):
    narrow = slots - LANES
    whole = LANES // narrow
    if q < whole:
        return [(0, samples, 0, q * narrow)]
    half = samples // 2
    lane = (q - whole) * narrow
    return [(0, half, samples, lane), (half, half, samples, LANES // 2 + lane)]


def pack_kernel(block_ref, rows_ref, columns_ref, valid_ref, packed_ref, lines_ref):
    mirrors, rows, slots, samples = block_ref.shape
    foot_line = mirrors + valid_ref.shape[1]
    lines_ref[...] = jnp.zeros(lines_ref.shape, lines_ref.dtype)
    lines_ref[mirrors:foot_line, :valid_ref.shape[2]] = valid_ref[0]
    for k in range(mirrors):
        lines_ref[k:k + 1, :columns_ref.shape[2]] = columns_ref[k]
        lines_ref[foot_line:foot_line + 1, k * rows:(k + 1) * rows] = rows_ref[k]
    identity = (
        lax.broadcasted_iota(jnp.int32, (samples, samples), 0) == lax.broadcasted_iota(jnp.int32, (samples, samples), 1)
    ).astype(jnp.float32).astype(jnp.bfloat16)
    wide = mirrors * rows * samples
    tails = {}
    for q in range(mirrors * rows):
        turned = lax.dot_general(
            identity, block_ref[q // rows, q % rows], (((1,), (1,)), ((), ())), preferred_element_type=jnp.float32
        ).astype(jnp.bfloat16)
        packed_ref[pl.ds(q * samples, samples), :] = turned[:, :LANES]
        for start, length, row, lane in narrow_places(q, slots, samples):
            tails.setdefault((row, length), {})[lane] = turned[start:start + length, LANES:]
    for (row, length), pieces in tails.items():
        packed_ref[pl.ds(wide + row, length), :] = jnp.concatenate([pieces[lane] for lane in sorted(pieces)], axis=1)


def pack(block, foot_rows, foot_columns, valid):
    mirrors, rows, slots, samples = block.shape
    vmem = pl.BlockSpec(memory_space=pltpu.VMEM)
    height = mirrors + valid.shape[1] + 1
    return pl.pallas_call(
        pack_kernel,
        out_shape=[
            jax.ShapeDtypeStruct((mirrors * rows * samples * slots // LANES, LANES), block.dtype),
            jax.ShapeDtypeStruct((-(-height // 8) * 8, WINDOW), jnp.int32),
        ],
        in_specs=[vmem] * 4,
        out_specs=[vmem] * 2,
        compiler_params=pltpu.CompilerParams(vmem_limit_bytes=VMEM_BYTES),
        cost_estimate=pl.CostEstimate(flops=0, bytes_accessed=3 * block.size, transcendentals=0),
        name="pack_influence",
    )(block, jnp.swapaxes(foot_rows, 0, 1), jnp.swapaxes(foot_columns, 0, 1), valid)


def column_of(row):
    return jnp.transpose(jnp.broadcast_to(row, (LANES, LANES)), (1, 0))


def own_side_of(table_ref, pokes_ref, codes_ref, words, own_signs, own_sums):
    planes = pokes_ref.shape[0]
    mirrors, rows, columns = table_ref.shape
    for line in range(codes_ref.shape[0]):
        pieces, at = [], line * LANES
        while at < (line + 1) * LANES:
            row, lane = divmod(at, columns)
            length = min(columns - lane, (line + 1) * LANES - at)
            pieces.append(table_ref[row // rows, row % rows:row % rows + 1, lane:lane + length])
            at += length
        codes_ref[line:line + 1, :] = jnp.concatenate(pieces, axis=1)
    half = LANES // 2
    own = own_signs.shape[0]
    plane = lax.broadcasted_iota(jnp.int32, pokes_ref.shape, 0)
    for bit in range(BITS):
        low = jnp.sum((pokes_ref[...] >> bit & 1) << plane, axis=0, keepdims=True)
        word = low | pltpu.roll(jnp.broadcast_to(low, (8, LANES)), half, 1)[:1] << planes
        words[bit] = column_of(word)[:half]
    count = codes_ref.shape[0] * LANES // (lax.axis_size("dir") * lax.axis_size("row"))
    first = (lax.axis_index("dir") * lax.axis_size("row") + lax.axis_index("row")) * count
    lane = lax.broadcasted_iota(jnp.int32, (8, LANES), 1)
    shift = first % LANES
    lines = [
        pltpu.roll(
            jnp.broadcast_to(
                codes_ref[pl.ds(jnp.minimum(first // LANES + n, codes_ref.shape[0] - 1), 1), :], (8, LANES)
            ),
            LANES - shift, 1,
        )
        for n in range(-(-own // LANES) + 1)
    ]
    own_column = jnp.concatenate(
        [column_of(jnp.where(lane < LANES - shift, lines[n], lines[n + 1])[:1]) for n in range(len(lines) - 1)],
        axis=0,
    )[:own]
    total = jnp.zeros((own, LANES), jnp.float32)
    for at in range(planes):
        signs = (1 - 2 * parity(own_column, pokes_ref[at:at + 1, :])).astype(jnp.float32)
        own_signs[:, at * LANES:(at + 1) * LANES] = signs.astype(NARROW)
        total = total + signs
    own_sums[...] = jnp.broadcast_to(jnp.sum(total, axis=1, keepdims=True), own_sums.shape)


def gram_kernel(
    row_shape, surface_rows, table_ref, pokes_ref, packed_ref, gram_out, first_ref, gram_ref, codes_ref, words,
    own_signs, own_sums, semaphores
):
    mirror = pl.program_id(0)
    half = LANES // 2
    own, pokes = own_signs.shape
    planes = pokes // LANES
    lines = codes_ref.shape[0] // row_shape[0]
    height = gram_ref.shape[0] // row_shape[0]

    @pl.when(mirror == 0)
    def _():
        own_side_of(table_ref, pokes_ref, codes_ref, words, own_signs, own_sums)

    def chunk(index, _):
        word = []
        for side in range(WINDOW // LANES):
            line = mirror * lines + index * (WINDOW // LANES) + side
            code = jnp.broadcast_to(codes_ref[pl.ds(line, 1), :], (8, LANES))
            value = None
            for bit in range(BITS):
                mask = jnp.concatenate([code << (31 - bit) >> 31] * (half // 8), axis=0)
                part = words[bit] & mask
                value = part if value is None else value ^ part
            word.append(value)
        word = jnp.concatenate(word, axis=1)
        bits = [None] * (2 * planes)
        for byte in range(0, 2 * planes, 8):
            part = (word >> byte).astype(jnp.int8)
            for bit in range(8):
                at = byte + bit
                hit = (part & np.uint8(1 << bit).astype(np.int8)) != 0
                bits[at % planes * 2 + at // planes] = jnp.where(hit, NARROW(1.0), NARROW(0.0))
        total = jnp.dot(own_signs[...], jnp.concatenate(bits, axis=0), preferred_element_type=jnp.float32)
        sums = jnp.concatenate([own_sums[...]] * (WINDOW // LANES), axis=1)
        turned = jnp.transpose((sums - 2.0 * total).astype(jnp.bfloat16))
        at = pl.multiple_of(mirror * height + index * WINDOW, WINDOW)
        gram_ref[pl.ds(at, WINDOW), :] = turned
        return 0

    lax.fori_loop(0, height // WINDOW, chunk, 0, unroll=3)

    def send(k):
        part = pl.ds(pl.multiple_of(k * height, height), height)
        return pltpu.make_async_copy(gram_ref.at[part], gram_out.at[part], semaphores.at[k])

    send(mirror).start()
    block = lax.axis_index("row")
    for l in range(row_shape[1]):
        for k in range(row_shape[0]):
            @pl.when(mirror == k)
            def _():
                first_ref[0, l] = band_product(
                    packed_ref, k * row_shape[1] + l, row_shape, block, surface_rows, gram_ref
                )

    @pl.when(mirror == pl.num_programs(0) - 1)
    def _():
        for k in range(row_shape[0]):
            send(k).wait()


def gram(table, pokes, packed, own, row_shape, surface_rows):
    own = -(-own // 32) * 32
    acts, count = table.size, pokes.size
    mirrors, shard_rows, slots, samples = row_shape
    vmem = pl.BlockSpec(memory_space=pltpu.VMEM)
    return pl.pallas_call(
        functools.partial(gram_kernel, row_shape, surface_rows),
        grid=(mirrors,),
        out_shape=[
            jax.ShapeDtypeStruct((acts, own), jnp.bfloat16),
            jax.ShapeDtypeStruct((1, mirrors * shard_rows, samples, own), jnp.bfloat16),
        ],
        in_specs=[vmem] * 3,
        out_specs=[
            pl.BlockSpec(memory_space=pl.ANY),
            pl.BlockSpec((1, shard_rows, samples, own), lambda s: (0, s, 0, 0)),
        ],
        scratch_shapes=[
            pltpu.VMEM((acts, own), jnp.bfloat16),
            pltpu.VMEM((acts // LANES, LANES), jnp.int32),
            pltpu.VMEM((BITS, LANES // 2, LANES), jnp.int32),
            pltpu.VMEM((own, count), NARROW),
            pltpu.VMEM((own, LANES), jnp.float32),
            pltpu.SemaphoreType.DMA((mirrors,)),
        ],
        compiler_params=pltpu.CompilerParams(vmem_limit_bytes=VMEM_BYTES),
        cost_estimate=pl.CostEstimate(
            flops=2 * own * acts * count, bytes_accessed=2 * own * acts, transcendentals=0
        ),
        name="gram_rows",
    )(table, pokes, packed)


def position(axis, staged):
    return lax.axis_index(axis) if staged else 0


def row_block(place, staged):
    if not staged:
        return place
    row = lax.axis_index("row")
    core = row & 1
    return row ^ [0, 1, 2 << core, 4 >> core, (4 >> core) | 1, (2 << core) | 1, 6, 7][place]


def row_place(block, staged):
    if not staged:
        return block
    row = lax.axis_index("row")
    core = row & 1
    distance = block ^ row
    near = jnp.where(distance == 2 << core, 2, 3)
    far = jnp.where(distance == (4 >> core) | 1, 4, 5)
    middle = jnp.where(distance & 1 == 0, near, far)
    return jnp.where((distance >= 2) & (distance < 6), middle, distance)


def band_product(source, q, row_shape, block, surface_rows, gram_ref):
    mirrors, shard_rows, slots, samples = row_shape
    own = gram_ref.shape[1]
    narrow = slots - LANES
    k, l = divmod(q, shard_rows)
    band = jnp.clip((block * shard_rows + l) * NAR // surface_rows - 1, 0, NAR - BAND)
    column = pl.multiple_of((k * NAR + band) * NA, 16)
    wide = mirrors * shard_rows * samples
    products = []
    for start, length, row, lane in narrow_places(q, slots, samples):
        left = jnp.concatenate(
            [source[pl.ds(q * samples + start, length), :], source[pl.ds(wide + row, length), :]], axis=1
        )
        right = [gram_ref[pl.ds(column, LANES), :]]
        if lane:
            right.append(jnp.zeros((lane, own), jnp.bfloat16))
        right.append(gram_ref[pl.ds(column + LANES, narrow), :])
        if lane + narrow < LANES:
            right.append(jnp.zeros((LANES - lane - narrow, own), jnp.bfloat16))
        products.append(
            jnp.dot(left, jnp.concatenate(right, axis=0), preferred_element_type=jnp.float32).astype(jnp.bfloat16)
        )
    return jnp.concatenate(products, axis=0)


def fetch_gram(gram_any, gram_ref, semaphores, mirrors):
    height = gram_ref.shape[0] // mirrors
    return [
        pltpu.make_async_copy(
            gram_any.at[pl.ds(k * height, height)], gram_ref.at[pl.ds(k * height, height)], semaphores.at[k]
        )
        for k in range(mirrors)
    ]


def bands_kernel(row_shape, surface_rows, first, counts, staged, gram_any, *refs):
    mirrors, shard_rows, slots, samples = row_shape
    sources = [ref.at[n] for ref, count in zip(refs, counts) for n in range(count)]
    refs = refs[len(counts):]
    *refs, gram_ref, blocks, gram_semaphores, block_semaphores = refs
    out_ref, = refs
    step = pl.program_id(0)
    gram_copies = fetch_gram(gram_any, gram_ref, gram_semaphores, mirrors)

    def fetch(n):
        return pltpu.make_async_copy(sources[n], blocks.at[n], block_semaphores.at[n])

    @pl.when(step == 0)
    def _():
        fetch(0).start()
        for copy in gram_copies:
            copy.start()
        for n in range(1, len(sources)):
            fetch(n).start()

    for n in range(len(sources)):
        @pl.when(step == n)
        def _():
            fetch(n).wait()
            block = row_block(first + n, staged)
            for q in range(mirrors * shard_rows):
                if n == 0 and q % shard_rows == 0:
                    gram_copies[q // shard_rows].wait()
                out_ref[0, q] = band_product(blocks.at[n], q, row_shape, block, surface_rows, gram_ref)


def bands(gram_rows, sources, first, staged, row_shape, surface_rows):
    acts, own = gram_rows.shape
    mirrors, shard_rows, slots, samples = row_shape
    counts = [source.shape[0] for source in sources]
    rows = mirrors * shard_rows
    flops = 2 * own * WINDOW * samples * rows * sum(counts)
    vmem, anywhere = pl.BlockSpec(memory_space=pltpu.VMEM), pl.BlockSpec(memory_space=pl.ANY)
    out_shape = [jax.ShapeDtypeStruct((sum(counts), rows, samples, own), jnp.bfloat16)]
    out_specs = [pl.BlockSpec((1, rows, samples, own), lambda s: (s, 0, 0, 0))]
    arguments, in_specs = [gram_rows, *sources], [anywhere] * (1 + len(sources))
    return pl.pallas_call(
        functools.partial(bands_kernel, row_shape, surface_rows, first, counts, staged),
        grid=(sum(counts),),
        out_shape=out_shape,
        in_specs=in_specs,
        out_specs=out_specs,
        scratch_shapes=[
            pltpu.VMEM((acts, own), jnp.bfloat16),
            pltpu.VMEM((sum(counts),) + sources[0].shape[1:], jnp.bfloat16),
            pltpu.SemaphoreType.DMA((mirrors,)),
            pltpu.SemaphoreType.DMA((sum(counts),)),
        ],
        compiler_params=pltpu.CompilerParams(vmem_limit_bytes=VMEM_BYTES),
        cost_estimate=pl.CostEstimate(
            flops=flops, bytes_accessed=2 * own * WINDOW * rows * sum(counts), transcendentals=0
        ),
        name="bands",
    )(*arguments)


def build_differences(columns, whole_ref, rest_ref, mirrors, samples):
    half = whole_ref.shape[2]
    pupil, depth = 2 * half, whole_ref.shape[3]
    remainder = mirrors * samples - depth
    pick = lax.broadcasted_iota(jnp.int32, (pupil, pupil), 0)
    lane = lax.broadcasted_iota(jnp.int32, (pupil, pupil), 1)
    pick = (lane == pick % half * 2 + pick // half).astype(jnp.float32).astype(jnp.bfloat16)
    lines = jnp.concatenate([ref[:, :pupil] for ref in columns], axis=0)
    height = columns[0].shape[0]
    turned = lax.dot_general(
        pick, lines.astype(jnp.float32).astype(jnp.bfloat16), (((1,), (1,)), ((), ())),
        preferred_element_type=jnp.float32,
    ).astype(jnp.int32)
    at = lax.broadcasted_iota(jnp.int32, (half, mirrors * samples), 1)
    for d in range(len(columns)):
        sides = []
        for side in range(2):
            wanted = None
            for k in range(mirrors):
                column = turned[side * half:(side + 1) * half, d * height + k:d * height + k + 1] + k * samples
                wanted = column if wanted is None else jnp.where(at < k * samples, wanted, column)
            sides.append((at == wanted).astype(jnp.float32))
        across, down = sides[1] - sides[0], sides[1] + sides[0]
        whole_ref[d, 0] = across[:, :depth].astype(jnp.bfloat16)
        whole_ref[d, 1] = down[:, :depth].astype(jnp.bfloat16)
        blank = jnp.zeros((half, remainder), jnp.float32)
        upper = jnp.concatenate([across[:, depth:], blank], axis=1)
        lower = jnp.concatenate([blank, down[:, depth:]], axis=1)
        rest_ref[d] = jnp.concatenate([upper, lower], axis=0).astype(jnp.bfloat16)


def decode_kernel(row_shape, surface_rows, own, staged, norm, counts, late, places, *refs):
    mirrors, shard_rows, slots, samples = row_shape
    columns_refs, refs = refs[:counts[3]], refs[counts[3]:]
    lines_refs, refs = refs[:counts[0]], refs[counts[0]:]
    late_refs, refs = refs[:counts[1]], refs[counts[1]:]
    ready_refs, refs = refs[:counts[2]], refs[counts[2]:]
    (gram_any, out_ref, gram_ref, decoded, whole_ref, rest_ref, total, lines, foot_rows, scalars, *refs) = refs
    late_blocks, refs = refs[:counts[1]], refs[counts[1]:]
    held_columns, refs = refs[:counts[3]], refs[counts[3]:]
    held_lines, refs = refs[:counts[0]], refs[counts[0]:]
    gram_semaphores, ready_semaphores, late_semaphores, scalar_semaphore, line_semaphores = refs
    group = pl.program_id(0)
    directions, pupil = whole_ref.shape[0], 2 * whole_ref.shape[2]
    depth = whole_ref.shape[3]
    phases = out_ref.shape[2] // pupil
    blocks = surface_rows // shard_rows
    ready = blocks - late
    count = shard_rows // 2
    rows = mirrors * shard_rows
    foot_line = mirrors + count

    @pl.when(group == 0)
    def _():
        def started(copies):
            for copy in copies:
                copy.start()
            return copies

        line_copies = started([
            pltpu.make_async_copy(source, target, line_semaphores.at[n])
            for n, (source, target) in enumerate(zip([*columns_refs, *lines_refs], [*held_columns, *held_lines]))
        ])
        late_copies = started([
            pltpu.make_async_copy(late_refs[n], late_blocks[n], late_semaphores.at[n]) for n in range(counts[1])
        ])
        gram_copies = started(fetch_gram(gram_any, gram_ref, gram_semaphores, mirrors)) if late else []
        ready_copies = started([
            pltpu.make_async_copy(block, decoded.at[pl.ds(n * rows, rows)], ready_semaphores.at[n])
            for n, block in enumerate([ref.at[m] for ref in ready_refs for m in range(ref.shape[0])])
        ])
        for copy in line_copies:
            copy.wait()
        held = [ref.at[n] for ref in held_lines for n in range(ref.shape[0])]
        feet = [None] * blocks
        for place, ref in zip(places, held):
            for d in range(directions):
                lines[place, d * count:(d + 1) * count] = ref[d, mirrors:foot_line, :LANES]
            pieces = [ref[d, foot_line:foot_line + 1, :rows] for d in range(directions)]
            pieces.append(jnp.zeros((1, LANES - rows * directions), jnp.int32))
            feet[place] = jnp.concatenate(pieces, axis=1)
        feet = jnp.concatenate(feet, axis=0)
        foot_rows[...] = row_place(feet // shard_rows, staged) * rows + feet % shard_rows
        to_scalars = pltpu.make_async_copy(foot_rows, scalars, scalar_semaphore.at[0])
        to_scalars.start()
        columns = [ref.at[n] for ref in held_columns for n in range(ref.shape[0])]
        build_differences(columns, whole_ref, rest_ref, mirrors, samples)
        for copy in late_copies:
            copy.wait()
        for n in range(late):
            source = late_blocks[n]
            for q in range(mirrors * shard_rows):
                if n == 0 and q % shard_rows == 0:
                    gram_copies[q // shard_rows].wait()
                decoded[(ready + n) * rows + q] = band_product(
                    source, q, row_shape, row_block(ready + n, staged), surface_rows, gram_ref
                )
        to_scalars.wait()
        for copy in ready_copies:
            copy.wait()

    for d in range(directions):
        held = d ^ position("dir", staged)
        products, factors = [], []
        for phase in range(phases):
            i = group * phases + phase
            block = row_place(2 * i // shard_rows, staged)
            sums, changes = [], []
            for k in range(mirrors):
                picked = []
                for y in range(2):
                    row = k * shard_rows + (2 * phase + y) % shard_rows
                    picked.append(decoded[scalars[block, held * rows + row] + k * shard_rows])
                sums.append(picked[0] + picked[1])
                changes.append(picked[1] - picked[0])
            right = [jnp.concatenate(part, axis=0) for part in (sums, changes)]
            mixed = jnp.concatenate([part[depth:] for part in right], axis=0)
            rest = jnp.dot(rest_ref[held], mixed, preferred_element_type=jnp.float32)
            for kind, part in enumerate(right):
                whole = jnp.dot(whole_ref[held, kind], part[:depth], preferred_element_type=jnp.float32)
                products.append(whole + rest[kind * pupil // 2:(kind + 1) * pupil // 2])
            valid = lines[block, pl.ds(held * count + phase % count, 1), :][:, :pupil // 2]
            factors += [valid.astype(jnp.float32)] * 2
        product = jnp.concatenate(products, axis=0)
        factor = jnp.concatenate(factors, axis=1)
        for tile in range(out_ref.shape[2] // LANES):
            at = tile * LANES
            value = jnp.transpose((product[at:at + LANES] * norm).astype(jnp.bfloat16))
            value = value.astype(jnp.float32)[:own] * factor[:, at:at + LANES]
            total[tile, pl.ds(d, own, stride=directions), :] = value
    for tile in range(out_ref.shape[2] // LANES):
        value = total[tile].reshape(own, directions, LANES)
        out_ref[:, :, tile * LANES:(tile + 1) * LANES] = value.astype(out_ref.dtype)


def decode(columns, lines, places, late, ready, gram_rows, own, row_shape, surface_rows, pupil, norm, staged):
    mirrors, shard_rows, slots, samples = row_shape
    acts, padded = gram_rows.shape
    directions = sum(line.shape[0] for line in columns)
    depth = mirrors * samples // WINDOW * WINDOW
    blocks = surface_rows // shard_rows
    phases = LANES // math.gcd(pupil, LANES)
    width = surface_rows // 2 * pupil
    lanes = phases * pupil
    flops = 2 * padded * mirrors * samples * pupil * directions * surface_rows // 2
    vmem, anywhere = pl.BlockSpec(memory_space=pltpu.VMEM), pl.BlockSpec(memory_space=pl.ANY)
    counts = (len(lines), len(late), len(ready), len(columns))
    semaphores = [mirrors, blocks, max(len(late), 1), 1, len(columns) + len(lines)]
    held = -(-directions * (shard_rows // 2) // 8) * 8
    return pl.pallas_call(
        functools.partial(
            decode_kernel, row_shape, surface_rows, own, staged, norm, counts, len(late), places
        ),
        grid=(width // lanes,),
        out_shape=jax.ShapeDtypeStruct((own, directions, width), jnp.bfloat16),
        in_specs=[anywhere] * (len(columns) + len(lines) + len(late) + len(ready) + 1),
        out_specs=pl.BlockSpec((own, directions, lanes), lambda s: (0, 0, s)),
        scratch_shapes=[
            pltpu.VMEM((acts, padded), jnp.bfloat16),
            pltpu.VMEM((blocks * mirrors * shard_rows, samples, padded), jnp.bfloat16),
            pltpu.VMEM((directions, 2, pupil // 2, depth), jnp.bfloat16),
            pltpu.VMEM((directions, pupil, 2 * (mirrors * samples - depth)), jnp.bfloat16),
            pltpu.VMEM((lanes // LANES, own * directions, LANES), jnp.float32),
            pltpu.VMEM((blocks, held, LANES), jnp.int32),
            pltpu.VMEM((blocks, LANES), jnp.int32),
            pltpu.SMEM((blocks, LANES), jnp.int32),
            *[pltpu.VMEM(block.shape, block.dtype) for block in [*late, *columns, *lines]],
            *[pltpu.SemaphoreType.DMA((count,)) for count in semaphores],
        ],
        compiler_params=pltpu.CompilerParams(vmem_limit_bytes=VMEM_BYTES),
        cost_estimate=pl.CostEstimate(flops=flops, bytes_accessed=2 * own * directions * width, transcendentals=0),
        name="decode",
    )(*columns, *lines, *late, *ready, gram_rows)


def swap(block, axis, distance):
    return lax.ppermute(block, axis, [(i, i ^ distance) for i in range(lax.axis_size(axis))])


def turn(block, even, odd):
    return lax.ppermute(
        block, "row", [(i, i ^ (odd if i % 2 else even)) for i in range(lax.axis_size("row"))]
    )


def shards(influence, foot_rows, foot_columns, actuator_codes, poke_rows, subaperture_valid):
    mirrors, shard_rows, samples, slots = influence.shape
    row_shape = (mirrors, shard_rows, slots, samples)
    directions, devices = lax.axis_size("dir"), lax.axis_size("row")
    surface_rows = shard_rows * devices
    pupil = foot_columns.shape[2]
    norm = 0.5 * poke_rows.shape[0] ** (-0.5)
    own = actuator_codes.size // (directions * devices)
    staged = devices == 8 and directions > 1 and directions & (directions - 1) == 0
    turned = jnp.swapaxes(influence, 2, 3)
    pokes = poke_rows.reshape(-1, LANES)
    packed, lines = pack(turned, foot_rows, foot_columns, subaperture_valid)
    if not staged:
        every = lax.all_gather(packed, "row")
        lines = lax.all_gather(lax.all_gather(lines, "dir"), "row")
        gram_rows, _ = gram(actuator_codes, pokes, packed, own, row_shape, surface_rows)
        ready, = bands(gram_rows, [every], 0, staged, row_shape, surface_rows)
        return decode(
            [lines[0]], [lines], list(range(devices)), [], [ready], gram_rows, own, row_shape, surface_rows, pupil,
            norm, staged,
        )

    first, second = turn(packed, 2, 4), turn(packed, 4, 2)
    sibling = swap(packed, "row", 1)
    lines, distance = [jnp.stack([lines, swap(lines, "dir", 1)])], 2
    lines[0], pokes = lax.optimization_barrier((lines[0], pokes))
    while distance < directions:
        lines.append(swap(jnp.concatenate(lines, axis=0), "dir", distance))
        distance *= 2
    held = jnp.concatenate(lines, axis=0)[None, :, :, :LANES]
    gram_rows, own_rows = gram(actuator_codes, pokes, packed, own, row_shape, surface_rows)
    gram_rows, first, second, held = lax.optimization_barrier((gram_rows, first, second, held))
    diagonal = turn(first, 4, 2)
    first_sibling = swap(first, "row", 1)
    mine = [held, turn(held, 2, 4), turn(held, 4, 2), swap(held, "row", 6)]
    sources = [source[None] for source in (sibling, first, second)]
    near, = bands(gram_rows, sources, 1, staged, row_shape, surface_rows)
    near, second = lax.optimization_barrier((near, second))
    second_sibling = swap(second, "row", 1)
    mine = jnp.concatenate(mine, axis=0)
    near, diagonal, mine = lax.optimization_barrier((near, diagonal, mine))
    theirs = swap(mine, "row", 1)
    late = [first_sibling, second_sibling, diagonal, swap(diagonal, "row", 1)]
    return decode(
        lines, [mine, theirs], [0, 2, 3, 6, 1, 4, 5, 7], late, [own_rows, near], gram_rows, own, row_shape,
        surface_rows, pupil, norm, staged,
    )


def solution(mesh):
    return jax.shard_map(
        shards,
        mesh=mesh,
        in_specs=(
            P(None, "row", None, None),
            P("dir", None, "row"),
            P("dir", None, None),
            P(),
            P(),
            P("dir", "row", None),
        ),
        out_specs=P(("dir", "row"), None, None),
        check_vma=False,
    )
```

```python
import functools
import math

import jax
import jax.numpy as jnp
import numpy as np
from jax import lax
from jax.experimental import pallas as pl
from jax.experimental.pallas import tpu as pltpu
from jax.sharding import PartitionSpec as P

NAR = 48
NA = 48
BAND = 3
REACH = 2
BITS = 13
NARROW = jnp.float8_e4m3fn
LANES = 128
WINDOW = 256
VMEM_BYTES = 127 * 512 * 1024


def parity(codes, rows):
    return lax.population_count(codes & rows) & 1


def narrow_places(q, slots, samples):
    narrow = slots - LANES
    whole = LANES // narrow
    if q < whole:
        return [(0, samples, 0, q * narrow)]
    half = samples // 2
    lane = (q - whole) * narrow
    return [(0, half, samples, lane), (half, half, samples, LANES // 2 + lane)]


def pack_kernel(block_ref, rows_ref, columns_ref, valid_ref, packed_ref, lines_ref):
    mirrors, rows, slots, samples = block_ref.shape
    foot_line = mirrors + valid_ref.shape[1]
    lines_ref[...] = jnp.zeros(lines_ref.shape, lines_ref.dtype)
    lines_ref[mirrors:foot_line, :valid_ref.shape[2]] = valid_ref[0]
    for k in range(mirrors):
        lines_ref[k:k + 1, :columns_ref.shape[2]] = columns_ref[k]
        lines_ref[foot_line:foot_line + 1, k * rows:(k + 1) * rows] = rows_ref[k]
    identity = (
        lax.broadcasted_iota(jnp.int32, (samples, samples), 0) == lax.broadcasted_iota(jnp.int32, (samples, samples), 1)
    ).astype(jnp.float32).astype(jnp.bfloat16)
    wide = mirrors * rows * samples
    tails = {}
    for q in range(mirrors * rows):
        turned = lax.dot_general(
            identity, block_ref[q // rows, q % rows], (((1,), (1,)), ((), ())), preferred_element_type=jnp.float32
        ).astype(jnp.bfloat16)
        packed_ref[pl.ds(q * samples, samples), :] = turned[:, :LANES]
        for start, length, row, lane in narrow_places(q, slots, samples):
            tails.setdefault((row, length), {})[lane] = turned[start:start + length, LANES:]
    for (row, length), pieces in tails.items():
        packed_ref[pl.ds(wide + row, length), :] = jnp.concatenate([pieces[lane] for lane in sorted(pieces)], axis=1)


def pack(block, foot_rows, foot_columns, valid):
    mirrors, rows, slots, samples = block.shape
    vmem = pl.BlockSpec(memory_space=pltpu.VMEM)
    height = mirrors + valid.shape[1] + 1
    return pl.pallas_call(
        pack_kernel,
        out_shape=[
            jax.ShapeDtypeStruct((mirrors * rows * samples * slots // LANES, LANES), block.dtype),
            jax.ShapeDtypeStruct((-(-height // 8) * 8, WINDOW), jnp.int32),
        ],
        in_specs=[vmem] * 4,
        out_specs=[vmem] * 2,
        compiler_params=pltpu.CompilerParams(vmem_limit_bytes=VMEM_BYTES),
        cost_estimate=pl.CostEstimate(flops=0, bytes_accessed=3 * block.size, transcendentals=0),
        name="pack_influence",
    )(block, jnp.swapaxes(foot_rows, 0, 1), jnp.swapaxes(foot_columns, 0, 1), valid)


def column_of(row):
    return jnp.transpose(jnp.broadcast_to(row, (LANES, LANES)), (1, 0))


def own_side_of(table_ref, pokes_ref, codes_ref, words, own_signs, own_sums):
    planes = pokes_ref.shape[0]
    mirrors, rows, columns = table_ref.shape
    for line in range(codes_ref.shape[0]):
        pieces, at = [], line * LANES
        while at < (line + 1) * LANES:
            row, lane = divmod(at, columns)
            length = min(columns - lane, (line + 1) * LANES - at)
            pieces.append(table_ref[row // rows, row % rows:row % rows + 1, lane:lane + length])
            at += length
        codes_ref[line:line + 1, :] = jnp.concatenate(pieces, axis=1)
    half = LANES // 2
    own = own_signs.shape[0]
    plane = lax.broadcasted_iota(jnp.int32, pokes_ref.shape, 0)
    for bit in range(BITS):
        low = jnp.sum((pokes_ref[...] >> bit & 1) << plane, axis=0, keepdims=True)
        word = low | pltpu.roll(jnp.broadcast_to(low, (8, LANES)), half, 1)[:1] << planes
        words[bit] = column_of(word)[:half]
    count = codes_ref.shape[0] * LANES // (lax.axis_size("dir") * lax.axis_size("row"))
    first = (lax.axis_index("dir") * lax.axis_size("row") + lax.axis_index("row")) * count
    lane = lax.broadcasted_iota(jnp.int32, (8, LANES), 1)
    shift = first % LANES
    lines = [
        pltpu.roll(
            jnp.broadcast_to(
                codes_ref[pl.ds(jnp.minimum(first // LANES + n, codes_ref.shape[0] - 1), 1), :], (8, LANES)
            ),
            LANES - shift, 1,
        )
        for n in range(-(-own // LANES) + 1)
    ]
    own_column = jnp.concatenate(
        [column_of(jnp.where(lane < LANES - shift, lines[n], lines[n + 1])[:1]) for n in range(len(lines) - 1)],
        axis=0,
    )[:own]
    total = jnp.zeros((own, LANES), jnp.float32)
    for at in range(planes):
        signs = (1 - 2 * parity(own_column, pokes_ref[at:at + 1, :])).astype(jnp.float32)
        own_signs[:, at * LANES:(at + 1) * LANES] = signs.astype(NARROW)
        total = total + signs
    own_sums[...] = jnp.broadcast_to(jnp.sum(total, axis=1, keepdims=True), own_sums.shape)


def gram_kernel(
    row_shape, surface_rows, table_ref, pokes_ref, packed_ref, gram_out, first_ref, gram_ref, codes_ref, words,
    own_signs, own_sums, semaphores
):
    mirror = pl.program_id(0)
    half = LANES // 2
    own, pokes = own_signs.shape
    planes = pokes // LANES
    lines = codes_ref.shape[0] // row_shape[0]
    height = gram_ref.shape[0] // row_shape[0]

    @pl.when(mirror == 0)
    def _():
        own_side_of(table_ref, pokes_ref, codes_ref, words, own_signs, own_sums)

    def chunk(index, _):
        word = []
        for side in range(WINDOW // LANES):
            line = mirror * lines + index * (WINDOW // LANES) + side
            code = jnp.broadcast_to(codes_ref[pl.ds(line, 1), :], (8, LANES))
            value = None
            for bit in range(BITS):
                mask = jnp.concatenate([code << (31 - bit) >> 31] * (half // 8), axis=0)
                part = words[bit] & mask
                value = part if value is None else value ^ part
            word.append(value)
        word = jnp.concatenate(word, axis=1)
        bits = [None] * (2 * planes)
        for byte in range(0, 2 * planes, 8):
            part = (word >> byte).astype(jnp.int8)
            for bit in range(8):
                at = byte + bit
                hit = (part & np.uint8(1 << bit).astype(np.int8)) != 0
                bits[at % planes * 2 + at // planes] = jnp.where(hit, NARROW(1.0), NARROW(0.0))
        total = jnp.dot(own_signs[...], jnp.concatenate(bits, axis=0), preferred_element_type=jnp.float32)
        sums = jnp.concatenate([own_sums[...]] * (WINDOW // LANES), axis=1)
        turned = jnp.transpose((sums - 2.0 * total).astype(jnp.bfloat16))
        at = pl.multiple_of(mirror * height + index * WINDOW, WINDOW)
        gram_ref[pl.ds(at, WINDOW), :] = turned
        return 0

    lax.fori_loop(0, height // WINDOW, chunk, 0, unroll=3)

    def send(k):
        part = pl.ds(pl.multiple_of(k * height, height), height)
        return pltpu.make_async_copy(gram_ref.at[part], gram_out.at[part], semaphores.at[k])

    send(mirror).start()
    block = lax.axis_index("row")
    for l in range(row_shape[1]):
        for k in range(row_shape[0]):
            @pl.when(mirror == k)
            def _():
                first_ref[0, l] = band_product(
                    packed_ref, k * row_shape[1] + l, row_shape, block, surface_rows, gram_ref
                )

    @pl.when(mirror == pl.num_programs(0) - 1)
    def _():
        for k in range(row_shape[0]):
            send(k).wait()


def gram(table, pokes, packed, own, row_shape, surface_rows):
    own = -(-own // 32) * 32
    acts, count = table.size, pokes.size
    mirrors, shard_rows, slots, samples = row_shape
    vmem = pl.BlockSpec(memory_space=pltpu.VMEM)
    return pl.pallas_call(
        functools.partial(gram_kernel, row_shape, surface_rows),
        grid=(mirrors,),
        out_shape=[
            jax.ShapeDtypeStruct((acts, own), jnp.bfloat16),
            jax.ShapeDtypeStruct((1, mirrors * shard_rows, samples, own), jnp.bfloat16),
        ],
        in_specs=[vmem] * 3,
        out_specs=[
            pl.BlockSpec(memory_space=pl.ANY),
            pl.BlockSpec((1, shard_rows, samples, own), lambda s: (0, s, 0, 0)),
        ],
        scratch_shapes=[
            pltpu.VMEM((acts, own), jnp.bfloat16),
            pltpu.VMEM((acts // LANES, LANES), jnp.int32),
            pltpu.VMEM((BITS, LANES // 2, LANES), jnp.int32),
            pltpu.VMEM((own, count), NARROW),
            pltpu.VMEM((own, LANES), jnp.float32),
            pltpu.SemaphoreType.DMA((mirrors,)),
        ],
        compiler_params=pltpu.CompilerParams(vmem_limit_bytes=VMEM_BYTES),
        cost_estimate=pl.CostEstimate(
            flops=2 * own * acts * count, bytes_accessed=2 * own * acts, transcendentals=0
        ),
        name="gram_rows",
    )(table, pokes, packed)


def position(axis, staged):
    return lax.axis_index(axis) if staged else 0


def row_block(place, staged):
    if not staged:
        return place
    row = lax.axis_index("row")
    core = row & 1
    return row ^ [0, 2 << core, 4 >> core, 1, (4 >> core) | 1, (2 << core) | 1, 6, 7][place]


def row_place(block, staged):
    if not staged:
        return block
    row = lax.axis_index("row")
    core = row & 1
    distance = block ^ row
    near = jnp.where(distance == 2 << core, 1, 2)
    far = jnp.where(distance == (4 >> core) | 1, 4, 5)
    middle = jnp.where(distance & 1 == 0, near, far)
    return jnp.where((distance >= 2) & (distance < 6), middle, jnp.where(distance == 1, 3, distance))


def band_product(source, q, row_shape, block, surface_rows, gram_ref):
    mirrors, shard_rows, slots, samples = row_shape
    own = gram_ref.shape[1]
    narrow = slots - LANES
    k, l = divmod(q, shard_rows)
    band = jnp.clip((block * shard_rows + l) * NAR // surface_rows - 1, 0, NAR - BAND)
    column = pl.multiple_of((k * NAR + band) * NA, 16)
    wide = mirrors * shard_rows * samples
    products = []
    for start, length, row, lane in narrow_places(q, slots, samples):
        left = jnp.concatenate(
            [source[pl.ds(q * samples + start, length), :], source[pl.ds(wide + row, length), :]], axis=1
        )
        right = [gram_ref[pl.ds(column, LANES), :]]
        if lane:
            right.append(jnp.zeros((lane, own), jnp.bfloat16))
        right.append(gram_ref[pl.ds(column + LANES, narrow), :])
        if lane + narrow < LANES:
            right.append(jnp.zeros((LANES - lane - narrow, own), jnp.bfloat16))
        products.append(
            jnp.dot(left, jnp.concatenate(right, axis=0), preferred_element_type=jnp.float32).astype(jnp.bfloat16)
        )
    return jnp.concatenate(products, axis=0)


def fetch_gram(gram_any, gram_ref, semaphores, mirrors):
    height = gram_ref.shape[0] // mirrors
    return [
        pltpu.make_async_copy(
            gram_any.at[pl.ds(k * height, height)], gram_ref.at[pl.ds(k * height, height)], semaphores.at[k]
        )
        for k in range(mirrors)
    ]


def bands_kernel(row_shape, surface_rows, first, counts, staged, gram_any, *refs):
    mirrors, shard_rows, slots, samples = row_shape
    sources = [ref.at[n] for ref, count in zip(refs, counts) for n in range(count)]
    refs = refs[len(counts):]
    *refs, gram_ref, blocks, gram_semaphores, block_semaphores = refs
    out_ref, = refs
    step = pl.program_id(0)
    gram_copies = fetch_gram(gram_any, gram_ref, gram_semaphores, mirrors)

    def fetch(n):
        return pltpu.make_async_copy(sources[n], blocks.at[n], block_semaphores.at[n])

    @pl.when(step == 0)
    def _():
        fetch(0).start()
        for copy in gram_copies:
            copy.start()
        for n in range(1, len(sources)):
            fetch(n).start()

    for n in range(len(sources)):
        @pl.when(step == n)
        def _():
            fetch(n).wait()
            block = row_block(first + n, staged)
            for q in range(mirrors * shard_rows):
                if n == 0 and q % shard_rows == 0:
                    gram_copies[q // shard_rows].wait()
                out_ref[0, q] = band_product(blocks.at[n], q, row_shape, block, surface_rows, gram_ref)


def bands(gram_rows, sources, first, staged, row_shape, surface_rows):
    acts, own = gram_rows.shape
    mirrors, shard_rows, slots, samples = row_shape
    counts = [source.shape[0] for source in sources]
    rows = mirrors * shard_rows
    flops = 2 * own * WINDOW * samples * rows * sum(counts)
    vmem, anywhere = pl.BlockSpec(memory_space=pltpu.VMEM), pl.BlockSpec(memory_space=pl.ANY)
    out_shape = [jax.ShapeDtypeStruct((sum(counts), rows, samples, own), jnp.bfloat16)]
    out_specs = [pl.BlockSpec((1, rows, samples, own), lambda s: (s, 0, 0, 0))]
    arguments, in_specs = [gram_rows, *sources], [anywhere] * (1 + len(sources))
    return pl.pallas_call(
        functools.partial(bands_kernel, row_shape, surface_rows, first, counts, staged),
        grid=(sum(counts),),
        out_shape=out_shape,
        in_specs=in_specs,
        out_specs=out_specs,
        scratch_shapes=[
            pltpu.VMEM((acts, own), jnp.bfloat16),
            pltpu.VMEM((sum(counts),) + sources[0].shape[1:], jnp.bfloat16),
            pltpu.SemaphoreType.DMA((mirrors,)),
            pltpu.SemaphoreType.DMA((sum(counts),)),
        ],
        compiler_params=pltpu.CompilerParams(vmem_limit_bytes=VMEM_BYTES),
        cost_estimate=pl.CostEstimate(
            flops=flops, bytes_accessed=2 * own * WINDOW * rows * sum(counts), transcendentals=0
        ),
        name="bands",
    )(*arguments)


def build_differences(columns, whole_ref, rest_ref, mirrors, samples):
    half = whole_ref.shape[2]
    pupil, depth = 2 * half, whole_ref.shape[3]
    remainder = mirrors * samples - depth
    pick = lax.broadcasted_iota(jnp.int32, (pupil, pupil), 0)
    lane = lax.broadcasted_iota(jnp.int32, (pupil, pupil), 1)
    pick = (lane == pick % half * 2 + pick // half).astype(jnp.float32).astype(jnp.bfloat16)
    lines = jnp.concatenate([ref[:, :pupil] for ref in columns], axis=0)
    height = columns[0].shape[0]
    turned = lax.dot_general(
        pick, lines.astype(jnp.float32).astype(jnp.bfloat16), (((1,), (1,)), ((), ())),
        preferred_element_type=jnp.float32,
    ).astype(jnp.int32)
    at = lax.broadcasted_iota(jnp.int32, (half, mirrors * samples), 1)
    for d in range(len(columns)):
        sides = []
        for side in range(2):
            wanted = None
            for k in range(mirrors):
                column = turned[side * half:(side + 1) * half, d * height + k:d * height + k + 1] + k * samples
                wanted = column if wanted is None else jnp.where(at < k * samples, wanted, column)
            sides.append((at == wanted).astype(jnp.float32))
        across, down = sides[1] - sides[0], sides[1] + sides[0]
        whole_ref[d, 0] = across[:, :depth].astype(jnp.bfloat16)
        whole_ref[d, 1] = down[:, :depth].astype(jnp.bfloat16)
        blank = jnp.zeros((half, remainder), jnp.float32)
        upper = jnp.concatenate([across[:, depth:], blank], axis=1)
        lower = jnp.concatenate([blank, down[:, depth:]], axis=1)
        rest_ref[d] = jnp.concatenate([upper, lower], axis=0).astype(jnp.bfloat16)


def decode_kernel(row_shape, surface_rows, own, staged, norm, counts, late, places, *refs):
    mirrors, shard_rows, slots, samples = row_shape
    columns_refs, refs = refs[:counts[3]], refs[counts[3]:]
    lines_refs, refs = refs[:counts[0]], refs[counts[0]:]
    late_refs, refs = refs[:counts[1]], refs[counts[1]:]
    ready_refs, refs = refs[:counts[2]], refs[counts[2]:]
    (gram_any, out_ref, gram_ref, decoded, whole_ref, rest_ref, total, lines, foot_rows, scalars, *refs) = refs
    late_blocks, refs = refs[:counts[1]], refs[counts[1]:]
    held_columns, refs = refs[:counts[3]], refs[counts[3]:]
    held_lines, refs = refs[:counts[0]], refs[counts[0]:]
    gram_semaphores, ready_semaphores, late_semaphores, scalar_semaphore, line_semaphores = refs
    group = pl.program_id(0)
    directions, pupil = whole_ref.shape[0], 2 * whole_ref.shape[2]
    depth = whole_ref.shape[3]
    phases = out_ref.shape[2] // pupil
    blocks = surface_rows // shard_rows
    ready = blocks - late
    count = shard_rows // 2
    rows = mirrors * shard_rows
    foot_line = mirrors + count

    @pl.when(group == 0)
    def _():
        def started(copies):
            for copy in copies:
                copy.start()
            return copies

        line_copies = started([
            pltpu.make_async_copy(source, target, line_semaphores.at[n])
            for n, (source, target) in enumerate(zip([*columns_refs, *lines_refs], [*held_columns, *held_lines]))
        ])
        late_copies = started([
            pltpu.make_async_copy(late_refs[n], late_blocks[n], late_semaphores.at[n]) for n in range(counts[1])
        ])
        gram_copies = started(fetch_gram(gram_any, gram_ref, gram_semaphores, mirrors)) if late else []
        ready_copies = started([
            pltpu.make_async_copy(block, decoded.at[pl.ds(n * rows, rows)], ready_semaphores.at[n])
            for n, block in enumerate([ref.at[m] for ref in ready_refs for m in range(ref.shape[0])])
        ])
        for copy in line_copies:
            copy.wait()
        held = [ref.at[n] for ref in held_lines for n in range(ref.shape[0])]
        feet = [None] * blocks
        for place, ref in zip(places, held):
            for d in range(directions):
                lines[place, d * count:(d + 1) * count] = ref[d, mirrors:foot_line, :LANES]
            pieces = [ref[d, foot_line:foot_line + 1, :rows] for d in range(directions)]
            pieces.append(jnp.zeros((1, LANES - rows * directions), jnp.int32))
            feet[place] = jnp.concatenate(pieces, axis=1)
        feet = jnp.concatenate(feet, axis=0)
        foot_rows[...] = row_place(feet // shard_rows, staged) * rows + feet % shard_rows
        to_scalars = pltpu.make_async_copy(foot_rows, scalars, scalar_semaphore.at[0])
        to_scalars.start()
        columns = [ref.at[n] for ref in held_columns for n in range(ref.shape[0])]
        build_differences(columns, whole_ref, rest_ref, mirrors, samples)
        for copy in late_copies:
            copy.wait()
        for n in range(late):
            source = late_blocks[n]
            for q in range(mirrors * shard_rows):
                if n == 0 and q % shard_rows == 0:
                    gram_copies[q // shard_rows].wait()
                decoded[(ready + n) * rows + q] = band_product(
                    source, q, row_shape, row_block(ready + n, staged), surface_rows, gram_ref
                )
        to_scalars.wait()
        for copy in ready_copies:
            copy.wait()

    for d in range(directions):
        held = d ^ position("dir", staged)
        products, factors = [], []
        for phase in range(phases):
            i = group * phases + phase
            block = row_place(2 * i // shard_rows, staged)
            sums, changes = [], []
            for k in range(mirrors):
                picked = []
                for y in range(2):
                    row = k * shard_rows + (2 * phase + y) % shard_rows
                    picked.append(decoded[scalars[block, held * rows + row] + k * shard_rows])
                sums.append(picked[0] + picked[1])
                changes.append(picked[1] - picked[0])
            right = [jnp.concatenate(part, axis=0) for part in (sums, changes)]
            mixed = jnp.concatenate([part[depth:] for part in right], axis=0)
            rest = jnp.dot(rest_ref[held], mixed, preferred_element_type=jnp.float32)
            for kind, part in enumerate(right):
                whole = jnp.dot(whole_ref[held, kind], part[:depth], preferred_element_type=jnp.float32)
                products.append(whole + rest[kind * pupil // 2:(kind + 1) * pupil // 2])
            valid = lines[block, pl.ds(held * count + phase % count, 1), :][:, :pupil // 2]
            factors += [valid.astype(jnp.float32)] * 2
        product = jnp.concatenate(products, axis=0)
        factor = jnp.concatenate(factors, axis=1)
        for tile in range(out_ref.shape[2] // LANES):
            at = tile * LANES
            value = jnp.transpose((product[at:at + LANES] * norm).astype(jnp.bfloat16))
            value = value.astype(jnp.float32)[:own] * factor[:, at:at + LANES]
            total[tile, pl.ds(d, own, stride=directions), :] = value
    for tile in range(out_ref.shape[2] // LANES):
        value = total[tile].reshape(own, directions, LANES)
        out_ref[:, :, tile * LANES:(tile + 1) * LANES] = value.astype(out_ref.dtype)


def decode(columns, lines, places, late, ready, gram_rows, own, row_shape, surface_rows, pupil, norm, staged):
    mirrors, shard_rows, slots, samples = row_shape
    acts, padded = gram_rows.shape
    directions = sum(line.shape[0] for line in columns)
    depth = mirrors * samples // WINDOW * WINDOW
    blocks = surface_rows // shard_rows
    phases = LANES // math.gcd(pupil, LANES)
    width = surface_rows // 2 * pupil
    lanes = phases * pupil
    flops = 2 * padded * mirrors * samples * pupil * directions * surface_rows // 2
    vmem, anywhere = pl.BlockSpec(memory_space=pltpu.VMEM), pl.BlockSpec(memory_space=pl.ANY)
    counts = (len(lines), len(late), len(ready), len(columns))
    semaphores = [mirrors, blocks, max(len(late), 1), 1, len(columns) + len(lines)]
    held = -(-directions * (shard_rows // 2) // 8) * 8
    return pl.pallas_call(
        functools.partial(
            decode_kernel, row_shape, surface_rows, own, staged, norm, counts, len(late), places
        ),
        grid=(width // lanes,),
        out_shape=jax.ShapeDtypeStruct((own, directions, width), jnp.bfloat16),
        in_specs=[anywhere] * (len(columns) + len(lines) + len(late) + len(ready) + 1),
        out_specs=pl.BlockSpec((own, directions, lanes), lambda s: (0, 0, s)),
        scratch_shapes=[
            pltpu.VMEM((acts, padded), jnp.bfloat16),
            pltpu.VMEM((blocks * mirrors * shard_rows, samples, padded), jnp.bfloat16),
            pltpu.VMEM((directions, 2, pupil // 2, depth), jnp.bfloat16),
            pltpu.VMEM((directions, pupil, 2 * (mirrors * samples - depth)), jnp.bfloat16),
            pltpu.VMEM((lanes // LANES, own * directions, LANES), jnp.float32),
            pltpu.VMEM((blocks, held, LANES), jnp.int32),
            pltpu.VMEM((blocks, LANES), jnp.int32),
            pltpu.SMEM((blocks, LANES), jnp.int32),
            *[pltpu.VMEM(block.shape, block.dtype) for block in [*late, *columns, *lines]],
            *[pltpu.SemaphoreType.DMA((count,)) for count in semaphores],
        ],
        compiler_params=pltpu.CompilerParams(vmem_limit_bytes=VMEM_BYTES),
        cost_estimate=pl.CostEstimate(flops=flops, bytes_accessed=2 * own * directions * width, transcendentals=0),
        name="decode",
    )(*columns, *lines, *late, *ready, gram_rows)


def swap(block, axis, distance):
    return lax.ppermute(block, axis, [(i, i ^ distance) for i in range(lax.axis_size(axis))])


def turn(block, even, odd):
    return lax.ppermute(
        block, "row", [(i, i ^ (odd if i % 2 else even)) for i in range(lax.axis_size("row"))]
    )


def shards(influence, foot_rows, foot_columns, actuator_codes, poke_rows, subaperture_valid):
    mirrors, shard_rows, samples, slots = influence.shape
    row_shape = (mirrors, shard_rows, slots, samples)
    directions, devices = lax.axis_size("dir"), lax.axis_size("row")
    surface_rows = shard_rows * devices
    pupil = foot_columns.shape[2]
    norm = 0.5 * poke_rows.shape[0] ** (-0.5)
    own = actuator_codes.size // (directions * devices)
    staged = devices == 8 and directions > 1 and directions & (directions - 1) == 0
    turned = jnp.swapaxes(influence, 2, 3)
    pokes = poke_rows.reshape(-1, LANES)
    packed, lines = pack(turned, foot_rows, foot_columns, subaperture_valid)
    if not staged:
        every = lax.all_gather(packed, "row")
        lines = lax.all_gather(lax.all_gather(lines, "dir"), "row")
        gram_rows, _ = gram(actuator_codes, pokes, packed, own, row_shape, surface_rows)
        ready, = bands(gram_rows, [every], 0, staged, row_shape, surface_rows)
        return decode(
            [lines[0]], [lines], list(range(devices)), [], [ready], gram_rows, own, row_shape, surface_rows, pupil,
            norm, staged,
        )

    first, second = turn(packed, 2, 4), turn(packed, 4, 2)
    sibling = swap(packed, "row", 1)
    lines, distance = [jnp.stack([lines, swap(lines, "dir", 1)])], 2
    lines[0], pokes = lax.optimization_barrier((lines[0], pokes))
    while distance < directions:
        lines.append(swap(jnp.concatenate(lines, axis=0), "dir", distance))
        distance *= 2
    held = jnp.concatenate(lines, axis=0)[None, :, :, :LANES]
    gram_rows, own_rows = gram(actuator_codes, pokes, packed, own, row_shape, surface_rows)
    gram_rows, first, second, held, sibling = lax.optimization_barrier(
        (gram_rows, first, second, held, sibling)
    )
    diagonal = turn(first, 4, 2)
    first_sibling = swap(first, "row", 1)
    mine = [held, turn(held, 2, 4), turn(held, 4, 2), swap(held, "row", 6)]
    sources = [source[None] for source in (first, second)]
    near, = bands(gram_rows, sources, 1, staged, row_shape, surface_rows)
    near, second = lax.optimization_barrier((near, second))
    second_sibling = swap(second, "row", 1)
    mine = jnp.concatenate(mine, axis=0)
    near, diagonal, mine = lax.optimization_barrier((near, diagonal, mine))
    theirs = swap(mine, "row", 1)
    late = [sibling, first_sibling, second_sibling, diagonal, swap(diagonal, "row", 1)]
    return decode(
        lines, [mine, theirs], [0, 1, 2, 6, 3, 4, 5, 7], late, [own_rows, near], gram_rows, own, row_shape,
        surface_rows, pupil, norm, staged,
    )


def solution(mesh):
    return jax.shard_map(
        shards,
        mesh=mesh,
        in_specs=(
            P(None, "row", None, None),
            P("dir", None, "row"),
            P("dir", None, None),
            P(),
            P(),
            P("dir", "row", None),
        ),
        out_specs=P(("dir", "row"), None, None),
        check_vma=False,
    )
```

```python
import functools
import math

import jax
import jax.numpy as jnp
import numpy as np
from jax import lax
from jax.experimental import pallas as pl
from jax.experimental.pallas import tpu as pltpu
from jax.sharding import PartitionSpec as P

NAR = 48
NA = 48
BAND = 3
REACH = 2
BITS = 13
NARROW = jnp.float8_e4m3fn
LANES = 128
WINDOW = 256
VMEM_BYTES = 127 * 512 * 1024


def parity(codes, rows):
    return lax.population_count(codes & rows) & 1


def narrow_places(q, slots, samples):
    narrow = slots - LANES
    whole = LANES // narrow
    if q < whole:
        return [(0, samples, 0, q * narrow)]
    half = samples // 2
    lane = (q - whole) * narrow
    return [(0, half, samples, lane), (half, half, samples, LANES // 2 + lane)]


def pack_kernel(block_ref, rows_ref, columns_ref, valid_ref, packed_ref, lines_ref):
    mirrors, rows, slots, samples = block_ref.shape
    foot_line = mirrors + valid_ref.shape[1]
    lines_ref[...] = jnp.zeros(lines_ref.shape, lines_ref.dtype)
    lines_ref[mirrors:foot_line, :valid_ref.shape[2]] = valid_ref[0]
    for k in range(mirrors):
        lines_ref[k:k + 1, :columns_ref.shape[2]] = columns_ref[k]
        lines_ref[foot_line:foot_line + 1, k * rows:(k + 1) * rows] = rows_ref[k]
    identity = (
        lax.broadcasted_iota(jnp.int32, (samples, samples), 0) == lax.broadcasted_iota(jnp.int32, (samples, samples), 1)
    ).astype(jnp.float32).astype(jnp.bfloat16)
    wide = mirrors * rows * samples
    tails = {}
    for q in range(mirrors * rows):
        turned = lax.dot_general(
            identity, block_ref[q // rows, q % rows], (((1,), (1,)), ((), ())), preferred_element_type=jnp.float32
        ).astype(jnp.bfloat16)
        packed_ref[pl.ds(q * samples, samples), :] = turned[:, :LANES]
        for start, length, row, lane in narrow_places(q, slots, samples):
            tails.setdefault((row, length), {})[lane] = turned[start:start + length, LANES:]
    for (row, length), pieces in tails.items():
        packed_ref[pl.ds(wide + row, length), :] = jnp.concatenate([pieces[lane] for lane in sorted(pieces)], axis=1)


def pack(block, foot_rows, foot_columns, valid):
    mirrors, rows, slots, samples = block.shape
    vmem = pl.BlockSpec(memory_space=pltpu.VMEM)
    height = mirrors + valid.shape[1] + 1
    return pl.pallas_call(
        pack_kernel,
        out_shape=[
            jax.ShapeDtypeStruct((mirrors * rows * samples * slots // LANES, LANES), block.dtype),
            jax.ShapeDtypeStruct((-(-height // 8) * 8, WINDOW), jnp.int32),
        ],
        in_specs=[vmem] * 4,
        out_specs=[vmem] * 2,
        compiler_params=pltpu.CompilerParams(vmem_limit_bytes=VMEM_BYTES),
        cost_estimate=pl.CostEstimate(flops=0, bytes_accessed=3 * block.size, transcendentals=0),
        name="pack_influence",
    )(block, jnp.swapaxes(foot_rows, 0, 1), jnp.swapaxes(foot_columns, 0, 1), valid)


def column_of(row):
    return jnp.transpose(jnp.broadcast_to(row, (LANES, LANES)), (1, 0))


def own_side_of(table_ref, pokes_ref, codes_ref, words, own_signs, own_sums):
    planes = pokes_ref.shape[0]
    mirrors, rows, columns = table_ref.shape
    for line in range(codes_ref.shape[0]):
        pieces, at = [], line * LANES
        while at < (line + 1) * LANES:
            row, lane = divmod(at, columns)
            length = min(columns - lane, (line + 1) * LANES - at)
            pieces.append(table_ref[row // rows, row % rows:row % rows + 1, lane:lane + length])
            at += length
        codes_ref[line:line + 1, :] = jnp.concatenate(pieces, axis=1)
    half = LANES // 2
    own = own_signs.shape[0]
    plane = lax.broadcasted_iota(jnp.int32, pokes_ref.shape, 0)
    for bit in range(BITS):
        low = jnp.sum((pokes_ref[...] >> bit & 1) << plane, axis=0, keepdims=True)
        word = low | pltpu.roll(jnp.broadcast_to(low, (8, LANES)), half, 1)[:1] << planes
        words[bit] = column_of(word)[:half]
    count = codes_ref.shape[0] * LANES // (lax.axis_size("dir") * lax.axis_size("row"))
    first = (lax.axis_index("dir") * lax.axis_size("row") + lax.axis_index("row")) * count
    lane = lax.broadcasted_iota(jnp.int32, (8, LANES), 1)
    shift = first % LANES
    lines = [
        pltpu.roll(
            jnp.broadcast_to(
                codes_ref[pl.ds(jnp.minimum(first // LANES + n, codes_ref.shape[0] - 1), 1), :], (8, LANES)
            ),
            LANES - shift, 1,
        )
        for n in range(-(-own // LANES) + 1)
    ]
    own_column = jnp.concatenate(
        [column_of(jnp.where(lane < LANES - shift, lines[n], lines[n + 1])[:1]) for n in range(len(lines) - 1)],
        axis=0,
    )[:own]
    total = jnp.zeros((own, LANES), jnp.float32)
    for at in range(planes):
        signs = (1 - 2 * parity(own_column, pokes_ref[at:at + 1, :])).astype(jnp.float32)
        own_signs[:, at * LANES:(at + 1) * LANES] = signs.astype(NARROW)
        total = total + signs
    own_sums[...] = jnp.broadcast_to(jnp.sum(total, axis=1, keepdims=True), own_sums.shape)


def gram_kernel(
    row_shape, surface_rows, table_ref, pokes_ref, packed_ref, gram_out, first_ref, gram_ref, codes_ref, words,
    own_signs, own_sums, semaphores
):
    mirror = pl.program_id(0)
    half = LANES // 2
    own, pokes = own_signs.shape
    planes = pokes // LANES
    lines = codes_ref.shape[0] // row_shape[0]
    height = gram_ref.shape[0] // row_shape[0]

    @pl.when(mirror == 0)
    def _():
        own_side_of(table_ref, pokes_ref, codes_ref, words, own_signs, own_sums)

    def chunk(index, _):
        word = []
        for side in range(WINDOW // LANES):
            line = mirror * lines + index * (WINDOW // LANES) + side
            code = jnp.broadcast_to(codes_ref[pl.ds(line, 1), :], (8, LANES))
            value = None
            for bit in range(BITS):
                mask = jnp.concatenate([code << (31 - bit) >> 31] * (half // 8), axis=0)
                part = words[bit] & mask
                value = part if value is None else value ^ part
            word.append(value)
        word = jnp.concatenate(word, axis=1)
        bits = [None] * (2 * planes)
        for byte in range(0, 2 * planes, 8):
            part = (word >> byte).astype(jnp.int8)
            for bit in range(8):
                at = byte + bit
                hit = (part & np.uint8(1 << bit).astype(np.int8)) != 0
                bits[at % planes * 2 + at // planes] = jnp.where(hit, NARROW(1.0), NARROW(0.0))
        total = jnp.dot(own_signs[...], jnp.concatenate(bits, axis=0), preferred_element_type=jnp.float32)
        sums = jnp.concatenate([own_sums[...]] * (WINDOW // LANES), axis=1)
        turned = jnp.transpose((sums - 2.0 * total).astype(jnp.bfloat16))
        at = pl.multiple_of(mirror * height + index * WINDOW, WINDOW)
        gram_ref[pl.ds(at, WINDOW), :] = turned
        return 0

    lax.fori_loop(0, height // WINDOW, chunk, 0, unroll=3)

    def send(k):
        part = pl.ds(pl.multiple_of(k * height, height), height)
        return pltpu.make_async_copy(gram_ref.at[part], gram_out.at[part], semaphores.at[k])

    send(mirror).start()
    block = lax.axis_index("row")
    for l in range(row_shape[1]):
        for k in range(row_shape[0]):
            @pl.when(mirror == k)
            def _():
                first_ref[0, l] = band_product(
                    packed_ref, k * row_shape[1] + l, row_shape, block, surface_rows, gram_ref
                )

    @pl.when(mirror == pl.num_programs(0) - 1)
    def _():
        for k in range(row_shape[0]):
            send(k).wait()


def gram(table, pokes, packed, own, row_shape, surface_rows):
    own = -(-own // 32) * 32
    acts, count = table.size, pokes.size
    mirrors, shard_rows, slots, samples = row_shape
    vmem = pl.BlockSpec(memory_space=pltpu.VMEM)
    return pl.pallas_call(
        functools.partial(gram_kernel, row_shape, surface_rows),
        grid=(mirrors,),
        out_shape=[
            jax.ShapeDtypeStruct((acts, own), jnp.bfloat16),
            jax.ShapeDtypeStruct((1, mirrors * shard_rows, samples, own), jnp.bfloat16),
        ],
        in_specs=[vmem] * 3,
        out_specs=[
            pl.BlockSpec(memory_space=pl.ANY),
            pl.BlockSpec((1, shard_rows, samples, own), lambda s: (0, s, 0, 0)),
        ],
        scratch_shapes=[
            pltpu.VMEM((acts, own), jnp.bfloat16),
            pltpu.VMEM((acts // LANES, LANES), jnp.int32),
            pltpu.VMEM((BITS, LANES // 2, LANES), jnp.int32),
            pltpu.VMEM((own, count), NARROW),
            pltpu.VMEM((own, LANES), jnp.float32),
            pltpu.SemaphoreType.DMA((mirrors,)),
        ],
        compiler_params=pltpu.CompilerParams(vmem_limit_bytes=VMEM_BYTES),
        cost_estimate=pl.CostEstimate(
            flops=2 * own * acts * count, bytes_accessed=2 * own * acts, transcendentals=0
        ),
        name="gram_rows",
    )(table, pokes, packed)


def position(axis, staged):
    return lax.axis_index(axis) if staged else 0


def row_block(place, staged):
    if not staged:
        return place
    row = lax.axis_index("row")
    core = row & 1
    return row ^ [0, 2 << core, 4 >> core, 1, (4 >> core) | 1, (2 << core) | 1, 6, 7][place]


def row_place(block, staged):
    if not staged:
        return block
    row = lax.axis_index("row")
    core = row & 1
    distance = block ^ row
    near = jnp.where(distance == 2 << core, 1, 2)
    far = jnp.where(distance == (4 >> core) | 1, 4, 5)
    middle = jnp.where(distance & 1 == 0, near, far)
    return jnp.where((distance >= 2) & (distance < 6), middle, jnp.where(distance == 1, 3, distance))


def band_product(source, q, row_shape, block, surface_rows, gram_ref):
    mirrors, shard_rows, slots, samples = row_shape
    own = gram_ref.shape[1]
    narrow = slots - LANES
    k, l = divmod(q, shard_rows)
    band = jnp.clip((block * shard_rows + l) * NAR // surface_rows - 1, 0, NAR - BAND)
    column = pl.multiple_of((k * NAR + band) * NA, 16)
    wide = mirrors * shard_rows * samples
    products = []
    for start, length, row, lane in narrow_places(q, slots, samples):
        left = jnp.concatenate(
            [source[pl.ds(q * samples + start, length), :], source[pl.ds(wide + row, length), :]], axis=1
        )
        right = [gram_ref[pl.ds(column, LANES), :]]
        if lane:
            right.append(jnp.zeros((lane, own), jnp.bfloat16))
        right.append(gram_ref[pl.ds(column + LANES, narrow), :])
        if lane + narrow < LANES:
            right.append(jnp.zeros((LANES - lane - narrow, own), jnp.bfloat16))
        products.append(
            jnp.dot(left, jnp.concatenate(right, axis=0), preferred_element_type=jnp.float32).astype(jnp.bfloat16)
        )
    return jnp.concatenate(products, axis=0)


def fetch_gram(gram_any, gram_ref, semaphores, mirrors):
    height = gram_ref.shape[0] // mirrors
    return [
        pltpu.make_async_copy(
            gram_any.at[pl.ds(k * height, height)], gram_ref.at[pl.ds(k * height, height)], semaphores.at[k]
        )
        for k in range(mirrors)
    ]


def bands_kernel(row_shape, surface_rows, first, counts, staged, gram_any, *refs):
    mirrors, shard_rows, slots, samples = row_shape
    sources = [ref.at[n] for ref, count in zip(refs, counts) for n in range(count)]
    refs = refs[len(counts):]
    *refs, gram_ref, blocks, gram_semaphores, block_semaphores = refs
    out_ref, = refs
    step = pl.program_id(0)
    gram_copies = fetch_gram(gram_any, gram_ref, gram_semaphores, mirrors)

    def fetch(n):
        return pltpu.make_async_copy(sources[n], blocks.at[n], block_semaphores.at[n])

    @pl.when(step == 0)
    def _():
        fetch(0).start()
        for copy in gram_copies:
            copy.start()
        for n in range(1, len(sources)):
            fetch(n).start()

    for n in range(len(sources)):
        @pl.when(step == n)
        def _():
            fetch(n).wait()
            block = row_block(first + n, staged)
            for q in range(mirrors * shard_rows):
                if n == 0 and q % shard_rows == 0:
                    gram_copies[q // shard_rows].wait()
                out_ref[0, q] = band_product(blocks.at[n], q, row_shape, block, surface_rows, gram_ref)


def bands(gram_rows, sources, first, staged, row_shape, surface_rows):
    acts, own = gram_rows.shape
    mirrors, shard_rows, slots, samples = row_shape
    counts = [source.shape[0] for source in sources]
    rows = mirrors * shard_rows
    flops = 2 * own * WINDOW * samples * rows * sum(counts)
    vmem, anywhere = pl.BlockSpec(memory_space=pltpu.VMEM), pl.BlockSpec(memory_space=pl.ANY)
    out_shape = [jax.ShapeDtypeStruct((sum(counts), rows, samples, own), jnp.bfloat16)]
    out_specs = [pl.BlockSpec((1, rows, samples, own), lambda s: (s, 0, 0, 0))]
    arguments, in_specs = [gram_rows, *sources], [anywhere] * (1 + len(sources))
    return pl.pallas_call(
        functools.partial(bands_kernel, row_shape, surface_rows, first, counts, staged),
        grid=(sum(counts),),
        out_shape=out_shape,
        in_specs=in_specs,
        out_specs=out_specs,
        scratch_shapes=[
            pltpu.VMEM((acts, own), jnp.bfloat16),
            pltpu.VMEM((sum(counts),) + sources[0].shape[1:], jnp.bfloat16),
            pltpu.SemaphoreType.DMA((mirrors,)),
            pltpu.SemaphoreType.DMA((sum(counts),)),
        ],
        compiler_params=pltpu.CompilerParams(vmem_limit_bytes=VMEM_BYTES),
        cost_estimate=pl.CostEstimate(
            flops=flops, bytes_accessed=2 * own * WINDOW * rows * sum(counts), transcendentals=0
        ),
        name="bands",
    )(*arguments)


def build_differences(columns, whole_ref, rest_ref, mirrors, samples):
    half = whole_ref.shape[2]
    pupil, depth = 2 * half, whole_ref.shape[3]
    remainder = mirrors * samples - depth
    pick = lax.broadcasted_iota(jnp.int32, (pupil, pupil), 0)
    lane = lax.broadcasted_iota(jnp.int32, (pupil, pupil), 1)
    pick = (lane == pick % half * 2 + pick // half).astype(jnp.float32).astype(jnp.bfloat16)
    lines = jnp.concatenate([ref[:, :pupil] for ref in columns], axis=0)
    height = columns[0].shape[0]
    turned = lax.dot_general(
        pick, lines.astype(jnp.float32).astype(jnp.bfloat16), (((1,), (1,)), ((), ())),
        preferred_element_type=jnp.float32,
    ).astype(jnp.int32)
    at = lax.broadcasted_iota(jnp.int32, (half, mirrors * samples), 1)
    for d in range(len(columns)):
        sides = []
        for side in range(2):
            wanted = None
            for k in range(mirrors):
                column = turned[side * half:(side + 1) * half, d * height + k:d * height + k + 1] + k * samples
                wanted = column if wanted is None else jnp.where(at < k * samples, wanted, column)
            sides.append((at == wanted).astype(jnp.float32))
        across, down = sides[1] - sides[0], sides[1] + sides[0]
        whole_ref[d, 0] = across[:, :depth].astype(jnp.bfloat16)
        whole_ref[d, 1] = down[:, :depth].astype(jnp.bfloat16)
        blank = jnp.zeros((half, remainder), jnp.float32)
        upper = jnp.concatenate([across[:, depth:], blank], axis=1)
        lower = jnp.concatenate([blank, down[:, depth:]], axis=1)
        rest_ref[d] = jnp.concatenate([upper, lower], axis=0).astype(jnp.bfloat16)


def decode_kernel(row_shape, surface_rows, own, staged, norm, counts, late, places, *refs):
    mirrors, shard_rows, slots, samples = row_shape
    columns_refs, refs = refs[:counts[3]], refs[counts[3]:]
    lines_refs, refs = refs[:counts[0]], refs[counts[0]:]
    late_refs, refs = refs[:counts[1]], refs[counts[1]:]
    ready_refs, refs = refs[:counts[2]], refs[counts[2]:]
    (gram_any, out_ref, gram_ref, decoded, whole_ref, rest_ref, total, lines, foot_rows, scalars, *refs) = refs
    late_blocks, refs = refs[:counts[1]], refs[counts[1]:]
    held_columns, refs = refs[:counts[3]], refs[counts[3]:]
    held_lines, refs = refs[:counts[0]], refs[counts[0]:]
    gram_semaphores, ready_semaphores, late_semaphores, scalar_semaphore, line_semaphores = refs
    group = pl.program_id(0)
    directions, pupil = whole_ref.shape[0], 2 * whole_ref.shape[2]
    depth = whole_ref.shape[3]
    phases = out_ref.shape[2] // pupil
    blocks = surface_rows // shard_rows
    ready = blocks - late
    count = shard_rows // 2
    rows = mirrors * shard_rows
    foot_line = mirrors + count

    @pl.when(group == 0)
    def _():
        def started(copies):
            for copy in copies:
                copy.start()
            return copies

        line_copies = started([
            pltpu.make_async_copy(source, target, line_semaphores.at[n])
            for n, (source, target) in enumerate(zip([*columns_refs, *lines_refs], [*held_columns, *held_lines]))
        ])
        late_copies = started([
            pltpu.make_async_copy(late_refs[n], late_blocks[n], late_semaphores.at[n]) for n in range(counts[1])
        ])
        gram_copies = started(fetch_gram(gram_any, gram_ref, gram_semaphores, mirrors)) if late else []
        ready_copies = started([
            pltpu.make_async_copy(block, decoded.at[pl.ds(n * rows, rows)], ready_semaphores.at[n])
            for n, block in enumerate([ref.at[m] for ref in ready_refs for m in range(ref.shape[0])])
        ])
        for copy in line_copies:
            copy.wait()
        held = [ref.at[n] for ref in held_lines for n in range(ref.shape[0])]
        feet = [None] * blocks
        for place, ref in zip(places, held):
            for d in range(directions):
                lines[place, d * count:(d + 1) * count] = ref[d, mirrors:foot_line, :LANES]
            pieces = [ref[d, foot_line:foot_line + 1, :rows] for d in range(directions)]
            pieces.append(jnp.zeros((1, LANES - rows * directions), jnp.int32))
            feet[place] = jnp.concatenate(pieces, axis=1)
        feet = jnp.concatenate(feet, axis=0)
        foot_rows[...] = row_place(feet // shard_rows, staged) * rows + feet % shard_rows
        to_scalars = pltpu.make_async_copy(foot_rows, scalars, scalar_semaphore.at[0])
        to_scalars.start()
        columns = [ref.at[n] for ref in held_columns for n in range(ref.shape[0])]
        build_differences(columns, whole_ref, rest_ref, mirrors, samples)
        for copy in late_copies:
            copy.wait()
        for n in range(late):
            source = late_blocks[n]
            for q in range(mirrors * shard_rows):
                if n == 0 and q % shard_rows == 0:
                    gram_copies[q // shard_rows].wait()
                decoded[(ready + n) * rows + q] = band_product(
                    source, q, row_shape, row_block(ready + n, staged), surface_rows, gram_ref
                )
        to_scalars.wait()
        for copy in ready_copies:
            copy.wait()

    for d in range(directions):
        held = d ^ position("dir", staged)
        products, factors = [], []
        for phase in range(phases):
            i = group * phases + phase
            block = row_place(2 * i // shard_rows, staged)
            sums, changes = [], []
            for k in range(mirrors):
                picked = []
                for y in range(2):
                    row = k * shard_rows + (2 * phase + y) % shard_rows
                    picked.append(decoded[scalars[block, held * rows + row] + k * shard_rows])
                sums.append(picked[0] + picked[1])
                changes.append(picked[1] - picked[0])
            right = [jnp.concatenate(part, axis=0) for part in (sums, changes)]
            mixed = jnp.concatenate([part[depth:] for part in right], axis=0)
            rest = jnp.dot(rest_ref[held], mixed, preferred_element_type=jnp.float32)
            for kind, part in enumerate(right):
                whole = jnp.dot(whole_ref[held, kind], part[:depth], preferred_element_type=jnp.float32)
                products.append(whole + rest[kind * pupil // 2:(kind + 1) * pupil // 2])
            valid = lines[block, pl.ds(held * count + phase % count, 1), :][:, :pupil // 2]
            factors += [valid.astype(jnp.float32)] * 2
        product = jnp.concatenate(products, axis=0)
        factor = jnp.concatenate(factors, axis=1)
        for tile in range(out_ref.shape[2] // LANES):
            at = tile * LANES
            value = jnp.transpose((product[at:at + LANES] * norm).astype(jnp.bfloat16))
            value = value.astype(jnp.float32)[:own] * factor[:, at:at + LANES]
            total[tile, pl.ds(d, own, stride=directions), :] = value
    for tile in range(out_ref.shape[2] // LANES):
        value = total[tile].reshape(own, directions, LANES)
        out_ref[:, :, tile * LANES:(tile + 1) * LANES] = value.astype(out_ref.dtype)


def decode(columns, lines, places, late, ready, gram_rows, own, row_shape, surface_rows, pupil, norm, staged):
    mirrors, shard_rows, slots, samples = row_shape
    acts, padded = gram_rows.shape
    directions = sum(line.shape[0] for line in columns)
    depth = mirrors * samples // WINDOW * WINDOW
    blocks = surface_rows // shard_rows
    phases = LANES // math.gcd(pupil, LANES)
    width = surface_rows // 2 * pupil
    lanes = phases * pupil
    flops = 2 * padded * mirrors * samples * pupil * directions * surface_rows // 2
    vmem, anywhere = pl.BlockSpec(memory_space=pltpu.VMEM), pl.BlockSpec(memory_space=pl.ANY)
    counts = (len(lines), len(late), len(ready), len(columns))
    semaphores = [mirrors, blocks, max(len(late), 1), 1, len(columns) + len(lines)]
    held = -(-directions * (shard_rows // 2) // 8) * 8
    return pl.pallas_call(
        functools.partial(
            decode_kernel, row_shape, surface_rows, own, staged, norm, counts, len(late), places
        ),
        grid=(width // lanes,),
        out_shape=jax.ShapeDtypeStruct((own, directions, width), jnp.bfloat16),
        in_specs=[anywhere] * (len(columns) + len(lines) + len(late) + len(ready) + 1),
        out_specs=pl.BlockSpec((own, directions, lanes), lambda s: (0, 0, s)),
        scratch_shapes=[
            pltpu.VMEM((acts, padded), jnp.bfloat16),
            pltpu.VMEM((blocks * mirrors * shard_rows, samples, padded), jnp.bfloat16),
            pltpu.VMEM((directions, 2, pupil // 2, depth), jnp.bfloat16),
            pltpu.VMEM((directions, pupil, 2 * (mirrors * samples - depth)), jnp.bfloat16),
            pltpu.VMEM((lanes // LANES, own * directions, LANES), jnp.float32),
            pltpu.VMEM((blocks, held, LANES), jnp.int32),
            pltpu.VMEM((blocks, LANES), jnp.int32),
            pltpu.SMEM((blocks, LANES), jnp.int32),
            *[pltpu.VMEM(block.shape, block.dtype) for block in [*late, *columns, *lines]],
            *[pltpu.SemaphoreType.DMA((count,)) for count in semaphores],
        ],
        compiler_params=pltpu.CompilerParams(vmem_limit_bytes=VMEM_BYTES),
        cost_estimate=pl.CostEstimate(flops=flops, bytes_accessed=2 * own * directions * width, transcendentals=0),
        name="decode",
    )(*columns, *lines, *late, *ready, gram_rows)


def swap(block, axis, distance):
    return lax.ppermute(block, axis, [(i, i ^ distance) for i in range(lax.axis_size(axis))])


def turn(block, even, odd):
    return lax.ppermute(
        block, "row", [(i, i ^ (odd if i % 2 else even)) for i in range(lax.axis_size("row"))]
    )


def shards(influence, foot_rows, foot_columns, actuator_codes, poke_rows, subaperture_valid):
    mirrors, shard_rows, samples, slots = influence.shape
    row_shape = (mirrors, shard_rows, slots, samples)
    directions, devices = lax.axis_size("dir"), lax.axis_size("row")
    surface_rows = shard_rows * devices
    pupil = foot_columns.shape[2]
    norm = 0.5 * poke_rows.shape[0] ** (-0.5)
    own = actuator_codes.size // (directions * devices)
    staged = devices == 8 and directions > 1 and directions & (directions - 1) == 0
    turned = jnp.swapaxes(influence, 2, 3)
    pokes = poke_rows.reshape(-1, LANES)
    packed, lines = pack(turned, foot_rows, foot_columns, subaperture_valid)
    if not staged:
        every = lax.all_gather(packed, "row")
        lines = lax.all_gather(lax.all_gather(lines, "dir"), "row")
        gram_rows, _ = gram(actuator_codes, pokes, packed, own, row_shape, surface_rows)
        ready, = bands(gram_rows, [every], 0, staged, row_shape, surface_rows)
        return decode(
            [lines[0]], [lines], list(range(devices)), [], [ready], gram_rows, own, row_shape, surface_rows, pupil,
            norm, staged,
        )

    first, second = turn(packed, 2, 4), turn(packed, 4, 2)
    sibling = swap(packed, "row", 1)
    lines, distance = [jnp.stack([lines, swap(lines, "dir", 1)])], 2
    lines[0], pokes = lax.optimization_barrier((lines[0], pokes))
    while distance < directions:
        lines.append(swap(jnp.concatenate(lines, axis=0), "dir", distance))
        distance *= 2
    held = jnp.concatenate(lines, axis=0)[None, :, :, :LANES]
    gram_rows, own_rows = gram(actuator_codes, pokes, packed, own, row_shape, surface_rows)
    gram_rows, first, second, held, sibling = lax.optimization_barrier(
        (gram_rows, first, second, held, sibling)
    )
    diagonal = turn(first, 4, 2)
    first_sibling = swap(first, "row", 1)
    mine = [held, turn(held, 2, 4), turn(held, 4, 2), swap(held, "row", 6)]
    second_sibling = swap(second, "row", 1)
    mine = jnp.concatenate(mine, axis=0)
    diagonal, mine = lax.optimization_barrier((diagonal, mine))
    theirs = swap(mine, "row", 1)
    late = [first, second, sibling, first_sibling, second_sibling, diagonal, swap(diagonal, "row", 1)]
    return decode(
        lines, [mine, theirs], [0, 1, 2, 6, 3, 4, 5, 7], late, [own_rows], gram_rows, own, row_shape,
        surface_rows, pupil, norm, staged,
    )


def solution(mesh):
    return jax.shard_map(
        shards,
        mesh=mesh,
        in_specs=(
            P(None, "row", None, None),
            P("dir", None, "row"),
            P("dir", None, None),
            P(),
            P(),
            P("dir", "row", None),
        ),
        out_specs=P(("dir", "row"), None, None),
        check_vma=False,
    )
```
